32 devices in a mesh: dp: 4 (over z), ctx: 2 (over y), exp: 4 (over x, core).
Axes of the slice: x: 2, y: 2, z: 4, core: 2. Of those that a mesh axis runs over, the one named last changes fastest.
Arguments:
- inputs: float32 [4096, 768], P(('dp', 'ctx', 'exp')), may hold values from -6 to 6
- w_query: bfloat16 [2, 768, 768], replicated, may hold values from -0.078125 to 0.078125
- w_key: bfloat16 [2, 768, 768], replicated, may hold values from -0.078125 to 0.078125
- w_value: bfloat16 [2, 768, 768], replicated, may hold values from -0.21875 to 0.21875
- w_out: bfloat16 [2, 768, 768], replicated, may hold values from -1.75 to 1.75
- norm_gain: float32 [4, 768], replicated, may hold values from 0.5 to 1.5
- bias_table: float32 [32, 12], replicated, may hold values from -9 to 9
- dense_in: bfloat16 [768, 3072], replicated, may hold values from -0.21875 to 0.21875
- dense_out: bfloat16 [3072, 768], replicated, may hold values from -0.109375 to 0.109375
- expert_in: bfloat16 [16, 768, 3072], P(('ctx', 'exp')), may hold values from -0.21875 to 0.21875
- expert_out: bfloat16 [16, 3072, 768], P(('ctx', 'exp')), may hold values from -0.21875 to 0.21875
- routes: int32 [4096, 1], P(('dp', 'ctx', 'exp')), may hold values from 0 to 15; in each aligned block of 128 rows (0 to 127, 128 to 255, ...) at most 16 rows name the same one
- gate_scale: float32 [4096, 1], P(('dp', 'ctx', 'exp')), may hold values from 0.45 to 1
- buckets: int32 [2048], replicated, may hold values from 0 to 31, as said below
- cotangent: float32 [4096, 768], P(('dp', 'ctx', 'exp')), may hold values from -6 to 6
Outputs:
- outputs: float32 [4096, 768], P(('dp', 'ctx', 'exp'))
- input_grad: float32 [4096, 768], P(('dp', 'ctx', 'exp'))
- w_query_grad: float32 [2, 768, 768], P(None, None, ('dp', 'ctx', 'exp'))
- w_key_grad: float32 [2, 768, 768], P(None, None, ('dp', 'ctx', 'exp'))
- w_value_grad: float32 [2, 768, 768], P(None, None, ('dp', 'ctx', 'exp'))
- w_out_grad: float32 [2, 768, 768], P(None, None, ('dp', 'ctx', 'exp'))
- norm_gain_grad: float32 [4, 768], P(None, ('dp', 'ctx', 'exp'))
- bias_table_grad: float32 [384], P(('dp', 'ctx', 'exp'))
- dense_in_grad: float32 [768, 3072], P(None, ('dp', 'ctx', 'exp'))
- dense_out_grad: float32 [3072, 768], P(('dp', 'ctx', 'exp'))
- expert_in_grad: float32 [16, 768, 3072], P(('ctx', 'exp'), None, 'dp')
- expert_out_grad: float32 [16, 3072, 768], P(('ctx', 'exp'), 'dp')
The draws below stay inside these ranges and needn't reach their ends.
Inputs may be any that keep to these rules, and one draw needn't show every extreme that they name: `routes`: at most 16 of the 128 tokens of one device go to one expert. Entry r is the bucket of the distance r - 1024 from a query to a key; distances of zero or less use buckets below 16, and on each side a bucket never falls as the distance moves away from zero.
All inputs are finite; a program needn't handle non-finite values.
Results may differ from the reference program's by a relative error of at most 0.035.
Values may be sent and summed in bfloat16 or wider, within the bound.
A program may use at most 832 MiB of HBM per device.

```python
import math
import jax
import jax.numpy as jnp
import numpy as np
from jax import lax

D = 768
HEADS = 12
HEAD = 64
FF = 3072
NB = 32
LAYERS = 2
GROUP = 128
EXPERTS = 16
LENGTH = 1024
TOKENS = 4096
CAP = 16
N_DP = 4


def draw_bias_table(key, part):
    table_values = jax.random.normal(jax.random.fold_in(key, 11), (NB, HEADS), jnp.float32)
    result_table = 1.5 * jnp.clip(table_values, -6.0, 6.0)
    return result_table


def side_boundaries(key, salt_value):
    half_count = NB // 2
    chosen = jax.random.permutation(jax.random.fold_in(key, salt_value), LENGTH - GROUP - 1)[:half_count - 2] + 1
    return jnp.concatenate([chosen.astype(jnp.int32), jnp.full((1,), LENGTH - GROUP, jnp.int32)])


def draw_buckets(key, part):
    half_count = NB // 2
    distance = jnp.arange(2 * LENGTH, dtype=jnp.int32) - LENGTH
    magnitude = jnp.abs(distance)
    lower_side = jnp.sum((magnitude[:, None] >= side_boundaries(key, 21)[None, :]).astype(jnp.int32), axis=1)
    upper_side = jnp.sum((magnitude[:, None] >= side_boundaries(key, 22)[None, :]).astype(jnp.int32), axis=1)
    return jnp.where(distance > 0, half_count + upper_side, lower_side).astype(jnp.int32)


def block_levels(own_key, extent, pieces, least, largest):
    factor_of = 1.0
    for dim, parts in pieces:
        heights = jax.random.uniform(jax.random.fold_in(jax.random.fold_in(own_key, 6), dim), (parts,), jnp.float32, least / len(pieces), largest / len(pieces))
        factor_of = factor_of * jnp.repeat(jnp.exp(heights), extent[dim] // parts).reshape((-1,) + (1,) * (len(extent) - 1 - dim))
    return factor_of


def routed_block(stream_key, own, number, rows, amount, top, most, slope):
    order = jax.random.permutation(stream_key, amount)
    packed, common = portions_of(amount, rows * top, most, slope, True), portions_of(amount, rows * top, most, slope, False)
    places = jnp.arange(amount)

    def named(lengths, offset_by):
        used = int((lengths > 0).sum())
        fixed = max(1, used // 4)
        moved = fixed + (places - fixed + offset_by * (used - fixed)) % max(1, amount - fixed)
        return jnp.zeros((amount,), jnp.int32).at[order[jnp.where(places < fixed, places, moved)]].set(jnp.asarray(lengths, jnp.int32))

    lengths = jnp.where(number % 4 == 0, named(packed, number // 4), named(common, number - number // 4 - 1))
    mixed = jax.random.permutation(jax.random.fold_in(own, 3), amount)
    giver, sink = mixed[0:amount // 2 * 2:2], mixed[1:amount // 2 * 2:2]
    slack = jnp.minimum(lengths[giver] - 1, most - lengths[sink]) // 2
    slack = jnp.where((giver == order[0]) | (sink == order[0]) | (lengths[sink] == 0), 0, jnp.maximum(slack, 0))
    moved = jax.random.randint(jax.random.fold_in(own, 4), (amount // 2,), 0, 1 << 20) % (slack + 1)
    lengths = lengths.at[giver].add(-moved).at[sink].add(moved)
    members = jnp.searchsorted(jnp.cumsum(lengths), jnp.arange(rows * top), side="right").astype(jnp.int32)
    listing = members.reshape(top, rows).T
    listing = listing[jax.random.permutation(jax.random.fold_in(own, 1), rows)]
    offset_by = jax.random.randint(jax.random.fold_in(own, 2), (rows, 1), 0, top)
    return jnp.take_along_axis(listing, (jnp.arange(top)[None, :] + offset_by) % top, axis=1)


def portions_of(number_of, total, most, lean, full):
    loads = [(1 << 20) // math.isqrt(standing ** lean) + 1 for standing in range(1, number_of + 1)]
    largest = most if full else min(most, max(-(-total // number_of), total * loads[0] // sum(loads)))
    least = 1 if total - largest >= number_of - 1 else 0
    counts, spare = [largest] + [least] * (number_of - 1), total - largest - least * (number_of - 1)
    while spare > 0:
        candidates = [i for i in range(1, number_of) if counts[i] < largest] or [i for i in range(1, number_of) if counts[i] < most]
        whole, remaining = sum([loads[i] for i in candidates]), spare
        for i in candidates:
            addition = min(most - counts[i], max(1, remaining * loads[i] // whole), spare)
            counts[i] = counts[i] + addition
            spare = spare - addition
    return np.array(counts)


def scatter_about(own_key, extent, scale, limit, cuts=(), kind=jnp.bfloat16):
    values = jax.random.normal(own_key, extent, jnp.float32) * scale
    if len(cuts) > 0:
        values = block_levels(own_key, extent, cuts, -0.22, 0.18) * values
    return jnp.clip(values, min=-limit, max=limit).astype(kind)


def setup_inputs(seed: int = 0) -> dict:
    keys = jax.random.split(jax.random.key(seed), 16)
    inputs = scatter_about(keys[0], (TOKENS, D), 1.0, 6.0, ((0, 32),), jnp.float32)
    w_query = scatter_about(keys[1], (LAYERS, D, D), (8 * D) ** -0.5, 0.078125)
    w_key = scatter_about(keys[2], (LAYERS, D, D), (8 * D) ** -0.5, 0.078125)
    w_value = scatter_about(keys[3], (LAYERS, D, D), D ** -0.5, 0.21875)
    w_out = scatter_about(keys[4], (LAYERS, D, D), (D // 64) ** -0.5, 1.75)
    norm_gain = jnp.clip(1.0 + 0.1 * jax.random.normal(keys[5], (2 * LAYERS, D), jnp.float32), 0.5, 1.5)
    bias_table = draw_bias_table(jax.random.fold_in(keys[15], 71), 0)
    dense_in = scatter_about(keys[7], (D, FF), D ** -0.5, 0.21875)
    dense_out = scatter_about(keys[8], (FF, D), FF ** -0.5, 0.109375)
    expert_in = scatter_about(keys[9], (EXPERTS, D, FF), D ** -0.5, 0.21875, ((0, 8),))
    expert_out = scatter_about(keys[10], (EXPERTS, FF, D), (FF // 4) ** -0.5, 0.21875, ((0, 8),))
    routes_keys = jax.random.split(jax.random.fold_in(keys[11], 1), TOKENS // GROUP)
    routes_turns = jax.random.permutation(jax.random.fold_in(keys[11], 3), TOKENS // GROUP)
    routes = jax.vmap(lambda own, number: routed_block(jax.random.fold_in(keys[11], 2), own, number, GROUP, EXPERTS, 1, CAP, 2))(routes_keys, routes_turns).reshape((TOKENS, 1))
    gate_scale = jnp.clip(0.45 + 0.55 * jax.random.uniform(keys[12], (TOKENS, 1), jnp.float32) ** block_levels(keys[12], (TOKENS, 1), ((0, 32),), -0.2, 0.2), 0.45, 1.0)
    buckets = draw_buckets(jax.random.fold_in(keys[15], 71), 0)
    cotangent = scatter_about(keys[14], (TOKENS, D), 1.0, 6.0, ((0, 32),), jnp.float32)
    return dict(inputs=inputs, w_query=w_query, w_key=w_key, w_value=w_value, w_out=w_out, norm_gain=norm_gain, bias_table=bias_table, dense_in=dense_in, dense_out=dense_out, expert_in=expert_in, expert_out=expert_out, routes=routes, gate_scale=gate_scale, buckets=buckets, cotangent=cotangent)


epsilon = 1e-06
highest = lax.Precision.HIGHEST

def to_half(values):
    return values.astype(jnp.bfloat16)

def widen(values):
    return values.astype(jnp.float32)

def smooth_act(values):
    return values * jax.nn.sigmoid(values)

def smooth_slope(values):
    sigma = jax.nn.sigmoid(values)
    return sigma * (1.0 + values * (1.0 - sigma))

def rms_forward(hidden, gains):
    inv_rms = lax.rsqrt(lax.optimization_barrier(jnp.mean(hidden * hidden, axis=-1, keepdims=True)) + epsilon)
    return (hidden * inv_rms * gains, inv_rms)

def rms_backward(hidden, inv_rms, gains, d_normed):
    d_scaled = d_normed * gains
    d_gains = lax.optimization_barrier(jnp.sum(d_normed * hidden * inv_rms, axis=0))
    d_hidden = inv_rms * d_scaled - hidden * inv_rms ** 3 * lax.optimization_barrier(jnp.mean(d_scaled * hidden, axis=-1, keepdims=True))
    return (d_hidden, d_gains)

def bucket_matrix(buckets):
    return (buckets[None, :] == jnp.arange(NB, dtype=jnp.int32)[:, None]).astype(jnp.float32)

def block_offsets(row_first, block_rows):
    return jnp.arange(LENGTH, dtype=jnp.int32)[None, :] - (row_first + jnp.arange(block_rows, dtype=jnp.int32))[:, None] + LENGTH

def sequence_forward(query_heads, key_heads, value_heads, bias_rows, block_rows):
    block_count = LENGTH // block_rows

    def one_block(block_index):
        row_first = block_index * block_rows
        query_block = lax.dynamic_slice_in_dim(query_heads, row_first, block_rows, 0)
        offsets = block_offsets(row_first, block_rows)
        scores = jnp.einsum('qhd,khd->hqk', query_block, key_heads, precision=highest) + bias_rows[:, offsets]
        top_score = lax.optimization_barrier(jnp.max(scores, axis=-1, keepdims=True))
        log_norm = top_score[:, :, 0] + jnp.log(lax.optimization_barrier(jnp.sum(jnp.exp(scores - top_score), axis=-1)))
        weights = jnp.exp(scores - log_norm[:, :, None])
        weights_half = widen(lax.optimization_barrier(to_half(weights)))
        attended = jnp.einsum('hqk,khd->qhd', weights_half, value_heads, precision=highest)
        return (to_half(attended), log_norm)
    attended, log_norm = lax.map(one_block, jnp.arange(block_count, dtype=jnp.int32))
    return (attended.reshape(LENGTH, HEADS * HEAD), jnp.transpose(log_norm, (1, 0, 2)).reshape(HEADS, LENGTH))

def sequence_backward(query_heads, key_heads, value_heads, grad_heads, log_norm, row_delta, bias_rows, block_rows):
    block_count = LENGTH // block_rows

    def one_block(running, block_index):
        d_keys, d_values, d_bias = running
        row_first = block_index * block_rows
        query_block = lax.dynamic_slice_in_dim(query_heads, row_first, block_rows, 0)
        grad_block = lax.dynamic_slice_in_dim(grad_heads, row_first, block_rows, 0)
        norm_block = lax.dynamic_slice_in_dim(log_norm, row_first, block_rows, 1)
        delta_block = lax.dynamic_slice_in_dim(row_delta, row_first, block_rows, 1)
        offsets = block_offsets(row_first, block_rows)
        scores = jnp.einsum('qhd,khd->hqk', query_block, key_heads, precision=highest) + bias_rows[:, offsets]
        weights = jnp.exp(scores - norm_block[:, :, None])
        d_weights = jnp.einsum('qhd,khd->hqk', grad_block, value_heads, precision=highest)
        d_scores = weights * (d_weights - delta_block[:, :, None])
        scores_half = widen(lax.optimization_barrier(to_half(d_scores)))
        weights_half = widen(lax.optimization_barrier(to_half(weights)))
        d_query = jnp.einsum('hqk,khd->qhd', scores_half, key_heads, precision=highest)
        d_keys = d_keys + jnp.einsum('hqk,qhd->khd', scores_half, query_block, precision=highest)
        d_values = d_values + jnp.einsum('hqk,qhd->khd', weights_half, grad_block, precision=highest)
        d_bias = d_bias.at[:, offsets].add(d_scores)
        return ((d_keys, d_values, d_bias), d_query)
    initial = (jnp.zeros_like(key_heads), jnp.zeros_like(value_heads), jnp.zeros(bias_rows.shape, jnp.float32))
    (d_keys, d_values, d_bias), d_query = lax.scan(one_block, initial, jnp.arange(block_count, dtype=jnp.int32))
    return (d_query.reshape(LENGTH, HEADS * HEAD), d_keys.reshape(LENGTH, HEADS * HEAD), d_values.reshape(LENGTH, HEADS * HEAD), d_bias)

def heads_of(values):
    return widen(values).reshape(values.shape[0], HEADS, HEAD)

def attention_forward(hidden, gains, weight_query, weight_key, weight_value, weight_out, bias_rows, block_rows):
    normed, inv_rms = rms_forward(hidden, gains)
    normed_half = to_half(normed)
    queries = to_half(jnp.dot(normed_half, weight_query, preferred_element_type=jnp.float32))
    keys_all = to_half(jnp.dot(normed_half, weight_key, preferred_element_type=jnp.float32))
    values_all = to_half(jnp.dot(normed_half, weight_value, preferred_element_type=jnp.float32))
    attended_parts = []
    norm_parts = []
    for sequence in range(N_DP):
        seq_first = sequence * LENGTH
        attended_seq, norm_seq = sequence_forward(heads_of(queries[seq_first:seq_first + LENGTH]), heads_of(keys_all[seq_first:seq_first + LENGTH]), heads_of(values_all[seq_first:seq_first + LENGTH]), bias_rows, block_rows)
        attended_parts.append(attended_seq)
        norm_parts.append(norm_seq)
    attended = jnp.concatenate(attended_parts, axis=0)
    output = hidden + jnp.dot(attended, weight_out, preferred_element_type=jnp.float32)
    return (output, (hidden, normed_half, inv_rms, queries, keys_all, values_all, attended, norm_parts))

def attention_backward(layer_cache, grad_out, gains, weight_query, weight_key, weight_value, weight_out, bias_rows, block_rows):
    hidden, normed_half, inv_rms, queries, keys_all, values_all, attended, norm_parts = layer_cache
    grad_half = to_half(grad_out)
    grad_wout = jnp.dot(attended.T, grad_half, preferred_element_type=jnp.float32)
    d_attended = to_half(jnp.dot(grad_half, weight_out.T, preferred_element_type=jnp.float32))
    row_delta = lax.optimization_barrier(jnp.sum(heads_of(d_attended) * heads_of(attended), axis=-1))
    query_parts = []
    key_parts = []
    value_parts = []
    d_bias = jnp.zeros(bias_rows.shape, jnp.float32)
    for sequence in range(N_DP):
        seq_first = sequence * LENGTH
        pick_rows = slice(seq_first, seq_first + LENGTH)
        d_query, d_keys, d_values, d_bias_seq = sequence_backward(heads_of(queries[pick_rows]), heads_of(keys_all[pick_rows]), heads_of(values_all[pick_rows]), heads_of(d_attended[pick_rows]), norm_parts[sequence], row_delta[pick_rows].T, bias_rows, block_rows)
        query_parts.append(d_query)
        key_parts.append(d_keys)
        value_parts.append(d_values)
        d_bias = d_bias + d_bias_seq
    dq_half = to_half(jnp.concatenate(query_parts, axis=0))
    dk_half = to_half(jnp.concatenate(key_parts, axis=0))
    dv_half = to_half(jnp.concatenate(value_parts, axis=0))
    grad_wq = jnp.dot(normed_half.T, dq_half, preferred_element_type=jnp.float32)
    grad_wk = jnp.dot(normed_half.T, dk_half, preferred_element_type=jnp.float32)
    grad_wv = jnp.dot(normed_half.T, dv_half, preferred_element_type=jnp.float32)
    d_normed = jnp.dot(dq_half, weight_query.T, preferred_element_type=jnp.float32) + jnp.dot(dk_half, weight_key.T, preferred_element_type=jnp.float32) + jnp.dot(dv_half, weight_value.T, preferred_element_type=jnp.float32)
    d_hidden, d_gains = rms_backward(hidden, inv_rms, gains, d_normed)
    return (grad_out + d_hidden, d_gains, grad_wq, grad_wk, grad_wv, grad_wout, d_bias)

def dense_forward(hidden, gains, dense_in, dense_out):
    normed, inv_rms = rms_forward(hidden, gains)
    normed_half = to_half(normed)
    pre_act = jnp.dot(normed_half, dense_in, preferred_element_type=jnp.float32)
    active = to_half(smooth_act(pre_act))
    output = hidden + jnp.dot(active, dense_out, preferred_element_type=jnp.float32)
    return (output, (hidden, normed_half, inv_rms, pre_act, active))

def dense_backward(layer_cache, grad_out, gains, dense_in, dense_out):
    hidden, normed_half, inv_rms, pre_act, active = layer_cache
    grad_half = to_half(grad_out)
    grad_dout = jnp.dot(active.T, grad_half, preferred_element_type=jnp.float32)
    d_active = jnp.dot(grad_half, dense_out.T, preferred_element_type=jnp.float32)
    d_pre = to_half(d_active * smooth_slope(pre_act))
    grad_din = jnp.dot(normed_half.T, d_pre, preferred_element_type=jnp.float32)
    d_normed = jnp.dot(d_pre, dense_in.T, preferred_element_type=jnp.float32)
    d_hidden, d_gains = rms_backward(hidden, inv_rms, gains, d_normed)
    return (grad_out + d_hidden, d_gains, grad_din, grad_dout)

def expert_targets(routes):
    block_total = TOKENS // GROUP
    block_routes = routes[:, 0].reshape(block_total, GROUP)
    route_hits = (block_routes[:, :, None] == jnp.arange(EXPERTS, dtype=jnp.int32)[None, None, :]).astype(jnp.int32)
    slot_order = lax.optimization_barrier(jnp.sum((jnp.cumsum(route_hits, axis=1) - 1) * route_hits, axis=2))
    block_ids = jnp.arange(block_total, dtype=jnp.int32)[:, None]
    return (block_routes * (block_total * CAP) + block_ids * CAP + slot_order).reshape(TOKENS).astype(jnp.int32)

def expert_rows_forward(operands):
    rows_in, weight_in, weight_out = operands
    pre_act = jnp.dot(rows_in, weight_in, preferred_element_type=jnp.float32)
    active = to_half(smooth_act(pre_act))
    return to_half(jnp.dot(active, weight_out, preferred_element_type=jnp.float32))

def expert_rows_backward(operands):
    rows_in, grad_rows, weight_in, weight_out = operands
    pre_act = jnp.dot(rows_in, weight_in, preferred_element_type=jnp.float32)
    active = to_half(smooth_act(pre_act))
    d_active = jnp.dot(grad_rows, weight_out.T, preferred_element_type=jnp.float32)
    d_pre = to_half(d_active * smooth_slope(pre_act))
    grad_in = jnp.dot(rows_in.T, d_pre, preferred_element_type=jnp.float32)
    grad_out = jnp.dot(active.T, grad_rows, preferred_element_type=jnp.float32)
    d_rows = to_half(jnp.dot(d_pre, weight_in.T, preferred_element_type=jnp.float32))
    return (grad_in, grad_out, d_rows)

def expert_forward(hidden, gains, expert_in, expert_out, target, gate_scale):
    normed, inv_rms = rms_forward(hidden, gains)
    normed_half = to_half(normed)
    slots_per = TOKENS // GROUP * CAP
    buffer = jnp.zeros((EXPERTS * slots_per, D), jnp.bfloat16).at[target].set(normed_half)
    produced = lax.map(expert_rows_forward, (buffer.reshape(EXPERTS, slots_per, D), expert_in, expert_out))
    gathered = widen(produced.reshape(EXPERTS * slots_per, D)[target])
    return (hidden + gate_scale * gathered, (hidden, inv_rms, buffer))

def expert_backward(layer_cache, grad_out, gains, expert_in, expert_out, target, gate_scale):
    hidden, inv_rms, buffer = layer_cache
    slots_per = TOKENS // GROUP * CAP
    sent_rows = to_half(gate_scale * grad_out)
    grad_buffer = jnp.zeros((EXPERTS * slots_per, D), jnp.bfloat16).at[target].set(sent_rows)
    grad_ein, grad_eout, d_rows = lax.map(expert_rows_backward, (buffer.reshape(EXPERTS, slots_per, D), grad_buffer.reshape(EXPERTS, slots_per, D), expert_in, expert_out))
    d_normed = widen(d_rows.reshape(EXPERTS * slots_per, D)[target])
    d_hidden, d_gains = rms_backward(hidden, inv_rms, gains, d_normed)
    return (grad_out + d_hidden, d_gains, grad_ein, grad_eout)

def reference(inputs, w_query, w_key, w_value, w_out, norm_gain, bias_table, dense_in, dense_out, expert_in, expert_out, routes, gate_scale, buckets, cotangent):
    bucket_picks = bucket_matrix(buckets)
    bias_rows = jnp.dot(bias_table.T, bucket_picks, precision=highest)
    block_rows = math.gcd(512, LENGTH)
    target = expert_targets(routes)
    out_one, cache_one = attention_forward(inputs, norm_gain[0], w_query[0], w_key[0], w_value[0], w_out[0], bias_rows, block_rows)
    out_two, cache_two = dense_forward(out_one, norm_gain[1], dense_in, dense_out)
    out_three, cache_three = attention_forward(out_two, norm_gain[2], w_query[1], w_key[1], w_value[1], w_out[1], bias_rows, block_rows)
    outputs, cache_four = expert_forward(out_three, norm_gain[3], expert_in, expert_out, target, gate_scale)
    grad_three, gains_four, grad_ein, grad_eout = expert_backward(cache_four, cotangent, norm_gain[3], expert_in, expert_out, target, gate_scale)
    grad_two, gains_three, wq_two, wk_two, wv_two, wo_two, bias_two = attention_backward(cache_three, grad_three, norm_gain[2], w_query[1], w_key[1], w_value[1], w_out[1], bias_rows, block_rows)
    grad_one, gains_two, grad_din, grad_dout = dense_backward(cache_two, grad_two, norm_gain[1], dense_in, dense_out)
    input_grad, gains_one, wq_one, wk_one, wv_one, wo_one, bias_one = attention_backward(cache_one, grad_one, norm_gain[0], w_query[0], w_key[0], w_value[0], w_out[0], bias_rows, block_rows)
    table_grad = jnp.dot(bucket_picks, (bias_one + bias_two).T, precision=highest).reshape(NB * HEADS)
    return (outputs, input_grad, jnp.stack([wq_one, wq_two]), jnp.stack([wk_one, wk_two]), jnp.stack([wv_one, wv_two]), jnp.stack([wo_one, wo_two]), jnp.stack([gains_one, gains_two, gains_three, gains_four]), table_grad, grad_din, grad_dout, grad_ein, grad_eout)
```

```python
import functools

import jax
import jax.numpy as jnp
from jax import lax
from jax.experimental import pallas as pl
from jax.experimental.pallas import tpu as pltpu
from jax.sharding import PartitionSpec as P

epsilon = 1e-06
highest = lax.Precision.HIGHEST
MESH = pl.DeviceIdType.MESH
VMEM = pltpu.VMEM


def to_half(values):
    return values.astype(jnp.bfloat16)


def widen(values):
    return values.astype(jnp.float32)


def dot_nn(a, b):
    return jnp.dot(a, b, preferred_element_type=jnp.float32)


def dot_nt(a, b):
    return lax.dot_general(a, b, (((1,), (1,)), ((), ())), preferred_element_type=jnp.float32)


def dot_tn(a, b):
    return lax.dot_general(a, b, (((0,), (0,)), ((), ())), preferred_element_type=jnp.float32)


def rotate(values, shift):
    width = values.shape[-1]
    shift = shift % width
    return values if shift == 0 else pltpu.roll(values, shift, values.ndim - 1)


def pad_lanes(values, width):
    if values.shape[1] == width:
        return values
    zeros = jnp.zeros((values.shape[0], width - values.shape[1]), values.dtype)
    return jnp.concatenate([values, zeros], axis=1)


class Plan:
    def __init__(self, cycle, exp_size, head_count, head_size, rows):
        self.cycle, self.exp_size, self.rows = cycle, exp_size, rows
        groups = 1
        while cycle % (groups * 2) == 0 and head_count % (groups * 2) == 0:
            groups *= 2
        self.groups, self.splits = groups, cycle // groups
        self.heads, self.head_size = head_count // groups, head_size
        self.width = self.heads * head_size
        self.model = head_count * head_size
        self.length = cycle * rows
        self.wide = -(-self.width // 128) * 128
        self.lead = self.wide - self.width
        self.pair = 2 * self.width
        self.tiled = self.heads if self.heads * rows * self.length * 8 <= 4 << 20 else 1
        assert self.pair % 128 == 0 and self.pair - self.wide == self.width - self.lead

    def place(self):
        c = lax.axis_index("ctx") * self.exp_size + lax.axis_index("exp")
        return c, c // self.splits, lax.rem(c, self.splits)

    def device(self, c):
        return (lax.axis_index("dp"), c // self.exp_size, lax.rem(c, self.exp_size))

    def peer(self, c, step):
        return lax.rem(c + step, self.cycle)


def greet(plan, c):
    barrier = pltpu.get_barrier_semaphore()
    for step in range(1, plan.cycle):
        pl.semaphore_signal(
            barrier, inc=1, device_id=plan.device(plan.peer(c, step)), device_id_type=MESH
        )
    return barrier


def rms_normed(hidden, gains):
    inv_rms = lax.rsqrt(jnp.mean(hidden * hidden, axis=-1, keepdims=True) + epsilon)
    return hidden * inv_rms * gains, inv_rms


def fill_bias(plan, rows_ref, tiles, heads):
    for head in heads:
        row = jnp.broadcast_to(rows_ref[head : head + 1, :], (plan.rows, 2 * plan.length))
        tiles[head % plan.tiled] = pltpu.roll(row, 0, 1, stride=1, stride_axis=0)


def bias_part(plan, tiles, head, key_block, split):
    parts = []
    head = head % plan.tiled
    for block in range(plan.groups):
        first = plan.length + (block * plan.splits + split - key_block) * plan.rows
        parts.append(tiles[head, :, pl.ds(pl.multiple_of(first, plan.rows), plan.rows)])
    return jnp.concatenate(parts, axis=1)


def lanes_between(shape, low, high):
    lane = lax.broadcasted_iota(jnp.int32, shape, 1)
    return (lane >= low) & (lane < high)


def natural(plan, blocks, lead):
    total = None
    for group, block in enumerate(blocks):
        moved = rotate(pad_lanes(block, plan.model), group * plan.width - lead)
        total = moved if total is None else total + moved
    return total


def remote(src, dst, send, recv, device):
    return pltpu.make_async_remote_copy(
        src_ref=src, dst_ref=dst, send_sem=send, recv_sem=recv, device_id=device, device_id_type=MESH
    )


def forward_kernel(
    plan,
    layer,
    x_ref,
    gain_ref,
    bias_ref,
    wq_hbm,
    wk_hbm,
    wv_hbm,
    wo_hbm,
    mid_ref,
    normed_ref,
    query_ref,
    pair_ref,
    heads_ref,
    attended_ref,
    norm_ref,
    weights,
    tiles,
    send_pair,
    send_query,
    scores,
    probs,
    att_in,
    load_sem,
    pair_send,
    pair_recv,
    query_send,
    query_recv,
    att_send,
    att_recv,
):
    c, group, split = plan.place()
    loads = []
    for slot, source in enumerate((wv_hbm, wk_hbm, wq_hbm, wo_hbm)):
        load = pltpu.make_async_copy(source.at[layer], weights.at[slot], load_sem.at[slot])
        load.start()
        loads.append(load)
    barrier = greet(plan, c)
    hidden = x_ref[...]
    normed, _ = rms_normed(hidden, gain_ref[layer * 2 : layer * 2 + 1, :])
    normed_half = to_half(normed)
    normed_ref[...] = normed_half
    loads[0].wait()
    values = dot_nn(normed_half, weights[0])
    loads[1].wait()
    keys = dot_nn(normed_half, weights[1])
    is_value = lanes_between((plan.rows, plan.pair), 0, plan.width)
    for g in range(plan.groups):
        value_part = rotate(values, -g * plan.width)[:, : plan.pair]
        key_part = rotate(keys, (1 - g) * plan.width)[:, : plan.pair]
        send_pair[g] = to_half(jnp.where(is_value, value_part, key_part))
    pl.semaphore_wait(barrier, plan.cycle - 1)
    copies = []
    for step in range(1, plan.cycle):
        to = plan.peer(c, step)
        copy = remote(
            send_pair.at[to // plan.splits],
            pair_ref.at[c],
            pair_send.at[step],
            pair_recv.at[step],
            plan.device(to),
        )
        copy.start()
        copies.append(copy)
    loads[2].wait()
    queries = dot_nn(normed_half, weights[2])
    is_query = lanes_between((plan.rows, plan.wide), plan.lead, plan.wide)
    for g in range(plan.groups):
        query_part = rotate(queries, plan.lead - g * plan.width)[:, : plan.wide]
        send_query[g] = to_half(jnp.where(is_query, query_part, 0.0))
    for step in range(1, plan.groups):
        to = plan.peer(c, step * plan.splits)
        copy = remote(
            send_query.at[to // plan.splits],
            query_ref.at[group],
            query_send.at[step],
            query_recv.at[step],
            plan.device(to),
        )
        copy.start()
        copies.append(copy)
    pair_ref[c] = send_pair[group]
    query_ref[group] = send_query[group]
    fill_bias(plan, bias_ref, tiles, range(plan.tiled))
    for copy in copies:
        copy.wait()

    total = plan.groups * plan.rows
    queries_all = query_ref[...].reshape(total, plan.wide)
    values_t = jnp.transpose(pair_ref[...].reshape(plan.length, plan.pair)[:, : plan.wide])
    rows_t = []
    for head in range(plan.heads):
        if head >= plan.tiled:
            fill_bias(plan, bias_ref, tiles, [head])
        low = plan.lead + head * plan.head_size
        picked = jnp.where(
            lanes_between(queries_all.shape, low, low + plan.head_size), queries_all, 0
        )

        def score_block(block, top):
            part = dot_nt(pair_ref[block][:, plan.pair - plan.wide :], picked)
            part = part + bias_part(plan, tiles, head, block, split)
            scores[pl.ds(pl.multiple_of(block * plan.rows, plan.rows), plan.rows), :] = part
            return jnp.maximum(top, jnp.max(part, axis=0, keepdims=True))

        top = lax.fori_loop(0, plan.cycle, score_block, jnp.full((1, total), -1e30, jnp.float32))

        def weight_block(block, norm):
            where = pl.ds(pl.multiple_of(block * plan.rows, plan.rows), plan.rows)
            part = jnp.exp(scores[where, :] - top)
            probs[where, :] = to_half(part)
            return norm + jnp.sum(part, axis=0, keepdims=True)

        norm = lax.fori_loop(0, plan.cycle, weight_block, jnp.zeros((1, total), jnp.float32))
        norm_ref[head : head + 1, :] = top + jnp.log(norm)
        mine = values_t[head * plan.head_size : (head + 1) * plan.head_size, :]
        rows_t.append(dot_nn(mine, probs[...]) / norm)
    rows_t.append(jnp.zeros((plan.lead, total), jnp.float32))
    heads_ref[...] = to_half(jnp.transpose(jnp.concatenate(rows_t, axis=0))).reshape(
        plan.groups, plan.rows, plan.wide
    )
    copies = []
    for step in range(1, plan.groups):
        to = plan.peer(c, step * plan.splits)
        copy = remote(
            heads_ref.at[to // plan.splits],
            att_in.at[group],
            att_send.at[step],
            att_recv.at[step],
            plan.device(to),
        )
        copy.start()
        copies.append(copy)
    att_in[group] = heads_ref[group]
    loads[3].wait()
    for copy in copies:
        copy.wait()
    attended = to_half(natural(plan, [widen(att_in[g]) for g in range(plan.groups)], 0))
    attended_ref[...] = attended
    mid_ref[...] = hidden + dot_nn(attended, weights[3])


def attention_forward(plan, layer, hidden, gains, bias_rows, wq, wk, wv, wo, collective):
    f32, half = jnp.float32, jnp.bfloat16
    total = plan.groups * plan.rows
    whole = pl.BlockSpec(memory_space=VMEM)
    hbm = pl.BlockSpec(memory_space=pl.ANY)
    dma = pltpu.SemaphoreType.DMA
    return pl.pallas_call(
        functools.partial(forward_kernel, plan, layer),
        out_shape=(
            jax.ShapeDtypeStruct((plan.rows, plan.model), f32),
            jax.ShapeDtypeStruct((plan.rows, plan.model), half),
            jax.ShapeDtypeStruct((plan.groups, plan.rows, plan.wide), half),
            jax.ShapeDtypeStruct((plan.cycle, plan.rows, plan.pair), half),
            jax.ShapeDtypeStruct((plan.groups, plan.rows, plan.wide), half),
            jax.ShapeDtypeStruct((plan.rows, plan.model), half),
            jax.ShapeDtypeStruct((plan.heads, total), f32),
        ),
        in_specs=[whole, whole, whole, hbm, hbm, hbm, hbm],
        out_specs=(whole,) * 7,
        scratch_shapes=[
            VMEM((4, plan.model, plan.model), half),
            VMEM((plan.tiled, plan.rows, 2 * plan.length), f32),
            VMEM((plan.groups, plan.rows, plan.pair), half),
            VMEM((plan.groups, plan.rows, plan.wide), half),
            VMEM((plan.length, total), f32),
            VMEM((plan.length, total), half),
            VMEM((plan.groups, plan.rows, plan.wide), half),
            dma((4,)),
            dma((plan.cycle,)),
            dma((plan.cycle,)),
            dma((plan.groups,)),
            dma((plan.groups,)),
            dma((plan.groups,)),
            dma((plan.groups,)),
        ],
        compiler_params=pltpu.CompilerParams(
            collective_id=collective, has_side_effects=True, vmem_limit_bytes=56 * 1024 * 1024
        ),
        name="attention_forward",
    )(hidden, gains, bias_rows, wq, wk, wv, wo)


def backward_kernel(
    plan,
    layer,
    grad_ref,
    x_ref,
    gain_ref,
    bias_ref,
    normed_ref,
    query_ref,
    pair_ref,
    heads_ref,
    attended_ref,
    norm_ref,
    wq_hbm,
    wk_hbm,
    wv_hbm,
    wo_hbm,
    out_ref,
    gain_grad_ref,
    weight_grad_ref,
    bias_grad_ref,
    weights,
    tiles,
    sums,
    send_grad,
    grad_in,
    probs,
    slopes,
    key_sum,
    value_sum,
    send_pair,
    pair_in,
    send_query,
    query_in,
    load_sem,
    grad_send,
    grad_recv,
    pair_send,
    pair_recv,
    query_send,
    query_recv,
):
    c, group, split = plan.place()
    total = plan.groups * plan.rows
    loads = []
    for slot, source in enumerate((wv_hbm, wk_hbm, wq_hbm, wo_hbm)):
        load = pltpu.make_async_copy(source.at[layer], weights.at[slot], load_sem.at[slot])
        loads.append(load)
    for slot in (3, 0, 1, 2):
        loads[slot].start()
    barrier = greet(plan, c)
    grad = grad_ref[...]
    grad_half = to_half(grad)
    loads[3].wait()
    d_attended = dot_nt(grad_half, weights[3])
    in_group = lanes_between((plan.rows, plan.wide), 0, plan.width)
    for g in range(plan.groups):
        part = rotate(d_attended, -g * plan.width)[:, : plan.wide]
        send_grad[g] = to_half(jnp.where(in_group, part, 0.0))
    pl.semaphore_wait(barrier, plan.cycle - 1)
    copies = []
    for step in range(1, plan.groups):
        to = plan.peer(c, step * plan.splits)
        copy = remote(
            send_grad.at[to // plan.splits],
            grad_in.at[group],
            grad_send.at[step],
            grad_recv.at[step],
            plan.device(to),
        )
        copy.start()
        copies.append(copy)
    grad_in[group] = send_grad[group]
    fill_bias(plan, bias_ref, tiles, range(plan.tiled))
    weight_grad_ref[3] = to_half(dot_tn(attended_ref[...], grad_half))
    queries_all = query_ref[...].reshape(total, plan.wide)
    keys_t = jnp.transpose(
        pair_ref[...].reshape(plan.length, plan.pair)[:, plan.pair - plan.wide :]
    )
    heads_t = jnp.transpose(widen(heads_ref[...].reshape(total, plan.wide)))
    for copy in copies:
        copy.wait()
    grads_all = grad_in[...].reshape(total, plan.wide)
    grads_t = jnp.transpose(widen(grads_all))
    products_t = grads_t * heads_t
    query_rows_t = [jnp.zeros((plan.lead, total), jnp.float32)]
    for head in range(plan.heads):
        if head >= plan.tiled:
            fill_bias(plan, bias_ref, tiles, [head])
        low, high = head * plan.head_size, (head + 1) * plan.head_size
        picked_queries = jnp.where(
            lanes_between(queries_all.shape, plan.lead + low, plan.lead + high), queries_all, 0
        )
        picked_grads = jnp.where(lanes_between(grads_all.shape, low, high), grads_all, 0)
        delta = jnp.sum(products_t[low:high, :], axis=0, keepdims=True)
        log_norm = norm_ref[head : head + 1, :]
        sums[...] = jnp.zeros_like(sums)

        def slope_block(block, carry):
            where = pl.ds(pl.multiple_of(block * plan.rows, plan.rows), plan.rows)
            part = dot_nt(pair_ref[block][:, plan.pair - plan.wide :], picked_queries)
            part = part + bias_part(plan, tiles, head, block, split)
            part = jnp.exp(part - log_norm)
            probs[where, :] = to_half(part)
            slope = part * (dot_nt(pair_ref[block][:, : plan.wide], picked_grads) - delta)
            slopes[where, :] = to_half(slope)
            for b in range(plan.groups):
                first = plan.length + (b * plan.splits + split - block) * plan.rows
                at = pl.ds(pl.multiple_of(first, plan.rows), plan.rows)
                sums[:, at] += slope[:, b * plan.rows : (b + 1) * plan.rows]
            return carry

        lax.fori_loop(0, plan.cycle, slope_block, 0)
        key_part = dot_nn(slopes[...], picked_queries)
        value_part = dot_nn(probs[...], picked_grads)
        if head == 0:
            key_sum[...], value_sum[...] = key_part, value_part
        else:
            key_sum[...] += key_part
            value_sum[...] += value_part
        query_rows_t.append(dot_nn(keys_t[plan.lead + low : plan.lead + high, :], slopes[...]))
        row = lax.broadcasted_iota(jnp.int32, (plan.rows, plan.rows), 0)
        column = lax.broadcasted_iota(jnp.int32, (plan.rows, plan.rows), 1)
        flip = (row + column == plan.rows - 1).astype(jnp.float32)
        flipped = jnp.dot(flip, sums[...], precision=highest, preferred_element_type=jnp.float32)
        skewed = pltpu.roll(
            flipped, 2 * plan.length - (plan.rows - 1), 1, stride=1, stride_axis=0
        )
        bias_grad_ref[head : head + 1, :] = jnp.sum(skewed, axis=0, keepdims=True)
    send_query[...] = to_half(jnp.transpose(jnp.concatenate(query_rows_t, axis=0))).reshape(
        plan.groups, plan.rows, plan.wide
    )
    value_all, key_all = value_sum[...], key_sum[...]
    low, gap = plan.pair - plan.wide, plan.wide - (plan.pair - plan.wide)
    middle = jnp.where(
        lanes_between((plan.length, gap), 0, plan.width - low), value_all[:, low:], key_all[:, :gap]
    )
    send_pair[...] = to_half(
        jnp.concatenate([value_all[:, :low], middle, key_all[:, gap:]], axis=1)
    ).reshape(plan.cycle, plan.rows, plan.pair)
    copies = []
    for step in range(1, plan.cycle):
        to = plan.peer(c, step)
        copy = remote(
            send_pair.at[to], pair_in.at[c], pair_send.at[step], pair_recv.at[step], plan.device(to)
        )
        copy.start()
        copies.append(copy)
    for step in range(1, plan.groups):
        to = plan.peer(c, step * plan.splits)
        copy = remote(
            send_query.at[to // plan.splits],
            query_in.at[group],
            query_send.at[step],
            query_recv.at[step],
            plan.device(to),
        )
        copy.start()
        copies.append(copy)
    pair_in[c] = send_pair[c]
    query_in[group] = send_query[group]
    hidden = x_ref[...]
    gains = gain_ref[layer * 2 : layer * 2 + 1, :]
    inv_rms = lax.rsqrt(jnp.mean(hidden * hidden, axis=-1, keepdims=True) + epsilon)
    for slot in range(3):
        loads[slot].wait()
    for copy in copies:
        copy.wait()
    is_value = lanes_between((plan.rows, plan.pair), 0, plan.width)
    value_blocks, key_blocks = [], []
    for g in range(plan.groups):
        block = widen(pair_in[g * plan.splits])
        for other in range(1, plan.splits):
            block = block + widen(pair_in[g * plan.splits + other])
        value_blocks.append(jnp.where(is_value, block, 0.0))
        key_blocks.append(jnp.where(is_value, 0.0, block))
    d_values = to_half(natural(plan, value_blocks, 0))
    d_keys = to_half(natural(plan, key_blocks, plan.width))
    d_queries = to_half(
        natural(plan, [widen(query_in[g]) for g in range(plan.groups)], plan.lead)
    )
    normed_half = normed_ref[...]
    d_normed = (
        dot_nt(d_queries, weights[2]) + dot_nt(d_keys, weights[1]) + dot_nt(d_values, weights[0])
    )
    weight_grad_ref[0] = to_half(dot_tn(normed_half, d_queries))
    weight_grad_ref[1] = to_half(dot_tn(normed_half, d_keys))
    weight_grad_ref[2] = to_half(dot_tn(normed_half, d_values))
    d_scaled = d_normed * gains
    gain_grad_ref[...] = jnp.sum(d_normed * hidden * inv_rms, axis=0, keepdims=True)
    out_ref[...] = (
        grad
        + inv_rms * d_scaled
        - hidden * (inv_rms * inv_rms * inv_rms) * jnp.mean(d_scaled * hidden, axis=-1, keepdims=True)
    )


def attention_backward(plan, layer, grad, cache, gains, bias_rows, wq, wk, wv, wo, collective):
    f32, half = jnp.float32, jnp.bfloat16
    total = plan.groups * plan.rows
    whole = pl.BlockSpec(memory_space=VMEM)
    hbm = pl.BlockSpec(memory_space=pl.ANY)
    dma = pltpu.SemaphoreType.DMA
    hidden, normed, query, pair, heads, attended, norm = cache
    block = (plan.groups, plan.rows, plan.wide)
    pairs = (plan.cycle, plan.rows, plan.pair)
    return pl.pallas_call(
        functools.partial(backward_kernel, plan, layer),
        out_shape=(
            jax.ShapeDtypeStruct((plan.rows, plan.model), f32),
            jax.ShapeDtypeStruct((1, plan.model), f32),
            jax.ShapeDtypeStruct((4, plan.model, plan.model), half),
            jax.ShapeDtypeStruct((plan.heads, 2 * plan.length), f32),
        ),
        in_specs=[whole] * 10 + [hbm] * 4,
        out_specs=(whole,) * 4,
        scratch_shapes=[
            VMEM((4, plan.model, plan.model), half),
            VMEM((plan.tiled, plan.rows, 2 * plan.length), f32),
            VMEM((plan.rows, 2 * plan.length), f32),
            VMEM(block, half),
            VMEM(block, half),
            VMEM((plan.length, total), half),
            VMEM((plan.length, total), half),
            VMEM((plan.length, plan.wide), f32),
            VMEM((plan.length, plan.wide), f32),
            VMEM(pairs, half),
            VMEM(pairs, half),
            VMEM(block, half),
            VMEM(block, half),
            dma((4,)),
            dma((plan.groups,)),
            dma((plan.groups,)),
            dma((plan.cycle,)),
            dma((plan.cycle,)),
            dma((plan.groups,)),
            dma((plan.groups,)),
        ],
        compiler_params=pltpu.CompilerParams(
            collective_id=collective, has_side_effects=True, vmem_limit_bytes=60 * 1024 * 1024
        ),
        name="attention_backward",
    )(grad, hidden, gains, bias_rows, normed, query, pair, heads, attended, norm, wq, wk, wv, wo)


def smooth_act(values):
    return values * jax.nn.sigmoid(values)


def smooth_slope(values):
    sigma = jax.nn.sigmoid(values)
    return sigma * (1.0 + values * (1.0 - sigma))


def rms_backward(hidden, inv_rms, gains, d_normed):
    d_scaled = d_normed * gains
    d_gains = jnp.sum(d_normed * hidden * inv_rms, axis=0)
    d_hidden = inv_rms * d_scaled - hidden * inv_rms**3 * jnp.mean(
        d_scaled * hidden, axis=-1, keepdims=True
    )
    return (d_hidden, d_gains)


def along_dp(values):
    count = lax.axis_size("dp")
    return [values] + [
        lax.ppermute(values, "dp", [(i, i ^ step) for i in range(count)]) for step in range(1, count)
    ]


def body(
    inputs,
    w_query,
    w_key,
    w_value,
    w_out,
    norm_gain,
    bias_table,
    dense_in,
    dense_out,
    expert_in,
    expert_out,
    routes,
    gate_scale,
    buckets,
    cotangent,
):
    group_rows, model_width = inputs.shape
    head_count = bias_table.shape[1]
    head_size = model_width // head_count
    bucket_count = bias_table.shape[0]
    cycle_size = lax.axis_size(("ctx", "exp"))
    plan = Plan(cycle_size, lax.axis_size("exp"), head_count, head_size, group_rows)
    my_group = lax.axis_index(("ctx", "exp")) // plan.splits
    reversed_buckets = jnp.roll(buckets[::-1], 1)
    bucket_picks = (
        reversed_buckets[None, :] == jnp.arange(bucket_count, dtype=jnp.int32)[:, None]
    ).astype(jnp.float32)
    my_table = lax.dynamic_slice_in_dim(bias_table.T, my_group * plan.heads, plan.heads, 0)
    bias_rows = jnp.dot(my_table, bucket_picks, precision=highest)

    local_experts = expert_in.shape[0]
    expert_total = local_experts * cycle_size
    capacity = 2 * group_rows // expert_total
    recv_rows = cycle_size * capacity
    flat_routes = routes[:, 0]
    route_hits = (
        flat_routes[:, None] == jnp.arange(expert_total, dtype=jnp.int32)[None, :]
    ).astype(jnp.int32)
    slot_order = jnp.sum((jnp.cumsum(route_hits, axis=0) - 1) * route_hits, axis=1)
    target = flat_routes * capacity + slot_order
    dispatch = (
        target[None, :] == jnp.arange(expert_total * capacity, dtype=jnp.int32)[:, None]
    ).astype(jnp.bfloat16)

    def to_owners(rows_half):
        placed = jnp.dot(dispatch, rows_half, preferred_element_type=jnp.float32)
        return lax.all_to_all(
            to_half(placed).reshape(cycle_size, local_experts, capacity, model_width),
            ("ctx", "exp"),
            split_axis=0,
            concat_axis=2,
            tiled=True,
        ).reshape(local_experts, recv_rows, model_width)

    def from_owners(produced):
        returned = lax.all_to_all(
            produced.reshape(1, local_experts, recv_rows, model_width),
            ("ctx", "exp"),
            split_axis=2,
            concat_axis=0,
            tiled=True,
        )
        return jnp.einsum(
            "sc,sd->cd",
            dispatch,
            returned.reshape(expert_total * capacity, model_width),
            preferred_element_type=jnp.float32,
        )

    grad_rows = to_owners(to_half(gate_scale * cotangent))
    grad_rows_all = jnp.concatenate(along_dp(grad_rows), axis=1)

    mid_zero, *cache_zero = attention_forward(
        plan, 0, inputs, norm_gain, bias_rows, w_query, w_key, w_value, w_out, 0
    )
    inv_rms_one = lax.rsqrt(jnp.mean(mid_zero * mid_zero, axis=-1, keepdims=True) + epsilon)
    normed_half = to_half(mid_zero * inv_rms_one * norm_gain[1])
    pre_act = jnp.dot(normed_half, dense_in, preferred_element_type=jnp.float32)
    active = to_half(smooth_act(pre_act))
    stream = mid_zero + jnp.dot(active, dense_out, preferred_element_type=jnp.float32)
    mid_one, *cache_one = attention_forward(
        plan, 1, stream, norm_gain, bias_rows, w_query, w_key, w_value, w_out, 1
    )
    inv_rms_three = lax.rsqrt(jnp.mean(mid_one * mid_one, axis=-1, keepdims=True) + epsilon)
    rows = to_owners(to_half(mid_one * inv_rms_three * norm_gain[3]))
    rows_all = jnp.concatenate(along_dp(rows), axis=1)
    expert_pre = jnp.einsum("erd,edf->erf", rows, expert_in, preferred_element_type=jnp.float32)
    expert_active = to_half(smooth_act(expert_pre))
    produced = to_half(
        jnp.einsum("erf,efd->erd", expert_active, expert_out, preferred_element_type=jnp.float32)
    )
    d_active = jnp.einsum("erd,efd->erf", grad_rows, expert_out, preferred_element_type=jnp.float32)
    d_pre = to_half(d_active * smooth_slope(expert_pre))
    d_rows = to_half(jnp.einsum("erf,edf->erd", d_pre, expert_in, preferred_element_type=jnp.float32))
    output = mid_one + gate_scale * from_owners(produced)
    d_hidden, gains_four = rms_backward(mid_one, inv_rms_three, norm_gain[3], from_owners(d_rows))
    grad_three = cotangent + d_hidden

    grad_two, gains_three, attn_two, bias_two = attention_backward(
        plan, 1, grad_three, [stream] + cache_one, norm_gain, bias_rows, w_query, w_key, w_value, w_out, 2
    )
    grad_half = to_half(grad_two)
    grad_dout = jnp.dot(active.T, grad_half, preferred_element_type=jnp.float32)
    d_active = jnp.dot(grad_half, dense_out.T, preferred_element_type=jnp.float32)
    d_pre = to_half(d_active * smooth_slope(pre_act))
    grad_din = jnp.dot(normed_half.T, d_pre, preferred_element_type=jnp.float32)
    d_normed = jnp.dot(d_pre, dense_in.T, preferred_element_type=jnp.float32)
    d_hidden, gains_two = rms_backward(mid_zero, inv_rms_one, norm_gain[1], d_normed)
    grad_one = grad_two + d_hidden
    input_grad, gains_one, attn_one, bias_one = attention_backward(
        plan, 0, grad_one, [inputs] + cache_zero, norm_gain, bias_rows, w_query, w_key, w_value, w_out, 3
    )

    shard = lax.axis_index("dp") * (expert_in.shape[2] // lax.axis_size("dp"))
    width = expert_in.shape[2] // lax.axis_size("dp")
    in_part = lax.dynamic_slice_in_dim(expert_in, shard, width, 2)
    out_part = lax.dynamic_slice_in_dim(expert_out, shard, width, 1)
    part_pre = jnp.einsum("erd,edf->erf", rows_all, in_part, preferred_element_type=jnp.float32)
    part_active = to_half(smooth_act(part_pre))
    part_d_active = jnp.einsum(
        "erd,efd->erf", grad_rows_all, out_part, preferred_element_type=jnp.float32
    )
    part_d_pre = to_half(part_d_active * smooth_slope(part_pre))
    grad_ein = jnp.einsum("erd,erf->edf", rows_all, part_d_pre, preferred_element_type=jnp.float32)
    grad_eout = jnp.einsum(
        "erf,erd->efd", part_active, grad_rows_all, preferred_element_type=jnp.float32
    )

    everyone = ("dp", "ctx", "exp")
    my_table_grad = jnp.dot(bucket_picks, (bias_one + bias_two).T, precision=highest)
    table_grad = lax.dynamic_update_slice(
        jnp.zeros((bucket_count, head_count), jnp.float32),
        my_table_grad,
        (0, my_group * plan.heads),
    ).reshape(bucket_count * head_count)
    attn = lax.psum_scatter(
        jnp.concatenate([attn_one, attn_two]), everyone, scatter_dimension=2, tiled=True
    ).astype(jnp.float32)
    gains = lax.psum_scatter(
        jnp.stack([gains_one[0], gains_two, gains_three[0], gains_four]),
        everyone,
        scatter_dimension=1,
        tiled=True,
    )
    table = lax.psum_scatter(table_grad, everyone, scatter_dimension=0, tiled=True)
    din = lax.psum_scatter(to_half(grad_din), everyone, scatter_dimension=1, tiled=True)
    dout = lax.psum_scatter(to_half(grad_dout), everyone, scatter_dimension=0, tiled=True)
    return (
        output,
        input_grad,
        attn[0::4],
        attn[1::4],
        attn[2::4],
        attn[3::4],
        gains,
        table,
        din.astype(jnp.float32),
        dout.astype(jnp.float32),
        grad_ein,
        grad_eout,
    )


def solution(mesh):
    in_specs = (
        P(("dp", "ctx", "exp"), None),
        P(),
        P(),
        P(),
        P(),
        P(),
        P(),
        P(),
        P(),
        P(("ctx", "exp"), None, None),
        P(("ctx", "exp"), None, None),
        P(("dp", "ctx", "exp"), None),
        P(("dp", "ctx", "exp"), None),
        P(),
        P(("dp", "ctx", "exp"), None),
    )
    out_specs = (
        P(("dp", "ctx", "exp"), None),
        P(("dp", "ctx", "exp"), None),
        P(None, None, ("dp", "ctx", "exp")),
        P(None, None, ("dp", "ctx", "exp")),
        P(None, None, ("dp", "ctx", "exp")),
        P(None, None, ("dp", "ctx", "exp")),
        P(None, ("dp", "ctx", "exp")),
        P(("dp", "ctx", "exp")),
        P(None, ("dp", "ctx", "exp")),
        P(("dp", "ctx", "exp"), None),
        P(("ctx", "exp"), None, "dp"),
        P(("ctx", "exp"), "dp", None),
    )
    return jax.shard_map(body, mesh=mesh, in_specs=in_specs, out_specs=out_specs, check_vma=False)
```

```python
import functools

import jax
import jax.numpy as jnp
from jax import lax
from jax.experimental import pallas as pl
from jax.experimental.pallas import tpu as pltpu
from jax.sharding import PartitionSpec as P

epsilon = 1e-06
highest = lax.Precision.HIGHEST
MESH = pl.DeviceIdType.MESH
VMEM = pltpu.VMEM


def to_half(values):
    return values.astype(jnp.bfloat16)


def widen(values):
    return values.astype(jnp.float32)


def dot_nn(a, b):
    return jnp.dot(a, b, preferred_element_type=jnp.float32)


def dot_nt(a, b):
    return lax.dot_general(a, b, (((1,), (1,)), ((), ())), preferred_element_type=jnp.float32)


def dot_tn(a, b):
    return lax.dot_general(a, b, (((0,), (0,)), ((), ())), preferred_element_type=jnp.float32)


def rotate(values, shift):
    width = values.shape[-1]
    shift = shift % width
    return values if shift == 0 else pltpu.roll(values, shift, values.ndim - 1)


def pad_lanes(values, width):
    if values.shape[1] == width:
        return values
    zeros = jnp.zeros((values.shape[0], width - values.shape[1]), values.dtype)
    return jnp.concatenate([values, zeros], axis=1)


class Plan:
    def __init__(self, copies, cycle, exp_size, head_count, head_size, rows, experts):
        self.copies, self.cycle, self.exp_size, self.rows = copies, cycle, exp_size, rows
        groups = 1
        while cycle % (groups * 2) == 0 and head_count % (groups * 2) == 0:
            groups *= 2
        self.groups, self.splits = groups, cycle // groups
        self.heads, self.head_size = head_count // groups, head_size
        self.width = self.heads * head_size
        self.model = head_count * head_size
        self.length = cycle * rows
        self.wide = -(-self.width // 128) * 128
        self.lead = self.wide - self.width
        self.pair = 2 * self.width
        self.tiled = self.heads if self.heads * rows * self.length * 8 <= 4 << 20 else 1
        self.chips = cycle // 2
        self.share = self.model // (copies * cycle)
        self.experts = experts
        self.capacity = 2 * rows // (experts * cycle)
        self.slab = experts * self.capacity
        self.fused = (2 * self.share) % 16 == 0 and self.capacity % 16 == 0 and copies & (copies - 1) == 0
        assert self.pair % 128 == 0 and self.pair - self.wide == self.width - self.lead

    def place(self):
        c = lax.axis_index("ctx") * self.exp_size + lax.axis_index("exp")
        return c, c // self.splits, lax.rem(c, self.splits)

    def device(self, c):
        return (lax.axis_index("dp"), c // self.exp_size, lax.rem(c, self.exp_size))

    def peer(self, c, step):
        return lax.rem(c + step, self.cycle)

    def copy_device(self, c, other):
        return (other, c // self.exp_size, lax.rem(c, self.exp_size))


def greet(plan, c):
    barrier = pltpu.get_barrier_semaphore()
    for step in range(1, plan.cycle):
        pl.semaphore_signal(
            barrier, inc=1, device_id=plan.device(plan.peer(c, step)), device_id_type=MESH
        )
    me = lax.axis_index("dp")
    for step in range(1, plan.copies):
        other = lax.rem(me + step, plan.copies)
        pl.semaphore_signal(
            barrier, inc=1, device_id=plan.copy_device(c, other), device_id_type=MESH
        )
    return barrier


def await_greetings(plan, barrier):
    pl.semaphore_wait(barrier, plan.cycle - 1 + plan.copies - 1)


def start_along_dp(plan, c, source, target, own_sem, send, recv):
    me = lax.axis_index("dp")
    own = pltpu.make_async_copy(source, target.at[me], own_sem.at[0])
    own.start()
    copies = [own]
    for step in range(1, plan.copies):
        other = lax.rem(me + step, plan.copies)
        copy = remote(
            source, target.at[me], send.at[step], recv.at[step], plan.copy_device(c, other)
        )
        copy.start()
        copies.append(copy)
    return copies


def start_slabs(plan, c, source, target, send, recv):
    copies = []
    for step in range(1, plan.cycle):
        to = plan.peer(c, step)
        copy = remote(source.at[to], target.at[c], send.at[step], recv.at[step], plan.device(to))
        copy.start()
        copies.append(copy)
    target[c] = source[c]
    return copies


def rms_normed(hidden, gains):
    inv_rms = lax.rsqrt(jnp.mean(hidden * hidden, axis=-1, keepdims=True) + epsilon)
    return hidden * inv_rms * gains, inv_rms


def fill_bias(plan, rows_ref, tiles, heads):
    for head in heads:
        row = jnp.broadcast_to(rows_ref[head : head + 1, :], (plan.rows, 2 * plan.length))
        tiles[head % plan.tiled] = pltpu.roll(row, 0, 1, stride=1, stride_axis=0)


def bias_part(plan, tiles, head, key_block, split):
    parts = []
    head = head % plan.tiled
    for block in range(plan.groups):
        first = plan.length + (block * plan.splits + split - key_block) * plan.rows
        parts.append(tiles[head, :, pl.ds(pl.multiple_of(first, plan.rows), plan.rows)])
    return jnp.concatenate(parts, axis=1)


def lanes_between(shape, low, high):
    lane = lax.broadcasted_iota(jnp.int32, shape, 1)
    return (lane >= low) & (lane < high)


def natural(plan, blocks, lead):
    total = None
    for group, block in enumerate(blocks):
        moved = rotate(pad_lanes(block, plan.model), group * plan.width - lead)
        total = moved if total is None else total + moved
    return total


def remote(src, dst, send, recv, device):
    return pltpu.make_async_remote_copy(
        src_ref=src, dst_ref=dst, send_sem=send, recv_sem=recv, device_id=device, device_id_type=MESH
    )


def forward_kernel(
    plan,
    layer,
    x_ref,
    gain_ref,
    bias_ref,
    wq_hbm,
    wk_hbm,
    wv_hbm,
    wo_hbm,
    extra_ref,
    placed_ref,
    mid_ref,
    normed_ref,
    query_ref,
    pair_ref,
    heads_ref,
    attended_ref,
    norm_ref,
    extra_out,
    weights,
    tiles,
    send_pair,
    send_query,
    scores,
    probs,
    att_in,
    slabs,
    load_sem,
    pair_send,
    pair_recv,
    query_send,
    query_recv,
    att_send,
    att_recv,
    own_sem,
    extra_send,
    extra_recv,
):
    c, group, split = plan.place()
    loads = []
    for slot, source in enumerate((wv_hbm, wk_hbm, wq_hbm, wo_hbm)):
        load = pltpu.make_async_copy(source.at[layer], weights.at[slot], load_sem.at[slot])
        load.start()
        loads.append(load)
    barrier = greet(plan, c)
    hidden = x_ref[...]
    normed, _ = rms_normed(hidden, gain_ref[layer * 2 : layer * 2 + 1, :])
    normed_half = to_half(normed)
    normed_ref[...] = normed_half
    loads[0].wait()
    values = dot_nn(normed_half, weights[0])
    loads[1].wait()
    keys = dot_nn(normed_half, weights[1])
    if layer == 0 and plan.fused:
        placed = dot_nn(placed_ref[...], extra_ref[...])
        slabs[...] = to_half(placed).reshape(plan.cycle, plan.slab, plan.model)
    is_value = lanes_between((plan.rows, plan.pair), 0, plan.width)
    for g in range(plan.groups):
        value_part = rotate(values, -g * plan.width)[:, : plan.pair]
        key_part = rotate(keys, (1 - g) * plan.width)[:, : plan.pair]
        send_pair[g] = to_half(jnp.where(is_value, value_part, key_part))
    await_greetings(plan, barrier)
    copies = []
    for step in range(1, plan.cycle):
        to = plan.peer(c, step)
        copy = remote(
            send_pair.at[to // plan.splits],
            pair_ref.at[c],
            pair_send.at[step],
            pair_recv.at[step],
            plan.device(to),
        )
        copy.start()
        copies.append(copy)
    loads[2].wait()
    queries = dot_nn(normed_half, weights[2])
    is_query = lanes_between((plan.rows, plan.wide), plan.lead, plan.wide)
    for g in range(plan.groups):
        query_part = rotate(queries, plan.lead - g * plan.width)[:, : plan.wide]
        send_query[g] = to_half(jnp.where(is_query, query_part, 0.0))
    for step in range(1, plan.groups):
        to = plan.peer(c, step * plan.splits)
        copy = remote(
            send_query.at[to // plan.splits],
            query_ref.at[group],
            query_send.at[step],
            query_recv.at[step],
            plan.device(to),
        )
        copy.start()
        copies.append(copy)
    extras = []
    if plan.fused and layer == 0:
        extras = start_slabs(plan, c, slabs, extra_out, extra_send, extra_recv)
    elif plan.fused:
        extras = start_along_dp(plan, c, extra_ref, extra_out, own_sem, extra_send, extra_recv)
    pair_ref[c] = send_pair[group]
    query_ref[group] = send_query[group]
    fill_bias(plan, bias_ref, tiles, range(plan.tiled))
    for copy in copies:
        copy.wait()

    total = plan.groups * plan.rows
    queries_all = query_ref[...].reshape(total, plan.wide)
    values_t = jnp.transpose(pair_ref[...].reshape(plan.length, plan.pair)[:, : plan.wide])
    rows_t = []
    for head in range(plan.heads):
        if head >= plan.tiled:
            fill_bias(plan, bias_ref, tiles, [head])
        low = plan.lead + head * plan.head_size
        picked = jnp.where(
            lanes_between(queries_all.shape, low, low + plan.head_size), queries_all, 0
        )

        def score_block(block, top):
            part = dot_nt(pair_ref[block][:, plan.pair - plan.wide :], picked)
            part = part + bias_part(plan, tiles, head, block, split)
            scores[pl.ds(pl.multiple_of(block * plan.rows, plan.rows), plan.rows), :] = part
            return jnp.maximum(top, jnp.max(part, axis=0, keepdims=True))

        top = lax.fori_loop(0, plan.cycle, score_block, jnp.full((1, total), -1e30, jnp.float32))

        def weight_block(block, norm):
            where = pl.ds(pl.multiple_of(block * plan.rows, plan.rows), plan.rows)
            part = jnp.exp(scores[where, :] - top)
            probs[where, :] = to_half(part)
            return norm + jnp.sum(part, axis=0, keepdims=True)

        norm = lax.fori_loop(0, plan.cycle, weight_block, jnp.zeros((1, total), jnp.float32))
        norm_ref[head : head + 1, :] = top + jnp.log(norm)
        mine = values_t[head * plan.head_size : (head + 1) * plan.head_size, :]
        rows_t.append(dot_nn(mine, probs[...]) / norm)
    rows_t.append(jnp.zeros((plan.lead, total), jnp.float32))
    heads_ref[...] = to_half(jnp.transpose(jnp.concatenate(rows_t, axis=0))).reshape(
        plan.groups, plan.rows, plan.wide
    )
    copies = []
    for step in range(1, plan.groups):
        to = plan.peer(c, step * plan.splits)
        copy = remote(
            heads_ref.at[to // plan.splits],
            att_in.at[group],
            att_send.at[step],
            att_recv.at[step],
            plan.device(to),
        )
        copy.start()
        copies.append(copy)
    att_in[group] = heads_ref[group]
    loads[3].wait()
    for copy in copies:
        copy.wait()
    attended = to_half(natural(plan, [widen(att_in[g]) for g in range(plan.groups)], 0))
    attended_ref[...] = attended
    mid_ref[...] = hidden + dot_nn(attended, weights[3])
    for copy in extras:
        copy.wait()


def attention_forward(plan, layer, hidden, gains, bias_rows, wq, wk, wv, wo, extra, placed, collective):
    f32, half = jnp.float32, jnp.bfloat16
    total = plan.groups * plan.rows
    whole = pl.BlockSpec(memory_space=VMEM)
    hbm = pl.BlockSpec(memory_space=pl.ANY)
    dma = pltpu.SemaphoreType.DMA
    slabs = (plan.cycle, plan.slab, plan.model)
    extra_shape = slabs if layer == 0 else (plan.copies,) + extra.shape
    return pl.pallas_call(
        functools.partial(forward_kernel, plan, layer),
        out_shape=(
            jax.ShapeDtypeStruct((plan.rows, plan.model), f32),
            jax.ShapeDtypeStruct((plan.rows, plan.model), half),
            jax.ShapeDtypeStruct((plan.groups, plan.rows, plan.wide), half),
            jax.ShapeDtypeStruct((plan.cycle, plan.rows, plan.pair), half),
            jax.ShapeDtypeStruct((plan.groups, plan.rows, plan.wide), half),
            jax.ShapeDtypeStruct((plan.rows, plan.model), half),
            jax.ShapeDtypeStruct((plan.heads, total), f32),
            jax.ShapeDtypeStruct(extra_shape, half),
        ),
        in_specs=[whole, whole, whole, hbm, hbm, hbm, hbm, hbm if layer else whole, whole],
        out_specs=(whole,) * 7 + (hbm if layer else whole,),
        scratch_shapes=[
            VMEM((4, plan.model, plan.model), half),
            VMEM((plan.tiled, plan.rows, 2 * plan.length), f32),
            VMEM((plan.groups, plan.rows, plan.pair), half),
            VMEM((plan.groups, plan.rows, plan.wide), half),
            VMEM((plan.length, total), f32),
            VMEM((plan.length, total), half),
            VMEM((plan.groups, plan.rows, plan.wide), half),
            VMEM(slabs, half),
            dma((4,)),
            dma((plan.cycle,)),
            dma((plan.cycle,)),
            dma((plan.groups,)),
            dma((plan.groups,)),
            dma((plan.groups,)),
            dma((plan.groups,)),
            dma((1,)),
            dma((plan.cycle,)),
            dma((plan.cycle,)),
        ],
        compiler_params=pltpu.CompilerParams(
            collective_id=collective, has_side_effects=True, vmem_limit_bytes=56 * 1024 * 1024
        ),
        name="attention_forward",
    )(hidden, gains, bias_rows, wq, wk, wv, wo, extra, placed)


def store_shares(plan, out_ref, stage, slot, *factors):
    for index, (rows, columns) in enumerate(factors):
        stage[index] = dot_tn(rows, columns)
    height = 2 * plan.share

    def one_share(device, carry):
        d, c = device // plan.cycle, lax.rem(device, plan.cycle)
        where = pl.ds(pl.multiple_of(device * plan.share, plan.share), plan.share)
        both = jnp.concatenate([stage[0, where, :], stage[1, where, :]], axis=0)
        out_ref[lax.rem(c, 2), c // 2, d, slot * height : (slot + 1) * height, :] = to_half(both)
        return carry

    lax.fori_loop(0, plan.copies * plan.cycle, one_share, 0)


def backward_kernel(
    plan,
    layer,
    grad_ref,
    x_ref,
    gain_ref,
    bias_ref,
    normed_ref,
    query_ref,
    pair_ref,
    heads_ref,
    attended_ref,
    norm_ref,
    wq_hbm,
    wk_hbm,
    wv_hbm,
    wo_hbm,
    extra_ref,
    out_ref,
    gain_grad_ref,
    weight_grad_ref,
    bias_grad_ref,
    extra_out,
    stage,
    weights,
    tiles,
    sums,
    send_grad,
    grad_in,
    probs,
    slopes,
    key_sum,
    value_sum,
    send_pair,
    pair_in,
    send_query,
    query_in,
    load_sem,
    grad_send,
    grad_recv,
    pair_send,
    pair_recv,
    query_send,
    query_recv,
    own_sem,
    extra_send,
    extra_recv,
):
    c, group, split = plan.place()
    total = plan.groups * plan.rows
    loads = []
    for slot, source in enumerate((wv_hbm, wk_hbm, wq_hbm, wo_hbm)):
        load = pltpu.make_async_copy(source.at[layer], weights.at[slot], load_sem.at[slot])
        loads.append(load)
    for slot in (3, 0, 1, 2):
        loads[slot].start()
    barrier = greet(plan, c)
    grad = grad_ref[...]
    grad_half = to_half(grad)
    loads[3].wait()
    d_attended = dot_nt(grad_half, weights[3])
    in_group = lanes_between((plan.rows, plan.wide), 0, plan.width)
    for g in range(plan.groups):
        part = rotate(d_attended, -g * plan.width)[:, : plan.wide]
        send_grad[g] = to_half(jnp.where(in_group, part, 0.0))
    await_greetings(plan, barrier)
    copies = []
    for step in range(1, plan.groups):
        to = plan.peer(c, step * plan.splits)
        copy = remote(
            send_grad.at[to // plan.splits],
            grad_in.at[group],
            grad_send.at[step],
            grad_recv.at[step],
            plan.device(to),
        )
        copy.start()
        copies.append(copy)
    grad_in[group] = send_grad[group]
    extras = []
    if plan.fused:
        extras = start_along_dp(plan, c, extra_ref, extra_out, own_sem, extra_send, extra_recv)
    fill_bias(plan, bias_ref, tiles, range(plan.tiled))
    if not plan.fused:
        weight_grad_ref[3] = to_half(dot_tn(attended_ref[...], grad_half))
    queries_all = query_ref[...].reshape(total, plan.wide)
    keys_t = jnp.transpose(
        pair_ref[...].reshape(plan.length, plan.pair)[:, plan.pair - plan.wide :]
    )
    heads_t = jnp.transpose(widen(heads_ref[...].reshape(total, plan.wide)))
    for copy in copies:
        copy.wait()
    grads_all = grad_in[...].reshape(total, plan.wide)
    grads_t = jnp.transpose(widen(grads_all))
    products_t = grads_t * heads_t
    query_rows_t = [jnp.zeros((plan.lead, total), jnp.float32)]
    for head in range(plan.heads):
        if head >= plan.tiled:
            fill_bias(plan, bias_ref, tiles, [head])
        low, high = head * plan.head_size, (head + 1) * plan.head_size
        picked_queries = jnp.where(
            lanes_between(queries_all.shape, plan.lead + low, plan.lead + high), queries_all, 0
        )
        picked_grads = jnp.where(lanes_between(grads_all.shape, low, high), grads_all, 0)
        delta = jnp.sum(products_t[low:high, :], axis=0, keepdims=True)
        log_norm = norm_ref[head : head + 1, :]
        sums[...] = jnp.zeros_like(sums)

        def slope_block(block, carry):
            where = pl.ds(pl.multiple_of(block * plan.rows, plan.rows), plan.rows)
            part = dot_nt(pair_ref[block][:, plan.pair - plan.wide :], picked_queries)
            part = part + bias_part(plan, tiles, head, block, split)
            part = jnp.exp(part - log_norm)
            probs[where, :] = to_half(part)
            slope = part * (dot_nt(pair_ref[block][:, : plan.wide], picked_grads) - delta)
            slopes[where, :] = to_half(slope)
            for b in range(plan.groups):
                first = plan.length + (b * plan.splits + split - block) * plan.rows
                at = pl.ds(pl.multiple_of(first, plan.rows), plan.rows)
                sums[:, at] += slope[:, b * plan.rows : (b + 1) * plan.rows]
            return carry

        lax.fori_loop(0, plan.cycle, slope_block, 0)
        key_part = dot_nn(slopes[...], picked_queries)
        value_part = dot_nn(probs[...], picked_grads)
        if head == 0:
            key_sum[...], value_sum[...] = key_part, value_part
        else:
            key_sum[...] += key_part
            value_sum[...] += value_part
        query_rows_t.append(dot_nn(keys_t[plan.lead + low : plan.lead + high, :], slopes[...]))
        row = lax.broadcasted_iota(jnp.int32, (plan.rows, plan.rows), 0)
        column = lax.broadcasted_iota(jnp.int32, (plan.rows, plan.rows), 1)
        flip = (row + column == plan.rows - 1).astype(jnp.float32)
        flipped = jnp.dot(flip, sums[...], precision=highest, preferred_element_type=jnp.float32)
        skewed = pltpu.roll(
            flipped, 2 * plan.length - (plan.rows - 1), 1, stride=1, stride_axis=0
        )
        bias_grad_ref[head : head + 1, :] = jnp.sum(skewed, axis=0, keepdims=True)
    send_query[...] = to_half(jnp.transpose(jnp.concatenate(query_rows_t, axis=0))).reshape(
        plan.groups, plan.rows, plan.wide
    )
    value_all, key_all = value_sum[...], key_sum[...]
    low, gap = plan.pair - plan.wide, plan.wide - (plan.pair - plan.wide)
    middle = jnp.where(
        lanes_between((plan.length, gap), 0, plan.width - low), value_all[:, low:], key_all[:, :gap]
    )
    send_pair[...] = to_half(
        jnp.concatenate([value_all[:, :low], middle, key_all[:, gap:]], axis=1)
    ).reshape(plan.cycle, plan.rows, plan.pair)
    copies = []
    for step in range(1, plan.cycle):
        to = plan.peer(c, step)
        copy = remote(
            send_pair.at[to], pair_in.at[c], pair_send.at[step], pair_recv.at[step], plan.device(to)
        )
        copy.start()
        copies.append(copy)
    for step in range(1, plan.groups):
        to = plan.peer(c, step * plan.splits)
        copy = remote(
            send_query.at[to // plan.splits],
            query_in.at[group],
            query_send.at[step],
            query_recv.at[step],
            plan.device(to),
        )
        copy.start()
        copies.append(copy)
    pair_in[c] = send_pair[c]
    query_in[group] = send_query[group]
    hidden = x_ref[...]
    gains = gain_ref[layer * 2 : layer * 2 + 1, :]
    inv_rms = lax.rsqrt(jnp.mean(hidden * hidden, axis=-1, keepdims=True) + epsilon)
    for slot in range(3):
        loads[slot].wait()
    for copy in copies:
        copy.wait()
    is_value = lanes_between((plan.rows, plan.pair), 0, plan.width)
    value_blocks, key_blocks = [], []
    for g in range(plan.groups):
        block = widen(pair_in[g * plan.splits])
        for other in range(1, plan.splits):
            block = block + widen(pair_in[g * plan.splits + other])
        value_blocks.append(jnp.where(is_value, block, 0.0))
        key_blocks.append(jnp.where(is_value, 0.0, block))
    d_values = to_half(natural(plan, value_blocks, 0))
    d_keys = to_half(natural(plan, key_blocks, plan.width))
    d_queries = to_half(
        natural(plan, [widen(query_in[g]) for g in range(plan.groups)], plan.lead)
    )
    normed_half = normed_ref[...]
    d_normed = (
        dot_nt(d_queries, weights[2]) + dot_nt(d_keys, weights[1]) + dot_nt(d_values, weights[0])
    )
    if plan.fused:
        store_shares(plan, weight_grad_ref, stage, 0, (d_queries, normed_half), (d_keys, normed_half))
        store_shares(plan, weight_grad_ref, stage, 1, (d_values, normed_half), (grad_half, attended_ref[...]))
    else:
        weight_grad_ref[0] = to_half(dot_tn(normed_half, d_queries))
        weight_grad_ref[1] = to_half(dot_tn(normed_half, d_keys))
        weight_grad_ref[2] = to_half(dot_tn(normed_half, d_values))
    d_scaled = d_normed * gains
    gain_grad_ref[...] = jnp.sum(d_normed * hidden * inv_rms, axis=0, keepdims=True)
    out_ref[...] = (
        grad
        + inv_rms * d_scaled
        - hidden * (inv_rms * inv_rms * inv_rms) * jnp.mean(d_scaled * hidden, axis=-1, keepdims=True)
    )
    for copy in extras:
        copy.wait()


def attention_backward(plan, layer, grad, cache, gains, bias_rows, wq, wk, wv, wo, extra, collective):
    f32, half = jnp.float32, jnp.bfloat16
    total = plan.groups * plan.rows
    whole = pl.BlockSpec(memory_space=VMEM)
    hbm = pl.BlockSpec(memory_space=pl.ANY)
    dma = pltpu.SemaphoreType.DMA
    hidden, normed, query, pair, heads, attended, norm = cache
    block = (plan.groups, plan.rows, plan.wide)
    pairs = (plan.cycle, plan.rows, plan.pair)
    grads_shape = (4, plan.model, plan.model)
    if plan.fused:
        grads_shape = (2, plan.chips, plan.copies, 4 * plan.share, plan.model)
    return pl.pallas_call(
        functools.partial(backward_kernel, plan, layer),
        out_shape=(
            jax.ShapeDtypeStruct((plan.rows, plan.model), f32),
            jax.ShapeDtypeStruct((1, plan.model), f32),
            jax.ShapeDtypeStruct(grads_shape, half),
            jax.ShapeDtypeStruct((plan.heads, 2 * plan.length), f32),
            jax.ShapeDtypeStruct((plan.copies,) + extra.shape, half),
        ),
        in_specs=[whole] * 10 + [hbm] * 5,
        out_specs=(whole,) * 4 + (hbm,),
        scratch_shapes=[
            VMEM((2, plan.model, plan.model) if plan.fused else (8, 128), f32),
            VMEM((4, plan.model, plan.model), half),
            VMEM((plan.tiled, plan.rows, 2 * plan.length), f32),
            VMEM((plan.rows, 2 * plan.length), f32),
            VMEM(block, half),
            VMEM(block, half),
            VMEM((plan.length, total), half),
            VMEM((plan.length, total), half),
            VMEM((plan.length, plan.wide), f32),
            VMEM((plan.length, plan.wide), f32),
            VMEM(pairs, half),
            VMEM(pairs, half),
            VMEM(block, half),
            VMEM(block, half),
            dma((4,)),
            dma((plan.groups,)),
            dma((plan.groups,)),
            dma((plan.cycle,)),
            dma((plan.cycle,)),
            dma((plan.groups,)),
            dma((plan.groups,)),
            dma((1,)),
            dma((plan.copies,)),
            dma((plan.copies,)),
        ],
        compiler_params=pltpu.CompilerParams(
            collective_id=collective, has_side_effects=True, vmem_limit_bytes=60 * 1024 * 1024
        ),
        name="attention_backward",
    )(grad, hidden, gains, bias_rows, normed, query, pair, heads, attended, norm, wq, wk, wv, wo, extra)


def smooth_act(values):
    return values * jax.nn.sigmoid(values)


def smooth_slope(values):
    sigma = jax.nn.sigmoid(values)
    return sigma * (1.0 + values * (1.0 - sigma))


def expert_kernel(
    plan,
    gain_row,
    mid_ref,
    gain_ref,
    placed_ref,
    gate_ref,
    cot_ref,
    cots_ref,
    ein_hbm,
    eout_hbm,
    extra_ref,
    output_ref,
    grad_ref,
    gain_grad_ref,
    rows_ref,
    extra_out,
    ein,
    eout,
    slabs,
    d_active,
    produced,
    d_rows,
    produced_in,
    d_rows_in,
    load_sem,
    row_send,
    row_recv,
    produced_send,
    produced_recv,
    d_row_send,
    d_row_recv,
    own_sem,
    extra_send,
    extra_recv,
):
    c, _, _ = plan.place()
    loads = []
    for e in range(plan.experts):
        load = pltpu.make_async_copy(eout_hbm.at[e], eout.at[e], load_sem.at[e])
        load.start()
        loads.append(load)
    for e in range(plan.experts):
        load = pltpu.make_async_copy(ein_hbm.at[e], ein.at[e], load_sem.at[plan.experts + e])
        load.start()
        loads.append(load)
    barrier = greet(plan, c)
    hidden = mid_ref[...]
    gains = gain_ref[gain_row : gain_row + 1, :]
    normed, inv_rms = rms_normed(hidden, gains)
    placed = placed_ref[...]
    slabs[...] = to_half(dot_nn(placed, to_half(normed))).reshape(
        plan.cycle, plan.slab, plan.model
    )
    await_greetings(plan, barrier)
    copies = start_slabs(plan, c, slabs, rows_ref, row_send, row_recv)
    extras = start_along_dp(plan, c, extra_ref, extra_out, own_sem, extra_send, extra_recv)
    count = plan.cycle * plan.capacity

    def of_expert(ref, e):
        return ref[:, e * plan.capacity : (e + 1) * plan.capacity, :].reshape(count, plan.model)

    for e in range(plan.experts):
        loads[e].wait()
        d_active[e] = dot_nt(of_expert(cots_ref, e), eout[e])
    for load in loads[plan.experts :]:
        load.wait()
    for copy in copies:
        copy.wait()
    active = []
    for e in range(plan.experts):
        pre = dot_nn(of_expert(rows_ref, e), ein[e])
        active.append(to_half(smooth_act(pre)))
        d_pre = to_half(d_active[e] * smooth_slope(pre))
        d_rows[:, e * plan.capacity : (e + 1) * plan.capacity, :] = to_half(
            dot_nt(d_pre, ein[e])
        ).reshape(plan.cycle, plan.capacity, plan.model)
    d_row_copies = start_slabs(plan, c, d_rows, d_rows_in, d_row_send, d_row_recv)
    for e in range(plan.experts):
        produced[:, e * plan.capacity : (e + 1) * plan.capacity, :] = to_half(
            dot_nn(active[e], eout[e])
        ).reshape(plan.cycle, plan.capacity, plan.model)
    produced_copies = start_slabs(plan, c, produced, produced_in, produced_send, produced_recv)
    for copy in d_row_copies:
        copy.wait()
    slots = plan.cycle * plan.slab
    d_normed = dot_tn(placed, d_rows_in[...].reshape(slots, plan.model))
    d_scaled = d_normed * gains
    gain_grad_ref[...] = jnp.sum(d_normed * hidden * inv_rms, axis=0, keepdims=True)
    grad_ref[...] = (
        cot_ref[...]
        + inv_rms * d_scaled
        - hidden * (inv_rms * inv_rms * inv_rms) * jnp.mean(d_scaled * hidden, axis=-1, keepdims=True)
    )
    for copy in produced_copies:
        copy.wait()
    output_ref[...] = hidden + gate_ref[...] * dot_tn(
        placed, produced_in[...].reshape(slots, plan.model)
    )
    for copy in extras:
        copy.wait()


def expert_layer(plan, gain_row, mid, gains, placed, gate, cot, cots, ein, eout, extra, collective):
    f32, half = jnp.float32, jnp.bfloat16
    whole = pl.BlockSpec(memory_space=VMEM)
    hbm = pl.BlockSpec(memory_space=pl.ANY)
    dma = pltpu.SemaphoreType.DMA
    slabs = (plan.cycle, plan.slab, plan.model)
    hidden_units = ein.shape[2]
    count = plan.cycle * plan.capacity
    row = jax.ShapeDtypeStruct((plan.rows, plan.model), f32)
    return pl.pallas_call(
        functools.partial(expert_kernel, plan, gain_row),
        out_shape=(
            row,
            row,
            jax.ShapeDtypeStruct((1, plan.model), f32),
            jax.ShapeDtypeStruct(slabs, half),
            jax.ShapeDtypeStruct((plan.copies,) + extra.shape, half),
        ),
        in_specs=[whole] * 6 + [hbm] * 3,
        out_specs=(whole,) * 4 + (hbm,),
        scratch_shapes=[
            VMEM(ein.shape, half),
            VMEM(eout.shape, half),
            VMEM(slabs, half),
            VMEM((plan.experts, count, hidden_units), f32),
            VMEM(slabs, half),
            VMEM(slabs, half),
            VMEM(slabs, half),
            VMEM(slabs, half),
            dma((2 * plan.experts,)),
        ]
        + [dma((plan.cycle,))] * 6
        + [dma((1,)), dma((plan.copies,)), dma((plan.copies,))],
        compiler_params=pltpu.CompilerParams(
            collective_id=collective, has_side_effects=True, vmem_limit_bytes=56 * 1024 * 1024
        ),
        name="expert_layer",
    )(mid, gains, placed, gate, cot, cots, ein, eout, extra)


def tail_kernel(
    plan,
    first_ref,
    second_ref,
    small_ref,
    normed_ref,
    grads_ref,
    rows_ref,
    cots_ref,
    din_hbm,
    dout_hbm,
    ein_hbm,
    eout_hbm,
    first_out,
    second_out,
    dense_out,
    small_out,
    ein_grad,
    eout_grad,
    din,
    dout,
    ein,
    eout,
    first_half,
    second_half,
    dense,
    dense_half,
    first_sum,
    second_sum,
    dense_sum,
    first_part,
    second_part,
    dense_part,
    first_row,
    second_row,
    first_in,
    second_in,
    small_half,
    small_sum,
    small_part,
    small_row,
    small_in,
    load_sem,
    pair_send,
    pair_recv,
    plane_send,
    plane_recv,
    line_send,
    line_recv,
):
    c, _, _ = plan.place()
    core, chip = lax.rem(c, 2), c // 2
    me = lax.axis_index("dp")
    partner = plan.device(c + 1 - 2 * core)
    part = din.shape[1]
    columns = pl.ds(pl.multiple_of(me * part, part), part)
    sources = [(din_hbm.at[:, columns], din), (dout_hbm.at[columns, :], dout)]
    sources += [(ein_hbm.at[:, :, columns], ein), (eout_hbm.at[:, columns, :], eout)]
    loads = []
    for slot, (source, target) in enumerate(sources):
        load = pltpu.make_async_copy(source, target, load_sem.at[slot])
        load.start()
        loads.append(load)
    barrier = pltpu.get_barrier_semaphore()
    pl.semaphore_signal(barrier, inc=1, device_id=partner, device_id_type=MESH)
    chips = [lax.rem(chip + step, plan.chips) for step in range(plan.chips)]
    lines = [lax.rem(me + step, plan.copies) for step in range(plan.copies)]
    for step in range(1, plan.chips):
        to = plan.device(2 * chips[step] + core)
        pl.semaphore_signal(barrier, inc=1, device_id=to, device_id_type=MESH)
    for step in range(1, plan.copies):
        to = plan.copy_device(c, lines[step])
        pl.semaphore_signal(barrier, inc=1, device_id=to, device_id_type=MESH)
    pl.semaphore_wait(barrier, 1 + plan.chips - 1 + plan.copies - 1)

    def to_partner(slot, source, target):
        copy = remote(source, target, pair_send.at[slot], pair_recv.at[slot], partner)
        copy.start()
        return copy

    def to_chips(slot, source, target):
        copies = []
        for step in range(1, plan.chips):
            at = slot * plan.chips + step
            copy = remote(
                source.at[chips[step]] if slot < 3 else source,
                target.at[step],
                plane_send.at[at],
                plane_recv.at[at],
                plan.device(2 * chips[step] + core),
            )
            copy.start()
            copies.append(copy)
        return copies

    def to_lines(slot, source, target):
        copies = []
        for step in range(1, plan.copies):
            at = slot * plan.copies + step
            copy = remote(
                source.at[lines[step]] if slot < 2 else source,
                target.at[step],
                line_send.at[at],
                line_recv.at[at],
                plan.copy_device(c, lines[step]),
            )
            copy.start()
            copies.append(copy)
        return copies

    small_pair = to_partner(3, small_ref, small_half)
    first_pair = to_partner(0, first_ref.at[1 - core], first_half)
    second_pair = to_partner(1, second_ref.at[1 - core], second_half)

    loads[0].wait()
    loads[1].wait()
    count = plan.copies * plan.rows
    normed = normed_ref[...].reshape(count, plan.model)
    grads = grads_ref[...].reshape(count, plan.model)
    pre = dot_nn(normed, din[...])
    active = to_half(smooth_act(pre))
    d_pre = to_half(dot_nt(grads, dout[...]) * smooth_slope(pre))
    share = part // plan.cycle
    shape = (plan.chips, 2, share, plan.model)
    in_grad = to_half(dot_tn(d_pre, normed)).reshape(shape)
    out_grad = to_half(dot_tn(active, grads)).reshape(shape)
    for side in range(2):
        dense[side, :, :share, :] = in_grad[:, side]
        dense[side, :, share:, :] = out_grad[:, side]
    dense_pair = to_partner(2, dense.at[1 - core], dense_half)

    small_pair.wait()
    small_sum[...] = small_ref[...] + small_half[...]
    small_plane = to_chips(3, small_sum, small_part)

    def join(mine, half, total):
        def one(i, carry):
            total[i] = to_half(widen(mine[core, i]) + widen(half[i]))
            return carry

        lax.fori_loop(0, plan.chips, one, 0)

    first_pair.wait()
    join(first_ref, first_half, first_sum)
    first_plane = to_chips(0, first_sum, first_part)
    second_pair.wait()
    join(second_ref, second_half, second_sum)
    second_plane = to_chips(1, second_sum, second_part)
    dense_pair.wait()
    join(dense, dense_half, dense_sum)
    dense_plane = to_chips(2, dense_sum, dense_part)

    loads[2].wait()
    loads[3].wait()
    slots = plan.copies * plan.cycle * plan.capacity
    for e in range(plan.experts):
        picked = slice(e * plan.capacity, (e + 1) * plan.capacity)
        rows = rows_ref[:, picked, :].reshape(slots, plan.model)
        cots = cots_ref[:, picked, :].reshape(slots, plan.model)
        pre = dot_nn(rows, ein[e])
        active = to_half(smooth_act(pre))
        d_pre = to_half(dot_nt(cots, eout[e]) * smooth_slope(pre))
        ein_grad[e] = dot_tn(rows, d_pre)
        eout_grad[e] = dot_tn(active, cots)

    for copy in small_plane:
        copy.wait()
    total = small_sum[...]
    for step in range(1, plan.chips):
        total = total + small_part[step]
    small_row[...] = total
    small_line = to_lines(2, small_row, small_in)

    def gather(total, part_ref):
        value = widen(total[chip])
        for step in range(1, plan.chips):
            value = value + widen(part_ref[step])
        return value

    def finish(row, row_in, out):
        value = widen(row[me])
        for step in range(1, plan.copies):
            value = value + widen(row_in[step])
        out[...] = value

    for copy in first_plane:
        copy.wait()
    first_row[...] = to_half(gather(first_sum, first_part))
    first_line = to_lines(0, first_row, first_in)
    for copy in second_plane:
        copy.wait()
    second_row[...] = to_half(gather(second_sum, second_part))
    second_line = to_lines(1, second_row, second_in)
    for copy in dense_plane:
        copy.wait()
    dense_out[...] = gather(dense_sum, dense_part)
    for copy in small_line:
        copy.wait()
    total = small_row[...]
    for step in range(1, plan.copies):
        total = total + small_in[step]
    small_out[...] = total
    for copy in first_line:
        copy.wait()
    finish(first_row, first_in, first_out)
    for copy in second_line:
        copy.wait()
    finish(second_row, second_in, second_out)


def tail(plan, first, second, small, normed, grads, rows, cots, din, dout, ein, eout, collective):
    f32, half = jnp.float32, jnp.bfloat16
    whole = pl.BlockSpec(memory_space=VMEM)
    hbm = pl.BlockSpec(memory_space=pl.ANY)
    dma = pltpu.SemaphoreType.DMA
    model, part = plan.model, din.shape[1] // plan.copies
    shares, dense_rows = 4 * plan.share, 2 * part // plan.cycle
    chip_shares = (plan.chips, plan.copies, shares, model)
    chip_dense = (plan.chips, dense_rows, model)
    line = (plan.copies, shares, model)
    many = (plan.copies * plan.cycle, plan.slab, model)
    return pl.pallas_call(
        functools.partial(tail_kernel, plan),
        out_shape=(
            jax.ShapeDtypeStruct((shares, model), f32),
            jax.ShapeDtypeStruct((shares, model), f32),
            jax.ShapeDtypeStruct((dense_rows, model), f32),
            jax.ShapeDtypeStruct(small.shape, f32),
            jax.ShapeDtypeStruct((plan.experts, model, part), f32),
            jax.ShapeDtypeStruct((plan.experts, part, model), f32),
        ),
        in_specs=[whole] * 7 + [hbm] * 4,
        out_specs=(whole,) * 6,
        scratch_shapes=[
            VMEM((model, part), half),
            VMEM((part, model), half),
            VMEM((plan.experts, model, part), half),
            VMEM((plan.experts, part, model), half),
            VMEM(chip_shares, half),
            VMEM(chip_shares, half),
            VMEM((2,) + chip_dense, half),
            VMEM(chip_dense, half),
            VMEM(chip_shares, half),
            VMEM(chip_shares, half),
            VMEM(chip_dense, half),
            VMEM((plan.chips,) + line, half),
            VMEM((plan.chips,) + line, half),
            VMEM((plan.chips,) + chip_dense[1:], half),
            VMEM(line, half),
            VMEM(line, half),
            VMEM((plan.copies,) + line[1:], half),
            VMEM((plan.copies,) + line[1:], half),
            VMEM(small.shape, f32),
            VMEM(small.shape, f32),
            VMEM((plan.chips,) + small.shape, f32),
            VMEM(small.shape, f32),
            VMEM((plan.copies,) + small.shape, f32),
            dma((4,)),
            dma((4,)),
            dma((4,)),
            dma((4 * plan.chips,)),
            dma((4 * plan.chips,)),
            dma((3 * plan.copies,)),
            dma((3 * plan.copies,)),
        ],
        compiler_params=pltpu.CompilerParams(
            collective_id=collective, has_side_effects=True, vmem_limit_bytes=60 * 1024 * 1024
        ),
        name="tail",
    )(first, second, small, normed, grads, rows.reshape(many), cots.reshape(many), din, dout, ein, eout)


def rms_backward(hidden, inv_rms, gains, d_normed):
    d_scaled = d_normed * gains
    d_gains = jnp.sum(d_normed * hidden * inv_rms, axis=0)
    d_hidden = inv_rms * d_scaled - hidden * inv_rms**3 * jnp.mean(
        d_scaled * hidden, axis=-1, keepdims=True
    )
    return (d_hidden, d_gains)


def body(
    inputs,
    w_query,
    w_key,
    w_value,
    w_out,
    norm_gain,
    bias_table,
    dense_in,
    dense_out,
    expert_in,
    expert_out,
    routes,
    gate_scale,
    buckets,
    cotangent,
):
    group_rows, model_width = inputs.shape
    head_count = bias_table.shape[1]
    head_size = model_width // head_count
    bucket_count = bias_table.shape[0]
    cycle_size = lax.axis_size(("ctx", "exp"))
    local_experts = expert_in.shape[0]
    plan = Plan(
        lax.axis_size("dp"),
        cycle_size,
        lax.axis_size("exp"),
        head_count,
        head_size,
        group_rows,
        local_experts,
    )
    my_group = lax.axis_index(("ctx", "exp")) // plan.splits
    reversed_buckets = jnp.roll(buckets[::-1], 1)
    bucket_picks = (
        reversed_buckets[None, :] == jnp.arange(bucket_count, dtype=jnp.int32)[:, None]
    ).astype(jnp.float32)
    my_table = lax.dynamic_slice_in_dim(bias_table.T, my_group * plan.heads, plan.heads, 0)
    bias_rows = jnp.dot(my_table, bucket_picks, precision=highest)

    expert_total = local_experts * cycle_size
    capacity = 2 * group_rows // expert_total
    recv_rows = cycle_size * capacity
    flat_routes = routes[:, 0]
    route_hits = (
        flat_routes[:, None] == jnp.arange(expert_total, dtype=jnp.int32)[None, :]
    ).astype(jnp.int32)
    slot_order = jnp.sum((jnp.cumsum(route_hits, axis=0) - 1) * route_hits, axis=1)
    target = flat_routes * capacity + slot_order
    dispatch = (
        target[None, :] == jnp.arange(expert_total * capacity, dtype=jnp.int32)[:, None]
    ).astype(jnp.bfloat16)

    def to_owners(rows_half):
        placed = jnp.dot(dispatch, rows_half, preferred_element_type=jnp.float32)
        return lax.all_to_all(
            to_half(placed).reshape(cycle_size, local_experts, capacity, model_width),
            ("ctx", "exp"),
            split_axis=0,
            concat_axis=2,
            tiled=True,
        ).reshape(local_experts, recv_rows, model_width)

    def from_owners(produced):
        returned = lax.all_to_all(
            produced.reshape(1, local_experts, recv_rows, model_width),
            ("ctx", "exp"),
            split_axis=2,
            concat_axis=0,
            tiled=True,
        )
        return jnp.einsum(
            "sc,sd->cd",
            dispatch,
            returned.reshape(expert_total * capacity, model_width),
            preferred_element_type=jnp.float32,
        )

    attention = (w_query, w_key, w_value, w_out)
    cot_rows = to_half(gate_scale * cotangent)
    spare = jnp.zeros((16, model_width), jnp.bfloat16)
    mid_zero, *cache_zero, grad_rows = attention_forward(
        plan, 0, inputs, norm_gain, bias_rows, *attention, cot_rows, dispatch, 0
    )
    inv_rms_one = lax.rsqrt(jnp.mean(mid_zero * mid_zero, axis=-1, keepdims=True) + epsilon)
    normed_half = to_half(mid_zero * inv_rms_one * norm_gain[1])
    pre_act = jnp.dot(normed_half, dense_in, preferred_element_type=jnp.float32)
    active = to_half(smooth_act(pre_act))
    stream = mid_zero + jnp.dot(active, dense_out, preferred_element_type=jnp.float32)
    extra = grad_rows.reshape(-1, model_width) if plan.fused else spare
    mid_one, *cache_one, grad_rows_all = attention_forward(
        plan, 1, stream, norm_gain, bias_rows, *attention, extra, dispatch, 1
    )
    if plan.fused:
        output, grad_three, gains_four, rows, normed_all = expert_layer(
            plan,
            3,
            mid_one,
            norm_gain,
            dispatch,
            gate_scale,
            cotangent,
            grad_rows,
            expert_in,
            expert_out,
            normed_half,
            4,
        )
        gains_four = gains_four[0]
        extra = rows.reshape(-1, model_width)
    else:
        grad_rows = to_owners(cot_rows)
        inv_rms_three = lax.rsqrt(jnp.mean(mid_one * mid_one, axis=-1, keepdims=True) + epsilon)
        rows = to_owners(to_half(mid_one * inv_rms_three * norm_gain[3]))
        expert_pre = jnp.einsum("erd,edf->erf", rows, expert_in, preferred_element_type=jnp.float32)
        expert_active = to_half(smooth_act(expert_pre))
        produced = to_half(
            jnp.einsum(
                "erf,efd->erd", expert_active, expert_out, preferred_element_type=jnp.float32
            )
        )
        d_active = jnp.einsum(
            "erd,efd->erf", grad_rows, expert_out, preferred_element_type=jnp.float32
        )
        expert_d_pre = to_half(d_active * smooth_slope(expert_pre))
        d_rows = to_half(
            jnp.einsum("erf,edf->erd", expert_d_pre, expert_in, preferred_element_type=jnp.float32)
        )
        output = mid_one + gate_scale * from_owners(produced)
        d_hidden, gains_four = rms_backward(
            mid_one, inv_rms_three, norm_gain[3], from_owners(d_rows)
        )
        grad_three = cotangent + d_hidden
        extra = spare

    grad_two, gains_three, attn_two, bias_two, rows_all = attention_backward(
        plan, 1, grad_three, [stream] + cache_one, norm_gain, bias_rows, *attention, extra, 2
    )
    grad_half = to_half(grad_two)
    d_active = jnp.dot(grad_half, dense_out.T, preferred_element_type=jnp.float32)
    d_pre = to_half(d_active * smooth_slope(pre_act))
    d_normed = jnp.dot(d_pre, dense_in.T, preferred_element_type=jnp.float32)
    d_hidden, gains_two = rms_backward(mid_zero, inv_rms_one, norm_gain[1], d_normed)
    grad_one = grad_two + d_hidden
    extra = grad_half if plan.fused else spare
    input_grad, gains_one, attn_one, bias_one, grads_all = attention_backward(
        plan, 0, grad_one, [inputs] + cache_zero, norm_gain, bias_rows, *attention, extra, 3
    )

    my_table_grad = jnp.dot(bucket_picks, (bias_one + bias_two).T, precision=highest)
    table_grad = lax.dynamic_update_slice(
        jnp.zeros((bucket_count, head_count), jnp.float32),
        my_table_grad,
        (0, my_group * plan.heads),
    ).reshape(bucket_count * head_count)
    gains_all = jnp.stack([gains_one[0], gains_two, gains_three[0], gains_four])
    everyone = ("dp", "ctx", "exp")
    if plan.fused:
        table_row = jnp.pad(table_grad, (0, model_width - bucket_count * head_count))
        small = jnp.concatenate([gains_all, table_row[None], jnp.zeros((3, model_width), jnp.float32)])
        share_two, share_one, dense_share, small, grad_ein, grad_eout = tail(
            plan,
            attn_two,
            attn_one,
            small,
            normed_all,
            grads_all,
            rows_all,
            grad_rows_all,
            dense_in,
            dense_out,
            expert_in,
            expert_out,
            5,
        )
        share = plan.share
        place = lax.axis_index(everyone)
        attn = jnp.stack([share_one, share_two]).reshape(2, 4, share, model_width)
        attn = jnp.transpose(attn, (1, 0, 3, 2))
        gains = lax.dynamic_slice_in_dim(small[:4], place * share, share, 1)
        table_share = bucket_count * head_count // (plan.copies * plan.cycle)
        table = lax.dynamic_slice_in_dim(small[4], place * table_share, table_share, 0)
        half_rows = dense_share.shape[0] // 2
        din, dout = dense_share[:half_rows].T, dense_share[half_rows:]
    else:
        grad_dout = jnp.dot(active.T, grad_half, preferred_element_type=jnp.float32)
        grad_din = jnp.dot(normed_half.T, d_pre, preferred_element_type=jnp.float32)
        grad_ein = jnp.einsum("erd,erf->edf", rows, expert_d_pre, preferred_element_type=jnp.float32)
        grad_eout = jnp.einsum(
            "erf,erd->efd", expert_active, grad_rows, preferred_element_type=jnp.float32
        )
        grad_ein = lax.psum_scatter(to_half(grad_ein), "dp", scatter_dimension=2, tiled=True)
        grad_eout = lax.psum_scatter(to_half(grad_eout), "dp", scatter_dimension=1, tiled=True)
        grad_ein, grad_eout = widen(grad_ein), widen(grad_eout)
        attn = lax.psum_scatter(
            jnp.stack([attn_one, attn_two], axis=1), everyone, scatter_dimension=3, tiled=True
        ).astype(jnp.float32)
        gains = lax.psum_scatter(gains_all, everyone, scatter_dimension=1, tiled=True)
        table = lax.psum_scatter(table_grad, everyone, scatter_dimension=0, tiled=True)
        din = lax.psum_scatter(to_half(grad_din), everyone, scatter_dimension=1, tiled=True)
        dout = lax.psum_scatter(to_half(grad_dout), everyone, scatter_dimension=0, tiled=True)
        din, dout = din.astype(jnp.float32), dout.astype(jnp.float32)
    return (
        output,
        input_grad,
        attn[0],
        attn[1],
        attn[2],
        attn[3],
        gains,
        table,
        din,
        dout,
        grad_ein,
        grad_eout,
    )


def solution(mesh):
    in_specs = (
        P(("dp", "ctx", "exp"), None),
        P(),
        P(),
        P(),
        P(),
        P(),
        P(),
        P(),
        P(),
        P(("ctx", "exp"), None, None),
        P(("ctx", "exp"), None, None),
        P(("dp", "ctx", "exp"), None),
        P(("dp", "ctx", "exp"), None),
        P(),
        P(("dp", "ctx", "exp"), None),
    )
    out_specs = (
        P(("dp", "ctx", "exp"), None),
        P(("dp", "ctx", "exp"), None),
        P(None, None, ("dp", "ctx", "exp")),
        P(None, None, ("dp", "ctx", "exp")),
        P(None, None, ("dp", "ctx", "exp")),
        P(None, None, ("dp", "ctx", "exp")),
        P(None, ("dp", "ctx", "exp")),
        P(("dp", "ctx", "exp")),
        P(None, ("dp", "ctx", "exp")),
        P(("dp", "ctx", "exp"), None),
        P(("ctx", "exp"), None, "dp"),
        P(("ctx", "exp"), "dp", None),
    )
    return jax.shard_map(body, mesh=mesh, in_specs=in_specs, out_specs=out_specs, check_vma=False)
```

```python
import functools

import jax
import jax.numpy as jnp
from jax import lax
from jax.experimental import pallas as pl
from jax.experimental.pallas import tpu as pltpu
from jax.sharding import PartitionSpec as P

epsilon = 1e-06
highest = lax.Precision.HIGHEST
MESH = pl.DeviceIdType.MESH
VMEM = pltpu.VMEM


def to_half(values):
    return values.astype(jnp.bfloat16)


def widen(values):
    return values.astype(jnp.float32)


def dot_nn(a, b):
    return jnp.dot(a, b, preferred_element_type=jnp.float32)


def dot_nt(a, b):
    return lax.dot_general(a, b, (((1,), (1,)), ((), ())), preferred_element_type=jnp.float32)


def dot_tn(a, b):
    return lax.dot_general(a, b, (((0,), (0,)), ((), ())), preferred_element_type=jnp.float32)


def rotate(values, shift):
    width = values.shape[-1]
    shift = shift % width
    return values if shift == 0 else pltpu.roll(values, shift, values.ndim - 1)


def pad_lanes(values, width):
    if values.shape[1] == width:
        return values
    zeros = jnp.zeros((values.shape[0], width - values.shape[1]), values.dtype)
    return jnp.concatenate([values, zeros], axis=1)


class Plan:
    def __init__(self, copies, cycle, exp_size, head_count, head_size, rows, experts):
        self.copies, self.cycle, self.exp_size, self.rows = copies, cycle, exp_size, rows
        groups = 1
        while cycle % (groups * 2) == 0 and head_count % (groups * 2) == 0:
            groups *= 2
        self.groups, self.splits = groups, cycle // groups
        self.heads, self.head_size = head_count // groups, head_size
        self.width = self.heads * head_size
        self.model = head_count * head_size
        self.length = cycle * rows
        self.wide = -(-self.width // 128) * 128
        self.lead = self.wide - self.width
        self.pair = 2 * self.width
        self.tiled = self.heads if self.heads * rows * self.length * 8 <= 4 << 20 else 1
        self.chips = cycle // 2
        self.share = self.model // (copies * cycle)
        self.experts = experts
        self.capacity = 2 * rows // (experts * cycle)
        self.slab = experts * self.capacity
        self.fused = (
            self.splits == 2
            and self.groups == copies
            and self.capacity % 16 == 0
            and (copies * self.share) % 16 == 0
            and self.width * copies == self.model
            and self.width + self.width % 128 <= self.wide
        )
        assert self.pair % 128 == 0 and self.pair - self.wide == self.width - self.lead

    def window(self, group):
        return group * self.width // 128 * 128

    def place(self):
        c = lax.axis_index("ctx") * self.exp_size + lax.axis_index("exp")
        return c, c // self.splits, lax.rem(c, self.splits)

    def device(self, c):
        return (lax.axis_index("dp"), c // self.exp_size, lax.rem(c, self.exp_size))

    def peer(self, c, step):
        return lax.rem(c + step, self.cycle)

    def copy_device(self, c, other):
        return (other, c // self.exp_size, lax.rem(c, self.exp_size))


def greet(plan, c):
    barrier = pltpu.get_barrier_semaphore()
    for step in range(1, plan.cycle):
        pl.semaphore_signal(
            barrier, inc=1, device_id=plan.device(plan.peer(c, step)), device_id_type=MESH
        )
    me = lax.axis_index("dp")
    for step in range(1, plan.copies):
        other = lax.rem(me + step, plan.copies)
        pl.semaphore_signal(
            barrier, inc=1, device_id=plan.copy_device(c, other), device_id_type=MESH
        )
    return barrier


def await_greetings(plan, barrier):
    pl.semaphore_wait(barrier, plan.cycle - 1 + plan.copies - 1)


def start_along_dp(plan, c, source, target, own_sem, send, recv):
    me = lax.axis_index("dp")
    own = pltpu.make_async_copy(source, target.at[me], own_sem.at[0])
    own.start()
    copies = [own]
    for step in range(1, plan.copies):
        other = lax.rem(me + step, plan.copies)
        copy = remote(
            source, target.at[me], send.at[step], recv.at[step], plan.copy_device(c, other)
        )
        copy.start()
        copies.append(copy)
    return copies


def start_slabs(plan, c, source, target, send, recv):
    copies = []
    for step in range(1, plan.cycle):
        to = plan.peer(c, step)
        copy = remote(source.at[to], target.at[c], send.at[step], recv.at[step], plan.device(to))
        copy.start()
        copies.append(copy)
    target[c] = source[c]
    return copies


def rms_normed(hidden, gains):
    inv_rms = lax.rsqrt(jnp.mean(hidden * hidden, axis=-1, keepdims=True) + epsilon)
    return hidden * inv_rms * gains, inv_rms


def fill_bias(plan, rows_ref, tiles, heads):
    for head in heads:
        row = jnp.broadcast_to(rows_ref[head : head + 1, :], (plan.rows, 2 * plan.length))
        tiles[head % plan.tiled] = pltpu.roll(row, 0, 1, stride=1, stride_axis=0)


def bias_part(plan, tiles, head, key_block, split):
    parts = []
    head = head % plan.tiled
    for block in range(plan.groups):
        first = plan.length + (block * plan.splits + split - key_block) * plan.rows
        parts.append(tiles[head, :, pl.ds(pl.multiple_of(first, plan.rows), plan.rows)])
    return jnp.concatenate(parts, axis=1)


def lanes_between(shape, low, high):
    lane = lax.broadcasted_iota(jnp.int32, shape, 1)
    return (lane >= low) & (lane < high)


def natural(plan, blocks, lead):
    total = None
    for group, block in enumerate(blocks):
        moved = rotate(pad_lanes(block, plan.model), group * plan.width - lead)
        total = moved if total is None else total + moved
    return total


def remote(src, dst, send, recv, device):
    return pltpu.make_async_remote_copy(
        src_ref=src, dst_ref=dst, send_sem=send, recv_sem=recv, device_id=device, device_id_type=MESH
    )


def forward_kernel(
    plan,
    layer,
    x_ref,
    gain_ref,
    bias_ref,
    wq_hbm,
    wk_hbm,
    wv_hbm,
    wo_hbm,
    mid_ref,
    normed_ref,
    query_ref,
    pair_ref,
    heads_ref,
    attended_ref,
    norm_ref,
    weights,
    tiles,
    send_pair,
    send_query,
    scores,
    probs,
    att_in,
    load_sem,
    pair_send,
    pair_recv,
    query_send,
    query_recv,
    att_send,
    att_recv,
):
    c, group, split = plan.place()
    loads = []
    for slot, source in enumerate((wv_hbm, wk_hbm, wq_hbm, wo_hbm)):
        load = pltpu.make_async_copy(source.at[layer], weights.at[slot], load_sem.at[slot])
        load.start()
        loads.append(load)
    barrier = greet(plan, c)
    hidden = x_ref[...]
    normed, _ = rms_normed(hidden, gain_ref[layer * 2 : layer * 2 + 1, :])
    normed_half = to_half(normed)
    normed_ref[...] = normed_half
    loads[0].wait()
    values = dot_nn(normed_half, weights[0])
    loads[1].wait()
    keys = dot_nn(normed_half, weights[1])
    is_value = lanes_between((plan.rows, plan.pair), 0, plan.width)
    for g in range(plan.groups):
        value_part = rotate(values, -g * plan.width)[:, : plan.pair]
        key_part = rotate(keys, (1 - g) * plan.width)[:, : plan.pair]
        send_pair[g] = to_half(jnp.where(is_value, value_part, key_part))
    await_greetings(plan, barrier)
    copies = []
    for step in range(1, plan.cycle):
        to = plan.peer(c, step)
        copy = remote(
            send_pair.at[to // plan.splits],
            pair_ref.at[c],
            pair_send.at[step],
            pair_recv.at[step],
            plan.device(to),
        )
        copy.start()
        copies.append(copy)
    loads[2].wait()
    queries = dot_nn(normed_half, weights[2])
    is_query = lanes_between((plan.rows, plan.wide), plan.lead, plan.wide)
    for g in range(plan.groups):
        query_part = rotate(queries, plan.lead - g * plan.width)[:, : plan.wide]
        send_query[g] = to_half(jnp.where(is_query, query_part, 0.0))
    for step in range(1, plan.groups):
        to = plan.peer(c, step * plan.splits)
        copy = remote(
            send_query.at[to // plan.splits],
            query_ref.at[group],
            query_send.at[step],
            query_recv.at[step],
            plan.device(to),
        )
        copy.start()
        copies.append(copy)
    pair_ref[c] = send_pair[group]
    query_ref[group] = send_query[group]
    fill_bias(plan, bias_ref, tiles, range(plan.tiled))
    for copy in copies:
        copy.wait()

    total = plan.groups * plan.rows
    queries_all = query_ref[...].reshape(total, plan.wide)
    values_t = jnp.transpose(pair_ref[...].reshape(plan.length, plan.pair)[:, : plan.wide])
    rows_t = []
    for head in range(plan.heads):
        if head >= plan.tiled:
            fill_bias(plan, bias_ref, tiles, [head])
        low = plan.lead + head * plan.head_size
        picked = jnp.where(
            lanes_between(queries_all.shape, low, low + plan.head_size), queries_all, 0
        )

        def score_block(block, top):
            part = dot_nt(pair_ref[block][:, plan.pair - plan.wide :], picked)
            part = part + bias_part(plan, tiles, head, block, split)
            scores[pl.ds(pl.multiple_of(block * plan.rows, plan.rows), plan.rows), :] = part
            return jnp.maximum(top, jnp.max(part, axis=0, keepdims=True))

        top = lax.fori_loop(0, plan.cycle, score_block, jnp.full((1, total), -1e30, jnp.float32))

        def weight_block(block, norm):
            where = pl.ds(pl.multiple_of(block * plan.rows, plan.rows), plan.rows)
            part = jnp.exp(scores[where, :] - top)
            probs[where, :] = to_half(part)
            return norm + jnp.sum(part, axis=0, keepdims=True)

        norm = lax.fori_loop(0, plan.cycle, weight_block, jnp.zeros((1, total), jnp.float32))
        norm_ref[head : head + 1, :] = top + jnp.log(norm)
        mine = values_t[head * plan.head_size : (head + 1) * plan.head_size, :]
        rows_t.append(dot_nn(mine, probs[...]) / norm)
    rows_t.append(jnp.zeros((plan.lead, total), jnp.float32))
    heads_ref[...] = to_half(jnp.transpose(jnp.concatenate(rows_t, axis=0))).reshape(
        plan.groups, plan.rows, plan.wide
    )
    copies = []
    for step in range(1, plan.groups):
        to = plan.peer(c, step * plan.splits)
        copy = remote(
            heads_ref.at[to // plan.splits],
            att_in.at[group],
            att_send.at[step],
            att_recv.at[step],
            plan.device(to),
        )
        copy.start()
        copies.append(copy)
    att_in[group] = heads_ref[group]
    loads[3].wait()
    for copy in copies:
        copy.wait()
    attended = to_half(natural(plan, [widen(att_in[g]) for g in range(plan.groups)], 0))
    attended_ref[...] = attended
    mid_ref[...] = hidden + dot_nn(attended, weights[3])


def attention_forward(plan, layer, hidden, gains, bias_rows, wq, wk, wv, wo, collective):
    f32, half = jnp.float32, jnp.bfloat16
    total = plan.groups * plan.rows
    whole = pl.BlockSpec(memory_space=VMEM)
    hbm = pl.BlockSpec(memory_space=pl.ANY)
    dma = pltpu.SemaphoreType.DMA
    return pl.pallas_call(
        functools.partial(forward_kernel, plan, layer),
        out_shape=(
            jax.ShapeDtypeStruct((plan.rows, plan.model), f32),
            jax.ShapeDtypeStruct((plan.rows, plan.model), half),
            jax.ShapeDtypeStruct((plan.groups, plan.rows, plan.wide), half),
            jax.ShapeDtypeStruct((plan.cycle, plan.rows, plan.pair), half),
            jax.ShapeDtypeStruct((plan.groups, plan.rows, plan.wide), half),
            jax.ShapeDtypeStruct((plan.rows, plan.model), half),
            jax.ShapeDtypeStruct((plan.heads, total), f32),
        ),
        in_specs=[whole, whole, whole, hbm, hbm, hbm, hbm],
        out_specs=(whole,) * 7,
        scratch_shapes=[
            VMEM((4, plan.model, plan.model), half),
            VMEM((plan.tiled, plan.rows, 2 * plan.length), f32),
            VMEM((plan.groups, plan.rows, plan.pair), half),
            VMEM((plan.groups, plan.rows, plan.wide), half),
            VMEM((plan.length, total), f32),
            VMEM((plan.length, total), half),
            VMEM((plan.groups, plan.rows, plan.wide), half),
            dma((4,)),
            dma((plan.cycle,)),
            dma((plan.cycle,)),
            dma((plan.groups,)),
            dma((plan.groups,)),
            dma((plan.groups,)),
            dma((plan.groups,)),
        ],
        compiler_params=pltpu.CompilerParams(
            collective_id=collective, has_side_effects=True, vmem_limit_bytes=56 * 1024 * 1024
        ),
        name="attention_forward",
    )(hidden, gains, bias_rows, wq, wk, wv, wo)


def backward_kernel(
    plan,
    layer,
    grad_ref,
    x_ref,
    gain_ref,
    bias_ref,
    normed_ref,
    query_ref,
    pair_ref,
    heads_ref,
    attended_ref,
    norm_ref,
    wq_hbm,
    wk_hbm,
    wv_hbm,
    wo_hbm,
    out_ref,
    gain_grad_ref,
    weight_grad_ref,
    bias_grad_ref,
    weights,
    tiles,
    sums,
    send_grad,
    grad_in,
    probs,
    slopes,
    key_sum,
    value_sum,
    send_pair,
    pair_in,
    send_query,
    query_in,
    load_sem,
    grad_send,
    grad_recv,
    pair_send,
    pair_recv,
    query_send,
    query_recv,
):
    c, group, split = plan.place()
    total = plan.groups * plan.rows
    loads = []
    for slot, source in enumerate((wv_hbm, wk_hbm, wq_hbm, wo_hbm)):
        load = pltpu.make_async_copy(source.at[layer], weights.at[slot], load_sem.at[slot])
        loads.append(load)
    for slot in (3, 0, 1, 2):
        loads[slot].start()
    barrier = greet(plan, c)
    grad = grad_ref[...]
    grad_half = to_half(grad)
    loads[3].wait()
    d_attended = dot_nt(grad_half, weights[3])
    in_group = lanes_between((plan.rows, plan.wide), 0, plan.width)
    for g in range(plan.groups):
        part = rotate(d_attended, -g * plan.width)[:, : plan.wide]
        send_grad[g] = to_half(jnp.where(in_group, part, 0.0))
    await_greetings(plan, barrier)
    copies = []
    for step in range(1, plan.groups):
        to = plan.peer(c, step * plan.splits)
        copy = remote(
            send_grad.at[to // plan.splits],
            grad_in.at[group],
            grad_send.at[step],
            grad_recv.at[step],
            plan.device(to),
        )
        copy.start()
        copies.append(copy)
    grad_in[group] = send_grad[group]
    fill_bias(plan, bias_ref, tiles, range(plan.tiled))
    weight_grad_ref[3] = to_half(dot_tn(attended_ref[...], grad_half))
    queries_all = query_ref[...].reshape(total, plan.wide)
    keys_t = jnp.transpose(
        pair_ref[...].reshape(plan.length, plan.pair)[:, plan.pair - plan.wide :]
    )
    heads_t = jnp.transpose(widen(heads_ref[...].reshape(total, plan.wide)))
    for copy in copies:
        copy.wait()
    grads_all = grad_in[...].reshape(total, plan.wide)
    grads_t = jnp.transpose(widen(grads_all))
    products_t = grads_t * heads_t
    query_rows_t = [jnp.zeros((plan.lead, total), jnp.float32)]
    for head in range(plan.heads):
        if head >= plan.tiled:
            fill_bias(plan, bias_ref, tiles, [head])
        low, high = head * plan.head_size, (head + 1) * plan.head_size
        picked_queries = jnp.where(
            lanes_between(queries_all.shape, plan.lead + low, plan.lead + high), queries_all, 0
        )
        picked_grads = jnp.where(lanes_between(grads_all.shape, low, high), grads_all, 0)
        delta = jnp.sum(products_t[low:high, :], axis=0, keepdims=True)
        log_norm = norm_ref[head : head + 1, :]
        sums[...] = jnp.zeros_like(sums)

        def slope_block(block, carry):
            where = pl.ds(pl.multiple_of(block * plan.rows, plan.rows), plan.rows)
            part = dot_nt(pair_ref[block][:, plan.pair - plan.wide :], picked_queries)
            part = part + bias_part(plan, tiles, head, block, split)
            part = jnp.exp(part - log_norm)
            probs[where, :] = to_half(part)
            slope = part * (dot_nt(pair_ref[block][:, : plan.wide], picked_grads) - delta)
            slopes[where, :] = to_half(slope)
            for b in range(plan.groups):
                first = plan.length + (b * plan.splits + split - block) * plan.rows
                at = pl.ds(pl.multiple_of(first, plan.rows), plan.rows)
                sums[:, at] += slope[:, b * plan.rows : (b + 1) * plan.rows]
            return carry

        lax.fori_loop(0, plan.cycle, slope_block, 0)
        key_part = dot_nn(slopes[...], picked_queries)
        value_part = dot_nn(probs[...], picked_grads)
        if head == 0:
            key_sum[...], value_sum[...] = key_part, value_part
        else:
            key_sum[...] += key_part
            value_sum[...] += value_part
        query_rows_t.append(dot_nn(keys_t[plan.lead + low : plan.lead + high, :], slopes[...]))
        row = lax.broadcasted_iota(jnp.int32, (plan.rows, plan.rows), 0)
        column = lax.broadcasted_iota(jnp.int32, (plan.rows, plan.rows), 1)
        flip = (row + column == plan.rows - 1).astype(jnp.float32)
        flipped = jnp.dot(flip, sums[...], precision=highest, preferred_element_type=jnp.float32)
        skewed = pltpu.roll(
            flipped, 2 * plan.length - (plan.rows - 1), 1, stride=1, stride_axis=0
        )
        bias_grad_ref[head : head + 1, :] = jnp.sum(skewed, axis=0, keepdims=True)
    send_query[...] = to_half(jnp.transpose(jnp.concatenate(query_rows_t, axis=0))).reshape(
        plan.groups, plan.rows, plan.wide
    )
    value_all, key_all = value_sum[...], key_sum[...]
    low, gap = plan.pair - plan.wide, plan.wide - (plan.pair - plan.wide)
    middle = jnp.where(
        lanes_between((plan.length, gap), 0, plan.width - low), value_all[:, low:], key_all[:, :gap]
    )
    send_pair[...] = to_half(
        jnp.concatenate([value_all[:, :low], middle, key_all[:, gap:]], axis=1)
    ).reshape(plan.cycle, plan.rows, plan.pair)
    copies = []
    for step in range(1, plan.cycle):
        to = plan.peer(c, step)
        copy = remote(
            send_pair.at[to], pair_in.at[c], pair_send.at[step], pair_recv.at[step], plan.device(to)
        )
        copy.start()
        copies.append(copy)
    for step in range(1, plan.groups):
        to = plan.peer(c, step * plan.splits)
        copy = remote(
            send_query.at[to // plan.splits],
            query_in.at[group],
            query_send.at[step],
            query_recv.at[step],
            plan.device(to),
        )
        copy.start()
        copies.append(copy)
    pair_in[c] = send_pair[c]
    query_in[group] = send_query[group]
    hidden = x_ref[...]
    gains = gain_ref[layer * 2 : layer * 2 + 1, :]
    inv_rms = lax.rsqrt(jnp.mean(hidden * hidden, axis=-1, keepdims=True) + epsilon)
    for slot in range(3):
        loads[slot].wait()
    for copy in copies:
        copy.wait()
    is_value = lanes_between((plan.rows, plan.pair), 0, plan.width)
    value_blocks, key_blocks = [], []
    for g in range(plan.groups):
        block = widen(pair_in[g * plan.splits])
        for other in range(1, plan.splits):
            block = block + widen(pair_in[g * plan.splits + other])
        value_blocks.append(jnp.where(is_value, block, 0.0))
        key_blocks.append(jnp.where(is_value, 0.0, block))
    d_values = to_half(natural(plan, value_blocks, 0))
    d_keys = to_half(natural(plan, key_blocks, plan.width))
    d_queries = to_half(
        natural(plan, [widen(query_in[g]) for g in range(plan.groups)], plan.lead)
    )
    normed_half = normed_ref[...]
    d_normed = (
        dot_nt(d_queries, weights[2]) + dot_nt(d_keys, weights[1]) + dot_nt(d_values, weights[0])
    )
    weight_grad_ref[0] = to_half(dot_tn(normed_half, d_queries))
    weight_grad_ref[1] = to_half(dot_tn(normed_half, d_keys))
    weight_grad_ref[2] = to_half(dot_tn(normed_half, d_values))
    d_scaled = d_normed * gains
    gain_grad_ref[...] = jnp.sum(d_normed * hidden * inv_rms, axis=0, keepdims=True)
    out_ref[...] = (
        grad
        + inv_rms * d_scaled
        - hidden * (inv_rms * inv_rms * inv_rms) * jnp.mean(d_scaled * hidden, axis=-1, keepdims=True)
    )


def attention_backward(plan, layer, grad, cache, gains, bias_rows, wq, wk, wv, wo, collective):
    f32, half = jnp.float32, jnp.bfloat16
    total = plan.groups * plan.rows
    whole = pl.BlockSpec(memory_space=VMEM)
    hbm = pl.BlockSpec(memory_space=pl.ANY)
    dma = pltpu.SemaphoreType.DMA
    hidden, normed, query, pair, heads, attended, norm = cache
    block = (plan.groups, plan.rows, plan.wide)
    pairs = (plan.cycle, plan.rows, plan.pair)
    return pl.pallas_call(
        functools.partial(backward_kernel, plan, layer),
        out_shape=(
            jax.ShapeDtypeStruct((plan.rows, plan.model), f32),
            jax.ShapeDtypeStruct((1, plan.model), f32),
            jax.ShapeDtypeStruct((4, plan.model, plan.model), half),
            jax.ShapeDtypeStruct((plan.heads, 2 * plan.length), f32),
        ),
        in_specs=[whole] * 10 + [hbm] * 4,
        out_specs=(whole,) * 4,
        scratch_shapes=[
            VMEM((4, plan.model, plan.model), half),
            VMEM((plan.tiled, plan.rows, 2 * plan.length), f32),
            VMEM((plan.rows, 2 * plan.length), f32),
            VMEM(block, half),
            VMEM(block, half),
            VMEM((plan.length, total), half),
            VMEM((plan.length, total), half),
            VMEM((plan.length, plan.wide), f32),
            VMEM((plan.length, plan.wide), f32),
            VMEM(pairs, half),
            VMEM(pairs, half),
            VMEM(block, half),
            VMEM(block, half),
            dma((4,)),
            dma((plan.groups,)),
            dma((plan.groups,)),
            dma((plan.cycle,)),
            dma((plan.cycle,)),
            dma((plan.groups,)),
            dma((plan.groups,)),
        ],
        compiler_params=pltpu.CompilerParams(
            collective_id=collective, has_side_effects=True, vmem_limit_bytes=60 * 1024 * 1024
        ),
        name="attention_backward",
    )(grad, hidden, gains, bias_rows, normed, query, pair, heads, attended, norm, wq, wk, wv, wo)


def smooth_act(values):
    return values * jax.nn.sigmoid(values)


def smooth_slope(values):
    sigma = jax.nn.sigmoid(values)
    return sigma * (1.0 + values * (1.0 - sigma))


class Links:
    def __init__(self, plan):
        self.plan = plan
        self.c, self.chip, self.core = plan.place()
        self.me = lax.axis_index("dp")
        self.lead = pl.multiple_of(lax.rem(self.chip * plan.width, 128), 64)
        self.first = pl.multiple_of(self.chip * plan.width // 128 * 128, 128)

    def pair(self):
        return self.plan.device(self.c + 1 - 2 * self.core)

    def at_chip(self, step):
        return lax.rem(self.chip + step, self.plan.groups)

    def chip_device(self, step):
        return self.plan.device(2 * self.at_chip(step) + self.core)

    def at_dp(self, step):
        return lax.rem(self.me + step, self.plan.copies)

    def dp_device(self, step):
        return self.plan.copy_device(self.c, self.at_dp(step))

    def head_lanes(self, shape, head):
        low = self.lead + head * self.plan.head_size
        return lanes_between(shape, low, low + self.plan.head_size)

    def head_rows(self, head):
        return pl.ds(
            pl.multiple_of(self.lead + head * self.plan.head_size, self.plan.head_size),
            self.plan.head_size,
        )


def wait_all(copies):
    for copy in copies:
        copy.wait()


def local(source, target, sem):
    copy = pltpu.make_async_copy(source, target, sem)
    copy.start()
    return copy


def started(copy):
    copy.start()
    return copy


def to_lines(links, source, target, send, recv, whole=False):
    copies = []
    for step in range(1, links.plan.copies):
        part = source if whole else source.at[links.at_dp(step)]
        copies.append(
            started(
                remote(part, target.at[step], send.at[step], recv.at[step], links.dp_device(step))
            )
        )
    return copies


def to_all_dp(links, source, target, send, recv):
    return [
        started(
            remote(
                source, target.at[links.me], send.at[step], recv.at[step], links.dp_device(step)
            )
        )
        for step in range(1, links.plan.copies)
    ]


def to_chips(links, source, target, send, recv, by_step=False, whole=False):
    copies = []
    for step in range(1, links.plan.chips):
        part = source if whole else source.at[links.at_chip(step)]
        slot = step if by_step else links.chip
        copies.append(
            started(
                remote(
                    part, target.at[slot], send.at[step], recv.at[step], links.chip_device(step)
                )
            )
        )
    return copies


def add_windows(plan, total, blocks):
    total[...] = jnp.zeros_like(total)
    for group, block in enumerate(blocks):
        first = plan.window(group)
        total[:, first : first + plan.wide] += block
    return total[...]


def bias_row_values(plan, links, table_ref, buckets_ref):
    picks = bucket_picks(table_ref.shape[0], buckets_ref)
    return lax.dot_general(
        table_ref[...],
        picks,
        (((0,), (0,)), ((), ())),
        precision=highest,
        preferred_element_type=jnp.float32,
    )


def bucket_picks(count, buckets_ref):
    shape = (count, buckets_ref.shape[1])
    hits = jnp.broadcast_to(buckets_ref[...], shape) == lax.broadcasted_iota(jnp.int32, shape, 0)
    return hits.astype(jnp.float32)


def fill_all_bias(plan, links, table_ref, buckets_ref, rows, tiles):
    rows[: table_ref.shape[1], :] = bias_row_values(plan, links, table_ref, buckets_ref)
    for head in range(plan.heads):
        row = rows[pl.ds(links.chip * plan.heads + head, 1), :]
        row = jnp.broadcast_to(row, (plan.rows, 2 * plan.length))
        tiles[head] = pltpu.roll(row, 0, 1, stride=1, stride_axis=0)


def place_tokens(plan, routes_ref):
    total = plan.experts * plan.cycle
    shape = (plan.rows, total)
    hits = (routes_ref[...] == lax.broadcasted_iota(jnp.int32, shape, 1)).astype(jnp.float32)
    square = (plan.rows, plan.rows)
    row = lax.broadcasted_iota(jnp.int32, square, 0)
    column = lax.broadcasted_iota(jnp.int32, square, 1)
    earlier = (column < row).astype(jnp.bfloat16)
    before = dot_nn(earlier, to_half(hits))
    expert = lax.broadcasted_iota(jnp.int32, shape, 1).astype(jnp.float32)
    slot = jnp.sum((before + expert * plan.capacity) * hits, axis=1, keepdims=True)
    slots = (plan.rows, total * plan.capacity)
    return (slot == lax.broadcasted_iota(jnp.int32, slots, 1).astype(jnp.float32)).astype(
        jnp.bfloat16
    )


def whole_forward_kernel(
    plan,
    x_ref,
    gain_ref,
    table_ref,
    buckets_ref,
    routes_ref,
    gate_ref,
    cot_ref,
    wq_hbm,
    wk_hbm,
    wv_hbm,
    wo_hbm,
    din_hbm,
    dout_hbm,
    ein_hbm,
    eout_hbm,
    output_ref,
    grad_ref,
    gain_grad_ref,
    stream_ref,
    mid_ref,
    normed_all,
    key_all,
    value_all,
    query_all,
    heads_all,
    attended_ref,
    norm_ref,
    dense_normed,
    cots_in,
    rows_in,
    cots_hbm,
    wq,
    wk,
    wv,
    wo,
    up,
    down,
    bias_rows,
    tiles,
    value_t,
    scores,
    probs,
    heads_t,
    att_in,
    natural_sum,
    cots_out,
    rows_out,
    d_active,
    produced,
    d_rows,
    produced_in,
    d_rows_in,
    load_sem,
    near_send,
    near_recv,
    far_send,
    far_recv,
    att_send,
    att_recv,
    cots_send,
    cots_recv,
    rows_send,
    rows_recv,
    produced_send,
    produced_recv,
    d_rows_send,
    d_rows_recv,
    line_send,
    line_recv,
    own_sem,
):
    links = Links(plan)
    c, chip, core = links.c, links.chip, links.core
    columns = pl.ds(links.first, plan.wide)
    loads = {}

    def load(name, source, target):
        loads[name] = local(source, target, load_sem.at[len(loads)])

    for layer in range(2):
        for name, source, target in (("k", wk_hbm, wk), ("v", wv_hbm, wv), ("q", wq_hbm, wq)):
            load((name, layer), source.at[layer, :, columns], target.at[layer])
        load(("o", layer), wo_hbm.at[layer], wo.at[layer])
        if layer == 0:
            load("din", din_hbm, up.at[0])
            load("dout", dout_hbm, down.at[0])
    load("eout1", eout_hbm.at[1], down.at[1])
    load("ein1", ein_hbm.at[1], up.at[1])
    barrier = greet(plan, c)
    placed = place_tokens(plan, routes_ref)
    total = plan.groups * plan.rows
    done_later = []

    def project(layer, block, with_query):
        normed = normed_all[layer, block // 2, lax.rem(block, 2)]
        key_all[layer, block] = to_half(dot_nn(normed, wk[layer]))
        value_all[layer, block] = to_half(dot_nn(normed, wv[layer]))
        if with_query:
            query_all[layer, block // 2] = to_half(dot_nn(normed, wq[layer]))

    def attention(layer, hidden):
        normed, _ = rms_normed(hidden, gain_ref[layer * 2 : layer * 2 + 1, :])
        normed_all[layer, chip, core] = to_half(normed)
        if layer == 0:
            await_greetings(plan, barrier)
        own = normed_all.at[layer, chip, core]
        far = []
        for step in range(1, plan.chips):
            far.append(
                started(
                    remote(
                        own,
                        own,
                        far_send.at[layer, step],
                        far_recv.at[layer, step],
                        links.chip_device(step),
                    )
                )
            )
        near = [
            started(
                remote(own, own, near_send.at[layer, 0], near_recv.at[layer, 0], links.pair())
            )
        ]
        for name in ("k", "v", "q"):
            loads[(name, layer)].wait()
        project(layer, c, True)
        if layer == 0:
            fill_all_bias(plan, links, table_ref, buckets_ref, bias_rows, tiles)
            cots = gate_ref[...] * cot_ref[...]
            cots_out[...] = to_half(dot_tn(placed, to_half(cots))).reshape(cots_out.shape)
        near[0].wait_recv()
        project(layer, 2 * chip + 1 - core, False)
        for step in range(1, plan.chips):
            far[step - 1].wait_recv()
            from_chip = lax.rem(chip + plan.chips - step, plan.chips)
            block = normed_all.at[layer, from_chip, core]
            near.append(
                started(
                    remote(
                        block,
                        block,
                        near_send.at[layer, step],
                        near_recv.at[layer, step],
                        links.pair(),
                    )
                )
            )
            project(layer, 2 * from_chip + core, True)
        for step in range(1, plan.chips):
            near[step].wait_recv()
            from_chip = lax.rem(chip + plan.chips - step, plan.chips)
            project(layer, 2 * from_chip + 1 - core, False)
        for copy in far + near:
            copy.wait_send()
        if layer == 0:
            done_later.extend(start_slabs(plan, c, cots_out, cots_in, cots_send, cots_recv))

        queries = query_all[layer].reshape(total, plan.wide)
        value_t[...] = jnp.transpose(value_all[layer].reshape(plan.length, plan.wide))
        heads_t[...] = jnp.zeros_like(heads_t)
        for head in range(plan.heads):
            picked = jnp.where(links.head_lanes(queries.shape, head), queries, 0)

            def score_block(block, top):
                part = dot_nt(key_all[layer, block], picked)
                part = part + bias_part(plan, tiles, head, block, core)
                scores[pl.ds(pl.multiple_of(block * plan.rows, plan.rows), plan.rows), :] = part
                return jnp.maximum(top, jnp.max(part, axis=0, keepdims=True))

            top = lax.fori_loop(
                0, plan.cycle, score_block, jnp.full((1, total), -1e30, jnp.float32)
            )

            def weight_block(block, norm):
                where = pl.ds(pl.multiple_of(block * plan.rows, plan.rows), plan.rows)
                part = jnp.exp(scores[where, :] - top)
                probs[where, :] = to_half(part)
                return norm + jnp.sum(part, axis=0, keepdims=True)

            norm = lax.fori_loop(0, plan.cycle, weight_block, jnp.zeros((1, total), jnp.float32))
            norm_ref[layer, head : head + 1, :] = top + jnp.log(norm)
            mine = links.head_rows(head)
            heads_t[mine, :] = dot_nn(value_t[mine, :], probs[...]) / norm
        heads_all[layer] = to_half(jnp.transpose(heads_t[...])).reshape(
            plan.groups, plan.rows, plan.wide
        )
        copies = to_chips(
            links, heads_all.at[layer], att_in.at[layer], att_send.at[layer], att_recv.at[layer]
        )
        att_in[layer, chip] = heads_all[layer, chip]
        loads[("o", layer)].wait()
        wait_all(copies)
        attended = to_half(
            add_windows(plan, natural_sum, [widen(att_in[layer, g]) for g in range(plan.groups)])
        )
        attended_ref[layer] = attended
        return hidden + dot_nn(attended, wo[layer])

    mid = attention(0, x_ref[...])
    mid_ref[...] = mid
    wait_all(done_later)
    lines = to_all_dp(links, cots_in, cots_hbm, line_send.at[0], line_recv.at[0])
    lines.append(local(cots_in, cots_hbm.at[links.me], own_sem.at[0]))
    normed, _ = rms_normed(mid, gain_ref[1:2, :])
    normed_half = to_half(normed)
    dense_normed[links.me] = normed_half
    mine = dense_normed.at[links.me]
    lines += to_all_dp(links, mine, dense_normed, line_send.at[1], line_recv.at[1])
    loads["din"].wait()
    active = to_half(smooth_act(dot_nn(normed_half, up[0])))
    loads["dout"].wait()
    stream = mid + dot_nn(active, down[0])
    stream_ref[...] = stream
    load("eout0", eout_hbm.at[0], down.at[0])
    load("ein0", ein_hbm.at[0], up.at[0])
    mid = attention(1, stream)

    gains = gain_ref[3:4, :]
    normed, inv_rms = rms_normed(mid, gains)
    rows_out[...] = to_half(dot_tn(placed, to_half(normed))).reshape(rows_out.shape)
    copies = start_slabs(plan, c, rows_out, rows_in, rows_send, rows_recv)
    count = plan.cycle * plan.capacity

    def of_expert(ref, e):
        return ref[:, e * plan.capacity : (e + 1) * plan.capacity, :].reshape(count, plan.model)

    for e in range(plan.experts):
        loads["eout%d" % e].wait()
        d_active[e] = dot_nt(of_expert(cots_in, e), down[e])
        loads["ein%d" % e].wait()
    wait_all(copies)
    actives = []
    for e in range(plan.experts):
        pre = dot_nn(of_expert(rows_in, e), up[e])
        actives.append(to_half(smooth_act(pre)))
        d_pre = to_half(d_active[e] * smooth_slope(pre))
        d_rows[:, e * plan.capacity : (e + 1) * plan.capacity, :] = to_half(
            dot_nt(d_pre, up[e])
        ).reshape(plan.cycle, plan.capacity, plan.model)
    d_row_copies = start_slabs(plan, c, d_rows, d_rows_in, d_rows_send, d_rows_recv)
    for e in range(plan.experts):
        produced[:, e * plan.capacity : (e + 1) * plan.capacity, :] = to_half(
            dot_nn(actives[e], down[e])
        ).reshape(plan.cycle, plan.capacity, plan.model)
    produced_copies = start_slabs(plan, c, produced, produced_in, produced_send, produced_recv)
    wait_all(d_row_copies)
    slots = plan.cycle * plan.slab
    d_normed = dot_nn(placed, d_rows_in[...].reshape(slots, plan.model))
    gain_grad_ref[...] = jnp.sum(d_normed * mid * inv_rms, axis=0, keepdims=True)
    grad_ref[...] = cot_ref[...] + norm_slope(mid, inv_rms, gains, d_normed)
    wait_all(produced_copies)
    output_ref[...] = mid + gate_ref[...] * dot_nn(
        placed, produced_in[...].reshape(slots, plan.model)
    )
    wait_all(lines)


def norm_slope(hidden, inv_rms, gains, d_normed):
    d_scaled = d_normed * gains
    mean = jnp.mean(d_scaled * hidden, axis=-1, keepdims=True)
    return inv_rms * d_scaled - hidden * (inv_rms * inv_rms * inv_rms) * mean


def whole_forward(plan, x, gains, table, buckets, routes, gate, cot, weights, dense, experts):
    f32, half = jnp.float32, jnp.bfloat16
    whole = pl.BlockSpec(memory_space=VMEM)
    hbm = pl.BlockSpec(memory_space=pl.ANY)
    dma = pltpu.SemaphoreType.DMA
    total = plan.groups * plan.rows
    units = dense[0].shape[1]
    slabs = (plan.cycle, plan.slab, plan.model)
    window = (plan.rows, plan.wide)
    row = (plan.rows, plan.model)
    outs = [
        (row, f32),
        (row, f32),
        ((1, plan.model), f32),
        (row, f32),
        (row, f32),
        ((2, plan.chips, 2) + row, half),
        ((2, plan.cycle) + window, half),
        ((2, plan.cycle) + window, half),
        ((2, plan.groups) + window, half),
        ((2, plan.groups) + window, half),
        ((2,) + row, half),
        ((2, plan.heads, total), f32),
        ((plan.copies,) + row, half),
        (slabs, half),
        (slabs, half),
        ((plan.copies,) + slabs, half),
    ]
    cycle_sems = [dma((plan.cycle,))] * 2
    return pl.pallas_call(
        functools.partial(whole_forward_kernel, plan),
        out_shape=tuple(jax.ShapeDtypeStruct(*out) for out in outs),
        in_specs=[whole] * 7 + [hbm] * 8,
        out_specs=(whole,) * 15 + (hbm,),
        scratch_shapes=[
            VMEM((2, plan.model, plan.wide), half),
            VMEM((2, plan.model, plan.wide), half),
            VMEM((2, plan.model, plan.wide), half),
            VMEM((2, plan.model, plan.model), half),
            VMEM((2, plan.model, units), half),
            VMEM((2, units, plan.model), half),
            VMEM((16, 2 * plan.length), f32),
            VMEM((plan.heads, plan.rows, 2 * plan.length), f32),
            VMEM((plan.wide, plan.length), half),
            VMEM((plan.length, total), f32),
            VMEM((plan.length, total), half),
            VMEM((plan.wide, total), f32),
            VMEM((2, plan.groups) + window, half),
            VMEM(row, f32),
            VMEM(slabs, half),
            VMEM(slabs, half),
            VMEM((plan.experts, plan.cycle * plan.capacity, units), f32),
            VMEM(slabs, half),
            VMEM(slabs, half),
            VMEM(slabs, half),
            VMEM(slabs, half),
            dma((14,)),
            dma((2, plan.chips)),
            dma((2, plan.chips)),
            dma((2, plan.chips)),
            dma((2, plan.chips)),
            dma((2, plan.chips)),
            dma((2, plan.chips)),
        ]
        + cycle_sems * 4
        + [dma((2, plan.copies)), dma((2, plan.copies)), dma((1,))],
        compiler_params=pltpu.CompilerParams(
            collective_id=0, has_side_effects=True, vmem_limit_bytes=60 * 1024 * 1024
        ),
        name="whole_forward",
    )(x, gains, table, buckets, routes, gate, cot, *weights, *dense, *experts)


def whole_backward_kernel(
    plan,
    grad_ref,
    stream_ref,
    x_ref,
    mid_ref,
    gain_ref,
    last_gain_ref,
    table_ref,
    buckets_ref,
    attended_ref,
    norm_ref,
    normed_z,
    normed_hbm,
    key_hbm,
    value_hbm,
    query_hbm,
    heads_hbm,
    cots_hbm,
    rows_hbm,
    wq_hbm,
    wk_hbm,
    wv_hbm,
    wo_hbm,
    din_hbm,
    dout_hbm,
    ein_hbm,
    eout_hbm,
    input_grad_ref,
    three_ref,
    out_ref,
    dense_ref,
    small_ref,
    ein_grad,
    eout_grad,
    normed_all,
    key_all,
    value_all,
    query_all,
    heads_all,
    weights,
    up,
    down,
    cots_all,
    rows_all,
    bias_rows,
    tiles,
    sums,
    grad_out,
    grad_in,
    key_t,
    products,
    picked_queries,
    picked_grads,
    key_part,
    value_part,
    pair_out,
    pair_in,
    own_out,
    own_in,
    query_t,
    query_out,
    query_in,
    natural_sum,
    stage,
    o_half,
    o_sum,
    o_part,
    o_row,
    o_in,
    three_pair,
    three_half,
    three_sum,
    three_part,
    three_in,
    grads_z,
    dense_pair,
    dense_half,
    dense_part,
    small_mine,
    small_half,
    small_sum,
    small_part,
    small_row,
    small_in,
    load_sem,
    own_sem,
    grad_send,
    grad_recv,
    pair_send,
    pair_recv,
    back_send,
    back_recv,
    query_send,
    query_recv,
    chain_send,
    chain_recv,
    plane_send,
    plane_recv,
    line_send,
    line_recv,
):
    links = Links(plan)
    c, chip, core, me = links.c, links.chip, links.core, links.me
    loads = {}

    def load(name, source, target):
        loads[name] = local(source, target, load_sem.at[len(loads)])

    def load_layer(layer):
        for name, source, target in (
            ("query", query_hbm, query_all),
            ("key", key_hbm, key_all),
            ("value", value_hbm, value_all),
            ("heads", heads_hbm, heads_all),
            ("normed", normed_hbm, normed_all),
        ):
            load((name, layer), source.at[layer], target)

    part = up.shape[1] // plan.copies
    mine = pl.ds(pl.multiple_of(me * part, part), part)
    load(("o", 1), wo_hbm.at[1], weights.at[3])
    load_layer(1)
    for slot, name, source in ((0, "v", wv_hbm), (1, "k", wk_hbm), (2, "q", wq_hbm)):
        load((name, 1), source.at[1], weights.at[slot])
    load("up", din_hbm, up)
    load("down", dout_hbm, down)
    load("cots", cots_hbm, cots_all)
    rows_own = local(rows_hbm, rows_all.at[me], own_sem.at[0])

    barrier = pltpu.get_barrier_semaphore()
    others = [links.pair()]
    others += [links.chip_device(step) for step in range(1, plan.chips)]
    others += [links.dp_device(step) for step in range(1, plan.copies)]
    for other in others:
        pl.semaphore_signal(barrier, inc=1, device_id=other, device_id_type=MESH)

    total = plan.groups * plan.rows
    rows_lines = []
    share = plan.share

    def o_start(layer, grad_half):
        stage[: plan.model, :] = dot_tn(grad_half, attended_ref[layer])

        def one(i, carry):
            side, to = lax.rem(i, 2), i // 2
            pieces = []
            for d in range(plan.copies):
                first = (d * plan.cycle + i) * share
                pieces.append(stage[pl.ds(pl.multiple_of(first, 8), share), :])
            dense_pair[side, to, : plan.copies * share, :] = to_half(jnp.concatenate(pieces, axis=0))
            return carry

        lax.fori_loop(0, plan.cycle, one, 0)
        return started(
            remote(
                dense_pair.at[1 - core, :, : plan.copies * share, :],
                o_half.at[layer],
                chain_send.at[layer, 0],
                chain_recv.at[layer, 0],
                links.pair(),
            )
        )

    def o_plane(layer, copy):
        copy.wait()
        o_sum[...] = to_half(
            widen(dense_pair[core, :, : plan.copies * share, :]) + widen(o_half[layer])
        )
        return to_chips(
            links,
            o_sum,
            o_part.at[layer],
            plane_send.at[layer],
            plane_recv.at[layer],
            by_step=True,
        )

    def o_line(layer, copies):
        wait_all(copies)
        value = widen(o_sum[chip])
        for step in range(1, plan.chips):
            value = value + widen(o_part[layer, step])
        pad = jnp.zeros((o_row.shape[2] - share, plan.model), jnp.float32)
        for d in range(plan.copies):
            piece = jnp.concatenate([value[d * share : (d + 1) * share, :], pad], axis=0)
            o_row[layer, d] = to_half(piece)
        return to_lines(
            links, o_row.at[layer], o_in.at[layer], line_send.at[layer], line_recv.at[layer]
        )

    def o_finish(layer, copies):
        wait_all(copies)
        value = widen(o_row[layer, me])
        for step in range(1, plan.copies):
            value = value + widen(o_in[layer, step])
        out_ref[layer] = value[:share, :]

    def three_start(layer):
        normed = normed_all[...].reshape(plan.length, plan.model)
        own_normed = normed_all[:, core].reshape(total, plan.model)
        stage[: plan.wide, :] = dot_tn(query_out[layer].reshape(total, plan.wide), own_normed)
        stage[plan.wide : 2 * plan.wide, :] = dot_tn(key_part[...].reshape(plan.length, plan.wide), normed)
        stage[2 * plan.wide : 3 * plan.wide, :] = dot_tn(value_part[...].reshape(plan.length, plan.wide), normed)
        for side in range(2):
            for slot in range(3):
                pieces = []
                for to in range(plan.chips):
                    first = slot * plan.wide + links.lead + (2 * to + side) * share
                    pieces.append(stage[pl.ds(pl.multiple_of(first, 8), share), :])
                three_pair[side, slot] = to_half(jnp.concatenate(pieces, axis=0))
        return started(
            remote(
                three_pair.at[1 - core],
                three_half.at[layer],
                chain_send.at[2 + layer, 0],
                chain_recv.at[2 + layer, 0],
                links.pair(),
            )
        )

    def three_plane(layer, copy):
        copy.wait()
        both = []
        for slot in range(3):
            both.append(widen(three_pair[core, slot]) + widen(three_half[layer, slot]))
        pad = jnp.zeros((three_sum.shape[2] - 3 * share, plan.model), jnp.float32)
        for to in range(plan.chips):
            pieces = [value[to * share : (to + 1) * share, :] for value in both]
            three_sum[layer, to] = to_half(jnp.concatenate(pieces + [pad], axis=0))
        three_part[layer, chip] = three_sum[layer, chip]
        return to_chips(
            links,
            three_sum.at[layer],
            three_part.at[layer],
            plane_send.at[2 + layer],
            plane_recv.at[2 + layer],
        )

    def three_line(layer, copies):
        wait_all(copies)
        return to_lines(
            links,
            three_part.at[layer],
            three_in.at[layer],
            line_send.at[2 + layer],
            line_recv.at[2 + layer],
        )

    def three_finish(layer, copies):
        wait_all(copies)
        value = widen(three_part[layer, me])
        for step in range(1, plan.copies):
            value = value + widen(three_in[layer, step])
        three_ref[layer] = value[: 3 * share, :]

    def attention(layer, grad, hidden):
        grad_half = to_half(grad)
        loads[("o", layer)].wait()
        d_attended = dot_nt(grad_half, weights[3])
        for g in range(plan.groups):
            first = plan.window(g)
            grad_out[layer, g] = to_half(d_attended[:, first : first + plan.wide])
        if layer == 1:
            pl.semaphore_wait(barrier, len(others))
            load(("o", 0), wo_hbm.at[0], weights.at[3])
        copies = to_chips(
            links, grad_out.at[layer], grad_in.at[layer], grad_send.at[layer], grad_recv.at[layer]
        )
        grad_in[layer, chip] = grad_out[layer, chip]
        if layer == 1:
            rows_lines.extend(
                to_all_dp(links, rows_hbm, rows_all, line_send.at[5], line_recv.at[5])
            )
        o_copy = o_start(layer, grad_half)
        if layer == 1:
            fill_all_bias(plan, links, table_ref, buckets_ref, bias_rows, tiles)
            sums[...] = jnp.zeros_like(sums)
        for name in ("query", "key", "heads", "value"):
            loads[(name, layer)].wait()
        queries = query_all[...].reshape(total, plan.wide)
        for head in range(plan.heads):
            picked_queries[head] = jnp.where(links.head_lanes(queries.shape, head), queries, 0)
        query_t[...] = jnp.zeros_like(query_t)
        key_t[...] = jnp.transpose(key_all[...].reshape(plan.length, plan.wide))
        products[...] = jnp.transpose(widen(heads_all[...].reshape(total, plan.wide)))
        wait_all(copies)
        grads = grad_in[layer].reshape(total, plan.wide)
        for head in range(plan.heads):
            picked_grads[head] = jnp.where(links.head_lanes(grads.shape, head), grads, 0)
        products[...] = products[...] * jnp.transpose(widen(grads))
        delta = [
            jnp.sum(products[links.head_rows(head), :], axis=0, keepdims=True)
            for head in range(plan.heads)
        ]
        log_norm = [norm_ref[layer, head : head + 1, :] for head in range(plan.heads)]

        def process(block):
            keys, values = key_all[block], value_all[block]
            d_keys = d_values = None
            for head in range(plan.heads):
                part = dot_nt(keys, picked_queries[head])
                part = jnp.exp(part + bias_part(plan, tiles, head, block, core) - log_norm[head])
                slope = part * (dot_nt(values, picked_grads[head]) - delta[head])
                for b in range(plan.groups):
                    first = plan.length + (b * plan.splits + core - block) * plan.rows
                    at = pl.ds(pl.multiple_of(first, plan.rows), plan.rows)
                    sums[head, :, at] += slope[:, b * plan.rows : (b + 1) * plan.rows]
                slope = to_half(slope)
                where = pl.ds(pl.multiple_of(block * plan.rows, plan.rows), plan.rows)
                query_t[links.head_rows(head), :] += dot_nn(
                    key_t[links.head_rows(head), where], slope
                )
                key_piece = dot_nn(slope, picked_queries[head])
                value_piece = dot_nn(to_half(part), picked_grads[head])
                d_keys = key_piece if head == 0 else d_keys + key_piece
                d_values = value_piece if head == 0 else d_values + value_piece
            key_part[block], value_part[block] = to_half(d_keys), to_half(d_values)
            return d_keys, d_values

        def pair_copy(step):
            return remote(
                pair_out.at[step],
                pair_in.at[layer, step],
                pair_send.at[layer, step],
                pair_recv.at[layer, step],
                links.pair(),
            )

        def for_pair(i, carry):
            step = lax.rem(i + 1, plan.chips)
            d_keys, d_values = process(2 * links.at_chip(step) + 1 - core)
            pair_out[step, 0] = to_half(d_keys)
            pair_out[step, 1] = to_half(d_values)
            pair_copy(step).start()
            return carry

        lax.fori_loop(0, plan.chips, for_pair, 0)

        def back_copy(step):
            return remote(
                own_out.at[step],
                own_in.at[layer, chip],
                back_send.at[layer, step],
                back_recv.at[layer, step],
                links.chip_device(step),
            )

        def for_owner(i, carry):
            step = lax.rem(i + 1, plan.chips)
            d_keys, d_values = process(2 * links.at_chip(step) + core)
            pair_copy(step).wait_recv()
            own_out[step, 0] = to_half(d_keys + widen(pair_in[layer, step, 0]))
            own_out[step, 1] = to_half(d_values + widen(pair_in[layer, step, 1]))

            @pl.when(step > 0)
            def _():
                back_copy(step).start()

            return carry

        lax.fori_loop(0, plan.chips, for_owner, 0)
        own_in[layer, chip] = own_out[0]
        query_out[layer] = to_half(jnp.transpose(query_t[...])).reshape(
            plan.groups, plan.rows, plan.wide
        )
        copies = to_chips(
            links,
            query_out.at[layer],
            query_in.at[layer],
            query_send.at[layer],
            query_recv.at[layer],
        )
        query_in[layer, chip] = query_out[layer, chip]
        o_copies = o_plane(layer, o_copy)
        loads[("normed", layer)].wait()
        three_copy = three_start(layer)
        inv_rms = lax.rsqrt(jnp.mean(hidden * hidden, axis=-1, keepdims=True) + epsilon)
        for name in ("v", "k", "q"):
            loads[(name, layer)].wait()
        wait_all(copies)
        for step in range(1, plan.chips):
            back_copy(step).wait()
        for step in range(plan.chips):
            pair_copy(step).wait_send()
        groups = range(plan.groups)
        d_queries = to_half(
            add_windows(plan, natural_sum, [widen(query_in[layer, g]) for g in groups])
        )
        d_keys = to_half(
            add_windows(plan, natural_sum, [widen(own_in[layer, g, 0]) for g in groups])
        )
        d_values = to_half(
            add_windows(plan, natural_sum, [widen(own_in[layer, g, 1]) for g in groups])
        )
        d_normed = (
            dot_nt(d_queries, weights[2])
            + dot_nt(d_keys, weights[1])
            + dot_nt(d_values, weights[0])
        )
        if layer == 1:
            load_layer(0)
            for slot, name, source in ((0, "v", wv_hbm), (1, "k", wk_hbm), (2, "q", wq_hbm)):
                load((name, 0), source.at[0], weights.at[slot])
        gains = gain_ref[2 * layer : 2 * layer + 1, :]
        small_mine[2 * layer : 2 * layer + 1, :] = jnp.sum(
            d_normed * hidden * inv_rms, axis=0, keepdims=True
        )
        result = grad + norm_slope(hidden, inv_rms, gains, d_normed)
        return result, o_copies, three_copy

    small_mine[...] = jnp.zeros_like(small_mine)
    small_mine[3:4, :] = last_gain_ref[...]
    grad, o_one, three_one = attention(1, grad_ref[...], stream_ref[...])

    grad_half = to_half(grad)
    grads_z[me] = grad_half
    grad_lines = to_all_dp(links, grads_z.at[me], grads_z, line_send.at[4], line_recv.at[4])
    mid = mid_ref[...]
    gains = gain_ref[1:2, :]
    normed, inv_rms = rms_normed(mid, gains)
    loads["up"].wait()
    loads["down"].wait()
    normed_half = to_half(normed)
    d_normed = jnp.zeros_like(normed)
    for slot in range(plan.copies):
        units = slice(slot * part, (slot + 1) * part)
        pre = dot_nn(normed_half, up[:, units])
        d_pre = to_half(dot_nt(grad_half, down[units, :]) * smooth_slope(pre))
        d_normed = d_normed + dot_nt(d_pre, up[:, units])
    pieces = [slice(slot * part, (slot + 1) * part) for slot in range(plan.experts + 1)]
    for e in range(plan.experts):
        load("ein%d" % e, ein_hbm.at[e, :, mine], up.at[:, pieces[e]])
        load("eout%d" % e, eout_hbm.at[e, mine, :], down.at[pieces[e], :])
    load("din", din_hbm.at[:, mine], up.at[:, pieces[-1]])
    load("dout", dout_hbm.at[mine, :], down.at[pieces[-1], :])
    small_mine[1:2, :] = jnp.sum(d_normed * mid * inv_rms, axis=0, keepdims=True)
    grad = grad + norm_slope(mid, inv_rms, gains, d_normed)

    three_one = three_plane(1, three_one)
    o_one = o_line(1, o_one)
    grad, o_zero, three_zero = attention(0, grad, x_ref[...])
    input_grad_ref[...] = grad

    three_zero = three_plane(0, three_zero)
    three_one = three_line(1, three_one)
    row = lax.broadcasted_iota(jnp.int32, (plan.rows, plan.rows), 0)
    column = lax.broadcasted_iota(jnp.int32, (plan.rows, plan.rows), 1)
    flip = (row + column == plan.rows - 1).astype(jnp.float32)
    diagonals = []
    for head in range(plan.heads):
        flipped = jnp.dot(
            flip, sums[head], precision=highest, preferred_element_type=jnp.float32
        )
        skewed = pltpu.roll(
            flipped, 2 * plan.length - (plan.rows - 1), 1, stride=1, stride_axis=0
        )
        diagonals.append(jnp.sum(skewed, axis=0, keepdims=True))
    diagonals.append(jnp.zeros((8 - plan.heads, 2 * plan.length), jnp.float32))
    buckets = table_ref.shape[0]
    table_grad = lax.dot_general(
        jnp.concatenate(diagonals, axis=0),
        bucket_picks(128, buckets_ref),
        (((1,), (1,)), ((), ())),
        precision=highest,
        preferred_element_type=jnp.float32,
    )
    lane = lax.broadcasted_iota(jnp.int32, (plan.heads, plan.model), 1)
    repeated = jnp.concatenate([table_grad[: plan.heads, :]] * (plan.model // 128), axis=1)
    small_mine[4 : 4 + plan.heads, :] = jnp.where(lane // 128 == chip, repeated, 0.0)
    small_copy = started(
        remote(
            small_mine, small_half, chain_send.at[5, 0], chain_recv.at[5, 0], links.pair()
        )
    )

    wait_all(grad_lines)
    count = plan.copies * plan.rows
    normed = normed_z[...].reshape(count, plan.model)
    grads = grads_z[...].reshape(count, plan.model)
    loads["din"].wait()
    loads["dout"].wait()
    height = part // plan.cycle
    some = part // plan.chips
    for to in range(plan.chips):
        units = slice(pieces[-1].start + to * some, pieces[-1].start + (to + 1) * some)
        pre = dot_nn(normed, up[:, units])
        active = to_half(smooth_act(pre))
        d_pre = to_half(dot_nt(grads, down[units, :]) * smooth_slope(pre))
        in_grad = to_half(dot_tn(d_pre, normed))
        out_grad = to_half(dot_tn(active, grads))
        for side in range(2):
            rows = slice(side * height, (side + 1) * height)
            dense_pair[side, to, :height, :] = in_grad[rows, :]
            dense_pair[side, to, height:, :] = out_grad[rows, :]
    dense_copy = started(
        remote(
            dense_pair.at[1 - core],
            dense_half,
            chain_send.at[4, 0],
            chain_recv.at[4, 0],
            links.pair(),
        )
    )
    three_zero = three_line(0, three_zero)
    small_copy.wait()
    small_sum[...] = small_mine[...] + small_half[...]
    small_copies = to_chips(
        links, small_sum, small_part, plane_send.at[5], plane_recv.at[5], by_step=True, whole=True
    )
    dense_copy.wait()

    def join(i, carry):
        dense_pair[core, i] = to_half(widen(dense_pair[core, i]) + widen(dense_half[i]))
        return carry

    lax.fori_loop(0, plan.chips, join, 0)
    dense_copies = to_chips(
        links, dense_pair.at[core], dense_part, plane_send.at[4], plane_recv.at[4], by_step=True
    )
    o_zero = o_line(0, o_zero)

    loads["cots"].wait()
    rows_own.wait()
    wait_all(rows_lines)
    slots = plan.copies * plan.cycle * plan.capacity
    stores = []
    for e in range(plan.experts):
        picked = slice(e * plan.capacity, (e + 1) * plan.capacity)
        rows = rows_all[:, :, picked, :].reshape(slots, plan.model)
        cots = cots_all[:, :, picked, :].reshape(slots, plan.model)
        loads["ein%d" % e].wait()
        loads["eout%d" % e].wait()
        for low in range(0, part, plan.wide):
            units = slice(e * part + low, e * part + low + plan.wide)
            pre = dot_nn(rows, up[:, units])
            active = to_half(smooth_act(pre))
            d_pre = to_half(dot_nt(cots, down[units, :]) * smooth_slope(pre))
            weights[e, :, low : low + plan.wide] = to_half(dot_tn(rows, d_pre))
            weights[plan.experts + e, low : low + plan.wide, :] = to_half(dot_tn(active, cots))
        stores.append(local(weights.at[e], ein_grad.at[e], own_sem.at[1 + 2 * e]))
        stores.append(
            local(weights.at[plan.experts + e], eout_grad.at[e], own_sem.at[2 + 2 * e])
        )
        if e == 0:
            wait_all(small_copies)
            value = small_sum[...]
            for step in range(1, plan.chips):
                value = value + small_part[step]
            small_row[...] = value
            small_copies = to_lines(
                links, small_row, small_in, line_send.at[6], line_recv.at[6], whole=True
            )

    wait_all(small_copies)
    value = small_row[...]
    for step in range(1, plan.copies):
        value = value + small_in[step]
    small_ref[...] = value
    three_finish(1, three_one)
    o_finish(1, o_one)
    wait_all(dense_copies)
    value = widen(dense_pair[core, chip])
    for step in range(1, plan.chips):
        value = value + widen(dense_part[step])
    dense_ref[...] = value
    three_finish(0, three_zero)
    o_finish(0, o_zero)
    wait_all(stores)


def whole_backward(plan, values, caches, weights, dense, experts):
    f32, half = jnp.float32, jnp.bfloat16
    whole = pl.BlockSpec(memory_space=VMEM)
    hbm = pl.BlockSpec(memory_space=pl.ANY)
    dma = pltpu.SemaphoreType.DMA
    total = plan.groups * plan.rows
    model, share = plan.model, plan.share
    units = dense[0].shape[1]
    part = units // plan.copies
    slabs = (plan.cycle, plan.slab, model)
    window = (plan.rows, plan.wide)
    row = (plan.rows, model)
    height = 2 * part // plan.cycle
    o_rows, three_rows = -(-share // 16) * 16, -(-3 * share // 16) * 16
    small = (8, model)
    outs = [
        (row, f32),
        ((2, 3 * share, model), f32),
        ((2, share, model), f32),
        ((height, model), f32),
        (small, f32),
        ((plan.experts, model, part), half),
        ((plan.experts, part, model), half),
    ]
    chip_o = (plan.chips, plan.copies * share, model)
    chip_dense = (plan.chips, height, model)
    scratch = [
        ((plan.chips, 2) + row, half),
        ((plan.cycle,) + window, half),
        ((plan.cycle,) + window, half),
        ((plan.groups,) + window, half),
        ((plan.groups,) + window, half),
        ((4, model, model), half),
        ((model, units), half),
        ((units, model), half),
        ((plan.copies,) + slabs, half),
        ((plan.copies,) + slabs, half),
        ((16, 2 * plan.length), f32),
        ((plan.heads, plan.rows, 2 * plan.length), f32),
        ((plan.heads, plan.rows, 2 * plan.length), f32),
        ((2, plan.groups) + window, half),
        ((2, plan.groups) + window, half),
        ((plan.wide, plan.length), half),
        ((plan.wide, total), f32),
        ((plan.heads, total, plan.wide), half),
        ((plan.heads, total, plan.wide), half),
        ((plan.cycle,) + window, half),
        ((plan.cycle,) + window, half),
        ((plan.chips, 2) + window, half),
        ((2, plan.chips, 2) + window, half),
        ((plan.chips, 2) + window, half),
        ((2, plan.groups, 2) + window, half),
        ((plan.wide, total), f32),
        ((2, plan.groups) + window, half),
        ((2, plan.groups) + window, half),
        (row, f32),
        ((max(model, 3 * plan.wide), model), f32),
        ((2,) + chip_o, half),
        (chip_o, half),
        ((2,) + chip_o, half),
        ((2, plan.copies, o_rows, model), half),
        ((2, plan.copies, o_rows, model), half),
        ((2, 3, plan.chips * share, model), half),
        ((2, 3, plan.chips * share, model), half),
        ((2, plan.chips, three_rows, model), half),
        ((2, plan.chips, three_rows, model), half),
        ((2, plan.copies, three_rows, model), half),
        ((plan.copies,) + row, half),
        ((2,) + chip_dense, half),
        (chip_dense, half),
        (chip_dense, half),
        (small, f32),
        (small, f32),
        (small, f32),
        ((plan.chips,) + small, f32),
        (small, f32),
        ((plan.copies,) + small, f32),
    ]
    chips, copies = plan.chips, plan.copies
    sems = [(28,), (1 + 2 * plan.experts,)]
    sems += [(2, chips)] * 8
    sems += [(6, 1)] * 2 + [(6, chips)] * 2 + [(7, copies)] * 2
    return pl.pallas_call(
        functools.partial(whole_backward_kernel, plan),
        out_shape=tuple(jax.ShapeDtypeStruct(*out) for out in outs),
        in_specs=[whole] * len(values) + [hbm] * (len(caches) + 8),
        out_specs=(whole,) * (len(outs) - 2) + (hbm,) * 2,
        scratch_shapes=[VMEM(*one) for one in scratch] + [dma(one) for one in sems],
        compiler_params=pltpu.CompilerParams(
            collective_id=1, has_side_effects=True, vmem_limit_bytes=63 * 1024 * 1024
        ),
        name="whole_backward",
    )(*values, *caches, *weights, *dense, *experts)


def rms_backward(hidden, inv_rms, gains, d_normed):
    d_gains = jnp.sum(d_normed * hidden * inv_rms, axis=0)
    return (norm_slope(hidden, inv_rms, gains, d_normed), d_gains)


def body(
    inputs,
    w_query,
    w_key,
    w_value,
    w_out,
    norm_gain,
    bias_table,
    dense_in,
    dense_out,
    expert_in,
    expert_out,
    routes,
    gate_scale,
    buckets,
    cotangent,
):
    group_rows, model_width = inputs.shape
    head_count = bias_table.shape[1]
    plan = Plan(
        lax.axis_size("dp"),
        lax.axis_size(("ctx", "exp")),
        lax.axis_size("exp"),
        head_count,
        model_width // head_count,
        group_rows,
        expert_in.shape[0],
    )
    reversed_buckets = jnp.concatenate([buckets[:1], buckets[:0:-1]])
    attention = (w_query, w_key, w_value, w_out)
    dense = (dense_in, dense_out)
    experts = (expert_in, expert_out)
    if not plan.fused:
        return separate_body(
            plan,
            inputs,
            attention,
            norm_gain,
            bias_table,
            dense,
            experts,
            routes,
            gate_scale,
            reversed_buckets,
            cotangent,
        )
    bucket_row = reversed_buckets[None]
    (
        output,
        grad,
        last_gain,
        stream,
        mid,
        normed_all,
        key_all,
        value_all,
        query_all,
        heads_all,
        attended,
        log_norm,
        dense_normed,
        _,
        rows,
        cots,
    ) = whole_forward(
        plan,
        inputs,
        norm_gain,
        bias_table,
        bucket_row,
        routes,
        gate_scale,
        cotangent,
        attention,
        dense,
        experts,
    )
    input_grad, three, out, dense_share, small, grad_ein, grad_eout = whole_backward(
        plan,
        (
            grad,
            stream,
            inputs,
            mid,
            norm_gain,
            last_gain,
            bias_table,
            bucket_row,
            attended,
            log_norm,
            dense_normed,
        ),
        (normed_all, key_all, value_all, query_all, heads_all, cots, rows),
        attention,
        dense,
        experts,
    )
    share = plan.share
    place = lax.axis_index(("dp", "ctx", "exp"))
    three = jnp.transpose(three.reshape(2, 3, share, model_width), (1, 0, 3, 2))
    gains = lax.dynamic_slice_in_dim(small[:4], place * share, share, 1)
    bucket_count = bias_table.shape[0]
    table = small[4 : 4 + plan.heads, : plan.groups * 128].reshape(plan.heads, plan.groups, 128)
    table = jnp.transpose(table[:, :, :bucket_count], (2, 1, 0)).reshape(bucket_count * head_count)
    table_share = bucket_count * head_count // (plan.copies * plan.cycle)
    table = lax.dynamic_slice_in_dim(table, place * table_share, table_share, 0)
    half_rows = dense_share.shape[0] // 2
    return (
        output,
        input_grad,
        three[0],
        three[1],
        three[2],
        jnp.transpose(out, (0, 2, 1)),
        gains,
        table,
        dense_share[:half_rows].T,
        dense_share[half_rows:],
        widen(grad_ein),
        widen(grad_eout),
    )


def separate_body(
    plan,
    inputs,
    attention,
    norm_gain,
    bias_table,
    dense,
    experts,
    routes,
    gate_scale,
    reversed_buckets,
    cotangent,
):
    group_rows, model_width = inputs.shape
    bucket_count, head_count = bias_table.shape
    dense_in, dense_out = dense
    expert_in, expert_out = experts
    cycle_size = plan.cycle
    my_group = lax.axis_index(("ctx", "exp")) // plan.splits
    bucket_hits = (
        reversed_buckets[None, :] == jnp.arange(bucket_count, dtype=jnp.int32)[:, None]
    ).astype(jnp.float32)
    my_table = lax.dynamic_slice_in_dim(bias_table.T, my_group * plan.heads, plan.heads, 0)
    bias_rows = jnp.dot(my_table, bucket_hits, precision=highest)
    local_experts = expert_in.shape[0]
    expert_total = local_experts * cycle_size
    capacity = 2 * group_rows // expert_total
    recv_rows = cycle_size * capacity
    flat_routes = routes[:, 0]
    route_hits = (
        flat_routes[:, None] == jnp.arange(expert_total, dtype=jnp.int32)[None, :]
    ).astype(jnp.int32)
    slot_order = jnp.sum((jnp.cumsum(route_hits, axis=0) - 1) * route_hits, axis=1)
    target = flat_routes * capacity + slot_order
    dispatch = (
        target[None, :] == jnp.arange(expert_total * capacity, dtype=jnp.int32)[:, None]
    ).astype(jnp.bfloat16)

    def to_owners(rows_half):
        placed = jnp.dot(dispatch, rows_half, preferred_element_type=jnp.float32)
        return lax.all_to_all(
            to_half(placed).reshape(cycle_size, local_experts, capacity, model_width),
            ("ctx", "exp"),
            split_axis=0,
            concat_axis=2,
            tiled=True,
        ).reshape(local_experts, recv_rows, model_width)

    def from_owners(produced):
        returned = lax.all_to_all(
            produced.reshape(1, local_experts, recv_rows, model_width),
            ("ctx", "exp"),
            split_axis=2,
            concat_axis=0,
            tiled=True,
        )
        return jnp.einsum(
            "sc,sd->cd",
            dispatch,
            returned.reshape(expert_total * capacity, model_width),
            preferred_element_type=jnp.float32,
        )

    mid_zero, *cache_zero = attention_forward(
        plan, 0, inputs, norm_gain, bias_rows, *attention, 0
    )
    inv_rms_one = lax.rsqrt(jnp.mean(mid_zero * mid_zero, axis=-1, keepdims=True) + epsilon)
    normed_half = to_half(mid_zero * inv_rms_one * norm_gain[1])
    pre_act = jnp.dot(normed_half, dense_in, preferred_element_type=jnp.float32)
    active = to_half(smooth_act(pre_act))
    stream = mid_zero + jnp.dot(active, dense_out, preferred_element_type=jnp.float32)
    mid_one, *cache_one = attention_forward(plan, 1, stream, norm_gain, bias_rows, *attention, 1)
    grad_rows = to_owners(to_half(gate_scale * cotangent))
    inv_rms_three = lax.rsqrt(jnp.mean(mid_one * mid_one, axis=-1, keepdims=True) + epsilon)
    rows = to_owners(to_half(mid_one * inv_rms_three * norm_gain[3]))
    expert_pre = jnp.einsum("erd,edf->erf", rows, expert_in, preferred_element_type=jnp.float32)
    expert_active = to_half(smooth_act(expert_pre))
    produced = to_half(
        jnp.einsum("erf,efd->erd", expert_active, expert_out, preferred_element_type=jnp.float32)
    )
    d_active = jnp.einsum("erd,efd->erf", grad_rows, expert_out, preferred_element_type=jnp.float32)
    expert_d_pre = to_half(d_active * smooth_slope(expert_pre))
    d_rows = to_half(
        jnp.einsum("erf,edf->erd", expert_d_pre, expert_in, preferred_element_type=jnp.float32)
    )
    output = mid_one + gate_scale * from_owners(produced)
    d_hidden, gains_four = rms_backward(mid_one, inv_rms_three, norm_gain[3], from_owners(d_rows))
    grad_three = cotangent + d_hidden

    grad_two, gains_three, attn_two, bias_two = attention_backward(
        plan, 1, grad_three, [stream] + cache_one, norm_gain, bias_rows, *attention, 2
    )
    grad_half = to_half(grad_two)
    d_active = jnp.dot(grad_half, dense_out.T, preferred_element_type=jnp.float32)
    d_pre = to_half(d_active * smooth_slope(pre_act))
    d_normed = jnp.dot(d_pre, dense_in.T, preferred_element_type=jnp.float32)
    d_hidden, gains_two = rms_backward(mid_zero, inv_rms_one, norm_gain[1], d_normed)
    input_grad, gains_one, attn_one, bias_one = attention_backward(
        plan, 0, grad_two + d_hidden, [inputs] + cache_zero, norm_gain, bias_rows, *attention, 3
    )

    my_table_grad = jnp.dot(bucket_hits, (bias_one + bias_two).T, precision=highest)
    table_grad = lax.dynamic_update_slice(
        jnp.zeros((bucket_count, head_count), jnp.float32),
        my_table_grad,
        (0, my_group * plan.heads),
    ).reshape(bucket_count * head_count)
    gains_all = jnp.stack([gains_one[0], gains_two, gains_three[0], gains_four])
    everyone = ("dp", "ctx", "exp")
    grad_dout = jnp.dot(active.T, grad_half, preferred_element_type=jnp.float32)
    grad_din = jnp.dot(normed_half.T, d_pre, preferred_element_type=jnp.float32)
    grad_ein = jnp.einsum("erd,erf->edf", rows, expert_d_pre, preferred_element_type=jnp.float32)
    grad_eout = jnp.einsum(
        "erf,erd->efd", expert_active, grad_rows, preferred_element_type=jnp.float32
    )
    grad_ein = lax.psum_scatter(to_half(grad_ein), "dp", scatter_dimension=2, tiled=True)
    grad_eout = lax.psum_scatter(to_half(grad_eout), "dp", scatter_dimension=1, tiled=True)
    attn = lax.psum_scatter(
        jnp.stack([attn_one, attn_two], axis=1), everyone, scatter_dimension=3, tiled=True
    ).astype(jnp.float32)
    gains = lax.psum_scatter(gains_all, everyone, scatter_dimension=1, tiled=True)
    table = lax.psum_scatter(table_grad, everyone, scatter_dimension=0, tiled=True)
    din = lax.psum_scatter(to_half(grad_din), everyone, scatter_dimension=1, tiled=True)
    dout = lax.psum_scatter(to_half(grad_dout), everyone, scatter_dimension=0, tiled=True)
    return (
        output,
        input_grad,
        attn[0],
        attn[1],
        attn[2],
        attn[3],
        gains,
        table,
        widen(din),
        widen(dout),
        widen(grad_ein),
        widen(grad_eout),
    )


def solution(mesh):
    in_specs = (
        P(("dp", "ctx", "exp"), None),
        P(),
        P(),
        P(),
        P(),
        P(),
        P(),
        P(),
        P(),
        P(("ctx", "exp"), None, None),
        P(("ctx", "exp"), None, None),
        P(("dp", "ctx", "exp"), None),
        P(("dp", "ctx", "exp"), None),
        P(),
        P(("dp", "ctx", "exp"), None),
    )
    out_specs = (
        P(("dp", "ctx", "exp"), None),
        P(("dp", "ctx", "exp"), None),
        P(None, None, ("dp", "ctx", "exp")),
        P(None, None, ("dp", "ctx", "exp")),
        P(None, None, ("dp", "ctx", "exp")),
        P(None, None, ("dp", "ctx", "exp")),
        P(None, ("dp", "ctx", "exp")),
        P(("dp", "ctx", "exp")),
        P(None, ("dp", "ctx", "exp")),
        P(("dp", "ctx", "exp"), None),
        P(("ctx", "exp"), None, "dp"),
        P(("ctx", "exp"), "dp", None),
    )
    return jax.shard_map(body, mesh=mesh, in_specs=in_specs, out_specs=out_specs, check_vma=False)
```

```python
import functools

import jax
import jax.numpy as jnp
from jax import lax
from jax.experimental import pallas as pl
from jax.experimental.pallas import tpu as pltpu
from jax.sharding import PartitionSpec as P

epsilon = 1e-06
highest = lax.Precision.HIGHEST
MESH = pl.DeviceIdType.MESH
VMEM = pltpu.VMEM


def to_half(values):
    return values.astype(jnp.bfloat16)


def widen(values):
    return values.astype(jnp.float32)


def dot_nn(a, b):
    return jnp.dot(a, b, preferred_element_type=jnp.float32)


def dot_nt(a, b):
    return lax.dot_general(a, b, (((1,), (1,)), ((), ())), preferred_element_type=jnp.float32)


def dot_tn(a, b):
    return lax.dot_general(a, b, (((0,), (0,)), ((), ())), preferred_element_type=jnp.float32)


def rotate(values, shift):
    width = values.shape[-1]
    shift = shift % width
    return values if shift == 0 else pltpu.roll(values, shift, values.ndim - 1)


def pad_lanes(values, width):
    if values.shape[1] == width:
        return values
    zeros = jnp.zeros((values.shape[0], width - values.shape[1]), values.dtype)
    return jnp.concatenate([values, zeros], axis=1)


class Plan:
    def __init__(self, copies, cycle, exp_size, head_count, head_size, rows, experts):
        self.copies, self.cycle, self.exp_size, self.rows = copies, cycle, exp_size, rows
        groups = 1
        while cycle % (groups * 2) == 0 and head_count % (groups * 2) == 0:
            groups *= 2
        self.groups, self.splits = groups, cycle // groups
        self.heads, self.head_size = head_count // groups, head_size
        self.width = self.heads * head_size
        self.model = head_count * head_size
        self.length = cycle * rows
        self.wide = -(-self.width // 128) * 128
        self.lead = self.wide - self.width
        self.pair = 2 * self.width
        self.tiled = self.heads if self.heads * rows * self.length * 8 <= 4 << 20 else 1
        self.chips = cycle // 2
        self.share = self.model // (copies * cycle)
        self.experts = experts
        self.capacity = 2 * rows // (experts * cycle)
        self.slab = experts * self.capacity
        self.early = cycle // 8
        self.fused = (
            self.splits == 2
            and self.groups == copies
            and self.capacity % 16 == 0
            and (copies * self.share) % 16 == 0
            and self.width * copies == self.model
            and self.width + self.width % 128 <= self.wide
        )
        assert self.pair % 128 == 0 and self.pair - self.wide == self.width - self.lead

    def window(self, group):
        return group * self.width // 128 * 128

    def place(self):
        c = lax.axis_index("ctx") * self.exp_size + lax.axis_index("exp")
        return c, c // self.splits, lax.rem(c, self.splits)

    def device(self, c):
        return (lax.axis_index("dp"), c // self.exp_size, lax.rem(c, self.exp_size))

    def peer(self, c, step):
        return lax.rem(c + step, self.cycle)

    def copy_device(self, c, other):
        return (other, c // self.exp_size, lax.rem(c, self.exp_size))


def greet(plan, c):
    barrier = pltpu.get_barrier_semaphore()
    for step in range(1, plan.cycle):
        pl.semaphore_signal(
            barrier, inc=1, device_id=plan.device(plan.peer(c, step)), device_id_type=MESH
        )
    me = lax.axis_index("dp")
    for step in range(1, plan.copies):
        other = lax.rem(me + step, plan.copies)
        pl.semaphore_signal(
            barrier, inc=1, device_id=plan.copy_device(c, other), device_id_type=MESH
        )
    return barrier


def await_greetings(plan, barrier):
    pl.semaphore_wait(barrier, plan.cycle - 1 + plan.copies - 1)


def start_along_dp(plan, c, source, target, own_sem, send, recv):
    me = lax.axis_index("dp")
    own = pltpu.make_async_copy(source, target.at[me], own_sem.at[0])
    own.start()
    copies = [own]
    for step in range(1, plan.copies):
        other = lax.rem(me + step, plan.copies)
        copy = remote(
            source, target.at[me], send.at[step], recv.at[step], plan.copy_device(c, other)
        )
        copy.start()
        copies.append(copy)
    return copies


def start_slabs(plan, c, source, target, send, recv):
    copies = []
    for step in range(1, plan.cycle):
        to = plan.peer(c, step)
        copy = remote(source.at[to], target.at[c], send.at[step], recv.at[step], plan.device(to))
        copy.start()
        copies.append(copy)
    target[c] = source[c]
    return copies


def rms_normed(hidden, gains):
    inv_rms = lax.rsqrt(jnp.mean(hidden * hidden, axis=-1, keepdims=True) + epsilon)
    return hidden * inv_rms * gains, inv_rms


def fill_bias(plan, rows_ref, tiles, heads):
    for head in heads:
        row = jnp.broadcast_to(rows_ref[head : head + 1, :], (plan.rows, 2 * plan.length))
        tiles[head % plan.tiled] = pltpu.roll(row, 0, 1, stride=1, stride_axis=0)


def bias_part(plan, tiles, head, key_block, split):
    parts = []
    head = head % plan.tiled
    for block in range(plan.groups):
        first = plan.length + (block * plan.splits + split - key_block) * plan.rows
        parts.append(tiles[head, :, pl.ds(pl.multiple_of(first, plan.rows), plan.rows)])
    return jnp.concatenate(parts, axis=1)


def lanes_between(shape, low, high):
    lane = lax.broadcasted_iota(jnp.int32, shape, 1)
    return (lane >= low) & (lane < high)


def natural(plan, blocks, lead):
    total = None
    for group, block in enumerate(blocks):
        moved = rotate(pad_lanes(block, plan.model), group * plan.width - lead)
        total = moved if total is None else total + moved
    return total


def remote(src, dst, send, recv, device):
    return pltpu.make_async_remote_copy(
        src_ref=src, dst_ref=dst, send_sem=send, recv_sem=recv, device_id=device, device_id_type=MESH
    )


def forward_kernel(
    plan,
    layer,
    x_ref,
    gain_ref,
    bias_ref,
    wq_hbm,
    wk_hbm,
    wv_hbm,
    wo_hbm,
    mid_ref,
    normed_ref,
    query_ref,
    pair_ref,
    heads_ref,
    attended_ref,
    norm_ref,
    weights,
    tiles,
    send_pair,
    send_query,
    scores,
    probs,
    att_in,
    load_sem,
    pair_send,
    pair_recv,
    query_send,
    query_recv,
    att_send,
    att_recv,
):
    c, group, split = plan.place()
    loads = []
    for slot, source in enumerate((wv_hbm, wk_hbm, wq_hbm, wo_hbm)):
        load = pltpu.make_async_copy(source.at[layer], weights.at[slot], load_sem.at[slot])
        load.start()
        loads.append(load)
    barrier = greet(plan, c)
    hidden = x_ref[...]
    normed, _ = rms_normed(hidden, gain_ref[layer * 2 : layer * 2 + 1, :])
    normed_half = to_half(normed)
    normed_ref[...] = normed_half
    loads[0].wait()
    values = dot_nn(normed_half, weights[0])
    loads[1].wait()
    keys = dot_nn(normed_half, weights[1])
    is_value = lanes_between((plan.rows, plan.pair), 0, plan.width)
    for g in range(plan.groups):
        value_part = rotate(values, -g * plan.width)[:, : plan.pair]
        key_part = rotate(keys, (1 - g) * plan.width)[:, : plan.pair]
        send_pair[g] = to_half(jnp.where(is_value, value_part, key_part))
    await_greetings(plan, barrier)
    copies = []
    for step in range(1, plan.cycle):
        to = plan.peer(c, step)
        copy = remote(
            send_pair.at[to // plan.splits],
            pair_ref.at[c],
            pair_send.at[step],
            pair_recv.at[step],
            plan.device(to),
        )
        copy.start()
        copies.append(copy)
    loads[2].wait()
    queries = dot_nn(normed_half, weights[2])
    is_query = lanes_between((plan.rows, plan.wide), plan.lead, plan.wide)
    for g in range(plan.groups):
        query_part = rotate(queries, plan.lead - g * plan.width)[:, : plan.wide]
        send_query[g] = to_half(jnp.where(is_query, query_part, 0.0))
    for step in range(1, plan.groups):
        to = plan.peer(c, step * plan.splits)
        copy = remote(
            send_query.at[to // plan.splits],
            query_ref.at[group],
            query_send.at[step],
            query_recv.at[step],
            plan.device(to),
        )
        copy.start()
        copies.append(copy)
    pair_ref[c] = send_pair[group]
    query_ref[group] = send_query[group]
    fill_bias(plan, bias_ref, tiles, range(plan.tiled))
    for copy in copies:
        copy.wait()

    total = plan.groups * plan.rows
    queries_all = query_ref[...].reshape(total, plan.wide)
    values_t = jnp.transpose(pair_ref[...].reshape(plan.length, plan.pair)[:, : plan.wide])
    rows_t = []
    for head in range(plan.heads):
        if head >= plan.tiled:
            fill_bias(plan, bias_ref, tiles, [head])
        low = plan.lead + head * plan.head_size
        picked = jnp.where(
            lanes_between(queries_all.shape, low, low + plan.head_size), queries_all, 0
        )

        def score_block(block, top):
            part = dot_nt(pair_ref[block][:, plan.pair - plan.wide :], picked)
            part = part + bias_part(plan, tiles, head, block, split)
            scores[pl.ds(pl.multiple_of(block * plan.rows, plan.rows), plan.rows), :] = part
            return jnp.maximum(top, jnp.max(part, axis=0, keepdims=True))

        top = lax.fori_loop(0, plan.cycle, score_block, jnp.full((1, total), -1e30, jnp.float32))

        def weight_block(block, norm):
            where = pl.ds(pl.multiple_of(block * plan.rows, plan.rows), plan.rows)
            part = jnp.exp(scores[where, :] - top)
            probs[where, :] = to_half(part)
            return norm + jnp.sum(part, axis=0, keepdims=True)

        norm = lax.fori_loop(0, plan.cycle, weight_block, jnp.zeros((1, total), jnp.float32))
        norm_ref[head : head + 1, :] = top + jnp.log(norm)
        mine = values_t[head * plan.head_size : (head + 1) * plan.head_size, :]
        rows_t.append(dot_nn(mine, probs[...]) / norm)
    rows_t.append(jnp.zeros((plan.lead, total), jnp.float32))
    heads_ref[...] = to_half(jnp.transpose(jnp.concatenate(rows_t, axis=0))).reshape(
        plan.groups, plan.rows, plan.wide
    )
    copies = []
    for step in range(1, plan.groups):
        to = plan.peer(c, step * plan.splits)
        copy = remote(
            heads_ref.at[to // plan.splits],
            att_in.at[group],
            att_send.at[step],
            att_recv.at[step],
            plan.device(to),
        )
        copy.start()
        copies.append(copy)
    att_in[group] = heads_ref[group]
    loads[3].wait()
    for copy in copies:
        copy.wait()
    attended = to_half(natural(plan, [widen(att_in[g]) for g in range(plan.groups)], 0))
    attended_ref[...] = attended
    mid_ref[...] = hidden + dot_nn(attended, weights[3])


def attention_forward(plan, layer, hidden, gains, bias_rows, wq, wk, wv, wo, collective):
    f32, half = jnp.float32, jnp.bfloat16
    total = plan.groups * plan.rows
    whole = pl.BlockSpec(memory_space=VMEM)
    hbm = pl.BlockSpec(memory_space=pl.ANY)
    dma = pltpu.SemaphoreType.DMA
    return pl.pallas_call(
        functools.partial(forward_kernel, plan, layer),
        out_shape=(
            jax.ShapeDtypeStruct((plan.rows, plan.model), f32),
            jax.ShapeDtypeStruct((plan.rows, plan.model), half),
            jax.ShapeDtypeStruct((plan.groups, plan.rows, plan.wide), half),
            jax.ShapeDtypeStruct((plan.cycle, plan.rows, plan.pair), half),
            jax.ShapeDtypeStruct((plan.groups, plan.rows, plan.wide), half),
            jax.ShapeDtypeStruct((plan.rows, plan.model), half),
            jax.ShapeDtypeStruct((plan.heads, total), f32),
        ),
        in_specs=[whole, whole, whole, hbm, hbm, hbm, hbm],
        out_specs=(whole,) * 7,
        scratch_shapes=[
            VMEM((4, plan.model, plan.model), half),
            VMEM((plan.tiled, plan.rows, 2 * plan.length), f32),
            VMEM((plan.groups, plan.rows, plan.pair), half),
            VMEM((plan.groups, plan.rows, plan.wide), half),
            VMEM((plan.length, total), f32),
            VMEM((plan.length, total), half),
            VMEM((plan.groups, plan.rows, plan.wide), half),
            dma((4,)),
            dma((plan.cycle,)),
            dma((plan.cycle,)),
            dma((plan.groups,)),
            dma((plan.groups,)),
            dma((plan.groups,)),
            dma((plan.groups,)),
        ],
        compiler_params=pltpu.CompilerParams(
            collective_id=collective, has_side_effects=True, vmem_limit_bytes=56 * 1024 * 1024
        ),
        name="attention_forward",
    )(hidden, gains, bias_rows, wq, wk, wv, wo)


def backward_kernel(
    plan,
    layer,
    grad_ref,
    x_ref,
    gain_ref,
    bias_ref,
    normed_ref,
    query_ref,
    pair_ref,
    heads_ref,
    attended_ref,
    norm_ref,
    wq_hbm,
    wk_hbm,
    wv_hbm,
    wo_hbm,
    out_ref,
    gain_grad_ref,
    weight_grad_ref,
    bias_grad_ref,
    weights,
    tiles,
    sums,
    send_grad,
    grad_in,
    probs,
    slopes,
    key_sum,
    value_sum,
    send_pair,
    pair_in,
    send_query,
    query_in,
    load_sem,
    grad_send,
    grad_recv,
    pair_send,
    pair_recv,
    query_send,
    query_recv,
):
    c, group, split = plan.place()
    total = plan.groups * plan.rows
    loads = []
    for slot, source in enumerate((wv_hbm, wk_hbm, wq_hbm, wo_hbm)):
        load = pltpu.make_async_copy(source.at[layer], weights.at[slot], load_sem.at[slot])
        loads.append(load)
    for slot in (3, 0, 1, 2):
        loads[slot].start()
    barrier = greet(plan, c)
    grad = grad_ref[...]
    grad_half = to_half(grad)
    loads[3].wait()
    d_attended = dot_nt(grad_half, weights[3])
    in_group = lanes_between((plan.rows, plan.wide), 0, plan.width)
    for g in range(plan.groups):
        part = rotate(d_attended, -g * plan.width)[:, : plan.wide]
        send_grad[g] = to_half(jnp.where(in_group, part, 0.0))
    await_greetings(plan, barrier)
    copies = []
    for step in range(1, plan.groups):
        to = plan.peer(c, step * plan.splits)
        copy = remote(
            send_grad.at[to // plan.splits],
            grad_in.at[group],
            grad_send.at[step],
            grad_recv.at[step],
            plan.device(to),
        )
        copy.start()
        copies.append(copy)
    grad_in[group] = send_grad[group]
    fill_bias(plan, bias_ref, tiles, range(plan.tiled))
    weight_grad_ref[3] = to_half(dot_tn(attended_ref[...], grad_half))
    queries_all = query_ref[...].reshape(total, plan.wide)
    keys_t = jnp.transpose(
        pair_ref[...].reshape(plan.length, plan.pair)[:, plan.pair - plan.wide :]
    )
    heads_t = jnp.transpose(widen(heads_ref[...].reshape(total, plan.wide)))
    for copy in copies:
        copy.wait()
    grads_all = grad_in[...].reshape(total, plan.wide)
    grads_t = jnp.transpose(widen(grads_all))
    products_t = grads_t * heads_t
    query_rows_t = [jnp.zeros((plan.lead, total), jnp.float32)]
    for head in range(plan.heads):
        if head >= plan.tiled:
            fill_bias(plan, bias_ref, tiles, [head])
        low, high = head * plan.head_size, (head + 1) * plan.head_size
        picked_queries = jnp.where(
            lanes_between(queries_all.shape, plan.lead + low, plan.lead + high), queries_all, 0
        )
        picked_grads = jnp.where(lanes_between(grads_all.shape, low, high), grads_all, 0)
        delta = jnp.sum(products_t[low:high, :], axis=0, keepdims=True)
        log_norm = norm_ref[head : head + 1, :]
        sums[...] = jnp.zeros_like(sums)

        def slope_block(block, carry):
            where = pl.ds(pl.multiple_of(block * plan.rows, plan.rows), plan.rows)
            part = dot_nt(pair_ref[block][:, plan.pair - plan.wide :], picked_queries)
            part = part + bias_part(plan, tiles, head, block, split)
            part = jnp.exp(part - log_norm)
            probs[where, :] = to_half(part)
            slope = part * (dot_nt(pair_ref[block][:, : plan.wide], picked_grads) - delta)
            slopes[where, :] = to_half(slope)
            for b in range(plan.groups):
                first = plan.length + (b * plan.splits + split - block) * plan.rows
                at = pl.ds(pl.multiple_of(first, plan.rows), plan.rows)
                sums[:, at] += slope[:, b * plan.rows : (b + 1) * plan.rows]
            return carry

        lax.fori_loop(0, plan.cycle, slope_block, 0)
        key_part = dot_nn(slopes[...], picked_queries)
        value_part = dot_nn(probs[...], picked_grads)
        if head == 0:
            key_sum[...], value_sum[...] = key_part, value_part
        else:
            key_sum[...] += key_part
            value_sum[...] += value_part
        query_rows_t.append(dot_nn(keys_t[plan.lead + low : plan.lead + high, :], slopes[...]))
        row = lax.broadcasted_iota(jnp.int32, (plan.rows, plan.rows), 0)
        column = lax.broadcasted_iota(jnp.int32, (plan.rows, plan.rows), 1)
        flip = (row + column == plan.rows - 1).astype(jnp.float32)
        flipped = jnp.dot(flip, sums[...], precision=highest, preferred_element_type=jnp.float32)
        skewed = pltpu.roll(
            flipped, 2 * plan.length - (plan.rows - 1), 1, stride=1, stride_axis=0
        )
        bias_grad_ref[head : head + 1, :] = jnp.sum(skewed, axis=0, keepdims=True)
    send_query[...] = to_half(jnp.transpose(jnp.concatenate(query_rows_t, axis=0))).reshape(
        plan.groups, plan.rows, plan.wide
    )
    value_all, key_all = value_sum[...], key_sum[...]
    low, gap = plan.pair - plan.wide, plan.wide - (plan.pair - plan.wide)
    middle = jnp.where(
        lanes_between((plan.length, gap), 0, plan.width - low), value_all[:, low:], key_all[:, :gap]
    )
    send_pair[...] = to_half(
        jnp.concatenate([value_all[:, :low], middle, key_all[:, gap:]], axis=1)
    ).reshape(plan.cycle, plan.rows, plan.pair)
    copies = []
    for step in range(1, plan.cycle):
        to = plan.peer(c, step)
        copy = remote(
            send_pair.at[to], pair_in.at[c], pair_send.at[step], pair_recv.at[step], plan.device(to)
        )
        copy.start()
        copies.append(copy)
    for step in range(1, plan.groups):
        to = plan.peer(c, step * plan.splits)
        copy = remote(
            send_query.at[to // plan.splits],
            query_in.at[group],
            query_send.at[step],
            query_recv.at[step],
            plan.device(to),
        )
        copy.start()
        copies.append(copy)
    pair_in[c] = send_pair[c]
    query_in[group] = send_query[group]
    hidden = x_ref[...]
    gains = gain_ref[layer * 2 : layer * 2 + 1, :]
    inv_rms = lax.rsqrt(jnp.mean(hidden * hidden, axis=-1, keepdims=True) + epsilon)
    for slot in range(3):
        loads[slot].wait()
    for copy in copies:
        copy.wait()
    is_value = lanes_between((plan.rows, plan.pair), 0, plan.width)
    value_blocks, key_blocks = [], []
    for g in range(plan.groups):
        block = widen(pair_in[g * plan.splits])
        for other in range(1, plan.splits):
            block = block + widen(pair_in[g * plan.splits + other])
        value_blocks.append(jnp.where(is_value, block, 0.0))
        key_blocks.append(jnp.where(is_value, 0.0, block))
    d_values = to_half(natural(plan, value_blocks, 0))
    d_keys = to_half(natural(plan, key_blocks, plan.width))
    d_queries = to_half(
        natural(plan, [widen(query_in[g]) for g in range(plan.groups)], plan.lead)
    )
    normed_half = normed_ref[...]
    d_normed = (
        dot_nt(d_queries, weights[2]) + dot_nt(d_keys, weights[1]) + dot_nt(d_values, weights[0])
    )
    weight_grad_ref[0] = to_half(dot_tn(normed_half, d_queries))
    weight_grad_ref[1] = to_half(dot_tn(normed_half, d_keys))
    weight_grad_ref[2] = to_half(dot_tn(normed_half, d_values))
    d_scaled = d_normed * gains
    gain_grad_ref[...] = jnp.sum(d_normed * hidden * inv_rms, axis=0, keepdims=True)
    out_ref[...] = (
        grad
        + inv_rms * d_scaled
        - hidden * (inv_rms * inv_rms * inv_rms) * jnp.mean(d_scaled * hidden, axis=-1, keepdims=True)
    )


def attention_backward(plan, layer, grad, cache, gains, bias_rows, wq, wk, wv, wo, collective):
    f32, half = jnp.float32, jnp.bfloat16
    total = plan.groups * plan.rows
    whole = pl.BlockSpec(memory_space=VMEM)
    hbm = pl.BlockSpec(memory_space=pl.ANY)
    dma = pltpu.SemaphoreType.DMA
    hidden, normed, query, pair, heads, attended, norm = cache
    block = (plan.groups, plan.rows, plan.wide)
    pairs = (plan.cycle, plan.rows, plan.pair)
    return pl.pallas_call(
        functools.partial(backward_kernel, plan, layer),
        out_shape=(
            jax.ShapeDtypeStruct((plan.rows, plan.model), f32),
            jax.ShapeDtypeStruct((1, plan.model), f32),
            jax.ShapeDtypeStruct((4, plan.model, plan.model), half),
            jax.ShapeDtypeStruct((plan.heads, 2 * plan.length), f32),
        ),
        in_specs=[whole] * 10 + [hbm] * 4,
        out_specs=(whole,) * 4,
        scratch_shapes=[
            VMEM((4, plan.model, plan.model), half),
            VMEM((plan.tiled, plan.rows, 2 * plan.length), f32),
            VMEM((plan.rows, 2 * plan.length), f32),
            VMEM(block, half),
            VMEM(block, half),
            VMEM((plan.length, total), half),
            VMEM((plan.length, total), half),
            VMEM((plan.length, plan.wide), f32),
            VMEM((plan.length, plan.wide), f32),
            VMEM(pairs, half),
            VMEM(pairs, half),
            VMEM(block, half),
            VMEM(block, half),
            dma((4,)),
            dma((plan.groups,)),
            dma((plan.groups,)),
            dma((plan.cycle,)),
            dma((plan.cycle,)),
            dma((plan.groups,)),
            dma((plan.groups,)),
        ],
        compiler_params=pltpu.CompilerParams(
            collective_id=collective, has_side_effects=True, vmem_limit_bytes=60 * 1024 * 1024
        ),
        name="attention_backward",
    )(grad, hidden, gains, bias_rows, normed, query, pair, heads, attended, norm, wq, wk, wv, wo)


def smooth_act(values):
    return values * jax.nn.sigmoid(values)


def smooth_slope(values):
    sigma = jax.nn.sigmoid(values)
    return sigma * (1.0 + values * (1.0 - sigma))


class Links:
    def __init__(self, plan):
        self.plan = plan
        self.c, self.chip, self.core = plan.place()
        self.me = lax.axis_index("dp")
        self.lead = pl.multiple_of(lax.rem(self.chip * plan.width, 128), 64)
        self.first = pl.multiple_of(self.chip * plan.width // 128 * 128, 128)

    def pair(self):
        return self.plan.device(self.c + 1 - 2 * self.core)

    def at_chip(self, step):
        return lax.rem(self.chip + step, self.plan.groups)

    def chip_device(self, step):
        return self.plan.device(2 * self.at_chip(step) + self.core)

    def at_dp(self, step):
        return lax.rem(self.me + step, self.plan.copies)

    def dp_device(self, step):
        return self.plan.copy_device(self.c, self.at_dp(step))

    def head_lanes(self, shape, head):
        low = self.lead + head * self.plan.head_size
        return lanes_between(shape, low, low + self.plan.head_size)

    def head_rows(self, head):
        return pl.ds(
            pl.multiple_of(self.lead + head * self.plan.head_size, self.plan.head_size),
            self.plan.head_size,
        )


def wait_all(copies):
    for copy in copies:
        copy.wait()


def local(source, target, sem):
    copy = pltpu.make_async_copy(source, target, sem)
    copy.start()
    return copy


def started(copy):
    copy.start()
    return copy


def to_lines(links, source, target, send, recv, whole=False):
    copies = []
    for step in range(1, links.plan.copies):
        part = source if whole else source.at[links.at_dp(step)]
        copies.append(
            started(
                remote(part, target.at[step], send.at[step], recv.at[step], links.dp_device(step))
            )
        )
    return copies


def to_all_dp(links, source, target, send, recv):
    return [
        started(
            remote(
                source, target.at[links.me], send.at[step], recv.at[step], links.dp_device(step)
            )
        )
        for step in range(1, links.plan.copies)
    ]


def to_chips(links, source, target, send, recv, by_step=False, whole=False):
    copies = []
    for step in range(1, links.plan.chips):
        part = source if whole else source.at[links.at_chip(step)]
        slot = step if by_step else links.chip
        copies.append(
            started(
                remote(
                    part, target.at[slot], send.at[step], recv.at[step], links.chip_device(step)
                )
            )
        )
    return copies


def add_windows(plan, total, blocks):
    total[...] = jnp.zeros_like(total)
    for group, block in enumerate(blocks):
        first = plan.window(group)
        total[:, first : first + plan.wide] += block
    return total[...]


def bucket_picks(count, buckets_ref):
    width = buckets_ref.shape[1]
    tiles = [buckets_ref[:, low : low + 128] for low in range(0, width, 128)]
    rows = jnp.concatenate(tiles, axis=0).astype(jnp.float32)
    square = (128, 128)
    row = lax.broadcasted_iota(jnp.int32, square, 0)
    column = lax.broadcasted_iota(jnp.int32, square, 1)
    flip = (row + column == 127).astype(jnp.bfloat16)
    rows = dot_nn(to_half(rows), flip)
    tiles = [rows[i : i + 1, :] for i in range(width // 128)][::-1]
    values = jnp.broadcast_to(jnp.concatenate(tiles, axis=1), (count, width))
    numbers = lax.broadcasted_iota(jnp.int32, (count, width), 0).astype(jnp.float32)
    return (values == numbers).astype(jnp.bfloat16)


def split_dot(exact, picks, dot):
    count = exact.shape[0]
    high = to_half(exact)
    rest = exact - widen(high)
    middle = to_half(rest)
    low = to_half(rest - widen(middle))
    parts = jnp.concatenate([widen(high), widen(middle), widen(low)], axis=0)
    result = dot(to_half(parts), picks)
    return result[:count] + (result[count : 2 * count] + result[2 * count :])


def fill_all_bias(plan, links, table_ref, buckets_ref, rows, tiles):
    rows[: table_ref.shape[0], :] = split_dot(
        table_ref[...], bucket_picks(table_ref.shape[1], buckets_ref), dot_nn
    )
    for head in range(plan.heads):
        row = rows[pl.ds(links.chip * plan.heads + head, 1), :]
        row = jnp.broadcast_to(row, (plan.rows, 2 * plan.length))
        tiles[head] = pltpu.roll(row, 1, 1, stride=1, stride_axis=0)


def as_column(row):
    count = row.shape[1]
    square = (count, count)
    same = lax.broadcasted_iota(jnp.int32, square, 0) == lax.broadcasted_iota(jnp.int32, square, 1)
    return jnp.sum(jnp.where(same, jnp.broadcast_to(row, square), 0.0), axis=1, keepdims=True)


def place_tokens(plan, routes_ref):
    total = plan.experts * plan.cycle
    shape = (plan.rows, total)
    routes = as_column(routes_ref[...].astype(jnp.float32))
    numbers = lax.broadcasted_iota(jnp.int32, shape, 1).astype(jnp.float32)
    hits = (routes == numbers).astype(jnp.float32)
    square = (plan.rows, plan.rows)
    row = lax.broadcasted_iota(jnp.int32, square, 0)
    column = lax.broadcasted_iota(jnp.int32, square, 1)
    earlier = (column < row).astype(jnp.bfloat16)
    before = dot_nn(earlier, to_half(hits))
    slot = jnp.sum((before + numbers * plan.capacity) * hits, axis=1, keepdims=True)
    slots = (plan.rows, total * plan.capacity)
    return (slot == lax.broadcasted_iota(jnp.int32, slots, 1).astype(jnp.float32)).astype(
        jnp.bfloat16
    )


def whole_forward_kernel(
    plan,
    x_ref,
    gain_ref,
    table_ref,
    buckets_ref,
    routes_ref,
    gate_ref,
    cot_ref,
    wq_hbm,
    wk_hbm,
    wv_hbm,
    wo_hbm,
    din_hbm,
    dout_hbm,
    ein_hbm,
    eout_hbm,
    output_ref,
    grad_ref,
    gain_grad_ref,
    stream_ref,
    mid_ref,
    attended_ref,
    norm_ref,
    dense_normed,
    cots_in,
    rows_in,
    cots_hbm,
    rows_early,
    normed_out,
    key_out,
    value_out,
    query_out,
    heads_out,
    normed_all,
    key_all,
    value_all,
    query_all,
    heads_all,
    wq,
    wk,
    wv,
    wo,
    up,
    down,
    bias_rows,
    tiles,
    value_t,
    scores,
    probs,
    heads_t,
    att_in,
    natural_sum,
    cots_out,
    rows_out,
    d_active,
    produced,
    d_rows,
    produced_in,
    d_rows_in,
    load_sem,
    near_send,
    near_recv,
    far_send,
    far_recv,
    att_send,
    att_recv,
    cots_send,
    cots_recv,
    rows_send,
    rows_recv,
    produced_send,
    produced_recv,
    d_rows_send,
    d_rows_recv,
    line_send,
    line_recv,
    own_sem,
    keep_sem,
):
    links = Links(plan)
    c, chip, core = links.c, links.chip, links.core
    columns = pl.ds(links.first, plan.wide)
    loads = {}

    def load(name, source, target):
        loads[name] = local(source, target, load_sem.at[len(loads)])

    for layer in range(2):
        for name, source, target in (("k", wk_hbm, wk), ("v", wv_hbm, wv), ("q", wq_hbm, wq)):
            load((name, layer), source.at[layer, :, columns], target.at[layer])
        load(("o", layer), wo_hbm.at[layer], wo.at[layer])
        if layer == 0:
            load("din", din_hbm, up.at[0])
            load("dout", dout_hbm, down.at[0])
    load("eout1", eout_hbm.at[1], down.at[1])
    load("ein1", ein_hbm.at[1], up.at[1])
    barrier = greet(plan, c)
    placed = place_tokens(plan, routes_ref)
    gate = as_column(gate_ref[...])
    total = plan.groups * plan.rows
    done_later, lines = [], []

    def project(layer, block, with_query):
        normed = normed_all[layer, block // 2, lax.rem(block, 2)]
        key_all[layer, block] = to_half(dot_nn(normed, wk[layer]))
        value_all[layer, block] = to_half(dot_nn(normed, wv[layer]))
        if with_query:
            query_all[layer, block // 2] = to_half(dot_nn(normed, wq[layer]))

    def attention(layer, hidden):
        normed, _ = rms_normed(hidden, gain_ref[layer * 2 : layer * 2 + 1, :])
        normed_all[layer, chip, core] = to_half(normed)
        if layer == 0:
            await_greetings(plan, barrier)
        own = normed_all.at[layer, chip, core]
        far = []
        for step in range(1, plan.chips):
            far.append(
                started(
                    remote(
                        own,
                        own,
                        far_send.at[layer, step],
                        far_recv.at[layer, step],
                        links.chip_device(step),
                    )
                )
            )
        near = [
            started(
                remote(own, own, near_send.at[layer, 0], near_recv.at[layer, 0], links.pair())
            )
        ]
        for name in ("k", "v", "q"):
            loads[(name, layer)].wait()
        project(layer, c, True)
        if layer == 0:
            fill_all_bias(plan, links, table_ref, buckets_ref, bias_rows, tiles)
            cots = gate * cot_ref[...]
            cots_out[...] = to_half(dot_tn(placed, to_half(cots))).reshape(cots_out.shape)
        near[0].wait_recv()
        project(layer, 2 * chip + 1 - core, False)
        for step in range(1, plan.chips):
            far[step - 1].wait_recv()
            from_chip = lax.rem(chip + plan.chips - step, plan.chips)
            block = normed_all.at[layer, from_chip, core]
            near.append(
                started(
                    remote(
                        block,
                        block,
                        near_send.at[layer, step],
                        near_recv.at[layer, step],
                        links.pair(),
                    )
                )
            )
            project(layer, 2 * from_chip + core, True)
        for step in range(1, plan.chips):
            near[step].wait_recv()
            from_chip = lax.rem(chip + plan.chips - step, plan.chips)
            project(layer, 2 * from_chip + 1 - core, False)
        for copy in far + near:
            copy.wait_send()
        if layer == 0:
            done_later.extend(start_slabs(plan, c, cots_out, cots_in, cots_send, cots_recv))

        queries = query_all[layer].reshape(total, plan.wide)
        value_t[...] = jnp.transpose(value_all[layer].reshape(plan.length, plan.wide))
        heads_t[...] = jnp.zeros_like(heads_t)
        for head in range(plan.heads):
            picked = jnp.where(links.head_lanes(queries.shape, head), queries, 0)

            top = jnp.full((1, total), -1e30, jnp.float32)
            many = plan.cycle // 2
            for first in range(0, plan.cycle, many):
                keys = key_all[layer, first : first + many].reshape(many * plan.rows, plan.wide)
                part = dot_nt(keys, picked)
                for block in range(many):
                    piece = part[block * plan.rows : (block + 1) * plan.rows, :]
                    piece = piece + bias_part(plan, tiles, head, first + block, core)
                    low = (first + block) * plan.rows
                    scores[low : low + plan.rows, :] = piece
                    top = jnp.maximum(top, jnp.max(piece, axis=0, keepdims=True))

            norm = jnp.zeros((1, total), jnp.float32)
            for block in range(plan.cycle):
                where = slice(block * plan.rows, (block + 1) * plan.rows)
                part = jnp.exp(scores[where, :] - top)
                probs[where, :] = to_half(part)
                norm = norm + jnp.sum(part, axis=0, keepdims=True)
            norm_ref[layer, head : head + 1, :] = top + jnp.log(norm)
            mine = links.head_rows(head)
            heads_t[mine, :] = dot_nn(value_t[mine, :], probs[...]) / norm
            if layer == 0 and head == 1:
                wait_all(done_later)
                lines.extend(
                    to_all_dp(links, cots_in, cots_hbm, line_send.at[0], line_recv.at[0])
                )
                lines.append(local(cots_in, cots_hbm.at[links.me], own_sem.at[0]))
        heads_all[layer] = to_half(jnp.transpose(heads_t[...])).reshape(
            plan.groups, plan.rows, plan.wide
        )
        copies = to_chips(
            links, heads_all.at[layer], att_in.at[layer], att_send.at[layer], att_recv.at[layer]
        )
        for slot, (kept, out) in enumerate(
            (
                (normed_all, normed_out),
                (key_all, key_out),
                (value_all, value_out),
                (query_all, query_out),
                (heads_all, heads_out),
            )
        ):
            lines.append(local(kept.at[layer], out.at[layer], keep_sem.at[layer, slot]))
        att_in[layer, chip] = heads_all[layer, chip]
        loads[("o", layer)].wait()
        wait_all(copies)
        attended = to_half(
            add_windows(plan, natural_sum, [widen(att_in[layer, g]) for g in range(plan.groups)])
        )
        attended_ref[layer] = attended
        return hidden + dot_nn(attended, wo[layer])

    mid = attention(0, x_ref[...])
    mid_ref[...] = mid
    normed, _ = rms_normed(mid, gain_ref[1:2, :])
    normed_half = to_half(normed)
    dense_normed[links.me] = normed_half
    mine = dense_normed.at[links.me]
    lines += to_all_dp(links, mine, dense_normed, line_send.at[1], line_recv.at[1])
    loads["din"].wait()
    active = to_half(smooth_act(dot_nn(normed_half, up[0])))
    loads["dout"].wait()
    stream = mid + dot_nn(active, down[0])
    stream_ref[...] = stream
    load("eout0", eout_hbm.at[0], down.at[0])
    load("ein0", ein_hbm.at[0], up.at[0])
    mid = attention(1, stream)

    gains = gain_ref[3:4, :]
    normed, inv_rms = rms_normed(mid, gains)
    rows_out[...] = to_half(dot_tn(placed, to_half(normed))).reshape(rows_out.shape)
    copies = start_slabs(plan, c, rows_out, rows_in, rows_send, rows_recv)
    count = plan.cycle * plan.capacity

    def of_expert(ref, e):
        return ref[:, e * plan.capacity : (e + 1) * plan.capacity, :].reshape(count, plan.model)

    for e in range(plan.experts):
        loads["eout%d" % e].wait()
        d_active[e] = dot_nt(of_expert(cots_in, e), down[e])
        loads["ein%d" % e].wait()
    wait_all(copies)
    early = rows_in.at[: plan.early]
    lines += to_all_dp(links, early, rows_early, line_send.at[2], line_recv.at[2])
    actives = []
    for e in range(plan.experts):
        pre = dot_nn(of_expert(rows_in, e), up[e])
        actives.append(to_half(smooth_act(pre)))
        d_pre = to_half(d_active[e] * smooth_slope(pre))
        d_rows[:, e * plan.capacity : (e + 1) * plan.capacity, :] = to_half(
            dot_nt(d_pre, up[e])
        ).reshape(plan.cycle, plan.capacity, plan.model)
    d_row_copies = start_slabs(plan, c, d_rows, d_rows_in, d_rows_send, d_rows_recv)
    for e in range(plan.experts):
        produced[:, e * plan.capacity : (e + 1) * plan.capacity, :] = to_half(
            dot_nn(actives[e], down[e])
        ).reshape(plan.cycle, plan.capacity, plan.model)
    produced_copies = start_slabs(plan, c, produced, produced_in, produced_send, produced_recv)
    wait_all(d_row_copies)
    slots = plan.cycle * plan.slab
    d_normed = dot_nn(placed, d_rows_in[...].reshape(slots, plan.model))
    gain_grad_ref[...] = jnp.sum(d_normed * mid * inv_rms, axis=0, keepdims=True)
    grad_ref[...] = cot_ref[...] + norm_slope(mid, inv_rms, gains, d_normed)
    wait_all(produced_copies)
    output_ref[...] = mid + gate * dot_nn(
        placed, produced_in[...].reshape(slots, plan.model)
    )
    wait_all(lines)


def norm_slope(hidden, inv_rms, gains, d_normed):
    d_scaled = d_normed * gains
    mean = jnp.mean(d_scaled * hidden, axis=-1, keepdims=True)
    return inv_rms * d_scaled - hidden * (inv_rms * inv_rms * inv_rms) * mean


def whole_forward(plan, x, gains, table, buckets, routes, gate, cot, weights, dense, experts):
    f32, half = jnp.float32, jnp.bfloat16
    whole = pl.BlockSpec(memory_space=VMEM)
    hbm = pl.BlockSpec(memory_space=pl.ANY)
    dma = pltpu.SemaphoreType.DMA
    total = plan.groups * plan.rows
    units = dense[0].shape[1]
    slabs = (plan.cycle, plan.slab, plan.model)
    window = (plan.rows, plan.wide)
    row = (plan.rows, plan.model)
    outs = [
        (row, f32),
        (row, f32),
        ((1, plan.model), f32),
        (row, f32),
        (row, f32),
        ((2,) + row, half),
        ((2, plan.heads, total), f32),
        ((plan.copies,) + row, half),
        (slabs, half),
        (slabs, half),
        ((plan.copies,) + slabs, half),
        ((plan.copies, plan.early) + slabs[1:], half),
    ]
    kept = [
        ((2, plan.chips, 2) + row, half),
        ((2, plan.cycle) + window, half),
        ((2, plan.cycle) + window, half),
        ((2, plan.groups) + window, half),
        ((2, plan.groups) + window, half),
    ]
    outs += kept
    cycle_sems = [dma((plan.cycle,))] * 2
    return pl.pallas_call(
        functools.partial(whole_forward_kernel, plan),
        out_shape=tuple(jax.ShapeDtypeStruct(*out) for out in outs),
        in_specs=[whole] * 7 + [hbm] * 8,
        out_specs=(whole,) * 10 + (hbm,) * 7,
        scratch_shapes=[VMEM(*one) for one in kept]
        + [
            VMEM((2, plan.model, plan.wide), half),
            VMEM((2, plan.model, plan.wide), half),
            VMEM((2, plan.model, plan.wide), half),
            VMEM((2, plan.model, plan.model), half),
            VMEM((2, plan.model, units), half),
            VMEM((2, units, plan.model), half),
            VMEM((16, 2 * plan.length), f32),
            VMEM((plan.heads, plan.rows, 2 * plan.length), f32),
            VMEM((plan.wide, plan.length), half),
            VMEM((plan.length, total), f32),
            VMEM((plan.length, total), half),
            VMEM((plan.wide, total), f32),
            VMEM((2, plan.groups) + window, half),
            VMEM(row, f32),
            VMEM(slabs, half),
            VMEM(slabs, half),
            VMEM((plan.experts, plan.cycle * plan.capacity, units), f32),
            VMEM(slabs, half),
            VMEM(slabs, half),
            VMEM(slabs, half),
            VMEM(slabs, half),
            dma((14,)),
            dma((2, plan.chips)),
            dma((2, plan.chips)),
            dma((2, plan.chips)),
            dma((2, plan.chips)),
            dma((2, plan.chips)),
            dma((2, plan.chips)),
        ]
        + cycle_sems * 4
        + [dma((3, plan.copies)), dma((3, plan.copies)), dma((1,)), dma((2, len(kept)))],
        compiler_params=pltpu.CompilerParams(
            collective_id=0, has_side_effects=True, vmem_limit_bytes=60 * 1024 * 1024
        ),
        name="whole_forward",
    )(x, gains, table, buckets, routes, gate, cot, *weights, *dense, *experts)


def whole_backward_kernel(
    plan,
    grad_ref,
    stream_ref,
    x_ref,
    mid_ref,
    gain_ref,
    last_gain_ref,
    table_ref,
    buckets_ref,
    attended_ref,
    norm_ref,
    normed_z,
    normed_hbm,
    key_hbm,
    value_hbm,
    query_hbm,
    heads_hbm,
    cots_hbm,
    rows_hbm,
    early_hbm,
    wq_hbm,
    wk_hbm,
    wv_hbm,
    wo_hbm,
    din_hbm,
    dout_hbm,
    ein_hbm,
    eout_hbm,
    input_grad_ref,
    three_ref,
    out_ref,
    dense_ref,
    small_ref,
    ein_grad,
    eout_grad,
    normed_all,
    key_all,
    value_all,
    query_all,
    heads_all,
    weights,
    up,
    down,
    cots_all,
    rows_all,
    bias_rows,
    tiles,
    sums,
    grad_out,
    grad_in,
    key_t,
    products,
    picked_queries,
    picked_grads,
    key_part,
    value_part,
    pair_out,
    pair_in,
    own_out,
    own_in,
    query_t,
    query_out,
    query_in,
    natural_sum,
    stage,
    o_half,
    o_sum,
    o_part,
    o_row,
    o_in,
    three_pair,
    three_half,
    three_sum,
    three_part,
    three_in,
    grads_z,
    dense_pair,
    dense_half,
    dense_part,
    small_mine,
    small_half,
    small_sum,
    small_part,
    small_row,
    small_in,
    load_sem,
    own_sem,
    grad_send,
    grad_recv,
    pair_send,
    pair_recv,
    back_send,
    back_recv,
    query_send,
    query_recv,
    chain_send,
    chain_recv,
    plane_send,
    plane_recv,
    line_send,
    line_recv,
):
    links = Links(plan)
    c, chip, core, me = links.c, links.chip, links.core, links.me
    loads = {}

    def load(name, source, target):
        loads[name] = local(source, target, load_sem.at[len(loads)])

    def load_layer(layer):
        for name, source, target in (
            ("query", query_hbm, query_all),
            ("key", key_hbm, key_all),
            ("value", value_hbm, value_all),
            ("heads", heads_hbm, heads_all),
            ("normed", normed_hbm, normed_all),
        ):
            load((name, layer), source.at[layer], target)

    part = up.shape[1] // plan.copies
    mine = pl.ds(pl.multiple_of(me * part, part), part)
    load(("o", 1), wo_hbm.at[1], weights.at[3])
    load_layer(1)
    for slot, name, source in ((0, "v", wv_hbm), (1, "k", wk_hbm), (2, "q", wq_hbm)):
        load((name, 1), source.at[1], weights.at[slot])
    load("up", din_hbm, up)
    load("down", dout_hbm, down)
    load("cots", cots_hbm, cots_all)
    rows_own = [local(rows_hbm, rows_all.at[me], own_sem.at[0])]
    for step in range(1, plan.copies):
        other = links.at_dp(step)
        target = rows_all.at[other, : plan.early]
        rows_own.append(
            local(early_hbm.at[other], target, own_sem.at[2 * plan.experts + step])
        )

    barrier = pltpu.get_barrier_semaphore()
    others = [links.pair()]
    others += [links.chip_device(step) for step in range(1, plan.chips)]
    others += [links.dp_device(step) for step in range(1, plan.copies)]
    for other in others:
        pl.semaphore_signal(barrier, inc=1, device_id=other, device_id_type=MESH)

    total = plan.groups * plan.rows
    rows_lines = []
    share = plan.share

    def send_rows(sems, first, last):
        for step in range(1, plan.copies):
            rows_lines.append(
                started(
                    remote(
                        rows_hbm.at[first:last],
                        rows_all.at[me, first:last],
                        line_send.at[sems, step],
                        line_recv.at[sems, step],
                        links.dp_device(step),
                    )
                )
            )

    def o_start(layer, grad_half):
        stage[: plan.model, :] = dot_tn(grad_half, attended_ref[layer])

        def one(i, carry):
            side, to = lax.rem(i, 2), i // 2
            pieces = []
            for d in range(plan.copies):
                first = (d * plan.cycle + i) * share
                pieces.append(stage[pl.ds(pl.multiple_of(first, 8), share), :])
            dense_pair[side, to, : plan.copies * share, :] = to_half(jnp.concatenate(pieces, axis=0))
            return carry

        lax.fori_loop(0, plan.cycle, one, 0)
        return started(
            remote(
                dense_pair.at[1 - core, :, : plan.copies * share, :],
                o_half.at[layer],
                chain_send.at[layer, 0],
                chain_recv.at[layer, 0],
                links.pair(),
            )
        )

    def o_plane(layer, copy):
        copy.wait()
        o_sum[...] = to_half(
            widen(dense_pair[core, :, : plan.copies * share, :]) + widen(o_half[layer])
        )
        return to_chips(
            links,
            o_sum,
            o_part.at[layer],
            plane_send.at[layer],
            plane_recv.at[layer],
            by_step=True,
        )

    def o_line(layer, copies):
        wait_all(copies)
        value = widen(o_sum[chip])
        for step in range(1, plan.chips):
            value = value + widen(o_part[layer, step])
        pad = jnp.zeros((o_row.shape[2] - share, plan.model), jnp.float32)
        for d in range(plan.copies):
            piece = jnp.concatenate([value[d * share : (d + 1) * share, :], pad], axis=0)
            o_row[layer, d] = to_half(piece)
        return to_lines(
            links, o_row.at[layer], o_in.at[layer], line_send.at[layer], line_recv.at[layer]
        )

    def o_finish(layer, copies):
        wait_all(copies)
        value = widen(o_row[layer, me])
        for step in range(1, plan.copies):
            value = value + widen(o_in[layer, step])
        out_ref[layer] = value[:share, :]

    def three_start(layer):
        normed = normed_all[...].reshape(plan.length, plan.model)
        own_normed = normed_all[:, core].reshape(total, plan.model)
        stage[: plan.wide, :] = dot_tn(query_out[layer].reshape(total, plan.wide), own_normed)
        stage[plan.wide : 2 * plan.wide, :] = dot_tn(key_part[...].reshape(plan.length, plan.wide), normed)
        stage[2 * plan.wide : 3 * plan.wide, :] = dot_tn(value_part[...].reshape(plan.length, plan.wide), normed)
        for side in range(2):
            for slot in range(3):
                pieces = []
                for to in range(plan.chips):
                    first = slot * plan.wide + links.lead + (2 * to + side) * share
                    pieces.append(stage[pl.ds(pl.multiple_of(first, 8), share), :])
                three_pair[side, slot] = to_half(jnp.concatenate(pieces, axis=0))
        return started(
            remote(
                three_pair.at[1 - core],
                three_half.at[layer],
                chain_send.at[2 + layer, 0],
                chain_recv.at[2 + layer, 0],
                links.pair(),
            )
        )

    def three_plane(layer, copy):
        copy.wait()
        both = []
        for slot in range(3):
            both.append(widen(three_pair[core, slot]) + widen(three_half[layer, slot]))
        pad = jnp.zeros((three_sum.shape[2] - 3 * share, plan.model), jnp.float32)
        for to in range(plan.chips):
            pieces = [value[to * share : (to + 1) * share, :] for value in both]
            three_sum[layer, to] = to_half(jnp.concatenate(pieces + [pad], axis=0))
        three_part[layer, chip] = three_sum[layer, chip]
        return to_chips(
            links,
            three_sum.at[layer],
            three_part.at[layer],
            plane_send.at[2 + layer],
            plane_recv.at[2 + layer],
        )

    def three_line(layer, copies):
        wait_all(copies)
        return to_lines(
            links,
            three_part.at[layer],
            three_in.at[layer],
            line_send.at[2 + layer],
            line_recv.at[2 + layer],
        )

    def three_finish(layer, copies):
        wait_all(copies)
        value = widen(three_part[layer, me])
        for step in range(1, plan.copies):
            value = value + widen(three_in[layer, step])
        three_ref[layer] = value[: 3 * share, :]

    def attention(layer, grad, hidden, before, between):
        grad_half = to_half(grad)
        loads[("o", layer)].wait()
        d_attended = dot_nt(grad_half, weights[3])
        for g in range(plan.groups):
            first = plan.window(g)
            grad_out[layer, g] = to_half(d_attended[:, first : first + plan.wide])
        if layer == 1:
            pl.semaphore_wait(barrier, len(others))
            load(("o", 0), wo_hbm.at[0], weights.at[3])
        copies = to_chips(
            links, grad_out.at[layer], grad_in.at[layer], grad_send.at[layer], grad_recv.at[layer]
        )
        grad_in[layer, chip] = grad_out[layer, chip]
        if layer == 1:
            send_rows(5, plan.early, plan.cycle // 2 + 1)
        o_copy = o_start(layer, grad_half)
        if layer == 1:
            fill_all_bias(plan, links, table_ref, buckets_ref, bias_rows, tiles)
            sums[...] = jnp.zeros_like(sums)
        for name in ("query", "key", "heads", "value"):
            loads[(name, layer)].wait()
        queries = query_all[...].reshape(total, plan.wide)
        for head in range(plan.heads):
            picked_queries[head] = jnp.where(links.head_lanes(queries.shape, head), queries, 0)
        query_t[...] = jnp.zeros_like(query_t)
        key_t[...] = jnp.transpose(key_all[...].reshape(plan.length, plan.wide))
        products[...] = jnp.transpose(widen(heads_all[...].reshape(total, plan.wide)))
        wait_all(copies)
        before()
        grads = grad_in[layer].reshape(total, plan.wide)
        for head in range(plan.heads):
            picked_grads[head] = jnp.where(links.head_lanes(grads.shape, head), grads, 0)
        products[...] = products[...] * jnp.transpose(widen(grads))
        delta = [
            jnp.sum(products[links.head_rows(head), :], axis=0, keepdims=True)
            for head in range(plan.heads)
        ]
        log_norm = [norm_ref[layer, head : head + 1, :] for head in range(plan.heads)]

        def process(blocks):
            keys = jnp.concatenate([key_all[block] for block in blocks], axis=0)
            values = jnp.concatenate([value_all[block] for block in blocks], axis=0)
            d_keys = d_values = None
            for head in range(plan.heads):
                bias = [bias_part(plan, tiles, head, block, core) for block in blocks]
                part = dot_nt(keys, picked_queries[head]) + jnp.concatenate(bias, axis=0)
                part = jnp.exp(part - log_norm[head])
                slope = part * (dot_nt(values, picked_grads[head]) - delta[head])
                for slot, block in enumerate(blocks):
                    rows = slice(slot * plan.rows, (slot + 1) * plan.rows)
                    for b in range(plan.groups):
                        first = plan.length + (b * plan.splits + core - block) * plan.rows
                        at = pl.ds(pl.multiple_of(first, plan.rows), plan.rows)
                        sums[head, :, at] += slope[rows, b * plan.rows : (b + 1) * plan.rows]
                slope = to_half(slope)
                keys_t = [
                    key_t[
                        links.head_rows(head),
                        pl.ds(pl.multiple_of(block * plan.rows, plan.rows), plan.rows),
                    ]
                    for block in blocks
                ]
                query_t[links.head_rows(head), :] += dot_nn(
                    jnp.concatenate(keys_t, axis=1), slope
                )
                key_piece = dot_nn(slope, picked_queries[head])
                value_piece = dot_nn(to_half(part), picked_grads[head])
                d_keys = key_piece if head == 0 else d_keys + key_piece
                d_values = value_piece if head == 0 else d_values + value_piece
            for slot, block in enumerate(blocks):
                rows = slice(slot * plan.rows, (slot + 1) * plan.rows)
                key_part[block] = to_half(d_keys[rows, :])
                value_part[block] = to_half(d_values[rows, :])
            return d_keys, d_values

        def pair_copy(step):
            return remote(
                pair_out.at[step],
                pair_in.at[layer, step],
                pair_send.at[layer, step],
                pair_recv.at[layer, step],
                links.pair(),
            )

        steps = [(i + 1) % plan.chips for i in range(plan.chips)]
        d_keys, d_values = process([2 * links.at_chip(step) + 1 - core for step in steps])
        for slot, step in enumerate(steps):
            rows = slice(slot * plan.rows, (slot + 1) * plan.rows)
            pair_out[step, 0] = to_half(d_keys[rows, :])
            pair_out[step, 1] = to_half(d_values[rows, :])
            pair_copy(step).start()

        def back_copy(step):
            return remote(
                own_out.at[step],
                own_in.at[layer, chip],
                back_send.at[layer, step],
                back_recv.at[layer, step],
                links.chip_device(step),
            )

        d_keys, d_values = process([2 * links.at_chip(step) + core for step in steps])
        for slot, step in enumerate(steps):
            rows = slice(slot * plan.rows, (slot + 1) * plan.rows)
            pair_copy(step).wait_recv()
            own_out[step, 0] = to_half(d_keys[rows, :] + widen(pair_in[layer, step, 0]))
            own_out[step, 1] = to_half(d_values[rows, :] + widen(pair_in[layer, step, 1]))
            if step > 0:
                back_copy(step).start()
        own_in[layer, chip] = own_out[0]
        query_out[layer] = to_half(jnp.transpose(query_t[...])).reshape(
            plan.groups, plan.rows, plan.wide
        )
        copies = to_chips(
            links,
            query_out.at[layer],
            query_in.at[layer],
            query_send.at[layer],
            query_recv.at[layer],
        )
        query_in[layer, chip] = query_out[layer, chip]
        loads[("normed", layer)].wait()
        three_copy = three_start(layer)
        o_copies = o_plane(layer, o_copy)
        between_result = between()
        inv_rms = lax.rsqrt(jnp.mean(hidden * hidden, axis=-1, keepdims=True) + epsilon)
        for name in ("v", "k", "q"):
            loads[(name, layer)].wait()
        wait_all(copies)
        for step in range(1, plan.chips):
            back_copy(step).wait()
        for step in range(plan.chips):
            pair_copy(step).wait_send()
        groups = range(plan.groups)
        d_queries = to_half(
            add_windows(plan, natural_sum, [widen(query_in[layer, g]) for g in groups])
        )
        d_keys = to_half(
            add_windows(plan, natural_sum, [widen(own_in[layer, g, 0]) for g in groups])
        )
        d_values = to_half(
            add_windows(plan, natural_sum, [widen(own_in[layer, g, 1]) for g in groups])
        )
        d_normed = (
            dot_nt(d_queries, weights[2])
            + dot_nt(d_keys, weights[1])
            + dot_nt(d_values, weights[0])
        )
        if layer == 1:
            load_layer(0)
            for slot, name, source in ((0, "v", wv_hbm), (1, "k", wk_hbm), (2, "q", wq_hbm)):
                load((name, 0), source.at[0], weights.at[slot])
        gains = gain_ref[2 * layer : 2 * layer + 1, :]
        small_mine[2 * layer : 2 * layer + 1, :] = jnp.sum(
            d_normed * hidden * inv_rms, axis=0, keepdims=True
        )
        result = grad + norm_slope(hidden, inv_rms, gains, d_normed)
        return result, o_copies, three_copy, between_result

    small_mine[...] = jnp.zeros_like(small_mine)
    small_mine[3:4, :] = last_gain_ref[...]
    grad, o_one, three_one, _ = attention(
        1, grad_ref[...], stream_ref[...], lambda: None, lambda: None
    )

    grad_half = to_half(grad)
    grads_z[me] = grad_half
    grad_lines = to_all_dp(links, grads_z.at[me], grads_z, line_send.at[4], line_recv.at[4])
    send_rows(7, plan.cycle // 2 + 1, plan.cycle)
    mid = mid_ref[...]
    gains = gain_ref[1:2, :]
    normed, inv_rms = rms_normed(mid, gains)
    loads["up"].wait()
    loads["down"].wait()
    normed_half = to_half(normed)
    d_normed = jnp.zeros_like(normed)
    for slot in range(plan.copies):
        units = slice(slot * part, (slot + 1) * part)
        pre = dot_nn(normed_half, up[:, units])
        d_pre = to_half(dot_nt(grad_half, down[units, :]) * smooth_slope(pre))
        d_normed = d_normed + dot_nt(d_pre, up[:, units])
    pieces = [slice(slot * part, (slot + 1) * part) for slot in range(plan.experts + 1)]
    for e in range(plan.experts):
        load("ein%d" % e, ein_hbm.at[e, :, mine], up.at[:, pieces[e]])
        load("eout%d" % e, eout_hbm.at[e, mine, :], down.at[pieces[e], :])
    load("din", din_hbm.at[:, mine], up.at[:, pieces[-1]])
    load("dout", dout_hbm.at[mine, :], down.at[pieces[-1], :])
    small_mine[1:2, :] = jnp.sum(d_normed * mid * inv_rms, axis=0, keepdims=True)
    grad = grad + norm_slope(mid, inv_rms, gains, d_normed)

    three_one = three_plane(1, three_one)
    o_one = o_line(1, o_one)
    three_lines = []

    def send_three():
        three_lines.extend(three_line(1, three_one))

    def dense_grads():
        wait_all(grad_lines)
        count = plan.copies * plan.rows
        normed = normed_z[...].reshape(count, plan.model)
        grads = grads_z[...].reshape(count, plan.model)
        loads["din"].wait()
        loads["dout"].wait()
        height = part // plan.cycle
        some = part // plan.chips
        for to in range(plan.chips):
            units = slice(pieces[-1].start + to * some, pieces[-1].start + (to + 1) * some)
            pre = dot_nn(normed, up[:, units])
            active = to_half(smooth_act(pre))
            d_pre = to_half(dot_nt(grads, down[units, :]) * smooth_slope(pre))
            in_grad = to_half(dot_tn(d_pre, normed))
            out_grad = to_half(dot_tn(active, grads))
            for side in range(2):
                rows = slice(side * height, (side + 1) * height)
                dense_pair[side, to, :height, :] = in_grad[rows, :]
                dense_pair[side, to, height:, :] = out_grad[rows, :]
        return started(
            remote(
                dense_pair.at[1 - core],
                dense_half,
                chain_send.at[4, 0],
                chain_recv.at[4, 0],
                links.pair(),
            )
        )

    grad, o_zero, three_zero, dense_copy = attention(
        0, grad, x_ref[...], lambda: None, dense_grads
    )
    input_grad_ref[...] = grad

    three_zero = three_plane(0, three_zero)
    dense_copy.wait()

    def join(i, carry):
        dense_pair[core, i] = to_half(widen(dense_pair[core, i]) + widen(dense_half[i]))
        return carry

    lax.fori_loop(0, plan.chips, join, 0)
    dense_copies = to_chips(
        links, dense_pair.at[core], dense_part, plane_send.at[4], plane_recv.at[4], by_step=True
    )
    send_three()
    diagonals = []
    for head in range(plan.heads):
        total_rows = None
        for first in range(0, plan.rows, 8):
            moved = rotate(sums[head, first : first + 8, :], -first - 1)
            total_rows = moved if first == 0 else total_rows + moved
        diagonal = total_rows[0:1, :]
        for r in range(1, 8):
            diagonal = diagonal + rotate(total_rows, -r)[r : r + 1, :]
        diagonals.append(diagonal)
    table_grad = split_dot(jnp.concatenate(diagonals, axis=0), bucket_picks(128, buckets_ref), dot_nt)
    lane = lax.broadcasted_iota(jnp.int32, (plan.heads, plan.model), 1)
    repeated = jnp.concatenate([table_grad] * (plan.model // 128), axis=1)
    small_mine[4 : 4 + plan.heads, :] = jnp.where(lane // 128 == chip, repeated, 0.0)
    small_copy = started(
        remote(
            small_mine, small_half, chain_send.at[5, 0], chain_recv.at[5, 0], links.pair()
        )
    )

    three_zero = three_line(0, three_zero)
    o_zero = o_line(0, o_zero)
    small_copy.wait()
    small_sum[...] = small_mine[...] + small_half[...]
    small_copies = to_chips(
        links, small_sum, small_part, plane_send.at[5], plane_recv.at[5], by_step=True, whole=True
    )

    loads["cots"].wait()
    wait_all(rows_own)
    wait_all(rows_lines)
    slots = plan.copies * plan.cycle * plan.capacity
    stores = []
    for e in range(plan.experts):
        picked = slice(e * plan.capacity, (e + 1) * plan.capacity)
        rows = rows_all[:, :, picked, :].reshape(slots, plan.model)
        cots = cots_all[:, :, picked, :].reshape(slots, plan.model)
        loads["ein%d" % e].wait()
        loads["eout%d" % e].wait()
        for low in range(0, part, plan.wide):
            units = slice(e * part + low, e * part + low + plan.wide)
            pre = dot_nn(rows, up[:, units])
            active = to_half(smooth_act(pre))
            d_pre = to_half(dot_nt(cots, down[units, :]) * smooth_slope(pre))
            weights[e, :, low : low + plan.wide] = to_half(dot_tn(rows, d_pre))
            weights[plan.experts + e, low : low + plan.wide, :] = to_half(dot_tn(active, cots))
        stores.append(local(weights.at[e], ein_grad.at[e], own_sem.at[1 + 2 * e]))
        stores.append(
            local(weights.at[plan.experts + e], eout_grad.at[e], own_sem.at[2 + 2 * e])
        )
        if e == 0:
            wait_all(small_copies)
            value = small_sum[...]
            for step in range(1, plan.chips):
                value = value + small_part[step]
            small_row[...] = value
            small_copies = to_lines(
                links, small_row, small_in, line_send.at[6], line_recv.at[6], whole=True
            )

    wait_all(small_copies)
    value = small_row[...]
    for step in range(1, plan.copies):
        value = value + small_in[step]
    small_ref[...] = value
    three_finish(1, three_lines)
    o_finish(1, o_one)
    wait_all(dense_copies)
    value = widen(dense_pair[core, chip])
    for step in range(1, plan.chips):
        value = value + widen(dense_part[step])
    dense_ref[...] = value
    three_finish(0, three_zero)
    o_finish(0, o_zero)
    wait_all(stores)


def whole_backward(plan, values, caches, weights, dense, experts):
    f32, half = jnp.float32, jnp.bfloat16
    whole = pl.BlockSpec(memory_space=VMEM)
    hbm = pl.BlockSpec(memory_space=pl.ANY)
    dma = pltpu.SemaphoreType.DMA
    total = plan.groups * plan.rows
    model, share = plan.model, plan.share
    units = dense[0].shape[1]
    part = units // plan.copies
    slabs = (plan.cycle, plan.slab, model)
    window = (plan.rows, plan.wide)
    row = (plan.rows, model)
    height = 2 * part // plan.cycle
    o_rows, three_rows = -(-share // 16) * 16, -(-3 * share // 16) * 16
    small = (8, model)
    outs = [
        (row, f32),
        ((2, 3 * share, model), f32),
        ((2, share, model), f32),
        ((height, model), f32),
        (small, f32),
        ((plan.experts, model, part), half),
        ((plan.experts, part, model), half),
    ]
    chip_o = (plan.chips, plan.copies * share, model)
    chip_dense = (plan.chips, height, model)
    scratch = [
        ((plan.chips, 2) + row, half),
        ((plan.cycle,) + window, half),
        ((plan.cycle,) + window, half),
        ((plan.groups,) + window, half),
        ((plan.groups,) + window, half),
        ((4, model, model), half),
        ((model, units), half),
        ((units, model), half),
        ((plan.copies,) + slabs, half),
        ((plan.copies,) + slabs, half),
        ((16, 2 * plan.length), f32),
        ((plan.heads, plan.rows, 2 * plan.length), f32),
        ((plan.heads, plan.rows, 2 * plan.length), f32),
        ((2, plan.groups) + window, half),
        ((2, plan.groups) + window, half),
        ((plan.wide, plan.length), half),
        ((plan.wide, total), f32),
        ((plan.heads, total, plan.wide), half),
        ((plan.heads, total, plan.wide), half),
        ((plan.cycle,) + window, half),
        ((plan.cycle,) + window, half),
        ((plan.chips, 2) + window, half),
        ((2, plan.chips, 2) + window, half),
        ((plan.chips, 2) + window, half),
        ((2, plan.groups, 2) + window, half),
        ((plan.wide, total), f32),
        ((2, plan.groups) + window, half),
        ((2, plan.groups) + window, half),
        (row, f32),
        ((max(model, 3 * plan.wide), model), f32),
        ((2,) + chip_o, half),
        (chip_o, half),
        ((2,) + chip_o, half),
        ((2, plan.copies, o_rows, model), half),
        ((2, plan.copies, o_rows, model), half),
        ((2, 3, plan.chips * share, model), half),
        ((2, 3, plan.chips * share, model), half),
        ((2, plan.chips, three_rows, model), half),
        ((2, plan.chips, three_rows, model), half),
        ((2, plan.copies, three_rows, model), half),
        ((plan.copies,) + row, half),
        ((2,) + chip_dense, half),
        (chip_dense, half),
        (chip_dense, half),
        (small, f32),
        (small, f32),
        (small, f32),
        ((plan.chips,) + small, f32),
        (small, f32),
        ((plan.copies,) + small, f32),
    ]
    chips, copies = plan.chips, plan.copies
    sems = [(28,), (2 * plan.experts + plan.copies,)]
    sems += [(2, chips)] * 8
    sems += [(6, 1)] * 2 + [(6, chips)] * 2 + [(8, copies)] * 2
    return pl.pallas_call(
        functools.partial(whole_backward_kernel, plan),
        out_shape=tuple(jax.ShapeDtypeStruct(*out) for out in outs),
        in_specs=[whole] * len(values) + [hbm] * (len(caches) + 8),
        out_specs=(whole,) * (len(outs) - 2) + (hbm,) * 2,
        scratch_shapes=[VMEM(*one) for one in scratch] + [dma(one) for one in sems],
        compiler_params=pltpu.CompilerParams(
            collective_id=1, has_side_effects=True, vmem_limit_bytes=63 * 1024 * 1024
        ),
        name="whole_backward",
    )(*values, *caches, *weights, *dense, *experts)


def rms_backward(hidden, inv_rms, gains, d_normed):
    d_gains = jnp.sum(d_normed * hidden * inv_rms, axis=0)
    return (norm_slope(hidden, inv_rms, gains, d_normed), d_gains)


def body(
    inputs,
    w_query,
    w_key,
    w_value,
    w_out,
    norm_gain,
    bias_table,
    dense_in,
    dense_out,
    expert_in,
    expert_out,
    routes,
    gate_scale,
    buckets,
    cotangent,
):
    group_rows, model_width = inputs.shape
    head_count = bias_table.shape[1]
    plan = Plan(
        lax.axis_size("dp"),
        lax.axis_size(("ctx", "exp")),
        lax.axis_size("exp"),
        head_count,
        model_width // head_count,
        group_rows,
        expert_in.shape[0],
    )
    attention = (w_query, w_key, w_value, w_out)
    dense = (dense_in, dense_out)
    experts = (expert_in, expert_out)
    if not plan.fused:
        return separate_body(
            plan,
            inputs,
            attention,
            norm_gain,
            bias_table,
            dense,
            experts,
            routes,
            gate_scale,
            jnp.concatenate([buckets[:1], buckets[:0:-1]]),
            cotangent,
        )
    bucket_row, table = buckets[None], bias_table.T
    (
        output,
        grad,
        last_gain,
        stream,
        mid,
        attended,
        log_norm,
        dense_normed,
        _,
        rows,
        cots,
        rows_early,
        *kept,
    ) = whole_forward(
        plan,
        inputs,
        norm_gain,
        table,
        bucket_row,
        routes.T,
        gate_scale.T,
        cotangent,
        attention,
        dense,
        experts,
    )
    input_grad, three, out, dense_share, small, grad_ein, grad_eout = whole_backward(
        plan,
        (
            grad,
            stream,
            inputs,
            mid,
            norm_gain,
            last_gain,
            table,
            bucket_row,
            attended,
            log_norm,
            dense_normed,
        ),
        (*kept, cots, rows, rows_early),
        attention,
        dense,
        experts,
    )
    share = plan.share
    place = lax.axis_index(("dp", "ctx", "exp"))
    three = jnp.transpose(three.reshape(2, 3, share, model_width), (1, 0, 3, 2))
    gains = lax.dynamic_slice_in_dim(small[:4], place * share, share, 1)
    bucket_count = bias_table.shape[0]
    table = small[4 : 4 + plan.heads, : plan.groups * 128].reshape(plan.heads, plan.groups, 128)
    table = jnp.transpose(table[:, :, :bucket_count], (2, 1, 0)).reshape(bucket_count * head_count)
    table_share = bucket_count * head_count // (plan.copies * plan.cycle)
    table = lax.dynamic_slice_in_dim(table, place * table_share, table_share, 0)
    half_rows = dense_share.shape[0] // 2
    return (
        output,
        input_grad,
        three[0],
        three[1],
        three[2],
        jnp.transpose(out, (0, 2, 1)),
        gains,
        table,
        dense_share[:half_rows].T,
        dense_share[half_rows:],
        widen(grad_ein),
        widen(grad_eout),
    )


def separate_body(
    plan,
    inputs,
    attention,
    norm_gain,
    bias_table,
    dense,
    experts,
    routes,
    gate_scale,
    reversed_buckets,
    cotangent,
):
    group_rows, model_width = inputs.shape
    bucket_count, head_count = bias_table.shape
    dense_in, dense_out = dense
    expert_in, expert_out = experts
    cycle_size = plan.cycle
    my_group = lax.axis_index(("ctx", "exp")) // plan.splits
    bucket_hits = (
        reversed_buckets[None, :] == jnp.arange(bucket_count, dtype=jnp.int32)[:, None]
    ).astype(jnp.float32)
    my_table = lax.dynamic_slice_in_dim(bias_table.T, my_group * plan.heads, plan.heads, 0)
    bias_rows = jnp.dot(my_table, bucket_hits, precision=highest)
    local_experts = expert_in.shape[0]
    expert_total = local_experts * cycle_size
    capacity = 2 * group_rows // expert_total
    recv_rows = cycle_size * capacity
    flat_routes = routes[:, 0]
    route_hits = (
        flat_routes[:, None] == jnp.arange(expert_total, dtype=jnp.int32)[None, :]
    ).astype(jnp.int32)
    slot_order = jnp.sum((jnp.cumsum(route_hits, axis=0) - 1) * route_hits, axis=1)
    target = flat_routes * capacity + slot_order
    dispatch = (
        target[None, :] == jnp.arange(expert_total * capacity, dtype=jnp.int32)[:, None]
    ).astype(jnp.bfloat16)

    def to_owners(rows_half):
        placed = jnp.dot(dispatch, rows_half, preferred_element_type=jnp.float32)
        return lax.all_to_all(
            to_half(placed).reshape(cycle_size, local_experts, capacity, model_width),
            ("ctx", "exp"),
            split_axis=0,
            concat_axis=2,
            tiled=True,
        ).reshape(local_experts, recv_rows, model_width)

    def from_owners(produced):
        returned = lax.all_to_all(
            produced.reshape(1, local_experts, recv_rows, model_width),
            ("ctx", "exp"),
            split_axis=2,
            concat_axis=0,
            tiled=True,
        )
        return jnp.einsum(
            "sc,sd->cd",
            dispatch,
            returned.reshape(expert_total * capacity, model_width),
            preferred_element_type=jnp.float32,
        )

    mid_zero, *cache_zero = attention_forward(
        plan, 0, inputs, norm_gain, bias_rows, *attention, 0
    )
    inv_rms_one = lax.rsqrt(jnp.mean(mid_zero * mid_zero, axis=-1, keepdims=True) + epsilon)
    normed_half = to_half(mid_zero * inv_rms_one * norm_gain[1])
    pre_act = jnp.dot(normed_half, dense_in, preferred_element_type=jnp.float32)
    active = to_half(smooth_act(pre_act))
    stream = mid_zero + jnp.dot(active, dense_out, preferred_element_type=jnp.float32)
    mid_one, *cache_one = attention_forward(plan, 1, stream, norm_gain, bias_rows, *attention, 1)
    grad_rows = to_owners(to_half(gate_scale * cotangent))
    inv_rms_three = lax.rsqrt(jnp.mean(mid_one * mid_one, axis=-1, keepdims=True) + epsilon)
    rows = to_owners(to_half(mid_one * inv_rms_three * norm_gain[3]))
    expert_pre = jnp.einsum("erd,edf->erf", rows, expert_in, preferred_element_type=jnp.float32)
    expert_active = to_half(smooth_act(expert_pre))
    produced = to_half(
        jnp.einsum("erf,efd->erd", expert_active, expert_out, preferred_element_type=jnp.float32)
    )
    d_active = jnp.einsum("erd,efd->erf", grad_rows, expert_out, preferred_element_type=jnp.float32)
    expert_d_pre = to_half(d_active * smooth_slope(expert_pre))
    d_rows = to_half(
        jnp.einsum("erf,edf->erd", expert_d_pre, expert_in, preferred_element_type=jnp.float32)
    )
    output = mid_one + gate_scale * from_owners(produced)
    d_hidden, gains_four = rms_backward(mid_one, inv_rms_three, norm_gain[3], from_owners(d_rows))
    grad_three = cotangent + d_hidden

    grad_two, gains_three, attn_two, bias_two = attention_backward(
        plan, 1, grad_three, [stream] + cache_one, norm_gain, bias_rows, *attention, 2
    )
    grad_half = to_half(grad_two)
    d_active = jnp.dot(grad_half, dense_out.T, preferred_element_type=jnp.float32)
    d_pre = to_half(d_active * smooth_slope(pre_act))
    d_normed = jnp.dot(d_pre, dense_in.T, preferred_element_type=jnp.float32)
    d_hidden, gains_two = rms_backward(mid_zero, inv_rms_one, norm_gain[1], d_normed)
    input_grad, gains_one, attn_one, bias_one = attention_backward(
        plan, 0, grad_two + d_hidden, [inputs] + cache_zero, norm_gain, bias_rows, *attention, 3
    )

    my_table_grad = jnp.dot(bucket_hits, (bias_one + bias_two).T, precision=highest)
    table_grad = lax.dynamic_update_slice(
        jnp.zeros((bucket_count, head_count), jnp.float32),
        my_table_grad,
        (0, my_group * plan.heads),
    ).reshape(bucket_count * head_count)
    gains_all = jnp.stack([gains_one[0], gains_two, gains_three[0], gains_four])
    everyone = ("dp", "ctx", "exp")
    grad_dout = jnp.dot(active.T, grad_half, preferred_element_type=jnp.float32)
    grad_din = jnp.dot(normed_half.T, d_pre, preferred_element_type=jnp.float32)
    grad_ein = jnp.einsum("erd,erf->edf", rows, expert_d_pre, preferred_element_type=jnp.float32)
    grad_eout = jnp.einsum(
        "erf,erd->efd", expert_active, grad_rows, preferred_element_type=jnp.float32
    )
    grad_ein = lax.psum_scatter(to_half(grad_ein), "dp", scatter_dimension=2, tiled=True)
    grad_eout = lax.psum_scatter(to_half(grad_eout), "dp", scatter_dimension=1, tiled=True)
    attn = lax.psum_scatter(
        jnp.stack([attn_one, attn_two], axis=1), everyone, scatter_dimension=3, tiled=True
    ).astype(jnp.float32)
    gains = lax.psum_scatter(gains_all, everyone, scatter_dimension=1, tiled=True)
    table = lax.psum_scatter(table_grad, everyone, scatter_dimension=0, tiled=True)
    din = lax.psum_scatter(to_half(grad_din), everyone, scatter_dimension=1, tiled=True)
    dout = lax.psum_scatter(to_half(grad_dout), everyone, scatter_dimension=0, tiled=True)
    return (
        output,
        input_grad,
        attn[0],
        attn[1],
        attn[2],
        attn[3],
        gains,
        table,
        widen(din),
        widen(dout),
        widen(grad_ein),
        widen(grad_eout),
    )


def solution(mesh):
    in_specs = (
        P(("dp", "ctx", "exp"), None),
        P(),
        P(),
        P(),
        P(),
        P(),
        P(),
        P(),
        P(),
        P(("ctx", "exp"), None, None),
        P(("ctx", "exp"), None, None),
        P(("dp", "ctx", "exp"), None),
        P(("dp", "ctx", "exp"), None),
        P(),
        P(("dp", "ctx", "exp"), None),
    )
    out_specs = (
        P(("dp", "ctx", "exp"), None),
        P(("dp", "ctx", "exp"), None),
        P(None, None, ("dp", "ctx", "exp")),
        P(None, None, ("dp", "ctx", "exp")),
        P(None, None, ("dp", "ctx", "exp")),
        P(None, None, ("dp", "ctx", "exp")),
        P(None, ("dp", "ctx", "exp")),
        P(("dp", "ctx", "exp")),
        P(None, ("dp", "ctx", "exp")),
        P(("dp", "ctx", "exp"), None),
        P(("ctx", "exp"), None, "dp"),
        P(("ctx", "exp"), "dp", None),
    )
    return jax.shard_map(body, mesh=mesh, in_specs=in_specs, out_specs=out_specs, check_vma=False)
```

```python
import functools

import jax
import jax.numpy as jnp
from jax import lax
from jax.experimental import pallas as pl
from jax.experimental.pallas import tpu as pltpu
from jax.sharding import PartitionSpec as P

epsilon = 1e-06
highest = lax.Precision.HIGHEST
MESH = pl.DeviceIdType.MESH
VMEM = pltpu.VMEM


def to_half(values):
    return values.astype(jnp.bfloat16)


def widen(values):
    return values.astype(jnp.float32)


def dot_nn(a, b):
    return jnp.dot(a, b, preferred_element_type=jnp.float32)


def dot_nt(a, b):
    return lax.dot_general(a, b, (((1,), (1,)), ((), ())), preferred_element_type=jnp.float32)


def dot_tn(a, b):
    return lax.dot_general(a, b, (((0,), (0,)), ((), ())), preferred_element_type=jnp.float32)


def rotate(values, shift):
    width = values.shape[-1]
    shift = shift % width
    return values if shift == 0 else pltpu.roll(values, shift, values.ndim - 1)


def pad_lanes(values, width):
    if values.shape[1] == width:
        return values
    zeros = jnp.zeros((values.shape[0], width - values.shape[1]), values.dtype)
    return jnp.concatenate([values, zeros], axis=1)


class Plan:
    def __init__(self, copies, cycle, exp_size, head_count, head_size, rows, experts):
        self.copies, self.cycle, self.exp_size, self.rows = copies, cycle, exp_size, rows
        groups = 1
        while cycle % (groups * 2) == 0 and head_count % (groups * 2) == 0:
            groups *= 2
        self.groups, self.splits = groups, cycle // groups
        self.heads, self.head_size = head_count // groups, head_size
        self.width = self.heads * head_size
        self.model = head_count * head_size
        self.length = cycle * rows
        self.wide = -(-self.width // 128) * 128
        self.lead = self.wide - self.width
        self.pair = 2 * self.width
        self.tiled = self.heads if self.heads * rows * self.length * 8 <= 4 << 20 else 1
        self.chips = cycle // 2
        self.share = self.model // (copies * cycle)
        self.experts = experts
        self.capacity = 2 * rows // (experts * cycle)
        self.slab = experts * self.capacity
        self.early = cycle // 4
        self.fused = (
            self.splits == 2
            and self.groups == copies
            and self.capacity % 16 == 0
            and (copies * self.share) % 16 == 0
            and self.width * copies == self.model
            and self.width + self.width % 128 <= self.wide
        )
        assert self.pair % 128 == 0 and self.pair - self.wide == self.width - self.lead

    def window(self, group):
        return group * self.width // 128 * 128

    def place(self):
        c = lax.axis_index("ctx") * self.exp_size + lax.axis_index("exp")
        return c, c // self.splits, lax.rem(c, self.splits)

    def device(self, c):
        return (lax.axis_index("dp"), c // self.exp_size, lax.rem(c, self.exp_size))

    def peer(self, c, step):
        return lax.rem(c + step, self.cycle)

    def copy_device(self, c, other):
        return (other, c // self.exp_size, lax.rem(c, self.exp_size))


def greet(plan, c):
    barrier = pltpu.get_barrier_semaphore()
    for step in range(1, plan.cycle):
        pl.semaphore_signal(
            barrier, inc=1, device_id=plan.device(plan.peer(c, step)), device_id_type=MESH
        )
    me = lax.axis_index("dp")
    for step in range(1, plan.copies):
        other = lax.rem(me + step, plan.copies)
        pl.semaphore_signal(
            barrier, inc=1, device_id=plan.copy_device(c, other), device_id_type=MESH
        )
    return barrier


def await_greetings(plan, barrier):
    pl.semaphore_wait(barrier, plan.cycle - 1 + plan.copies - 1)


def start_along_dp(plan, c, source, target, own_sem, send, recv):
    me = lax.axis_index("dp")
    own = pltpu.make_async_copy(source, target.at[me], own_sem.at[0])
    own.start()
    copies = [own]
    for step in range(1, plan.copies):
        other = lax.rem(me + step, plan.copies)
        copy = remote(
            source, target.at[me], send.at[step], recv.at[step], plan.copy_device(c, other)
        )
        copy.start()
        copies.append(copy)
    return copies


def start_slabs(plan, c, source, target, send, recv):
    copies = []
    for step in range(1, plan.cycle):
        to = plan.peer(c, step)
        copy = remote(source.at[to], target.at[c], send.at[step], recv.at[step], plan.device(to))
        copy.start()
        copies.append(copy)
    target[c] = source[c]
    return copies


def rms_normed(hidden, gains):
    inv_rms = lax.rsqrt(jnp.mean(hidden * hidden, axis=-1, keepdims=True) + epsilon)
    return hidden * inv_rms * gains, inv_rms


def fill_bias(plan, rows_ref, tiles, heads):
    for head in heads:
        row = jnp.broadcast_to(rows_ref[head : head + 1, :], (plan.rows, 2 * plan.length))
        tiles[head % plan.tiled] = pltpu.roll(row, 0, 1, stride=1, stride_axis=0)


def bias_part(plan, tiles, head, key_block, split):
    parts = []
    head = head % plan.tiled
    for block in range(plan.groups):
        first = plan.length + (block * plan.splits + split - key_block) * plan.rows
        parts.append(tiles[head, :, pl.ds(pl.multiple_of(first, plan.rows), plan.rows)])
    return jnp.concatenate(parts, axis=1)


def lanes_between(shape, low, high):
    lane = lax.broadcasted_iota(jnp.int32, shape, 1)
    return (lane >= low) & (lane < high)


def natural(plan, blocks, lead):
    total = None
    for group, block in enumerate(blocks):
        moved = rotate(pad_lanes(block, plan.model), group * plan.width - lead)
        total = moved if total is None else total + moved
    return total


def remote(src, dst, send, recv, device):
    return pltpu.make_async_remote_copy(
        src_ref=src, dst_ref=dst, send_sem=send, recv_sem=recv, device_id=device, device_id_type=MESH
    )


def forward_kernel(
    plan,
    layer,
    x_ref,
    gain_ref,
    bias_ref,
    wq_hbm,
    wk_hbm,
    wv_hbm,
    wo_hbm,
    mid_ref,
    normed_ref,
    query_ref,
    pair_ref,
    heads_ref,
    attended_ref,
    norm_ref,
    weights,
    tiles,
    send_pair,
    send_query,
    scores,
    probs,
    att_in,
    load_sem,
    pair_send,
    pair_recv,
    query_send,
    query_recv,
    att_send,
    att_recv,
):
    c, group, split = plan.place()
    loads = []
    for slot, source in enumerate((wv_hbm, wk_hbm, wq_hbm, wo_hbm)):
        load = pltpu.make_async_copy(source.at[layer], weights.at[slot], load_sem.at[slot])
        load.start()
        loads.append(load)
    barrier = greet(plan, c)
    hidden = x_ref[...]
    normed, _ = rms_normed(hidden, gain_ref[layer * 2 : layer * 2 + 1, :])
    normed_half = to_half(normed)
    normed_ref[...] = normed_half
    loads[0].wait()
    values = dot_nn(normed_half, weights[0])
    loads[1].wait()
    keys = dot_nn(normed_half, weights[1])
    is_value = lanes_between((plan.rows, plan.pair), 0, plan.width)
    for g in range(plan.groups):
        value_part = rotate(values, -g * plan.width)[:, : plan.pair]
        key_part = rotate(keys, (1 - g) * plan.width)[:, : plan.pair]
        send_pair[g] = to_half(jnp.where(is_value, value_part, key_part))
    await_greetings(plan, barrier)
    copies = []
    for step in range(1, plan.cycle):
        to = plan.peer(c, step)
        copy = remote(
            send_pair.at[to // plan.splits],
            pair_ref.at[c],
            pair_send.at[step],
            pair_recv.at[step],
            plan.device(to),
        )
        copy.start()
        copies.append(copy)
    loads[2].wait()
    queries = dot_nn(normed_half, weights[2])
    is_query = lanes_between((plan.rows, plan.wide), plan.lead, plan.wide)
    for g in range(plan.groups):
        query_part = rotate(queries, plan.lead - g * plan.width)[:, : plan.wide]
        send_query[g] = to_half(jnp.where(is_query, query_part, 0.0))
    for step in range(1, plan.groups):
        to = plan.peer(c, step * plan.splits)
        copy = remote(
            send_query.at[to // plan.splits],
            query_ref.at[group],
            query_send.at[step],
            query_recv.at[step],
            plan.device(to),
        )
        copy.start()
        copies.append(copy)
    pair_ref[c] = send_pair[group]
    query_ref[group] = send_query[group]
    fill_bias(plan, bias_ref, tiles, range(plan.tiled))
    for copy in copies:
        copy.wait()

    total = plan.groups * plan.rows
    queries_all = query_ref[...].reshape(total, plan.wide)
    values_t = jnp.transpose(pair_ref[...].reshape(plan.length, plan.pair)[:, : plan.wide])
    rows_t = []
    for head in range(plan.heads):
        if head >= plan.tiled:
            fill_bias(plan, bias_ref, tiles, [head])
        low = plan.lead + head * plan.head_size
        picked = jnp.where(
            lanes_between(queries_all.shape, low, low + plan.head_size), queries_all, 0
        )

        def score_block(block, top):
            part = dot_nt(pair_ref[block][:, plan.pair - plan.wide :], picked)
            part = part + bias_part(plan, tiles, head, block, split)
            scores[pl.ds(pl.multiple_of(block * plan.rows, plan.rows), plan.rows), :] = part
            return jnp.maximum(top, jnp.max(part, axis=0, keepdims=True))

        top = lax.fori_loop(0, plan.cycle, score_block, jnp.full((1, total), -1e30, jnp.float32))

        def weight_block(block, norm):
            where = pl.ds(pl.multiple_of(block * plan.rows, plan.rows), plan.rows)
            part = jnp.exp(scores[where, :] - top)
            probs[where, :] = to_half(part)
            return norm + jnp.sum(part, axis=0, keepdims=True)

        norm = lax.fori_loop(0, plan.cycle, weight_block, jnp.zeros((1, total), jnp.float32))
        norm_ref[head : head + 1, :] = top + jnp.log(norm)
        mine = values_t[head * plan.head_size : (head + 1) * plan.head_size, :]
        rows_t.append(dot_nn(mine, probs[...]) / norm)
    rows_t.append(jnp.zeros((plan.lead, total), jnp.float32))
    heads_ref[...] = to_half(jnp.transpose(jnp.concatenate(rows_t, axis=0))).reshape(
        plan.groups, plan.rows, plan.wide
    )
    copies = []
    for step in range(1, plan.groups):
        to = plan.peer(c, step * plan.splits)
        copy = remote(
            heads_ref.at[to // plan.splits],
            att_in.at[group],
            att_send.at[step],
            att_recv.at[step],
            plan.device(to),
        )
        copy.start()
        copies.append(copy)
    att_in[group] = heads_ref[group]
    loads[3].wait()
    for copy in copies:
        copy.wait()
    attended = to_half(natural(plan, [widen(att_in[g]) for g in range(plan.groups)], 0))
    attended_ref[...] = attended
    mid_ref[...] = hidden + dot_nn(attended, weights[3])


def attention_forward(plan, layer, hidden, gains, bias_rows, wq, wk, wv, wo, collective):
    f32, half = jnp.float32, jnp.bfloat16
    total = plan.groups * plan.rows
    whole = pl.BlockSpec(memory_space=VMEM)
    hbm = pl.BlockSpec(memory_space=pl.ANY)
    dma = pltpu.SemaphoreType.DMA
    return pl.pallas_call(
        functools.partial(forward_kernel, plan, layer),
        out_shape=(
            jax.ShapeDtypeStruct((plan.rows, plan.model), f32),
            jax.ShapeDtypeStruct((plan.rows, plan.model), half),
            jax.ShapeDtypeStruct((plan.groups, plan.rows, plan.wide), half),
            jax.ShapeDtypeStruct((plan.cycle, plan.rows, plan.pair), half),
            jax.ShapeDtypeStruct((plan.groups, plan.rows, plan.wide), half),
            jax.ShapeDtypeStruct((plan.rows, plan.model), half),
            jax.ShapeDtypeStruct((plan.heads, total), f32),
        ),
        in_specs=[whole, whole, whole, hbm, hbm, hbm, hbm],
        out_specs=(whole,) * 7,
        scratch_shapes=[
            VMEM((4, plan.model, plan.model), half),
            VMEM((plan.tiled, plan.rows, 2 * plan.length), f32),
            VMEM((plan.groups, plan.rows, plan.pair), half),
            VMEM((plan.groups, plan.rows, plan.wide), half),
            VMEM((plan.length, total), f32),
            VMEM((plan.length, total), half),
            VMEM((plan.groups, plan.rows, plan.wide), half),
            dma((4,)),
            dma((plan.cycle,)),
            dma((plan.cycle,)),
            dma((plan.groups,)),
            dma((plan.groups,)),
            dma((plan.groups,)),
            dma((plan.groups,)),
        ],
        compiler_params=pltpu.CompilerParams(
            collective_id=collective, has_side_effects=True, vmem_limit_bytes=56 * 1024 * 1024
        ),
        name="attention_forward",
    )(hidden, gains, bias_rows, wq, wk, wv, wo)


def backward_kernel(
    plan,
    layer,
    grad_ref,
    x_ref,
    gain_ref,
    bias_ref,
    normed_ref,
    query_ref,
    pair_ref,
    heads_ref,
    attended_ref,
    norm_ref,
    wq_hbm,
    wk_hbm,
    wv_hbm,
    wo_hbm,
    out_ref,
    gain_grad_ref,
    weight_grad_ref,
    bias_grad_ref,
    weights,
    tiles,
    sums,
    send_grad,
    grad_in,
    probs,
    slopes,
    key_sum,
    value_sum,
    send_pair,
    pair_in,
    send_query,
    query_in,
    load_sem,
    grad_send,
    grad_recv,
    pair_send,
    pair_recv,
    query_send,
    query_recv,
):
    c, group, split = plan.place()
    total = plan.groups * plan.rows
    loads = []
    for slot, source in enumerate((wv_hbm, wk_hbm, wq_hbm, wo_hbm)):
        load = pltpu.make_async_copy(source.at[layer], weights.at[slot], load_sem.at[slot])
        loads.append(load)
    for slot in (3, 0, 1, 2):
        loads[slot].start()
    barrier = greet(plan, c)
    grad = grad_ref[...]
    grad_half = to_half(grad)
    loads[3].wait()
    d_attended = dot_nt(grad_half, weights[3])
    in_group = lanes_between((plan.rows, plan.wide), 0, plan.width)
    for g in range(plan.groups):
        part = rotate(d_attended, -g * plan.width)[:, : plan.wide]
        send_grad[g] = to_half(jnp.where(in_group, part, 0.0))
    await_greetings(plan, barrier)
    copies = []
    for step in range(1, plan.groups):
        to = plan.peer(c, step * plan.splits)
        copy = remote(
            send_grad.at[to // plan.splits],
            grad_in.at[group],
            grad_send.at[step],
            grad_recv.at[step],
            plan.device(to),
        )
        copy.start()
        copies.append(copy)
    grad_in[group] = send_grad[group]
    fill_bias(plan, bias_ref, tiles, range(plan.tiled))
    weight_grad_ref[3] = to_half(dot_tn(attended_ref[...], grad_half))
    queries_all = query_ref[...].reshape(total, plan.wide)
    keys_t = jnp.transpose(
        pair_ref[...].reshape(plan.length, plan.pair)[:, plan.pair - plan.wide :]
    )
    heads_t = jnp.transpose(widen(heads_ref[...].reshape(total, plan.wide)))
    for copy in copies:
        copy.wait()
    grads_all = grad_in[...].reshape(total, plan.wide)
    grads_t = jnp.transpose(widen(grads_all))
    products_t = grads_t * heads_t
    query_rows_t = [jnp.zeros((plan.lead, total), jnp.float32)]
    for head in range(plan.heads):
        if head >= plan.tiled:
            fill_bias(plan, bias_ref, tiles, [head])
        low, high = head * plan.head_size, (head + 1) * plan.head_size
        picked_queries = jnp.where(
            lanes_between(queries_all.shape, plan.lead + low, plan.lead + high), queries_all, 0
        )
        picked_grads = jnp.where(lanes_between(grads_all.shape, low, high), grads_all, 0)
        delta = jnp.sum(products_t[low:high, :], axis=0, keepdims=True)
        log_norm = norm_ref[head : head + 1, :]
        sums[...] = jnp.zeros_like(sums)

        def slope_block(block, carry):
            where = pl.ds(pl.multiple_of(block * plan.rows, plan.rows), plan.rows)
            part = dot_nt(pair_ref[block][:, plan.pair - plan.wide :], picked_queries)
            part = part + bias_part(plan, tiles, head, block, split)
            part = jnp.exp(part - log_norm)
            probs[where, :] = to_half(part)
            slope = part * (dot_nt(pair_ref[block][:, : plan.wide], picked_grads) - delta)
            slopes[where, :] = to_half(slope)
            for b in range(plan.groups):
                first = plan.length + (b * plan.splits + split - block) * plan.rows
                at = pl.ds(pl.multiple_of(first, plan.rows), plan.rows)
                sums[:, at] += slope[:, b * plan.rows : (b + 1) * plan.rows]
            return carry

        lax.fori_loop(0, plan.cycle, slope_block, 0)
        key_part = dot_nn(slopes[...], picked_queries)
        value_part = dot_nn(probs[...], picked_grads)
        if head == 0:
            key_sum[...], value_sum[...] = key_part, value_part
        else:
            key_sum[...] += key_part
            value_sum[...] += value_part
        query_rows_t.append(dot_nn(keys_t[plan.lead + low : plan.lead + high, :], slopes[...]))
        row = lax.broadcasted_iota(jnp.int32, (plan.rows, plan.rows), 0)
        column = lax.broadcasted_iota(jnp.int32, (plan.rows, plan.rows), 1)
        flip = (row + column == plan.rows - 1).astype(jnp.float32)
        flipped = jnp.dot(flip, sums[...], precision=highest, preferred_element_type=jnp.float32)
        skewed = pltpu.roll(
            flipped, 2 * plan.length - (plan.rows - 1), 1, stride=1, stride_axis=0
        )
        bias_grad_ref[head : head + 1, :] = jnp.sum(skewed, axis=0, keepdims=True)
    send_query[...] = to_half(jnp.transpose(jnp.concatenate(query_rows_t, axis=0))).reshape(
        plan.groups, plan.rows, plan.wide
    )
    value_all, key_all = value_sum[...], key_sum[...]
    low, gap = plan.pair - plan.wide, plan.wide - (plan.pair - plan.wide)
    middle = jnp.where(
        lanes_between((plan.length, gap), 0, plan.width - low), value_all[:, low:], key_all[:, :gap]
    )
    send_pair[...] = to_half(
        jnp.concatenate([value_all[:, :low], middle, key_all[:, gap:]], axis=1)
    ).reshape(plan.cycle, plan.rows, plan.pair)
    copies = []
    for step in range(1, plan.cycle):
        to = plan.peer(c, step)
        copy = remote(
            send_pair.at[to], pair_in.at[c], pair_send.at[step], pair_recv.at[step], plan.device(to)
        )
        copy.start()
        copies.append(copy)
    for step in range(1, plan.groups):
        to = plan.peer(c, step * plan.splits)
        copy = remote(
            send_query.at[to // plan.splits],
            query_in.at[group],
            query_send.at[step],
            query_recv.at[step],
            plan.device(to),
        )
        copy.start()
        copies.append(copy)
    pair_in[c] = send_pair[c]
    query_in[group] = send_query[group]
    hidden = x_ref[...]
    gains = gain_ref[layer * 2 : layer * 2 + 1, :]
    inv_rms = lax.rsqrt(jnp.mean(hidden * hidden, axis=-1, keepdims=True) + epsilon)
    for slot in range(3):
        loads[slot].wait()
    for copy in copies:
        copy.wait()
    is_value = lanes_between((plan.rows, plan.pair), 0, plan.width)
    value_blocks, key_blocks = [], []
    for g in range(plan.groups):
        block = widen(pair_in[g * plan.splits])
        for other in range(1, plan.splits):
            block = block + widen(pair_in[g * plan.splits + other])
        value_blocks.append(jnp.where(is_value, block, 0.0))
        key_blocks.append(jnp.where(is_value, 0.0, block))
    d_values = to_half(natural(plan, value_blocks, 0))
    d_keys = to_half(natural(plan, key_blocks, plan.width))
    d_queries = to_half(
        natural(plan, [widen(query_in[g]) for g in range(plan.groups)], plan.lead)
    )
    normed_half = normed_ref[...]
    d_normed = (
        dot_nt(d_queries, weights[2]) + dot_nt(d_keys, weights[1]) + dot_nt(d_values, weights[0])
    )
    weight_grad_ref[0] = to_half(dot_tn(normed_half, d_queries))
    weight_grad_ref[1] = to_half(dot_tn(normed_half, d_keys))
    weight_grad_ref[2] = to_half(dot_tn(normed_half, d_values))
    d_scaled = d_normed * gains
    gain_grad_ref[...] = jnp.sum(d_normed * hidden * inv_rms, axis=0, keepdims=True)
    out_ref[...] = (
        grad
        + inv_rms * d_scaled
        - hidden * (inv_rms * inv_rms * inv_rms) * jnp.mean(d_scaled * hidden, axis=-1, keepdims=True)
    )


def attention_backward(plan, layer, grad, cache, gains, bias_rows, wq, wk, wv, wo, collective):
    f32, half = jnp.float32, jnp.bfloat16
    total = plan.groups * plan.rows
    whole = pl.BlockSpec(memory_space=VMEM)
    hbm = pl.BlockSpec(memory_space=pl.ANY)
    dma = pltpu.SemaphoreType.DMA
    hidden, normed, query, pair, heads, attended, norm = cache
    block = (plan.groups, plan.rows, plan.wide)
    pairs = (plan.cycle, plan.rows, plan.pair)
    return pl.pallas_call(
        functools.partial(backward_kernel, plan, layer),
        out_shape=(
            jax.ShapeDtypeStruct((plan.rows, plan.model), f32),
            jax.ShapeDtypeStruct((1, plan.model), f32),
            jax.ShapeDtypeStruct((4, plan.model, plan.model), half),
            jax.ShapeDtypeStruct((plan.heads, 2 * plan.length), f32),
        ),
        in_specs=[whole] * 10 + [hbm] * 4,
        out_specs=(whole,) * 4,
        scratch_shapes=[
            VMEM((4, plan.model, plan.model), half),
            VMEM((plan.tiled, plan.rows, 2 * plan.length), f32),
            VMEM((plan.rows, 2 * plan.length), f32),
            VMEM(block, half),
            VMEM(block, half),
            VMEM((plan.length, total), half),
            VMEM((plan.length, total), half),
            VMEM((plan.length, plan.wide), f32),
            VMEM((plan.length, plan.wide), f32),
            VMEM(pairs, half),
            VMEM(pairs, half),
            VMEM(block, half),
            VMEM(block, half),
            dma((4,)),
            dma((plan.groups,)),
            dma((plan.groups,)),
            dma((plan.cycle,)),
            dma((plan.cycle,)),
            dma((plan.groups,)),
            dma((plan.groups,)),
        ],
        compiler_params=pltpu.CompilerParams(
            collective_id=collective, has_side_effects=True, vmem_limit_bytes=60 * 1024 * 1024
        ),
        name="attention_backward",
    )(grad, hidden, gains, bias_rows, normed, query, pair, heads, attended, norm, wq, wk, wv, wo)


def smooth_act(values):
    return values * jax.nn.sigmoid(values)


def smooth_slope(values):
    sigma = jax.nn.sigmoid(values)
    return sigma * (1.0 + values * (1.0 - sigma))


class Links:
    def __init__(self, plan):
        self.plan = plan
        self.c, self.chip, self.core = plan.place()
        self.me = lax.axis_index("dp")
        self.lead = pl.multiple_of(lax.rem(self.chip * plan.width, 128), 64)
        self.first = pl.multiple_of(self.chip * plan.width // 128 * 128, 128)

    def pair(self):
        return self.plan.device(self.c + 1 - 2 * self.core)

    def at_chip(self, step):
        return lax.rem(self.chip + step, self.plan.groups)

    def chip_device(self, step):
        return self.plan.device(2 * self.at_chip(step) + self.core)

    def at_dp(self, step):
        return lax.rem(self.me + step, self.plan.copies)

    def dp_device(self, step):
        return self.plan.copy_device(self.c, self.at_dp(step))

    def head_lanes(self, shape, head):
        low = self.lead + head * self.plan.head_size
        return lanes_between(shape, low, low + self.plan.head_size)

    def head_rows(self, head):
        return pl.ds(
            pl.multiple_of(self.lead + head * self.plan.head_size, self.plan.head_size),
            self.plan.head_size,
        )


def wait_all(copies):
    for copy in copies:
        copy.wait()


def local(source, target, sem):
    copy = pltpu.make_async_copy(source, target, sem)
    copy.start()
    return copy


def started(copy):
    copy.start()
    return copy


def to_lines(links, source, target, send, recv, whole=False):
    copies = []
    for step in range(1, links.plan.copies):
        part = source if whole else source.at[links.at_dp(step)]
        copies.append(
            started(
                remote(part, target.at[step], send.at[step], recv.at[step], links.dp_device(step))
            )
        )
    return copies


def to_all_dp(links, source, target, send, recv):
    return [
        started(
            remote(
                source, target.at[links.me], send.at[step], recv.at[step], links.dp_device(step)
            )
        )
        for step in range(1, links.plan.copies)
    ]


def to_chips(links, source, target, send, recv, by_step=False, whole=False):
    copies = []
    for step in range(1, links.plan.chips):
        part = source if whole else source.at[links.at_chip(step)]
        slot = step if by_step else links.chip
        copies.append(
            started(
                remote(
                    part, target.at[slot], send.at[step], recv.at[step], links.chip_device(step)
                )
            )
        )
    return copies


def add_windows(plan, total, blocks):
    total[...] = jnp.zeros_like(total)
    for group, block in enumerate(blocks):
        first = plan.window(group)
        total[:, first : first + plan.wide] += block
    return total[...]


def bucket_picks(count, buckets_ref):
    width = buckets_ref.shape[1]
    tiles = [buckets_ref[:, low : low + 128] for low in range(0, width, 128)]
    rows = jnp.concatenate(tiles, axis=0).astype(jnp.float32)
    square = (128, 128)
    row = lax.broadcasted_iota(jnp.int32, square, 0)
    column = lax.broadcasted_iota(jnp.int32, square, 1)
    flip = (row + column == 127).astype(jnp.bfloat16)
    rows = dot_nn(to_half(rows), flip)
    tiles = [rows[i : i + 1, :] for i in range(width // 128)][::-1]
    values = jnp.broadcast_to(jnp.concatenate(tiles, axis=1), (count, width))
    numbers = lax.broadcasted_iota(jnp.int32, (count, width), 0).astype(jnp.float32)
    return (values == numbers).astype(jnp.bfloat16)


def split_dot(exact, picks, dot):
    count = exact.shape[0]
    high = to_half(exact)
    rest = exact - widen(high)
    middle = to_half(rest)
    low = to_half(rest - widen(middle))
    parts = jnp.concatenate([widen(high), widen(middle), widen(low)], axis=0)
    result = dot(to_half(parts), picks)
    return result[:count] + (result[count : 2 * count] + result[2 * count :])


def fill_all_bias(plan, links, table_ref, buckets_ref, rows, tiles):
    rows[: table_ref.shape[0], :] = split_dot(
        table_ref[...], bucket_picks(table_ref.shape[1], buckets_ref), dot_nn
    )
    for head in range(plan.heads):
        row = rows[pl.ds(links.chip * plan.heads + head, 1), :]
        row = jnp.broadcast_to(row, (plan.rows, 2 * plan.length))
        tiles[head] = pltpu.roll(row, 1, 1, stride=1, stride_axis=0)


def as_column(row):
    count = row.shape[1]
    square = (count, count)
    same = lax.broadcasted_iota(jnp.int32, square, 0) == lax.broadcasted_iota(jnp.int32, square, 1)
    return jnp.sum(jnp.where(same, jnp.broadcast_to(row, square), 0.0), axis=1, keepdims=True)


def place_tokens(plan, routes_ref):
    total = plan.experts * plan.cycle
    shape = (plan.rows, total)
    routes = as_column(routes_ref[...].astype(jnp.float32))
    numbers = lax.broadcasted_iota(jnp.int32, shape, 1).astype(jnp.float32)
    hits = (routes == numbers).astype(jnp.float32)
    square = (plan.rows, plan.rows)
    row = lax.broadcasted_iota(jnp.int32, square, 0)
    column = lax.broadcasted_iota(jnp.int32, square, 1)
    earlier = (column < row).astype(jnp.bfloat16)
    before = dot_nn(earlier, to_half(hits))
    slot = jnp.sum((before + numbers * plan.capacity) * hits, axis=1, keepdims=True)
    slots = (plan.rows, total * plan.capacity)
    return (slot == lax.broadcasted_iota(jnp.int32, slots, 1).astype(jnp.float32)).astype(
        jnp.bfloat16
    )


def whole_forward_kernel(
    plan,
    x_ref,
    gain_ref,
    table_ref,
    buckets_ref,
    routes_ref,
    gate_ref,
    cot_ref,
    wq_hbm,
    wk_hbm,
    wv_hbm,
    wo_hbm,
    din_hbm,
    dout_hbm,
    ein_hbm,
    eout_hbm,
    last_mid_ref,
    grad_ref,
    gain_grad_ref,
    stream_ref,
    mid_ref,
    attended_ref,
    norm_ref,
    dense_normed,
    cots_in,
    rows_in,
    produced,
    cots_hbm,
    rows_early,
    normed_out,
    key_out,
    value_out,
    query_out,
    heads_out,
    normed_all,
    key_all,
    value_all,
    query_all,
    heads_all,
    wq,
    wk,
    wv,
    wo,
    up,
    down,
    bias_rows,
    tiles,
    value_t,
    scores,
    probs,
    heads_t,
    att_in,
    natural_sum,
    cots_out,
    rows_out,
    d_active,
    d_rows,
    d_rows_in,
    load_sem,
    near_send,
    near_recv,
    far_send,
    far_recv,
    att_send,
    att_recv,
    cots_send,
    cots_recv,
    rows_send,
    rows_recv,
    d_rows_send,
    d_rows_recv,
    line_send,
    line_recv,
    own_sem,
    keep_sem,
):
    links = Links(plan)
    c, chip, core = links.c, links.chip, links.core
    columns = pl.ds(links.first, plan.wide)
    loads = {}

    def load(name, source, target):
        loads[name] = local(source, target, load_sem.at[len(loads)])

    for layer in range(2):
        for name, source, target in (("k", wk_hbm, wk), ("v", wv_hbm, wv), ("q", wq_hbm, wq)):
            load((name, layer), source.at[layer, :, columns], target.at[layer])
        load(("o", layer), wo_hbm.at[layer], wo.at[layer])
        if layer == 0:
            load("din", din_hbm, up.at[0])
            load("dout", dout_hbm, down.at[0])
    load("eout1", eout_hbm.at[1], down.at[1])
    load("ein1", ein_hbm.at[1], up.at[1])
    barrier = greet(plan, c)
    placed = place_tokens(plan, routes_ref)
    gate = as_column(gate_ref[...])
    total = plan.groups * plan.rows
    done_later, lines = [], []

    def project(layer, block, with_query):
        normed = normed_all[layer, block // 2, lax.rem(block, 2)]
        key_all[layer, block] = to_half(dot_nn(normed, wk[layer]))
        value_all[layer, block] = to_half(dot_nn(normed, wv[layer]))
        if with_query:
            query_all[layer, block // 2] = to_half(dot_nn(normed, wq[layer]))

    def attention(layer, hidden):
        normed, _ = rms_normed(hidden, gain_ref[layer * 2 : layer * 2 + 1, :])
        normed_all[layer, chip, core] = to_half(normed)
        if layer == 0:
            cots = gate * cot_ref[...]
            cots_out[...] = to_half(dot_tn(placed, to_half(cots))).reshape(cots_out.shape)
            await_greetings(plan, barrier)
            done_later.extend(start_slabs(plan, c, cots_out, cots_in, cots_send, cots_recv))
        own = normed_all.at[layer, chip, core]
        far = []
        for step in range(1, plan.chips):
            far.append(
                started(
                    remote(
                        own,
                        own,
                        far_send.at[layer, step],
                        far_recv.at[layer, step],
                        links.chip_device(step),
                    )
                )
            )
        near = [
            started(
                remote(own, own, near_send.at[layer, 0], near_recv.at[layer, 0], links.pair())
            )
        ]
        for name in ("k", "v", "q"):
            loads[(name, layer)].wait()
        project(layer, c, True)
        if layer == 0:
            fill_all_bias(plan, links, table_ref, buckets_ref, bias_rows, tiles)
        near[0].wait_recv()
        project(layer, 2 * chip + 1 - core, False)
        if layer == 0:
            wait_all(done_later)
            lines.extend(to_all_dp(links, cots_in, cots_hbm, line_send.at[0], line_recv.at[0]))
            lines.append(local(cots_in, cots_hbm.at[links.me], own_sem.at[0]))
        for step in range(1, plan.chips):
            far[step - 1].wait_recv()
            from_chip = lax.rem(chip + plan.chips - step, plan.chips)
            block = normed_all.at[layer, from_chip, core]
            near.append(
                started(
                    remote(
                        block,
                        block,
                        near_send.at[layer, step],
                        near_recv.at[layer, step],
                        links.pair(),
                    )
                )
            )
            project(layer, 2 * from_chip + core, True)
        blocks = []
        for step in range(1, plan.chips):
            near[step].wait_recv()
            from_chip = lax.rem(chip + plan.chips - step, plan.chips)
            blocks.append((2 * from_chip + 1 - core, normed_all[layer, from_chip, 1 - core]))
        normed = jnp.concatenate([values for _, values in blocks], axis=0)
        keys = to_half(dot_nn(normed, wk[layer]))
        values = to_half(dot_nn(normed, wv[layer]))
        for slot, (block, _) in enumerate(blocks):
            rows = slice(slot * plan.rows, (slot + 1) * plan.rows)
            key_all[layer, block] = keys[rows, :]
            value_all[layer, block] = values[rows, :]
        for copy in far + near:
            copy.wait_send()

        queries = query_all[layer].reshape(total, plan.wide)
        value_t[...] = jnp.transpose(value_all[layer].reshape(plan.length, plan.wide))
        heads_t[...] = jnp.zeros_like(heads_t)
        for head in range(plan.heads):
            picked = jnp.where(links.head_lanes(queries.shape, head), queries, 0)

            top = jnp.full((1, total), -1e30, jnp.float32)
            many = plan.cycle // 2
            for first in range(0, plan.cycle, many):
                keys = key_all[layer, first : first + many].reshape(many * plan.rows, plan.wide)
                part = dot_nt(keys, picked)
                for block in range(many):
                    piece = part[block * plan.rows : (block + 1) * plan.rows, :]
                    piece = piece + bias_part(plan, tiles, head, first + block, core)
                    low = (first + block) * plan.rows
                    scores[low : low + plan.rows, :] = piece
                    top = jnp.maximum(top, jnp.max(piece, axis=0, keepdims=True))

            norm = jnp.zeros((1, total), jnp.float32)
            for block in range(plan.cycle):
                where = slice(block * plan.rows, (block + 1) * plan.rows)
                part = jnp.exp(scores[where, :] - top)
                probs[where, :] = to_half(part)
                norm = norm + jnp.sum(part, axis=0, keepdims=True)
            norm_ref[layer, head : head + 1, :] = top + jnp.log(norm)
            mine = links.head_rows(head)
            heads_t[mine, :] = dot_nn(value_t[mine, :], probs[...]) / norm
        heads_all[layer] = to_half(jnp.transpose(heads_t[...])).reshape(
            plan.groups, plan.rows, plan.wide
        )
        copies = to_chips(
            links, heads_all.at[layer], att_in.at[layer], att_send.at[layer], att_recv.at[layer]
        )
        for slot, (kept, out) in enumerate(
            (
                (normed_all, normed_out),
                (key_all, key_out),
                (value_all, value_out),
                (query_all, query_out),
                (heads_all, heads_out),
            )
        ):
            lines.append(local(kept.at[layer], out.at[layer], keep_sem.at[layer, slot]))
        att_in[layer, chip] = heads_all[layer, chip]
        loads[("o", layer)].wait()
        wait_all(copies)
        attended = to_half(
            add_windows(plan, natural_sum, [widen(att_in[layer, g]) for g in range(plan.groups)])
        )
        attended_ref[layer] = attended
        return hidden + dot_nn(attended, wo[layer])

    mid = attention(0, x_ref[...])
    mid_ref[...] = mid
    normed, _ = rms_normed(mid, gain_ref[1:2, :])
    normed_half = to_half(normed)
    dense_normed[links.me] = normed_half
    mine = dense_normed.at[links.me]
    lines += to_all_dp(links, mine, dense_normed, line_send.at[1], line_recv.at[1])
    loads["din"].wait()
    active = to_half(smooth_act(dot_nn(normed_half, up[0])))
    loads["dout"].wait()
    stream = mid + dot_nn(active, down[0])
    stream_ref[...] = stream
    load("eout0", eout_hbm.at[0], down.at[0])
    load("ein0", ein_hbm.at[0], up.at[0])
    mid = attention(1, stream)
    last_mid_ref[...] = mid

    gains = gain_ref[3:4, :]
    normed, inv_rms = rms_normed(mid, gains)
    rows_out[...] = to_half(dot_tn(placed, to_half(normed))).reshape(rows_out.shape)
    copies = start_slabs(plan, c, rows_out, rows_in, rows_send, rows_recv)
    count = plan.cycle * plan.capacity

    def of_expert(ref, e):
        return ref[:, e * plan.capacity : (e + 1) * plan.capacity, :].reshape(count, plan.model)

    for e in range(plan.experts):
        loads["eout%d" % e].wait()
        d_active[e] = dot_nt(of_expert(cots_in, e), down[e])
        loads["ein%d" % e].wait()
    wait_all(copies)
    early = rows_in.at[: plan.early]
    lines += to_all_dp(links, early, rows_early, line_send.at[2], line_recv.at[2])
    actives = []
    for e in range(plan.experts):
        pre = dot_nn(of_expert(rows_in, e), up[e])
        actives.append(to_half(smooth_act(pre)))
        d_pre = to_half(d_active[e] * smooth_slope(pre))
        d_rows[:, e * plan.capacity : (e + 1) * plan.capacity, :] = to_half(
            dot_nt(d_pre, up[e])
        ).reshape(plan.cycle, plan.capacity, plan.model)
    d_row_copies = start_slabs(plan, c, d_rows, d_rows_in, d_rows_send, d_rows_recv)
    for e in range(plan.experts):
        produced[:, e * plan.capacity : (e + 1) * plan.capacity, :] = to_half(
            dot_nn(actives[e], down[e])
        ).reshape(plan.cycle, plan.capacity, plan.model)
    wait_all(d_row_copies)
    slots = plan.cycle * plan.slab
    d_normed = dot_nn(placed, d_rows_in[...].reshape(slots, plan.model))
    gain_grad_ref[...] = jnp.sum(d_normed * mid * inv_rms, axis=0, keepdims=True)
    grad_ref[...] = cot_ref[...] + norm_slope(mid, inv_rms, gains, d_normed)
    wait_all(lines)


def norm_slope(hidden, inv_rms, gains, d_normed):
    d_scaled = d_normed * gains
    mean = jnp.mean(d_scaled * hidden, axis=-1, keepdims=True)
    return inv_rms * d_scaled - hidden * (inv_rms * inv_rms * inv_rms) * mean


def whole_forward(plan, x, gains, table, buckets, routes, gate, cot, weights, dense, experts):
    f32, half = jnp.float32, jnp.bfloat16
    whole = pl.BlockSpec(memory_space=VMEM)
    hbm = pl.BlockSpec(memory_space=pl.ANY)
    dma = pltpu.SemaphoreType.DMA
    total = plan.groups * plan.rows
    units = dense[0].shape[1]
    slabs = (plan.cycle, plan.slab, plan.model)
    window = (plan.rows, plan.wide)
    row = (plan.rows, plan.model)
    outs = [
        (row, f32),
        (row, f32),
        ((1, plan.model), f32),
        (row, f32),
        (row, f32),
        ((2,) + row, half),
        ((2, plan.heads, total), f32),
        ((plan.copies,) + row, half),
        (slabs, half),
        (slabs, half),
        (slabs, half),
        ((plan.copies,) + slabs, half),
        ((plan.copies, plan.early) + slabs[1:], half),
    ]
    kept = [
        ((2, plan.chips, 2) + row, half),
        ((2, plan.cycle) + window, half),
        ((2, plan.cycle) + window, half),
        ((2, plan.groups) + window, half),
        ((2, plan.groups) + window, half),
    ]
    outs += kept
    cycle_sems = [dma((plan.cycle,))] * 2
    return pl.pallas_call(
        functools.partial(whole_forward_kernel, plan),
        out_shape=tuple(jax.ShapeDtypeStruct(*out) for out in outs),
        in_specs=[whole] * 7 + [hbm] * 8,
        out_specs=(whole,) * 11 + (hbm,) * 7,
        scratch_shapes=[VMEM(*one) for one in kept]
        + [
            VMEM((2, plan.model, plan.wide), half),
            VMEM((2, plan.model, plan.wide), half),
            VMEM((2, plan.model, plan.wide), half),
            VMEM((2, plan.model, plan.model), half),
            VMEM((2, plan.model, units), half),
            VMEM((2, units, plan.model), half),
            VMEM((16, 2 * plan.length), f32),
            VMEM((plan.heads, plan.rows, 2 * plan.length), f32),
            VMEM((plan.wide, plan.length), half),
            VMEM((plan.length, total), f32),
            VMEM((plan.length, total), half),
            VMEM((plan.wide, total), f32),
            VMEM((2, plan.groups) + window, half),
            VMEM(row, f32),
            VMEM(slabs, half),
            VMEM(slabs, half),
            VMEM((plan.experts, plan.cycle * plan.capacity, units), f32),
            VMEM(slabs, half),
            VMEM(slabs, half),
            dma((14,)),
            dma((2, plan.chips)),
            dma((2, plan.chips)),
            dma((2, plan.chips)),
            dma((2, plan.chips)),
            dma((2, plan.chips)),
            dma((2, plan.chips)),
        ]
        + cycle_sems * 3
        + [dma((3, plan.copies)), dma((3, plan.copies)), dma((1,)), dma((2, len(kept)))],
        compiler_params=pltpu.CompilerParams(
            collective_id=0, has_side_effects=True, vmem_limit_bytes=60 * 1024 * 1024
        ),
        name="whole_forward",
    )(x, gains, table, buckets, routes, gate, cot, *weights, *dense, *experts)


def whole_backward_kernel(
    plan,
    grad_ref,
    stream_ref,
    x_ref,
    mid_ref,
    gain_ref,
    last_gain_ref,
    table_ref,
    buckets_ref,
    attended_ref,
    norm_ref,
    normed_z,
    last_mid_ref,
    produced_ref,
    routes_ref,
    gate_ref,
    normed_hbm,
    key_hbm,
    value_hbm,
    query_hbm,
    heads_hbm,
    cots_hbm,
    rows_hbm,
    early_hbm,
    wq_hbm,
    wk_hbm,
    wv_hbm,
    wo_hbm,
    din_hbm,
    dout_hbm,
    ein_hbm,
    eout_hbm,
    output_ref,
    input_grad_ref,
    three_ref,
    out_ref,
    dense_ref,
    small_ref,
    ein_grad,
    eout_grad,
    produced_in,
    normed_all,
    key_all,
    value_all,
    query_all,
    heads_all,
    weights,
    up,
    down,
    cots_all,
    rows_all,
    bias_rows,
    tiles,
    sums,
    grad_out,
    grad_in,
    key_t,
    products,
    picked_queries,
    picked_grads,
    key_part,
    value_part,
    pair_out,
    pair_in,
    own_out,
    own_in,
    query_t,
    query_out,
    query_in,
    natural_sum,
    stage,
    o_half,
    o_sum,
    o_part,
    o_row,
    o_in,
    three_pair,
    three_half,
    three_sum,
    three_part,
    three_in,
    grads_z,
    dense_pair,
    dense_half,
    dense_part,
    small_mine,
    small_half,
    small_sum,
    small_part,
    small_row,
    small_in,
    load_sem,
    own_sem,
    grad_send,
    grad_recv,
    pair_send,
    pair_recv,
    back_send,
    back_recv,
    query_send,
    query_recv,
    chain_send,
    chain_recv,
    plane_send,
    plane_recv,
    line_send,
    line_recv,
    produced_send,
    produced_recv,
):
    links = Links(plan)
    c, chip, core, me = links.c, links.chip, links.core, links.me
    loads = {}

    def load(name, source, target):
        loads[name] = local(source, target, load_sem.at[len(loads)])

    def load_layer(layer):
        for name, source, target in (
            ("query", query_hbm, query_all),
            ("key", key_hbm, key_all),
            ("value", value_hbm, value_all),
            ("heads", heads_hbm, heads_all),
            ("normed", normed_hbm, normed_all),
        ):
            load((name, layer), source.at[layer], target)

    part = up.shape[1] // plan.copies
    mine = pl.ds(pl.multiple_of(me * part, part), part)
    load(("o", 1), wo_hbm.at[1], weights.at[3])
    load_layer(1)
    for slot, name, source in ((0, "v", wv_hbm), (1, "k", wk_hbm), (2, "q", wq_hbm)):
        load((name, 1), source.at[1], weights.at[slot])
    load("up", din_hbm, up)
    load("down", dout_hbm, down)
    load("cots", cots_hbm, cots_all)
    rows_own = [local(rows_hbm, rows_all.at[me], own_sem.at[0])]
    for step in range(1, plan.copies):
        other = links.at_dp(step)
        target = rows_all.at[other, : plan.early]
        rows_own.append(
            local(early_hbm.at[other], target, own_sem.at[2 * plan.experts + step])
        )

    barrier = greet(plan, c)
    total = plan.groups * plan.rows
    rows_lines, returned = [], []
    share = plan.share

    def send_rows(sems, first, last):
        for step in range(1, plan.copies):
            rows_lines.append(
                started(
                    remote(
                        rows_hbm.at[first:last],
                        rows_all.at[me, first:last],
                        line_send.at[sems, step],
                        line_recv.at[sems, step],
                        links.dp_device(step),
                    )
                )
            )

    def o_start(layer, grad_half):
        stage[: plan.model, :] = dot_tn(grad_half, attended_ref[layer])

        def one(i, carry):
            side, to = lax.rem(i, 2), i // 2
            pieces = []
            for d in range(plan.copies):
                first = (d * plan.cycle + i) * share
                pieces.append(stage[pl.ds(pl.multiple_of(first, 8), share), :])
            dense_pair[side, to, : plan.copies * share, :] = to_half(jnp.concatenate(pieces, axis=0))
            return carry

        lax.fori_loop(0, plan.cycle, one, 0)
        return started(
            remote(
                dense_pair.at[1 - core, :, : plan.copies * share, :],
                o_half.at[layer],
                chain_send.at[layer, 0],
                chain_recv.at[layer, 0],
                links.pair(),
            )
        )

    def o_plane(layer, copy):
        copy.wait()
        o_sum[...] = to_half(
            widen(dense_pair[core, :, : plan.copies * share, :]) + widen(o_half[layer])
        )
        return to_chips(
            links,
            o_sum,
            o_part.at[layer],
            plane_send.at[layer],
            plane_recv.at[layer],
            by_step=True,
        )

    def o_line(layer, copies):
        wait_all(copies)
        value = widen(o_sum[chip])
        for step in range(1, plan.chips):
            value = value + widen(o_part[layer, step])
        pad = jnp.zeros((o_row.shape[2] - share, plan.model), jnp.float32)
        for d in range(plan.copies):
            piece = jnp.concatenate([value[d * share : (d + 1) * share, :], pad], axis=0)
            o_row[layer, d] = to_half(piece)
        return to_lines(
            links, o_row.at[layer], o_in.at[layer], line_send.at[layer], line_recv.at[layer]
        )

    def o_finish(layer, copies):
        wait_all(copies)
        value = widen(o_row[layer, me])
        for step in range(1, plan.copies):
            value = value + widen(o_in[layer, step])
        out_ref[layer] = value[:share, :]

    def three_start(layer):
        normed = normed_all[...].reshape(plan.length, plan.model)
        own_normed = normed_all[:, core].reshape(total, plan.model)
        stage[: plan.wide, :] = dot_tn(query_out[layer].reshape(total, plan.wide), own_normed)
        stage[plan.wide : 2 * plan.wide, :] = dot_tn(key_part[...].reshape(plan.length, plan.wide), normed)
        stage[2 * plan.wide : 3 * plan.wide, :] = dot_tn(value_part[...].reshape(plan.length, plan.wide), normed)
        for side in range(2):
            for slot in range(3):
                pieces = []
                for to in range(plan.chips):
                    first = slot * plan.wide + links.lead + (2 * to + side) * share
                    pieces.append(stage[pl.ds(pl.multiple_of(first, 8), share), :])
                three_pair[side, slot] = to_half(jnp.concatenate(pieces, axis=0))
        return started(
            remote(
                three_pair.at[1 - core],
                three_half.at[layer],
                chain_send.at[2 + layer, 0],
                chain_recv.at[2 + layer, 0],
                links.pair(),
            )
        )

    def three_plane(layer, copy):
        copy.wait()
        both = []
        for slot in range(3):
            both.append(widen(three_pair[core, slot]) + widen(three_half[layer, slot]))
        pad = jnp.zeros((three_sum.shape[2] - 3 * share, plan.model), jnp.float32)
        for to in range(plan.chips):
            pieces = [value[to * share : (to + 1) * share, :] for value in both]
            three_sum[layer, to] = to_half(jnp.concatenate(pieces + [pad], axis=0))
        three_part[layer, chip] = three_sum[layer, chip]
        return to_chips(
            links,
            three_sum.at[layer],
            three_part.at[layer],
            plane_send.at[2 + layer],
            plane_recv.at[2 + layer],
        )

    def three_line(layer, copies):
        wait_all(copies)
        return to_lines(
            links,
            three_part.at[layer],
            three_in.at[layer],
            line_send.at[2 + layer],
            line_recv.at[2 + layer],
        )

    def three_finish(layer, copies):
        wait_all(copies)
        value = widen(three_part[layer, me])
        for step in range(1, plan.copies):
            value = value + widen(three_in[layer, step])
        three_ref[layer] = value[: 3 * share, :]

    def attention(layer, grad, hidden, between):
        grad_half = to_half(grad)
        loads[("o", layer)].wait()
        d_attended = dot_nt(grad_half, weights[3])
        for g in range(plan.groups):
            first = plan.window(g)
            grad_out[layer, g] = to_half(d_attended[:, first : first + plan.wide])
        if layer == 1:
            await_greetings(plan, barrier)
            load(("o", 0), wo_hbm.at[0], weights.at[3])
        copies = to_chips(
            links, grad_out.at[layer], grad_in.at[layer], grad_send.at[layer], grad_recv.at[layer]
        )
        grad_in[layer, chip] = grad_out[layer, chip]
        if layer == 1:
            send_rows(5, plan.early, plan.cycle - 1)
        o_copy = o_start(layer, grad_half)
        if layer == 1:
            fill_all_bias(plan, links, table_ref, buckets_ref, bias_rows, tiles)
            sums[...] = jnp.zeros_like(sums)
        for name in ("query", "key", "heads", "value"):
            loads[(name, layer)].wait()
        queries = query_all[...].reshape(total, plan.wide)
        for head in range(plan.heads):
            picked_queries[head] = jnp.where(links.head_lanes(queries.shape, head), queries, 0)
        query_t[...] = jnp.zeros_like(query_t)
        key_t[...] = jnp.transpose(key_all[...].reshape(plan.length, plan.wide))
        products[...] = jnp.transpose(widen(heads_all[...].reshape(total, plan.wide)))
        wait_all(copies)
        if layer == 0:
            o_copies = o_plane(layer, o_copy)
        if layer == 1:
            returned.extend(
                start_slabs(plan, c, produced_ref, produced_in, produced_send, produced_recv)
            )
        grads = grad_in[layer].reshape(total, plan.wide)
        for head in range(plan.heads):
            picked_grads[head] = jnp.where(links.head_lanes(grads.shape, head), grads, 0)
        products[...] = products[...] * jnp.transpose(widen(grads))
        delta = [
            jnp.sum(products[links.head_rows(head), :], axis=0, keepdims=True)
            for head in range(plan.heads)
        ]
        log_norm = [norm_ref[layer, head : head + 1, :] for head in range(plan.heads)]

        def process(blocks):
            keys = jnp.concatenate([key_all[block] for block in blocks], axis=0)
            values = jnp.concatenate([value_all[block] for block in blocks], axis=0)
            d_keys = d_values = None
            for head in range(plan.heads):
                bias = [bias_part(plan, tiles, head, block, core) for block in blocks]
                part = dot_nt(keys, picked_queries[head]) + jnp.concatenate(bias, axis=0)
                part = jnp.exp(part - log_norm[head])
                slope = part * (dot_nt(values, picked_grads[head]) - delta[head])
                for slot, block in enumerate(blocks):
                    rows = slice(slot * plan.rows, (slot + 1) * plan.rows)
                    for b in range(plan.groups):
                        first = plan.length + (b * plan.splits + core - block) * plan.rows
                        at = pl.ds(pl.multiple_of(first, plan.rows), plan.rows)
                        sums[head, :, at] += slope[rows, b * plan.rows : (b + 1) * plan.rows]
                slope = to_half(slope)
                keys_t = [
                    key_t[
                        links.head_rows(head),
                        pl.ds(pl.multiple_of(block * plan.rows, plan.rows), plan.rows),
                    ]
                    for block in blocks
                ]
                query_t[links.head_rows(head), :] += dot_nn(
                    jnp.concatenate(keys_t, axis=1), slope
                )
                key_piece = dot_nn(slope, picked_queries[head])
                value_piece = dot_nn(to_half(part), picked_grads[head])
                d_keys = key_piece if head == 0 else d_keys + key_piece
                d_values = value_piece if head == 0 else d_values + value_piece
            for slot, block in enumerate(blocks):
                rows = slice(slot * plan.rows, (slot + 1) * plan.rows)
                key_part[block] = to_half(d_keys[rows, :])
                value_part[block] = to_half(d_values[rows, :])
            return d_keys, d_values

        def pair_copy(step):
            return remote(
                pair_out.at[step],
                pair_in.at[layer, step],
                pair_send.at[layer, step],
                pair_recv.at[layer, step],
                links.pair(),
            )

        steps = [(i + 1) % plan.chips for i in range(plan.chips)]
        d_keys, d_values = process([2 * links.at_chip(step) + 1 - core for step in steps])
        for slot, step in enumerate(steps):
            rows = slice(slot * plan.rows, (slot + 1) * plan.rows)
            pair_out[step, 0] = to_half(d_keys[rows, :])
            pair_out[step, 1] = to_half(d_values[rows, :])
            pair_copy(step).start()

        def back_copy(step):
            return remote(
                own_out.at[step],
                own_in.at[layer, chip],
                back_send.at[layer, step],
                back_recv.at[layer, step],
                links.chip_device(step),
            )

        d_keys, d_values = process([2 * links.at_chip(step) + core for step in steps])
        for slot, step in enumerate(steps):
            rows = slice(slot * plan.rows, (slot + 1) * plan.rows)
            pair_copy(step).wait_recv()
            own_out[step, 0] = to_half(d_keys[rows, :] + widen(pair_in[layer, step, 0]))
            own_out[step, 1] = to_half(d_values[rows, :] + widen(pair_in[layer, step, 1]))
            if step > 0:
                back_copy(step).start()
        own_in[layer, chip] = own_out[0]
        query_out[layer] = to_half(jnp.transpose(query_t[...])).reshape(
            plan.groups, plan.rows, plan.wide
        )
        copies = to_chips(
            links,
            query_out.at[layer],
            query_in.at[layer],
            query_send.at[layer],
            query_recv.at[layer],
        )
        query_in[layer, chip] = query_out[layer, chip]
        loads[("normed", layer)].wait()
        three_copy = three_start(layer)
        if layer == 1:
            o_copies = o_plane(layer, o_copy)
        between_result = between(three_copy, o_copies)
        inv_rms = lax.rsqrt(jnp.mean(hidden * hidden, axis=-1, keepdims=True) + epsilon)
        for name in ("v", "k", "q"):
            loads[(name, layer)].wait()
        wait_all(copies)
        for step in range(1, plan.chips):
            back_copy(step).wait()
        for step in range(plan.chips):
            pair_copy(step).wait_send()
        groups = range(plan.groups)
        d_queries = to_half(
            add_windows(plan, natural_sum, [widen(query_in[layer, g]) for g in groups])
        )
        d_keys = to_half(
            add_windows(plan, natural_sum, [widen(own_in[layer, g, 0]) for g in groups])
        )
        d_values = to_half(
            add_windows(plan, natural_sum, [widen(own_in[layer, g, 1]) for g in groups])
        )
        d_normed = (
            dot_nt(d_queries, weights[2])
            + dot_nt(d_keys, weights[1])
            + dot_nt(d_values, weights[0])
        )
        if layer == 1:
            load_layer(0)
            for slot, name, source in ((0, "v", wv_hbm), (1, "k", wk_hbm), (2, "q", wq_hbm)):
                load((name, 0), source.at[0], weights.at[slot])
        gains = gain_ref[2 * layer : 2 * layer + 1, :]
        small_mine[2 * layer : 2 * layer + 1, :] = jnp.sum(
            d_normed * hidden * inv_rms, axis=0, keepdims=True
        )
        result = grad + norm_slope(hidden, inv_rms, gains, d_normed)
        return result, o_copies, three_copy, between_result

    small_mine[...] = jnp.zeros_like(small_mine)
    small_mine[3:4, :] = last_gain_ref[...]
    grad, o_one, three_one, _ = attention(
        1, grad_ref[...], stream_ref[...], lambda *_: None
    )

    grad_half = to_half(grad)
    grads_z[me] = grad_half
    grad_lines = to_all_dp(links, grads_z.at[me], grads_z, line_send.at[4], line_recv.at[4])
    send_rows(7, plan.cycle - 1, plan.cycle)
    mid = mid_ref[...]
    gains = gain_ref[1:2, :]
    normed, inv_rms = rms_normed(mid, gains)
    loads["up"].wait()
    loads["down"].wait()
    normed_half = to_half(normed)
    d_normed = jnp.zeros_like(normed)
    for slot in range(plan.copies):
        units = slice(slot * part, (slot + 1) * part)
        pre = dot_nn(normed_half, up[:, units])
        d_pre = to_half(dot_nt(grad_half, down[units, :]) * smooth_slope(pre))
        d_normed = d_normed + dot_nt(d_pre, up[:, units])
    pieces = [slice(slot * part, (slot + 1) * part) for slot in range(plan.experts + 1)]
    for e in range(plan.experts):
        load("ein%d" % e, ein_hbm.at[e, :, mine], up.at[:, pieces[e]])
        load("eout%d" % e, eout_hbm.at[e, mine, :], down.at[pieces[e], :])
    load("din", din_hbm.at[:, mine], up.at[:, pieces[-1]])
    load("dout", dout_hbm.at[mine, :], down.at[pieces[-1], :])
    small_mine[1:2, :] = jnp.sum(d_normed * mid * inv_rms, axis=0, keepdims=True)
    grad = grad + norm_slope(mid, inv_rms, gains, d_normed)

    three_one = three_plane(1, three_one)
    o_one = o_line(1, o_one)
    three_lines = []

    def send_three():
        three_lines.extend(three_line(1, three_one))

    def dense_grads():
        wait_all(grad_lines)
        count = plan.copies * plan.rows
        normed = normed_z[...].reshape(count, plan.model)
        grads = grads_z[...].reshape(count, plan.model)
        loads["din"].wait()
        loads["dout"].wait()
        height = part // plan.cycle
        some = part // plan.chips
        for to in range(plan.chips):
            units = slice(pieces[-1].start + to * some, pieces[-1].start + (to + 1) * some)
            pre = dot_nn(normed, up[:, units])
            active = to_half(smooth_act(pre))
            d_pre = to_half(dot_nt(grads, down[units, :]) * smooth_slope(pre))
            in_grad = to_half(dot_tn(d_pre, normed))
            out_grad = to_half(dot_tn(active, grads))
            for side in range(2):
                rows = slice(side * height, (side + 1) * height)
                dense_pair[side, to, :height, :] = in_grad[rows, :]
                dense_pair[side, to, height:, :] = out_grad[rows, :]
        return started(
            remote(
                dense_pair.at[1 - core],
                dense_half,
                chain_send.at[4, 0],
                chain_recv.at[4, 0],
                links.pair(),
            )
        )

    def last_sums(three_copy, o_copies):
        o_copies = o_line(0, o_copies)
        three = three_plane(0, three_copy)
        send_three()
        dense_copy = dense_grads()
        dense_copy.wait()

        def join(i, carry):
            dense_pair[core, i] = to_half(widen(dense_pair[core, i]) + widen(dense_half[i]))
            return carry

        lax.fori_loop(0, plan.chips, join, 0)
        dense = to_chips(
            links,
            dense_pair.at[core],
            dense_part,
            plane_send.at[4],
            plane_recv.at[4],
            by_step=True,
        )
        return three, dense, o_copies

    grad, _, _, (three_zero, dense_copies, o_zero) = attention(0, grad, x_ref[...], last_sums)
    input_grad_ref[...] = grad
    three_zero = three_line(0, three_zero)
    wait_all(returned)
    output_ref[...] = last_mid_ref[...] + as_column(gate_ref[...]) * dot_nn(
        place_tokens(plan, routes_ref),
        produced_in[...].reshape(plan.cycle * plan.slab, plan.model),
    )
    diagonals = []
    for head in range(plan.heads):
        total_rows = None
        for first in range(0, plan.rows, 8):
            moved = rotate(sums[head, first : first + 8, :], -first - 1)
            total_rows = moved if first == 0 else total_rows + moved
        diagonal = total_rows[0:1, :]
        for r in range(1, 8):
            diagonal = diagonal + rotate(total_rows, -r)[r : r + 1, :]
        diagonals.append(diagonal)
    table_grad = split_dot(jnp.concatenate(diagonals, axis=0), bucket_picks(128, buckets_ref), dot_nt)
    shape = (128, plan.model)
    bucket = lax.broadcasted_iota(jnp.int32, shape, 0)
    lane = lax.broadcasted_iota(jnp.int32, shape, 1)
    heads = plan.heads * plan.groups
    row = jnp.zeros((1, plan.model), jnp.float32)
    for head in range(plan.heads):
        places = (lane == bucket * heads + chip * plan.heads + head) & (lane < heads * table_ref.shape[1])
        row = row + split_dot(
            table_grad[head : head + 1, :], places.astype(jnp.float32).astype(jnp.bfloat16), dot_nn
        )
    small_mine[4:5, :] = row
    small_copy = started(
        remote(
            small_mine, small_half, chain_send.at[5, 0], chain_recv.at[5, 0], links.pair()
        )
    )

    small_copy.wait()
    small_sum[...] = small_mine[...] + small_half[...]
    small_copies = to_chips(
        links, small_sum, small_part, plane_send.at[5], plane_recv.at[5], by_step=True, whole=True
    )

    loads["cots"].wait()
    wait_all(rows_own)
    wait_all(rows_lines)
    slots = plan.copies * plan.cycle * plan.capacity
    stores = []
    for e in range(plan.experts):
        picked = slice(e * plan.capacity, (e + 1) * plan.capacity)
        rows = rows_all[:, :, picked, :].reshape(slots, plan.model)
        cots = cots_all[:, :, picked, :].reshape(slots, plan.model)
        loads["ein%d" % e].wait()
        loads["eout%d" % e].wait()
        for low in range(0, part, plan.wide):
            units = slice(e * part + low, e * part + low + plan.wide)
            pre = dot_nn(rows, up[:, units])
            active = to_half(smooth_act(pre))
            d_pre = to_half(dot_nt(cots, down[units, :]) * smooth_slope(pre))
            weights[e, :, low : low + plan.wide] = to_half(dot_tn(rows, d_pre))
            weights[plan.experts + e, low : low + plan.wide, :] = to_half(dot_tn(active, cots))
        stores.append(local(weights.at[e], ein_grad.at[e], own_sem.at[1 + 2 * e]))
        stores.append(
            local(weights.at[plan.experts + e], eout_grad.at[e], own_sem.at[2 + 2 * e])
        )
        if e == 0:
            wait_all(small_copies)
            value = small_sum[...]
            for step in range(1, plan.chips):
                value = value + small_part[step]
            small_row[...] = value
            small_copies = to_lines(
                links, small_row, small_in, line_send.at[6], line_recv.at[6], whole=True
            )

    wait_all(small_copies)
    value = small_row[...]
    for step in range(1, plan.copies):
        value = value + small_in[step]
    small_ref[...] = value
    three_finish(1, three_lines)
    o_finish(1, o_one)
    wait_all(dense_copies)
    value = widen(dense_pair[core, chip])
    for step in range(1, plan.chips):
        value = value + widen(dense_part[step])
    dense_ref[...] = value
    three_finish(0, three_zero)
    o_finish(0, o_zero)
    wait_all(stores)


def whole_backward(plan, values, caches, weights, dense, experts):
    f32, half = jnp.float32, jnp.bfloat16
    whole = pl.BlockSpec(memory_space=VMEM)
    hbm = pl.BlockSpec(memory_space=pl.ANY)
    dma = pltpu.SemaphoreType.DMA
    total = plan.groups * plan.rows
    model, share = plan.model, plan.share
    units = dense[0].shape[1]
    part = units // plan.copies
    slabs = (plan.cycle, plan.slab, model)
    window = (plan.rows, plan.wide)
    row = (plan.rows, model)
    height = 2 * part // plan.cycle
    o_rows, three_rows = -(-share // 16) * 16, -(-3 * share // 16) * 16
    small = (8, model)
    outs = [
        (row, f32),
        (row, f32),
        ((2, 3 * share, model), f32),
        ((2, share, model), f32),
        ((height, model), f32),
        (small, f32),
        ((plan.experts, model, part), half),
        ((plan.experts, part, model), half),
    ]
    chip_o = (plan.chips, plan.copies * share, model)
    chip_dense = (plan.chips, height, model)
    scratch = [
        (slabs, half),
        ((plan.chips, 2) + row, half),
        ((plan.cycle,) + window, half),
        ((plan.cycle,) + window, half),
        ((plan.groups,) + window, half),
        ((plan.groups,) + window, half),
        ((4, model, model), half),
        ((model, units), half),
        ((units, model), half),
        ((plan.copies,) + slabs, half),
        ((plan.copies,) + slabs, half),
        ((16, 2 * plan.length), f32),
        ((plan.heads, plan.rows, 2 * plan.length), f32),
        ((plan.heads, plan.rows, 2 * plan.length), f32),
        ((2, plan.groups) + window, half),
        ((2, plan.groups) + window, half),
        ((plan.wide, plan.length), half),
        ((plan.wide, total), f32),
        ((plan.heads, total, plan.wide), half),
        ((plan.heads, total, plan.wide), half),
        ((plan.cycle,) + window, half),
        ((plan.cycle,) + window, half),
        ((plan.chips, 2) + window, half),
        ((2, plan.chips, 2) + window, half),
        ((plan.chips, 2) + window, half),
        ((2, plan.groups, 2) + window, half),
        ((plan.wide, total), f32),
        ((2, plan.groups) + window, half),
        ((2, plan.groups) + window, half),
        (row, f32),
        ((max(model, 3 * plan.wide), model), f32),
        ((2,) + chip_o, half),
        (chip_o, half),
        ((2,) + chip_o, half),
        ((2, plan.copies, o_rows, model), half),
        ((2, plan.copies, o_rows, model), half),
        ((2, 3, plan.chips * share, model), half),
        ((2, 3, plan.chips * share, model), half),
        ((2, plan.chips, three_rows, model), half),
        ((2, plan.chips, three_rows, model), half),
        ((2, plan.copies, three_rows, model), half),
        ((plan.copies,) + row, half),
        ((2,) + chip_dense, half),
        (chip_dense, half),
        (chip_dense, half),
        (small, f32),
        (small, f32),
        (small, f32),
        ((plan.chips,) + small, f32),
        (small, f32),
        ((plan.copies,) + small, f32),
    ]
    chips, copies = plan.chips, plan.copies
    sems = [(28,), (2 * plan.experts + plan.copies,)]
    sems += [(2, chips)] * 8
    sems += [(6, 1)] * 2 + [(6, chips)] * 2 + [(8, copies)] * 2
    sems += [(plan.cycle,)] * 2
    return pl.pallas_call(
        functools.partial(whole_backward_kernel, plan),
        out_shape=tuple(jax.ShapeDtypeStruct(*out) for out in outs),
        in_specs=[whole] * len(values) + [hbm] * (len(caches) + 8),
        out_specs=(whole,) * (len(outs) - 2) + (hbm,) * 2,
        scratch_shapes=[VMEM(*one) for one in scratch] + [dma(one) for one in sems],
        compiler_params=pltpu.CompilerParams(
            collective_id=1, has_side_effects=True, vmem_limit_bytes=63 * 1024 * 1024
        ),
        name="whole_backward",
    )(*values, *caches, *weights, *dense, *experts)


def rms_backward(hidden, inv_rms, gains, d_normed):
    d_gains = jnp.sum(d_normed * hidden * inv_rms, axis=0)
    return (norm_slope(hidden, inv_rms, gains, d_normed), d_gains)


def body(
    inputs,
    w_query,
    w_key,
    w_value,
    w_out,
    norm_gain,
    bias_table,
    dense_in,
    dense_out,
    expert_in,
    expert_out,
    routes,
    gate_scale,
    buckets,
    cotangent,
):
    group_rows, model_width = inputs.shape
    head_count = bias_table.shape[1]
    plan = Plan(
        lax.axis_size("dp"),
        lax.axis_size(("ctx", "exp")),
        lax.axis_size("exp"),
        head_count,
        model_width // head_count,
        group_rows,
        expert_in.shape[0],
    )
    attention = (w_query, w_key, w_value, w_out)
    dense = (dense_in, dense_out)
    experts = (expert_in, expert_out)
    if not plan.fused:
        return separate_body(
            plan,
            inputs,
            attention,
            norm_gain,
            bias_table,
            dense,
            experts,
            routes,
            gate_scale,
            jnp.concatenate([buckets[:1], buckets[:0:-1]]),
            cotangent,
        )
    bucket_row, table = buckets[None], bias_table.T
    (
        last_mid,
        grad,
        last_gain,
        stream,
        mid,
        attended,
        log_norm,
        dense_normed,
        _,
        rows,
        produced,
        cots,
        rows_early,
        *kept,
    ) = whole_forward(
        plan,
        inputs,
        norm_gain,
        table,
        bucket_row,
        routes.T,
        gate_scale.T,
        cotangent,
        attention,
        dense,
        experts,
    )
    output, input_grad, three, out, dense_share, small, grad_ein, grad_eout = whole_backward(
        plan,
        (
            grad,
            stream,
            inputs,
            mid,
            norm_gain,
            last_gain,
            table,
            bucket_row,
            attended,
            log_norm,
            dense_normed,
            last_mid,
            produced,
            routes.T,
            gate_scale.T,
        ),
        (*kept, cots, rows, rows_early),
        attention,
        dense,
        experts,
    )
    share = plan.share
    place = lax.axis_index(("dp", "ctx", "exp"))
    three = jnp.transpose(three.reshape(2, 3, share, model_width), (1, 0, 3, 2))
    gains = lax.dynamic_slice_in_dim(small[:4], place * share, share, 1)
    bucket_count = bias_table.shape[0]
    table_share = bucket_count * head_count // (plan.copies * plan.cycle)
    table = lax.dynamic_slice_in_dim(small[4], place * table_share, table_share, 0)
    half_rows = dense_share.shape[0] // 2
    return (
        output,
        input_grad,
        three[0],
        three[1],
        three[2],
        jnp.transpose(out, (0, 2, 1)),
        gains,
        table,
        dense_share[:half_rows].T,
        dense_share[half_rows:],
        widen(grad_ein),
        widen(grad_eout),
    )


def separate_body(
    plan,
    inputs,
    attention,
    norm_gain,
    bias_table,
    dense,
    experts,
    routes,
    gate_scale,
    reversed_buckets,
    cotangent,
):
    group_rows, model_width = inputs.shape
    bucket_count, head_count = bias_table.shape
    dense_in, dense_out = dense
    expert_in, expert_out = experts
    cycle_size = plan.cycle
    my_group = lax.axis_index(("ctx", "exp")) // plan.splits
    bucket_hits = (
        reversed_buckets[None, :] == jnp.arange(bucket_count, dtype=jnp.int32)[:, None]
    ).astype(jnp.float32)
    my_table = lax.dynamic_slice_in_dim(bias_table.T, my_group * plan.heads, plan.heads, 0)
    bias_rows = jnp.dot(my_table, bucket_hits, precision=highest)
    local_experts = expert_in.shape[0]
    expert_total = local_experts * cycle_size
    capacity = 2 * group_rows // expert_total
    recv_rows = cycle_size * capacity
    flat_routes = routes[:, 0]
    route_hits = (
        flat_routes[:, None] == jnp.arange(expert_total, dtype=jnp.int32)[None, :]
    ).astype(jnp.int32)
    slot_order = jnp.sum((jnp.cumsum(route_hits, axis=0) - 1) * route_hits, axis=1)
    target = flat_routes * capacity + slot_order
    dispatch = (
        target[None, :] == jnp.arange(expert_total * capacity, dtype=jnp.int32)[:, None]
    ).astype(jnp.bfloat16)

    def to_owners(rows_half):
        placed = jnp.dot(dispatch, rows_half, preferred_element_type=jnp.float32)
        return lax.all_to_all(
            to_half(placed).reshape(cycle_size, local_experts, capacity, model_width),
            ("ctx", "exp"),
            split_axis=0,
            concat_axis=2,
            tiled=True,
        ).reshape(local_experts, recv_rows, model_width)

    def from_owners(produced):
        returned = lax.all_to_all(
            produced.reshape(1, local_experts, recv_rows, model_width),
            ("ctx", "exp"),
            split_axis=2,
            concat_axis=0,
            tiled=True,
        )
        return jnp.einsum(
            "sc,sd->cd",
            dispatch,
            returned.reshape(expert_total * capacity, model_width),
            preferred_element_type=jnp.float32,
        )

    mid_zero, *cache_zero = attention_forward(
        plan, 0, inputs, norm_gain, bias_rows, *attention, 0
    )
    inv_rms_one = lax.rsqrt(jnp.mean(mid_zero * mid_zero, axis=-1, keepdims=True) + epsilon)
    normed_half = to_half(mid_zero * inv_rms_one * norm_gain[1])
    pre_act = jnp.dot(normed_half, dense_in, preferred_element_type=jnp.float32)
    active = to_half(smooth_act(pre_act))
    stream = mid_zero + jnp.dot(active, dense_out, preferred_element_type=jnp.float32)
    mid_one, *cache_one = attention_forward(plan, 1, stream, norm_gain, bias_rows, *attention, 1)
    grad_rows = to_owners(to_half(gate_scale * cotangent))
    inv_rms_three = lax.rsqrt(jnp.mean(mid_one * mid_one, axis=-1, keepdims=True) + epsilon)
    rows = to_owners(to_half(mid_one * inv_rms_three * norm_gain[3]))
    expert_pre = jnp.einsum("erd,edf->erf", rows, expert_in, preferred_element_type=jnp.float32)
    expert_active = to_half(smooth_act(expert_pre))
    produced = to_half(
        jnp.einsum("erf,efd->erd", expert_active, expert_out, preferred_element_type=jnp.float32)
    )
    d_active = jnp.einsum("erd,efd->erf", grad_rows, expert_out, preferred_element_type=jnp.float32)
    expert_d_pre = to_half(d_active * smooth_slope(expert_pre))
    d_rows = to_half(
        jnp.einsum("erf,edf->erd", expert_d_pre, expert_in, preferred_element_type=jnp.float32)
    )
    output = mid_one + gate_scale * from_owners(produced)
    d_hidden, gains_four = rms_backward(mid_one, inv_rms_three, norm_gain[3], from_owners(d_rows))
    grad_three = cotangent + d_hidden

    grad_two, gains_three, attn_two, bias_two = attention_backward(
        plan, 1, grad_three, [stream] + cache_one, norm_gain, bias_rows, *attention, 2
    )
    grad_half = to_half(grad_two)
    d_active = jnp.dot(grad_half, dense_out.T, preferred_element_type=jnp.float32)
    d_pre = to_half(d_active * smooth_slope(pre_act))
    d_normed = jnp.dot(d_pre, dense_in.T, preferred_element_type=jnp.float32)
    d_hidden, gains_two = rms_backward(mid_zero, inv_rms_one, norm_gain[1], d_normed)
    input_grad, gains_one, attn_one, bias_one = attention_backward(
        plan, 0, grad_two + d_hidden, [inputs] + cache_zero, norm_gain, bias_rows, *attention, 3
    )

    my_table_grad = jnp.dot(bucket_hits, (bias_one + bias_two).T, precision=highest)
    table_grad = lax.dynamic_update_slice(
        jnp.zeros((bucket_count, head_count), jnp.float32),
        my_table_grad,
        (0, my_group * plan.heads),
    ).reshape(bucket_count * head_count)
    gains_all = jnp.stack([gains_one[0], gains_two, gains_three[0], gains_four])
    everyone = ("dp", "ctx", "exp")
    grad_dout = jnp.dot(active.T, grad_half, preferred_element_type=jnp.float32)
    grad_din = jnp.dot(normed_half.T, d_pre, preferred_element_type=jnp.float32)
    grad_ein = jnp.einsum("erd,erf->edf", rows, expert_d_pre, preferred_element_type=jnp.float32)
    grad_eout = jnp.einsum(
        "erf,erd->efd", expert_active, grad_rows, preferred_element_type=jnp.float32
    )
    grad_ein = lax.psum_scatter(to_half(grad_ein), "dp", scatter_dimension=2, tiled=True)
    grad_eout = lax.psum_scatter(to_half(grad_eout), "dp", scatter_dimension=1, tiled=True)
    attn = lax.psum_scatter(
        jnp.stack([attn_one, attn_two], axis=1), everyone, scatter_dimension=3, tiled=True
    ).astype(jnp.float32)
    gains = lax.psum_scatter(gains_all, everyone, scatter_dimension=1, tiled=True)
    table = lax.psum_scatter(table_grad, everyone, scatter_dimension=0, tiled=True)
    din = lax.psum_scatter(to_half(grad_din), everyone, scatter_dimension=1, tiled=True)
    dout = lax.psum_scatter(to_half(grad_dout), everyone, scatter_dimension=0, tiled=True)
    return (
        output,
        input_grad,
        attn[0],
        attn[1],
        attn[2],
        attn[3],
        gains,
        table,
        widen(din),
        widen(dout),
        widen(grad_ein),
        widen(grad_eout),
    )


def solution(mesh):
    in_specs = (
        P(("dp", "ctx", "exp"), None),
        P(),
        P(),
        P(),
        P(),
        P(),
        P(),
        P(),
        P(),
        P(("ctx", "exp"), None, None),
        P(("ctx", "exp"), None, None),
        P(("dp", "ctx", "exp"), None),
        P(("dp", "ctx", "exp"), None),
        P(),
        P(("dp", "ctx", "exp"), None),
    )
    out_specs = (
        P(("dp", "ctx", "exp"), None),
        P(("dp", "ctx", "exp"), None),
        P(None, None, ("dp", "ctx", "exp")),
        P(None, None, ("dp", "ctx", "exp")),
        P(None, None, ("dp", "ctx", "exp")),
        P(None, None, ("dp", "ctx", "exp")),
        P(None, ("dp", "ctx", "exp")),
        P(("dp", "ctx", "exp")),
        P(None, ("dp", "ctx", "exp")),
        P(("dp", "ctx", "exp"), None),
        P(("ctx", "exp"), None, "dp"),
        P(("ctx", "exp"), "dp", None),
    )
    return jax.shard_map(body, mesh=mesh, in_specs=in_specs, out_specs=out_specs, check_vma=False)
```

```python
import functools

import jax
import jax.numpy as jnp
from jax import lax
from jax.experimental import pallas as pl
from jax.experimental.pallas import tpu as pltpu
from jax.sharding import PartitionSpec as P

epsilon = 1e-06
highest = lax.Precision.HIGHEST
MESH = pl.DeviceIdType.MESH
VMEM = pltpu.VMEM


def to_half(values):
    return values.astype(jnp.bfloat16)


def widen(values):
    return values.astype(jnp.float32)


def dot_nn(a, b):
    return jnp.dot(a, b, preferred_element_type=jnp.float32)


def dot_nt(a, b):
    return lax.dot_general(a, b, (((1,), (1,)), ((), ())), preferred_element_type=jnp.float32)


def dot_tn(a, b):
    return lax.dot_general(a, b, (((0,), (0,)), ((), ())), preferred_element_type=jnp.float32)


def rotate(values, shift):
    width = values.shape[-1]
    shift = shift % width
    return values if shift == 0 else pltpu.roll(values, shift, values.ndim - 1)


def pad_lanes(values, width):
    if values.shape[1] == width:
        return values
    zeros = jnp.zeros((values.shape[0], width - values.shape[1]), values.dtype)
    return jnp.concatenate([values, zeros], axis=1)


class Plan:
    def __init__(self, copies, cycle, exp_size, head_count, head_size, rows, experts):
        self.copies, self.cycle, self.exp_size, self.rows = copies, cycle, exp_size, rows
        groups = 1
        while cycle % (groups * 2) == 0 and head_count % (groups * 2) == 0:
            groups *= 2
        self.groups, self.splits = groups, cycle // groups
        self.heads, self.head_size = head_count // groups, head_size
        self.width = self.heads * head_size
        self.model = head_count * head_size
        self.length = cycle * rows
        self.wide = -(-self.width // 128) * 128
        self.lead = self.wide - self.width
        self.pair = 2 * self.width
        self.tiled = self.heads if self.heads * rows * self.length * 8 <= 4 << 20 else 1
        self.chips = cycle // 2
        self.share = self.model // (copies * cycle)
        self.experts = experts
        self.capacity = 2 * rows // (experts * cycle)
        self.slab = experts * self.capacity
        self.early = cycle // 4
        self.fused = (
            self.splits == 2
            and self.groups == copies
            and self.capacity % 16 == 0
            and (copies * self.share) % 16 == 0
            and self.width * copies == self.model
            and self.width + self.width % 128 <= self.wide
        )
        assert self.pair % 128 == 0 and self.pair - self.wide == self.width - self.lead

    def window(self, group):
        return group * self.width // 128 * 128

    def place(self):
        c = lax.axis_index("ctx") * self.exp_size + lax.axis_index("exp")
        return c, c // self.splits, lax.rem(c, self.splits)

    def device(self, c):
        return (lax.axis_index("dp"), c // self.exp_size, lax.rem(c, self.exp_size))

    def peer(self, c, step):
        return lax.rem(c + step, self.cycle)

    def copy_device(self, c, other):
        return (other, c // self.exp_size, lax.rem(c, self.exp_size))


def greet(plan, c):
    barrier = pltpu.get_barrier_semaphore()
    for step in range(1, plan.cycle):
        pl.semaphore_signal(
            barrier, inc=1, device_id=plan.device(plan.peer(c, step)), device_id_type=MESH
        )
    me = lax.axis_index("dp")
    for step in range(1, plan.copies):
        other = lax.rem(me + step, plan.copies)
        pl.semaphore_signal(
            barrier, inc=1, device_id=plan.copy_device(c, other), device_id_type=MESH
        )
    return barrier


def await_greetings(plan, barrier):
    pl.semaphore_wait(barrier, plan.cycle - 1 + plan.copies - 1)


def start_along_dp(plan, c, source, target, own_sem, send, recv):
    me = lax.axis_index("dp")
    own = pltpu.make_async_copy(source, target.at[me], own_sem.at[0])
    own.start()
    copies = [own]
    for step in range(1, plan.copies):
        other = lax.rem(me + step, plan.copies)
        copy = remote(
            source, target.at[me], send.at[step], recv.at[step], plan.copy_device(c, other)
        )
        copy.start()
        copies.append(copy)
    return copies


def start_slabs(plan, c, source, target, send, recv):
    copies = []
    for step in range(1, plan.cycle):
        to = plan.peer(c, step)
        copy = remote(source.at[to], target.at[c], send.at[step], recv.at[step], plan.device(to))
        copy.start()
        copies.append(copy)
    target[c] = source[c]
    return copies


def rms_normed(hidden, gains):
    inv_rms = lax.rsqrt(jnp.mean(hidden * hidden, axis=-1, keepdims=True) + epsilon)
    return hidden * inv_rms * gains, inv_rms


def fill_bias(plan, rows_ref, tiles, heads):
    for head in heads:
        row = jnp.broadcast_to(rows_ref[head : head + 1, :], (plan.rows, 2 * plan.length))
        tiles[head % plan.tiled] = pltpu.roll(row, 0, 1, stride=1, stride_axis=0)


def bias_part(plan, tiles, head, key_block, split):
    parts = []
    head = head % plan.tiled
    for block in range(plan.groups):
        first = plan.length + (block * plan.splits + split - key_block) * plan.rows
        parts.append(tiles[head, :, pl.ds(pl.multiple_of(first, plan.rows), plan.rows)])
    return jnp.concatenate(parts, axis=1)


def lanes_between(shape, low, high):
    lane = lax.broadcasted_iota(jnp.int32, shape, 1)
    return (lane >= low) & (lane < high)


def natural(plan, blocks, lead):
    total = None
    for group, block in enumerate(blocks):
        moved = rotate(pad_lanes(block, plan.model), group * plan.width - lead)
        total = moved if total is None else total + moved
    return total


def remote(src, dst, send, recv, device):
    return pltpu.make_async_remote_copy(
        src_ref=src, dst_ref=dst, send_sem=send, recv_sem=recv, device_id=device, device_id_type=MESH
    )


def forward_kernel(
    plan,
    layer,
    x_ref,
    gain_ref,
    bias_ref,
    wq_hbm,
    wk_hbm,
    wv_hbm,
    wo_hbm,
    mid_ref,
    normed_ref,
    query_ref,
    pair_ref,
    heads_ref,
    attended_ref,
    norm_ref,
    weights,
    tiles,
    send_pair,
    send_query,
    scores,
    probs,
    att_in,
    load_sem,
    pair_send,
    pair_recv,
    query_send,
    query_recv,
    att_send,
    att_recv,
):
    c, group, split = plan.place()
    loads = []
    for slot, source in enumerate((wv_hbm, wk_hbm, wq_hbm, wo_hbm)):
        load = pltpu.make_async_copy(source.at[layer], weights.at[slot], load_sem.at[slot])
        load.start()
        loads.append(load)
    barrier = greet(plan, c)
    hidden = x_ref[...]
    normed, _ = rms_normed(hidden, gain_ref[layer * 2 : layer * 2 + 1, :])
    normed_half = to_half(normed)
    normed_ref[...] = normed_half
    loads[0].wait()
    values = dot_nn(normed_half, weights[0])
    loads[1].wait()
    keys = dot_nn(normed_half, weights[1])
    is_value = lanes_between((plan.rows, plan.pair), 0, plan.width)
    for g in range(plan.groups):
        value_part = rotate(values, -g * plan.width)[:, : plan.pair]
        key_part = rotate(keys, (1 - g) * plan.width)[:, : plan.pair]
        send_pair[g] = to_half(jnp.where(is_value, value_part, key_part))
    await_greetings(plan, barrier)
    copies = []
    for step in range(1, plan.cycle):
        to = plan.peer(c, step)
        copy = remote(
            send_pair.at[to // plan.splits],
            pair_ref.at[c],
            pair_send.at[step],
            pair_recv.at[step],
            plan.device(to),
        )
        copy.start()
        copies.append(copy)
    loads[2].wait()
    queries = dot_nn(normed_half, weights[2])
    is_query = lanes_between((plan.rows, plan.wide), plan.lead, plan.wide)
    for g in range(plan.groups):
        query_part = rotate(queries, plan.lead - g * plan.width)[:, : plan.wide]
        send_query[g] = to_half(jnp.where(is_query, query_part, 0.0))
    for step in range(1, plan.groups):
        to = plan.peer(c, step * plan.splits)
        copy = remote(
            send_query.at[to // plan.splits],
            query_ref.at[group],
            query_send.at[step],
            query_recv.at[step],
            plan.device(to),
        )
        copy.start()
        copies.append(copy)
    pair_ref[c] = send_pair[group]
    query_ref[group] = send_query[group]
    fill_bias(plan, bias_ref, tiles, range(plan.tiled))
    for copy in copies:
        copy.wait()

    total = plan.groups * plan.rows
    queries_all = query_ref[...].reshape(total, plan.wide)
    values_t = jnp.transpose(pair_ref[...].reshape(plan.length, plan.pair)[:, : plan.wide])
    rows_t = []
    for head in range(plan.heads):
        if head >= plan.tiled:
            fill_bias(plan, bias_ref, tiles, [head])
        low = plan.lead + head * plan.head_size
        picked = jnp.where(
            lanes_between(queries_all.shape, low, low + plan.head_size), queries_all, 0
        )

        def score_block(block, top):
            part = dot_nt(pair_ref[block][:, plan.pair - plan.wide :], picked)
            part = part + bias_part(plan, tiles, head, block, split)
            scores[pl.ds(pl.multiple_of(block * plan.rows, plan.rows), plan.rows), :] = part
            return jnp.maximum(top, jnp.max(part, axis=0, keepdims=True))

        top = lax.fori_loop(0, plan.cycle, score_block, jnp.full((1, total), -1e30, jnp.float32))

        def weight_block(block, norm):
            where = pl.ds(pl.multiple_of(block * plan.rows, plan.rows), plan.rows)
            part = jnp.exp(scores[where, :] - top)
            probs[where, :] = to_half(part)
            return norm + jnp.sum(part, axis=0, keepdims=True)

        norm = lax.fori_loop(0, plan.cycle, weight_block, jnp.zeros((1, total), jnp.float32))
        norm_ref[head : head + 1, :] = top + jnp.log(norm)
        mine = values_t[head * plan.head_size : (head + 1) * plan.head_size, :]
        rows_t.append(dot_nn(mine, probs[...]) / norm)
    rows_t.append(jnp.zeros((plan.lead, total), jnp.float32))
    heads_ref[...] = to_half(jnp.transpose(jnp.concatenate(rows_t, axis=0))).reshape(
        plan.groups, plan.rows, plan.wide
    )
    copies = []
    for step in range(1, plan.groups):
        to = plan.peer(c, step * plan.splits)
        copy = remote(
            heads_ref.at[to // plan.splits],
            att_in.at[group],
            att_send.at[step],
            att_recv.at[step],
            plan.device(to),
        )
        copy.start()
        copies.append(copy)
    att_in[group] = heads_ref[group]
    loads[3].wait()
    for copy in copies:
        copy.wait()
    attended = to_half(natural(plan, [widen(att_in[g]) for g in range(plan.groups)], 0))
    attended_ref[...] = attended
    mid_ref[...] = hidden + dot_nn(attended, weights[3])


def attention_forward(plan, layer, hidden, gains, bias_rows, wq, wk, wv, wo, collective):
    f32, half = jnp.float32, jnp.bfloat16
    total = plan.groups * plan.rows
    whole = pl.BlockSpec(memory_space=VMEM)
    hbm = pl.BlockSpec(memory_space=pl.ANY)
    dma = pltpu.SemaphoreType.DMA
    return pl.pallas_call(
        functools.partial(forward_kernel, plan, layer),
        out_shape=(
            jax.ShapeDtypeStruct((plan.rows, plan.model), f32),
            jax.ShapeDtypeStruct((plan.rows, plan.model), half),
            jax.ShapeDtypeStruct((plan.groups, plan.rows, plan.wide), half),
            jax.ShapeDtypeStruct((plan.cycle, plan.rows, plan.pair), half),
            jax.ShapeDtypeStruct((plan.groups, plan.rows, plan.wide), half),
            jax.ShapeDtypeStruct((plan.rows, plan.model), half),
            jax.ShapeDtypeStruct((plan.heads, total), f32),
        ),
        in_specs=[whole, whole, whole, hbm, hbm, hbm, hbm],
        out_specs=(whole,) * 7,
        scratch_shapes=[
            VMEM((4, plan.model, plan.model), half),
            VMEM((plan.tiled, plan.rows, 2 * plan.length), f32),
            VMEM((plan.groups, plan.rows, plan.pair), half),
            VMEM((plan.groups, plan.rows, plan.wide), half),
            VMEM((plan.length, total), f32),
            VMEM((plan.length, total), half),
            VMEM((plan.groups, plan.rows, plan.wide), half),
            dma((4,)),
            dma((plan.cycle,)),
            dma((plan.cycle,)),
            dma((plan.groups,)),
            dma((plan.groups,)),
            dma((plan.groups,)),
            dma((plan.groups,)),
        ],
        compiler_params=pltpu.CompilerParams(
            collective_id=collective, has_side_effects=True, vmem_limit_bytes=56 * 1024 * 1024
        ),
        name="attention_forward",
    )(hidden, gains, bias_rows, wq, wk, wv, wo)


def backward_kernel(
    plan,
    layer,
    grad_ref,
    x_ref,
    gain_ref,
    bias_ref,
    normed_ref,
    query_ref,
    pair_ref,
    heads_ref,
    attended_ref,
    norm_ref,
    wq_hbm,
    wk_hbm,
    wv_hbm,
    wo_hbm,
    out_ref,
    gain_grad_ref,
    weight_grad_ref,
    bias_grad_ref,
    weights,
    tiles,
    sums,
    send_grad,
    grad_in,
    probs,
    slopes,
    key_sum,
    value_sum,
    send_pair,
    pair_in,
    send_query,
    query_in,
    load_sem,
    grad_send,
    grad_recv,
    pair_send,
    pair_recv,
    query_send,
    query_recv,
):
    c, group, split = plan.place()
    total = plan.groups * plan.rows
    loads = []
    for slot, source in enumerate((wv_hbm, wk_hbm, wq_hbm, wo_hbm)):
        load = pltpu.make_async_copy(source.at[layer], weights.at[slot], load_sem.at[slot])
        loads.append(load)
    for slot in (3, 0, 1, 2):
        loads[slot].start()
    barrier = greet(plan, c)
    grad = grad_ref[...]
    grad_half = to_half(grad)
    loads[3].wait()
    d_attended = dot_nt(grad_half, weights[3])
    in_group = lanes_between((plan.rows, plan.wide), 0, plan.width)
    for g in range(plan.groups):
        part = rotate(d_attended, -g * plan.width)[:, : plan.wide]
        send_grad[g] = to_half(jnp.where(in_group, part, 0.0))
    await_greetings(plan, barrier)
    copies = []
    for step in range(1, plan.groups):
        to = plan.peer(c, step * plan.splits)
        copy = remote(
            send_grad.at[to // plan.splits],
            grad_in.at[group],
            grad_send.at[step],
            grad_recv.at[step],
            plan.device(to),
        )
        copy.start()
        copies.append(copy)
    grad_in[group] = send_grad[group]
    fill_bias(plan, bias_ref, tiles, range(plan.tiled))
    weight_grad_ref[3] = to_half(dot_tn(attended_ref[...], grad_half))
    queries_all = query_ref[...].reshape(total, plan.wide)
    keys_t = jnp.transpose(
        pair_ref[...].reshape(plan.length, plan.pair)[:, plan.pair - plan.wide :]
    )
    heads_t = jnp.transpose(widen(heads_ref[...].reshape(total, plan.wide)))
    for copy in copies:
        copy.wait()
    grads_all = grad_in[...].reshape(total, plan.wide)
    grads_t = jnp.transpose(widen(grads_all))
    products_t = grads_t * heads_t
    query_rows_t = [jnp.zeros((plan.lead, total), jnp.float32)]
    for head in range(plan.heads):
        if head >= plan.tiled:
            fill_bias(plan, bias_ref, tiles, [head])
        low, high = head * plan.head_size, (head + 1) * plan.head_size
        picked_queries = jnp.where(
            lanes_between(queries_all.shape, plan.lead + low, plan.lead + high), queries_all, 0
        )
        picked_grads = jnp.where(lanes_between(grads_all.shape, low, high), grads_all, 0)
        delta = jnp.sum(products_t[low:high, :], axis=0, keepdims=True)
        log_norm = norm_ref[head : head + 1, :]
        sums[...] = jnp.zeros_like(sums)

        def slope_block(block, carry):
            where = pl.ds(pl.multiple_of(block * plan.rows, plan.rows), plan.rows)
            part = dot_nt(pair_ref[block][:, plan.pair - plan.wide :], picked_queries)
            part = part + bias_part(plan, tiles, head, block, split)
            part = jnp.exp(part - log_norm)
            probs[where, :] = to_half(part)
            slope = part * (dot_nt(pair_ref[block][:, : plan.wide], picked_grads) - delta)
            slopes[where, :] = to_half(slope)
            for b in range(plan.groups):
                first = plan.length + (b * plan.splits + split - block) * plan.rows
                at = pl.ds(pl.multiple_of(first, plan.rows), plan.rows)
                sums[:, at] += slope[:, b * plan.rows : (b + 1) * plan.rows]
            return carry

        lax.fori_loop(0, plan.cycle, slope_block, 0)
        key_part = dot_nn(slopes[...], picked_queries)
        value_part = dot_nn(probs[...], picked_grads)
        if head == 0:
            key_sum[...], value_sum[...] = key_part, value_part
        else:
            key_sum[...] += key_part
            value_sum[...] += value_part
        query_rows_t.append(dot_nn(keys_t[plan.lead + low : plan.lead + high, :], slopes[...]))
        row = lax.broadcasted_iota(jnp.int32, (plan.rows, plan.rows), 0)
        column = lax.broadcasted_iota(jnp.int32, (plan.rows, plan.rows), 1)
        flip = (row + column == plan.rows - 1).astype(jnp.float32)
        flipped = jnp.dot(flip, sums[...], precision=highest, preferred_element_type=jnp.float32)
        skewed = pltpu.roll(
            flipped, 2 * plan.length - (plan.rows - 1), 1, stride=1, stride_axis=0
        )
        bias_grad_ref[head : head + 1, :] = jnp.sum(skewed, axis=0, keepdims=True)
    send_query[...] = to_half(jnp.transpose(jnp.concatenate(query_rows_t, axis=0))).reshape(
        plan.groups, plan.rows, plan.wide
    )
    value_all, key_all = value_sum[...], key_sum[...]
    low, gap = plan.pair - plan.wide, plan.wide - (plan.pair - plan.wide)
    middle = jnp.where(
        lanes_between((plan.length, gap), 0, plan.width - low), value_all[:, low:], key_all[:, :gap]
    )
    send_pair[...] = to_half(
        jnp.concatenate([value_all[:, :low], middle, key_all[:, gap:]], axis=1)
    ).reshape(plan.cycle, plan.rows, plan.pair)
    copies = []
    for step in range(1, plan.cycle):
        to = plan.peer(c, step)
        copy = remote(
            send_pair.at[to], pair_in.at[c], pair_send.at[step], pair_recv.at[step], plan.device(to)
        )
        copy.start()
        copies.append(copy)
    for step in range(1, plan.groups):
        to = plan.peer(c, step * plan.splits)
        copy = remote(
            send_query.at[to // plan.splits],
            query_in.at[group],
            query_send.at[step],
            query_recv.at[step],
            plan.device(to),
        )
        copy.start()
        copies.append(copy)
    pair_in[c] = send_pair[c]
    query_in[group] = send_query[group]
    hidden = x_ref[...]
    gains = gain_ref[layer * 2 : layer * 2 + 1, :]
    inv_rms = lax.rsqrt(jnp.mean(hidden * hidden, axis=-1, keepdims=True) + epsilon)
    for slot in range(3):
        loads[slot].wait()
    for copy in copies:
        copy.wait()
    is_value = lanes_between((plan.rows, plan.pair), 0, plan.width)
    value_blocks, key_blocks = [], []
    for g in range(plan.groups):
        block = widen(pair_in[g * plan.splits])
        for other in range(1, plan.splits):
            block = block + widen(pair_in[g * plan.splits + other])
        value_blocks.append(jnp.where(is_value, block, 0.0))
        key_blocks.append(jnp.where(is_value, 0.0, block))
    d_values = to_half(natural(plan, value_blocks, 0))
    d_keys = to_half(natural(plan, key_blocks, plan.width))
    d_queries = to_half(
        natural(plan, [widen(query_in[g]) for g in range(plan.groups)], plan.lead)
    )
    normed_half = normed_ref[...]
    d_normed = (
        dot_nt(d_queries, weights[2]) + dot_nt(d_keys, weights[1]) + dot_nt(d_values, weights[0])
    )
    weight_grad_ref[0] = to_half(dot_tn(normed_half, d_queries))
    weight_grad_ref[1] = to_half(dot_tn(normed_half, d_keys))
    weight_grad_ref[2] = to_half(dot_tn(normed_half, d_values))
    d_scaled = d_normed * gains
    gain_grad_ref[...] = jnp.sum(d_normed * hidden * inv_rms, axis=0, keepdims=True)
    out_ref[...] = (
        grad
        + inv_rms * d_scaled
        - hidden * (inv_rms * inv_rms * inv_rms) * jnp.mean(d_scaled * hidden, axis=-1, keepdims=True)
    )


def attention_backward(plan, layer, grad, cache, gains, bias_rows, wq, wk, wv, wo, collective):
    f32, half = jnp.float32, jnp.bfloat16
    total = plan.groups * plan.rows
    whole = pl.BlockSpec(memory_space=VMEM)
    hbm = pl.BlockSpec(memory_space=pl.ANY)
    dma = pltpu.SemaphoreType.DMA
    hidden, normed, query, pair, heads, attended, norm = cache
    block = (plan.groups, plan.rows, plan.wide)
    pairs = (plan.cycle, plan.rows, plan.pair)
    return pl.pallas_call(
        functools.partial(backward_kernel, plan, layer),
        out_shape=(
            jax.ShapeDtypeStruct((plan.rows, plan.model), f32),
            jax.ShapeDtypeStruct((1, plan.model), f32),
            jax.ShapeDtypeStruct((4, plan.model, plan.model), half),
            jax.ShapeDtypeStruct((plan.heads, 2 * plan.length), f32),
        ),
        in_specs=[whole] * 10 + [hbm] * 4,
        out_specs=(whole,) * 4,
        scratch_shapes=[
            VMEM((4, plan.model, plan.model), half),
            VMEM((plan.tiled, plan.rows, 2 * plan.length), f32),
            VMEM((plan.rows, 2 * plan.length), f32),
            VMEM(block, half),
            VMEM(block, half),
            VMEM((plan.length, total), half),
            VMEM((plan.length, total), half),
            VMEM((plan.length, plan.wide), f32),
            VMEM((plan.length, plan.wide), f32),
            VMEM(pairs, half),
            VMEM(pairs, half),
            VMEM(block, half),
            VMEM(block, half),
            dma((4,)),
            dma((plan.groups,)),
            dma((plan.groups,)),
            dma((plan.cycle,)),
            dma((plan.cycle,)),
            dma((plan.groups,)),
            dma((plan.groups,)),
        ],
        compiler_params=pltpu.CompilerParams(
            collective_id=collective, has_side_effects=True, vmem_limit_bytes=60 * 1024 * 1024
        ),
        name="attention_backward",
    )(grad, hidden, gains, bias_rows, normed, query, pair, heads, attended, norm, wq, wk, wv, wo)


def smooth_act(values):
    return values * jax.nn.sigmoid(values)


def smooth_slope(values):
    sigma = jax.nn.sigmoid(values)
    return sigma * (1.0 + values * (1.0 - sigma))


class Links:
    def __init__(self, plan):
        self.plan = plan
        self.c, self.chip, self.core = plan.place()
        self.me = lax.axis_index("dp")
        self.lead = pl.multiple_of(lax.rem(self.chip * plan.width, 128), 64)
        self.first = pl.multiple_of(self.chip * plan.width // 128 * 128, 128)

    def pair(self):
        return self.plan.device(self.c + 1 - 2 * self.core)

    def at_chip(self, step):
        return lax.rem(self.chip + step, self.plan.groups)

    def chip_device(self, step):
        return self.plan.device(2 * self.at_chip(step) + self.core)

    def at_dp(self, step):
        return lax.rem(self.me + step, self.plan.copies)

    def dp_device(self, step):
        return self.plan.copy_device(self.c, self.at_dp(step))

    def head_lanes(self, shape, head):
        low = self.lead + head * self.plan.head_size
        return lanes_between(shape, low, low + self.plan.head_size)

    def head_rows(self, head):
        return pl.ds(
            pl.multiple_of(self.lead + head * self.plan.head_size, self.plan.head_size),
            self.plan.head_size,
        )


def wait_all(copies):
    for copy in copies:
        copy.wait()


def local(source, target, sem):
    copy = pltpu.make_async_copy(source, target, sem)
    copy.start()
    return copy


def started(copy):
    copy.start()
    return copy


def to_lines(links, source, target, send, recv, whole=False):
    copies = []
    for step in range(1, links.plan.copies):
        part = source if whole else source.at[links.at_dp(step)]
        copies.append(
            started(
                remote(part, target.at[step], send.at[step], recv.at[step], links.dp_device(step))
            )
        )
    return copies


def to_all_dp(links, source, target, send, recv):
    return [
        started(
            remote(
                source, target.at[links.me], send.at[step], recv.at[step], links.dp_device(step)
            )
        )
        for step in range(1, links.plan.copies)
    ]


def to_chips(links, source, target, send, recv, by_step=False, whole=False):
    copies = []
    for step in range(1, links.plan.chips):
        part = source if whole else source.at[links.at_chip(step)]
        slot = step if by_step else links.chip
        copies.append(
            started(
                remote(
                    part, target.at[slot], send.at[step], recv.at[step], links.chip_device(step)
                )
            )
        )
    return copies


def add_windows(plan, total, blocks):
    total[...] = jnp.zeros_like(total)
    for group, block in enumerate(blocks):
        first = plan.window(group)
        total[:, first : first + plan.wide] += block
    return total[...]


def bucket_picks(count, buckets_ref):
    width = buckets_ref.shape[1]
    tiles = [buckets_ref[:, low : low + 128] for low in range(0, width, 128)]
    rows = jnp.concatenate(tiles, axis=0).astype(jnp.float32)
    square = (128, 128)
    row = lax.broadcasted_iota(jnp.int32, square, 0)
    column = lax.broadcasted_iota(jnp.int32, square, 1)
    flip = (row + column == 127).astype(jnp.bfloat16)
    rows = dot_nn(to_half(rows), flip)
    tiles = [rows[i : i + 1, :] for i in range(width // 128)][::-1]
    values = jnp.broadcast_to(jnp.concatenate(tiles, axis=1), (count, width))
    numbers = lax.broadcasted_iota(jnp.int32, (count, width), 0).astype(jnp.float32)
    return (values == numbers).astype(jnp.bfloat16)


def split_dot(exact, picks, dot):
    count = exact.shape[0]
    high = to_half(exact)
    rest = exact - widen(high)
    middle = to_half(rest)
    low = to_half(rest - widen(middle))
    parts = jnp.concatenate([widen(high), widen(middle), widen(low)], axis=0)
    result = dot(to_half(parts), picks)
    return result[:count] + (result[count : 2 * count] + result[2 * count :])


def fill_all_bias(plan, links, table_ref, buckets_ref, rows, tiles):
    rows[: table_ref.shape[0], :] = split_dot(
        table_ref[...], bucket_picks(table_ref.shape[1], buckets_ref), dot_nn
    )
    for head in range(plan.heads):
        row = rows[pl.ds(links.chip * plan.heads + head, 1), :]
        row = jnp.broadcast_to(row, (plan.rows, 2 * plan.length))
        tiles[head] = pltpu.roll(row, 1, 1, stride=1, stride_axis=0)


def as_column(row):
    count = row.shape[1]
    square = (count, count)
    same = lax.broadcasted_iota(jnp.int32, square, 0) == lax.broadcasted_iota(jnp.int32, square, 1)
    return jnp.sum(jnp.where(same, jnp.broadcast_to(row, square), 0.0), axis=1, keepdims=True)


def place_tokens(plan, routes_ref):
    total = plan.experts * plan.cycle
    shape = (plan.rows, total)
    routes = as_column(routes_ref[...].astype(jnp.float32))
    numbers = lax.broadcasted_iota(jnp.int32, shape, 1).astype(jnp.float32)
    hits = (routes == numbers).astype(jnp.float32)
    square = (plan.rows, plan.rows)
    row = lax.broadcasted_iota(jnp.int32, square, 0)
    column = lax.broadcasted_iota(jnp.int32, square, 1)
    earlier = (column < row).astype(jnp.bfloat16)
    before = dot_nn(earlier, to_half(hits))
    slot = jnp.sum((before + numbers * plan.capacity) * hits, axis=1, keepdims=True)
    slots = (plan.rows, total * plan.capacity)
    return (slot == lax.broadcasted_iota(jnp.int32, slots, 1).astype(jnp.float32)).astype(
        jnp.bfloat16
    )


def whole_forward_kernel(
    plan,
    x_ref,
    gain_ref,
    table_ref,
    buckets_ref,
    routes_ref,
    gate_ref,
    cot_ref,
    wq_hbm,
    wk_hbm,
    wv_hbm,
    wo_hbm,
    din_hbm,
    dout_hbm,
    ein_hbm,
    eout_hbm,
    last_mid_ref,
    grad_ref,
    gain_grad_ref,
    stream_ref,
    mid_ref,
    attended_ref,
    norm_ref,
    dense_normed,
    cots_in,
    rows_in,
    produced,
    cots_hbm,
    rows_early,
    normed_out,
    key_out,
    value_out,
    query_out,
    heads_out,
    normed_all,
    key_all,
    value_all,
    query_all,
    heads_all,
    wq,
    wk,
    wv,
    wo,
    up,
    down,
    bias_rows,
    tiles,
    value_t,
    scores,
    probs,
    heads_t,
    att_in,
    natural_sum,
    cots_out,
    rows_out,
    d_active,
    d_rows,
    d_rows_in,
    load_sem,
    near_send,
    near_recv,
    far_send,
    far_recv,
    att_send,
    att_recv,
    cots_send,
    cots_recv,
    rows_send,
    rows_recv,
    d_rows_send,
    d_rows_recv,
    line_send,
    line_recv,
    own_sem,
    keep_sem,
):
    links = Links(plan)
    c, chip, core = links.c, links.chip, links.core
    columns = pl.ds(links.first, plan.wide)
    loads = {}

    def load(name, source, target):
        loads[name] = local(source, target, load_sem.at[len(loads)])

    for layer in range(2):
        for name, source, target in (("k", wk_hbm, wk), ("v", wv_hbm, wv), ("q", wq_hbm, wq)):
            load((name, layer), source.at[layer, :, columns], target.at[layer])
        load(("o", layer), wo_hbm.at[layer], wo.at[layer])
        if layer == 0:
            load("din", din_hbm, up.at[0])
            load("dout", dout_hbm, down.at[0])
    load("eout1", eout_hbm.at[1], down.at[1])
    load("ein1", ein_hbm.at[1], up.at[1])
    barrier = greet(plan, c)
    placed = place_tokens(plan, routes_ref)
    gate = as_column(gate_ref[...])
    total = plan.groups * plan.rows
    done_later, lines = [], []

    def project(layer, block, with_query):
        normed = normed_all[layer, block // 2, lax.rem(block, 2)]
        key_all[layer, block] = to_half(dot_nn(normed, wk[layer]))
        value_all[layer, block] = to_half(dot_nn(normed, wv[layer]))
        if with_query:
            query_all[layer, block // 2] = to_half(dot_nn(normed, wq[layer]))

    def attention(layer, hidden):
        normed, _ = rms_normed(hidden, gain_ref[layer * 2 : layer * 2 + 1, :])
        normed_all[layer, chip, core] = to_half(normed)
        if layer == 0:
            cots = gate * cot_ref[...]
            cots_out[...] = to_half(dot_tn(placed, to_half(cots))).reshape(cots_out.shape)
            await_greetings(plan, barrier)
            done_later.extend(start_slabs(plan, c, cots_out, cots_in, cots_send, cots_recv))
        own = normed_all.at[layer, chip, core]
        far = []
        for step in range(1, plan.chips):
            far.append(
                started(
                    remote(
                        own,
                        own,
                        far_send.at[layer, step],
                        far_recv.at[layer, step],
                        links.chip_device(step),
                    )
                )
            )
        near = [
            started(
                remote(own, own, near_send.at[layer, 0], near_recv.at[layer, 0], links.pair())
            )
        ]
        for name in ("k", "v", "q"):
            loads[(name, layer)].wait()
        project(layer, c, True)
        if layer == 0:
            fill_all_bias(plan, links, table_ref, buckets_ref, bias_rows, tiles)
        near[0].wait_recv()
        project(layer, 2 * chip + 1 - core, False)
        if layer == 0:
            wait_all(done_later)
            lines.extend(to_all_dp(links, cots_in, cots_hbm, line_send.at[0], line_recv.at[0]))
            lines.append(local(cots_in, cots_hbm.at[links.me], own_sem.at[0]))
        for step in range(1, plan.chips):
            far[step - 1].wait_recv()
            from_chip = lax.rem(chip + plan.chips - step, plan.chips)
            block = normed_all.at[layer, from_chip, core]
            near.append(
                started(
                    remote(
                        block,
                        block,
                        near_send.at[layer, step],
                        near_recv.at[layer, step],
                        links.pair(),
                    )
                )
            )
            project(layer, 2 * from_chip + core, True)
        blocks = []
        for step in range(1, plan.chips):
            near[step].wait_recv()
            from_chip = lax.rem(chip + plan.chips - step, plan.chips)
            blocks.append((2 * from_chip + 1 - core, normed_all[layer, from_chip, 1 - core]))
        normed = jnp.concatenate([values for _, values in blocks], axis=0)
        keys = to_half(dot_nn(normed, wk[layer]))
        values = to_half(dot_nn(normed, wv[layer]))
        for slot, (block, _) in enumerate(blocks):
            rows = slice(slot * plan.rows, (slot + 1) * plan.rows)
            key_all[layer, block] = keys[rows, :]
            value_all[layer, block] = values[rows, :]
        for copy in far + near:
            copy.wait_send()

        queries = query_all[layer].reshape(total, plan.wide)
        value_t[...] = jnp.transpose(value_all[layer].reshape(plan.length, plan.wide))
        heads_t[...] = jnp.zeros_like(heads_t)
        for head in range(plan.heads):
            picked = jnp.where(links.head_lanes(queries.shape, head), queries, 0)

            top = jnp.full((1, total), -1e30, jnp.float32)
            many = plan.cycle // 2
            for first in range(0, plan.cycle, many):
                keys = key_all[layer, first : first + many].reshape(many * plan.rows, plan.wide)
                part = dot_nt(keys, picked)
                for block in range(many):
                    piece = part[block * plan.rows : (block + 1) * plan.rows, :]
                    piece = piece + bias_part(plan, tiles, head, first + block, core)
                    low = (first + block) * plan.rows
                    scores[low : low + plan.rows, :] = piece
                    top = jnp.maximum(top, jnp.max(piece, axis=0, keepdims=True))

            norm = jnp.zeros((1, total), jnp.float32)
            for block in range(plan.cycle):
                where = slice(block * plan.rows, (block + 1) * plan.rows)
                part = jnp.exp(scores[where, :] - top)
                probs[where, :] = to_half(part)
                norm = norm + jnp.sum(part, axis=0, keepdims=True)
            norm_ref[layer, head : head + 1, :] = top + jnp.log(norm)
            mine = links.head_rows(head)
            heads_t[mine, :] = dot_nn(value_t[mine, :], probs[...]) / norm
        heads_all[layer] = to_half(jnp.transpose(heads_t[...])).reshape(
            plan.groups, plan.rows, plan.wide
        )
        copies = to_chips(
            links, heads_all.at[layer], att_in.at[layer], att_send.at[layer], att_recv.at[layer]
        )
        for slot, (kept, out) in enumerate(
            (
                (normed_all, normed_out),
                (key_all, key_out),
                (value_all, value_out),
                (query_all, query_out),
                (heads_all, heads_out),
            )
        ):
            lines.append(local(kept.at[layer], out.at[layer], keep_sem.at[layer, slot]))
        att_in[layer, chip] = heads_all[layer, chip]
        loads[("o", layer)].wait()
        wait_all(copies)
        attended = to_half(
            add_windows(plan, natural_sum, [widen(att_in[layer, g]) for g in range(plan.groups)])
        )
        attended_ref[layer] = attended
        return hidden + dot_nn(attended, wo[layer])

    mid = attention(0, x_ref[...])
    mid_ref[...] = mid
    normed, _ = rms_normed(mid, gain_ref[1:2, :])
    normed_half = to_half(normed)
    dense_normed[links.me] = normed_half
    mine = dense_normed.at[links.me]
    lines += to_all_dp(links, mine, dense_normed, line_send.at[1], line_recv.at[1])
    loads["din"].wait()
    active = to_half(smooth_act(dot_nn(normed_half, up[0])))
    loads["dout"].wait()
    stream = mid + dot_nn(active, down[0])
    stream_ref[...] = stream
    load("eout0", eout_hbm.at[0], down.at[0])
    load("ein0", ein_hbm.at[0], up.at[0])
    mid = attention(1, stream)
    last_mid_ref[...] = mid

    gains = gain_ref[3:4, :]
    normed, inv_rms = rms_normed(mid, gains)
    rows_out[...] = to_half(dot_tn(placed, to_half(normed))).reshape(rows_out.shape)
    copies = start_slabs(plan, c, rows_out, rows_in, rows_send, rows_recv)
    count = plan.cycle * plan.capacity

    def of_expert(ref, e):
        return ref[:, e * plan.capacity : (e + 1) * plan.capacity, :].reshape(count, plan.model)

    for e in range(plan.experts):
        loads["eout%d" % e].wait()
        d_active[e] = dot_nt(of_expert(cots_in, e), down[e])
        loads["ein%d" % e].wait()
    wait_all(copies)
    early = rows_in.at[: plan.early]
    lines += to_all_dp(links, early, rows_early, line_send.at[2], line_recv.at[2])
    actives = []
    for e in range(plan.experts):
        pre = dot_nn(of_expert(rows_in, e), up[e])
        actives.append(to_half(smooth_act(pre)))
        d_pre = to_half(d_active[e] * smooth_slope(pre))
        d_rows[:, e * plan.capacity : (e + 1) * plan.capacity, :] = to_half(
            dot_nt(d_pre, up[e])
        ).reshape(plan.cycle, plan.capacity, plan.model)
    d_row_copies = start_slabs(plan, c, d_rows, d_rows_in, d_rows_send, d_rows_recv)
    for e in range(plan.experts):
        produced[:, e * plan.capacity : (e + 1) * plan.capacity, :] = to_half(
            dot_nn(actives[e], down[e])
        ).reshape(plan.cycle, plan.capacity, plan.model)
    wait_all(d_row_copies)
    slots = plan.cycle * plan.slab
    d_normed = dot_nn(placed, d_rows_in[...].reshape(slots, plan.model))
    gain_grad_ref[...] = jnp.sum(d_normed * mid * inv_rms, axis=0, keepdims=True)
    grad_ref[...] = cot_ref[...] + norm_slope(mid, inv_rms, gains, d_normed)
    wait_all(lines)


def norm_slope(hidden, inv_rms, gains, d_normed):
    d_scaled = d_normed * gains
    mean = jnp.mean(d_scaled * hidden, axis=-1, keepdims=True)
    return inv_rms * d_scaled - hidden * (inv_rms * inv_rms * inv_rms) * mean


def whole_forward(plan, x, gains, table, buckets, routes, gate, cot, weights, dense, experts):
    f32, half = jnp.float32, jnp.bfloat16
    whole = pl.BlockSpec(memory_space=VMEM)
    hbm = pl.BlockSpec(memory_space=pl.ANY)
    dma = pltpu.SemaphoreType.DMA
    total = plan.groups * plan.rows
    units = dense[0].shape[1]
    slabs = (plan.cycle, plan.slab, plan.model)
    window = (plan.rows, plan.wide)
    row = (plan.rows, plan.model)
    outs = [
        (row, f32),
        (row, f32),
        ((1, plan.model), f32),
        (row, f32),
        (row, f32),
        ((2,) + row, half),
        ((2, plan.heads, total), f32),
        ((plan.copies,) + row, half),
        (slabs, half),
        (slabs, half),
        (slabs, half),
        ((plan.copies,) + slabs, half),
        ((plan.copies, plan.early) + slabs[1:], half),
    ]
    kept = [
        ((2, plan.chips, 2) + row, half),
        ((2, plan.cycle) + window, half),
        ((2, plan.cycle) + window, half),
        ((2, plan.groups) + window, half),
        ((2, plan.groups) + window, half),
    ]
    outs += kept
    cycle_sems = [dma((plan.cycle,))] * 2
    return pl.pallas_call(
        functools.partial(whole_forward_kernel, plan),
        out_shape=tuple(jax.ShapeDtypeStruct(*out) for out in outs),
        in_specs=[whole] * 7 + [hbm] * 8,
        out_specs=(whole,) * 11 + (hbm,) * 7,
        scratch_shapes=[VMEM(*one) for one in kept]
        + [
            VMEM((2, plan.model, plan.wide), half),
            VMEM((2, plan.model, plan.wide), half),
            VMEM((2, plan.model, plan.wide), half),
            VMEM((2, plan.model, plan.model), half),
            VMEM((2, plan.model, units), half),
            VMEM((2, units, plan.model), half),
            VMEM((16, 2 * plan.length), f32),
            VMEM((plan.heads, plan.rows, 2 * plan.length), f32),
            VMEM((plan.wide, plan.length), half),
            VMEM((plan.length, total), f32),
            VMEM((plan.length, total), half),
            VMEM((plan.wide, total), f32),
            VMEM((2, plan.groups) + window, half),
            VMEM(row, f32),
            VMEM(slabs, half),
            VMEM(slabs, half),
            VMEM((plan.experts, plan.cycle * plan.capacity, units), f32),
            VMEM(slabs, half),
            VMEM(slabs, half),
            dma((14,)),
            dma((2, plan.chips)),
            dma((2, plan.chips)),
            dma((2, plan.chips)),
            dma((2, plan.chips)),
            dma((2, plan.chips)),
            dma((2, plan.chips)),
        ]
        + cycle_sems * 3
        + [dma((3, plan.copies)), dma((3, plan.copies)), dma((1,)), dma((2, len(kept)))],
        compiler_params=pltpu.CompilerParams(
            collective_id=0, has_side_effects=True, vmem_limit_bytes=60 * 1024 * 1024
        ),
        name="whole_forward",
    )(x, gains, table, buckets, routes, gate, cot, *weights, *dense, *experts)


def whole_backward_kernel(
    plan,
    grad_ref,
    stream_ref,
    x_ref,
    mid_ref,
    gain_ref,
    last_gain_ref,
    table_ref,
    buckets_ref,
    attended_ref,
    norm_ref,
    normed_z,
    last_mid_ref,
    produced_ref,
    routes_ref,
    gate_ref,
    normed_hbm,
    key_hbm,
    value_hbm,
    query_hbm,
    heads_hbm,
    cots_hbm,
    rows_hbm,
    early_hbm,
    wq_hbm,
    wk_hbm,
    wv_hbm,
    wo_hbm,
    din_hbm,
    dout_hbm,
    ein_hbm,
    eout_hbm,
    output_ref,
    input_grad_ref,
    three_ref,
    out_ref,
    dense_ref,
    small_ref,
    ein_grad,
    eout_grad,
    produced_in,
    normed_all,
    key_all,
    value_all,
    query_all,
    heads_all,
    weights,
    up,
    down,
    cots_all,
    rows_all,
    bias_rows,
    tiles,
    sums,
    grad_out,
    grad_in,
    key_t,
    products,
    picked_queries,
    picked_grads,
    key_part,
    value_part,
    pair_out,
    pair_in,
    own_out,
    own_in,
    query_t,
    query_out,
    query_in,
    natural_sum,
    stage,
    o_half,
    o_sum,
    o_part,
    o_row,
    o_in,
    three_pair,
    three_half,
    three_sum,
    three_part,
    three_in,
    grads_z,
    dense_pair,
    dense_half,
    dense_part,
    small_mine,
    small_half,
    small_sum,
    small_part,
    small_row,
    small_in,
    load_sem,
    own_sem,
    grad_send,
    grad_recv,
    pair_send,
    pair_recv,
    back_send,
    back_recv,
    query_send,
    query_recv,
    chain_send,
    chain_recv,
    plane_send,
    plane_recv,
    line_send,
    line_recv,
    produced_send,
    produced_recv,
):
    links = Links(plan)
    c, chip, core, me = links.c, links.chip, links.core, links.me
    loads = {}

    def load(name, source, target):
        loads[name] = local(source, target, load_sem.at[len(loads)])

    def load_layer(layer):
        for name, source, target in (
            ("query", query_hbm, query_all),
            ("key", key_hbm, key_all),
            ("value", value_hbm, value_all),
            ("heads", heads_hbm, heads_all),
            ("normed", normed_hbm, normed_all),
        ):
            load((name, layer), source.at[layer], target)

    part = up.shape[1] // plan.copies
    mine = pl.ds(pl.multiple_of(me * part, part), part)
    load(("o", 1), wo_hbm.at[1], weights.at[3])
    load_layer(1)
    for slot, name, source in ((0, "v", wv_hbm), (1, "k", wk_hbm), (2, "q", wq_hbm)):
        load((name, 1), source.at[1], weights.at[slot])
    load("up", din_hbm, up)
    load("down", dout_hbm, down)
    load("cots", cots_hbm, cots_all)
    rows_own = [local(rows_hbm, rows_all.at[me], own_sem.at[0])]
    for step in range(1, plan.copies):
        other = links.at_dp(step)
        target = rows_all.at[other, : plan.early]
        rows_own.append(
            local(early_hbm.at[other], target, own_sem.at[2 * plan.experts + step])
        )

    barrier = greet(plan, c)
    total = plan.groups * plan.rows
    rows_lines, returned = [], []
    share = plan.share

    def send_rows(sems, first, last):
        for step in range(1, plan.copies):
            rows_lines.append(
                started(
                    remote(
                        rows_hbm.at[first:last],
                        rows_all.at[me, first:last],
                        line_send.at[sems, step],
                        line_recv.at[sems, step],
                        links.dp_device(step),
                    )
                )
            )

    def o_start(layer, grad_half):
        stage[: plan.model, :] = dot_tn(grad_half, attended_ref[layer])

        def one(i, carry):
            side, to = lax.rem(i, 2), i // 2
            pieces = []
            for d in range(plan.copies):
                first = (d * plan.cycle + i) * share
                pieces.append(stage[pl.ds(pl.multiple_of(first, 8), share), :])
            dense_pair[side, to, : plan.copies * share, :] = to_half(jnp.concatenate(pieces, axis=0))
            return carry

        lax.fori_loop(0, plan.cycle, one, 0)
        return started(
            remote(
                dense_pair.at[1 - core, :, : plan.copies * share, :],
                o_half.at[layer],
                chain_send.at[layer, 0],
                chain_recv.at[layer, 0],
                links.pair(),
            )
        )

    def o_plane(layer, copy):
        copy.wait()
        o_sum[layer] = to_half(
            widen(dense_pair[core, :, : plan.copies * share, :]) + widen(o_half[layer])
        )
        return to_chips(
            links,
            o_sum.at[layer],
            o_part.at[layer],
            plane_send.at[layer],
            plane_recv.at[layer],
            by_step=True,
        )

    def o_line(layer, copies):
        wait_all(copies)
        value = widen(o_sum[layer, chip])
        for step in range(1, plan.chips):
            value = value + widen(o_part[layer, step])
        pad = jnp.zeros((o_row.shape[2] - share, plan.model), jnp.float32)
        for d in range(plan.copies):
            piece = jnp.concatenate([value[d * share : (d + 1) * share, :], pad], axis=0)
            o_row[layer, d] = to_half(piece)
        return to_lines(
            links, o_row.at[layer], o_in.at[layer], line_send.at[layer], line_recv.at[layer]
        )

    def o_finish(layer, copies):
        wait_all(copies)
        value = widen(o_row[layer, me])
        for step in range(1, plan.copies):
            value = value + widen(o_in[layer, step])
        out_ref[layer] = value[:share, :]

    def three_start(layer):
        normed = normed_all[...].reshape(plan.length, plan.model)
        own_normed = normed_all[:, core].reshape(total, plan.model)
        stage[: plan.wide, :] = dot_tn(query_out[layer].reshape(total, plan.wide), own_normed)
        stage[plan.wide : 2 * plan.wide, :] = dot_tn(key_part[...].reshape(plan.length, plan.wide), normed)
        stage[2 * plan.wide : 3 * plan.wide, :] = dot_tn(value_part[...].reshape(plan.length, plan.wide), normed)
        for side in range(2):
            for slot in range(3):
                pieces = []
                for to in range(plan.chips):
                    first = slot * plan.wide + links.lead + (2 * to + side) * share
                    pieces.append(stage[pl.ds(pl.multiple_of(first, 8), share), :])
                three_pair[side, slot] = to_half(jnp.concatenate(pieces, axis=0))
        return started(
            remote(
                three_pair.at[1 - core],
                three_half.at[layer],
                chain_send.at[2 + layer, 0],
                chain_recv.at[2 + layer, 0],
                links.pair(),
            )
        )

    def three_plane(layer, copy):
        copy.wait()
        both = []
        for slot in range(3):
            both.append(widen(three_pair[core, slot]) + widen(three_half[layer, slot]))
        pad = jnp.zeros((three_sum.shape[2] - 3 * share, plan.model), jnp.float32)
        for to in range(plan.chips):
            pieces = [value[to * share : (to + 1) * share, :] for value in both]
            three_sum[layer, to] = to_half(jnp.concatenate(pieces + [pad], axis=0))
        three_part[layer, chip] = three_sum[layer, chip]
        return to_chips(
            links,
            three_sum.at[layer],
            three_part.at[layer],
            plane_send.at[2 + layer],
            plane_recv.at[2 + layer],
        )

    def three_line(layer, copies):
        wait_all(copies)
        return to_lines(
            links,
            three_part.at[layer],
            three_in.at[layer],
            line_send.at[2 + layer],
            line_recv.at[2 + layer],
        )

    def three_finish(layer, copies):
        wait_all(copies)
        value = widen(three_part[layer, me])
        for step in range(1, plan.copies):
            value = value + widen(three_in[layer, step])
        three_ref[layer] = value[: 3 * share, :]

    def attention(layer, grad, hidden, waiting, between):
        grad_half = to_half(grad)
        loads[("o", layer)].wait()
        d_attended = dot_nt(grad_half, weights[3])
        for g in range(plan.groups):
            first = plan.window(g)
            grad_out[layer, g] = to_half(d_attended[:, first : first + plan.wide])
        if layer == 1:
            await_greetings(plan, barrier)
            load(("o", 0), wo_hbm.at[0], weights.at[3])
        copies = to_chips(
            links, grad_out.at[layer], grad_in.at[layer], grad_send.at[layer], grad_recv.at[layer]
        )
        grad_in[layer, chip] = grad_out[layer, chip]
        if layer == 1:
            send_rows(5, plan.early, plan.cycle - 1)
        o_copy = o_start(layer, grad_half)
        waiting()
        if layer == 1:
            fill_all_bias(plan, links, table_ref, buckets_ref, bias_rows, tiles)
            sums[...] = jnp.zeros_like(sums)
        for name in ("query", "key", "heads", "value"):
            loads[(name, layer)].wait()
        queries = query_all[...].reshape(total, plan.wide)
        for head in range(plan.heads):
            picked_queries[head] = jnp.where(links.head_lanes(queries.shape, head), queries, 0)
        query_t[...] = jnp.zeros_like(query_t)
        key_t[...] = jnp.transpose(key_all[...].reshape(plan.length, plan.wide))
        products[...] = jnp.transpose(widen(heads_all[...].reshape(total, plan.wide)))
        wait_all(copies)
        if layer == 0:
            o_copies = o_plane(layer, o_copy)
        if layer == 1:
            returned.extend(
                start_slabs(plan, c, produced_ref, produced_in, produced_send, produced_recv)
            )
        grads = grad_in[layer].reshape(total, plan.wide)
        for head in range(plan.heads):
            picked_grads[head] = jnp.where(links.head_lanes(grads.shape, head), grads, 0)
        products[...] = products[...] * jnp.transpose(widen(grads))
        delta = [
            jnp.sum(products[links.head_rows(head), :], axis=0, keepdims=True)
            for head in range(plan.heads)
        ]
        log_norm = [norm_ref[layer, head : head + 1, :] for head in range(plan.heads)]

        def process(blocks):
            keys = jnp.concatenate([key_all[block] for block in blocks], axis=0)
            values = jnp.concatenate([value_all[block] for block in blocks], axis=0)
            d_keys = d_values = None
            for head in range(plan.heads):
                bias = [bias_part(plan, tiles, head, block, core) for block in blocks]
                part = dot_nt(keys, picked_queries[head]) + jnp.concatenate(bias, axis=0)
                part = jnp.exp(part - log_norm[head])
                slope = part * (dot_nt(values, picked_grads[head]) - delta[head])
                for slot, block in enumerate(blocks):
                    rows = slice(slot * plan.rows, (slot + 1) * plan.rows)
                    for b in range(plan.groups):
                        first = plan.length + (b * plan.splits + core - block) * plan.rows
                        at = pl.ds(pl.multiple_of(first, plan.rows), plan.rows)
                        sums[head, :, at] += slope[rows, b * plan.rows : (b + 1) * plan.rows]
                slope = to_half(slope)
                keys_t = [
                    key_t[
                        links.head_rows(head),
                        pl.ds(pl.multiple_of(block * plan.rows, plan.rows), plan.rows),
                    ]
                    for block in blocks
                ]
                query_t[links.head_rows(head), :] += dot_nn(
                    jnp.concatenate(keys_t, axis=1), slope
                )
                key_piece = dot_nn(slope, picked_queries[head])
                value_piece = dot_nn(to_half(part), picked_grads[head])
                d_keys = key_piece if head == 0 else d_keys + key_piece
                d_values = value_piece if head == 0 else d_values + value_piece
            for slot, block in enumerate(blocks):
                rows = slice(slot * plan.rows, (slot + 1) * plan.rows)
                key_part[block] = to_half(d_keys[rows, :])
                value_part[block] = to_half(d_values[rows, :])
            return d_keys, d_values

        def pair_copy(step):
            return remote(
                pair_out.at[step],
                pair_in.at[layer, step],
                pair_send.at[layer, step],
                pair_recv.at[layer, step],
                links.pair(),
            )

        steps = [(i + 1) % plan.chips for i in range(plan.chips)]
        d_keys, d_values = process([2 * links.at_chip(step) + 1 - core for step in steps])
        for slot, step in enumerate(steps):
            rows = slice(slot * plan.rows, (slot + 1) * plan.rows)
            pair_out[step, 0] = to_half(d_keys[rows, :])
            pair_out[step, 1] = to_half(d_values[rows, :])
            pair_copy(step).start()

        def back_copy(step):
            return remote(
                own_out.at[step],
                own_in.at[layer, chip],
                back_send.at[layer, step],
                back_recv.at[layer, step],
                links.chip_device(step),
            )

        d_keys, d_values = process([2 * links.at_chip(step) + core for step in steps])
        for slot, step in enumerate(steps):
            rows = slice(slot * plan.rows, (slot + 1) * plan.rows)
            pair_copy(step).wait_recv()
            own_out[step, 0] = to_half(d_keys[rows, :] + widen(pair_in[layer, step, 0]))
            own_out[step, 1] = to_half(d_values[rows, :] + widen(pair_in[layer, step, 1]))
            if step > 0:
                back_copy(step).start()
        own_in[layer, chip] = own_out[0]
        query_out[layer] = to_half(jnp.transpose(query_t[...])).reshape(
            plan.groups, plan.rows, plan.wide
        )
        copies = to_chips(
            links,
            query_out.at[layer],
            query_in.at[layer],
            query_send.at[layer],
            query_recv.at[layer],
        )
        query_in[layer, chip] = query_out[layer, chip]
        loads[("normed", layer)].wait()
        three_copy = three_start(layer)
        if layer == 1:
            o_copies = None
        between_result = between(three_copy, o_copies)
        inv_rms = lax.rsqrt(jnp.mean(hidden * hidden, axis=-1, keepdims=True) + epsilon)
        for name in ("v", "k", "q"):
            loads[(name, layer)].wait()
        wait_all(copies)
        for step in range(1, plan.chips):
            back_copy(step).wait()
        for step in range(plan.chips):
            pair_copy(step).wait_send()
        if layer == 1:
            o_copies = o_plane(layer, o_copy)
        groups = range(plan.groups)
        d_queries = to_half(
            add_windows(plan, natural_sum, [widen(query_in[layer, g]) for g in groups])
        )
        d_keys = to_half(
            add_windows(plan, natural_sum, [widen(own_in[layer, g, 0]) for g in groups])
        )
        d_values = to_half(
            add_windows(plan, natural_sum, [widen(own_in[layer, g, 1]) for g in groups])
        )
        d_normed = (
            dot_nt(d_queries, weights[2])
            + dot_nt(d_keys, weights[1])
            + dot_nt(d_values, weights[0])
        )
        if layer == 1:
            load_layer(0)
            for slot, name, source in ((0, "v", wv_hbm), (1, "k", wk_hbm), (2, "q", wq_hbm)):
                load((name, 0), source.at[0], weights.at[slot])
        gains = gain_ref[2 * layer : 2 * layer + 1, :]
        small_mine[2 * layer : 2 * layer + 1, :] = jnp.sum(
            d_normed * hidden * inv_rms, axis=0, keepdims=True
        )
        result = grad + norm_slope(hidden, inv_rms, gains, d_normed)
        return result, o_copies, three_copy, between_result

    small_mine[...] = jnp.zeros_like(small_mine)
    small_mine[3:4, :] = last_gain_ref[...]
    grad, o_one, three_one, _ = attention(
        1, grad_ref[...], stream_ref[...], lambda: None, lambda *_: None
    )

    grad_half = to_half(grad)
    grads_z[me] = grad_half
    grad_lines = to_all_dp(links, grads_z.at[me], grads_z, line_send.at[4], line_recv.at[4])
    send_rows(7, plan.cycle - 1, plan.cycle)
    mid = mid_ref[...]
    gains = gain_ref[1:2, :]
    normed, inv_rms = rms_normed(mid, gains)
    loads["up"].wait()
    loads["down"].wait()
    normed_half = to_half(normed)
    d_normed = jnp.zeros_like(normed)
    for slot in range(plan.copies):
        units = slice(slot * part, (slot + 1) * part)
        pre = dot_nn(normed_half, up[:, units])
        d_pre = to_half(dot_nt(grad_half, down[units, :]) * smooth_slope(pre))
        d_normed = d_normed + dot_nt(d_pre, up[:, units])
    pieces = [slice(slot * part, (slot + 1) * part) for slot in range(plan.experts + 1)]
    for e in range(plan.experts):
        load("ein%d" % e, ein_hbm.at[e, :, mine], up.at[:, pieces[e]])
        load("eout%d" % e, eout_hbm.at[e, mine, :], down.at[pieces[e], :])
    load("din", din_hbm.at[:, mine], up.at[:, pieces[-1]])
    load("dout", dout_hbm.at[mine, :], down.at[pieces[-1], :])
    small_mine[1:2, :] = jnp.sum(d_normed * mid * inv_rms, axis=0, keepdims=True)
    grad = grad + norm_slope(mid, inv_rms, gains, d_normed)

    three_lines, one_lines = [], []

    def send_one():
        one_lines.append(three_plane(1, three_one))

    def send_three():
        three_lines.extend(three_line(1, one_lines[0]))

    def dense_grads():
        wait_all(grad_lines)
        count = plan.copies * plan.rows
        normed = normed_z[...].reshape(count, plan.model)
        grads = grads_z[...].reshape(count, plan.model)
        loads["din"].wait()
        loads["dout"].wait()
        height = part // plan.cycle
        some = part // plan.chips
        for to in range(plan.chips):
            units = slice(pieces[-1].start + to * some, pieces[-1].start + (to + 1) * some)
            pre = dot_nn(normed, up[:, units])
            active = to_half(smooth_act(pre))
            d_pre = to_half(dot_nt(grads, down[units, :]) * smooth_slope(pre))
            in_grad = to_half(dot_tn(d_pre, normed))
            out_grad = to_half(dot_tn(active, grads))
            for side in range(2):
                rows = slice(side * height, (side + 1) * height)
                dense_pair[side, to, :height, :] = in_grad[rows, :]
                dense_pair[side, to, height:, :] = out_grad[rows, :]
        return started(
            remote(
                dense_pair.at[1 - core],
                dense_half,
                chain_send.at[4, 0],
                chain_recv.at[4, 0],
                links.pair(),
            )
        )

    def last_sums(three_copy, o_copies):
        one_lines.append(o_line(1, o_one))
        o_copies = o_line(0, o_copies)
        three = three_plane(0, three_copy)
        send_three()
        dense_copy = dense_grads()
        dense_copy.wait()

        def join(i, carry):
            dense_pair[core, i] = to_half(widen(dense_pair[core, i]) + widen(dense_half[i]))
            return carry

        lax.fori_loop(0, plan.chips, join, 0)
        dense = to_chips(
            links,
            dense_pair.at[core],
            dense_part,
            plane_send.at[4],
            plane_recv.at[4],
            by_step=True,
        )
        return three, dense, o_copies

    grad, _, _, (three_zero, dense_copies, o_zero) = attention(
        0, grad, x_ref[...], send_one, last_sums
    )
    input_grad_ref[...] = grad
    three_zero = three_line(0, three_zero)
    wait_all(returned)
    output_ref[...] = last_mid_ref[...] + as_column(gate_ref[...]) * dot_nn(
        place_tokens(plan, routes_ref),
        produced_in[...].reshape(plan.cycle * plan.slab, plan.model),
    )
    diagonals = []
    for head in range(plan.heads):
        total_rows = None
        for first in range(0, plan.rows, 8):
            moved = rotate(sums[head, first : first + 8, :], -first - 1)
            total_rows = moved if first == 0 else total_rows + moved
        diagonal = total_rows[0:1, :]
        for r in range(1, 8):
            diagonal = diagonal + rotate(total_rows, -r)[r : r + 1, :]
        diagonals.append(diagonal)
    table_grad = split_dot(jnp.concatenate(diagonals, axis=0), bucket_picks(128, buckets_ref), dot_nt)
    shape = (128, plan.model)
    bucket = lax.broadcasted_iota(jnp.int32, shape, 0)
    lane = lax.broadcasted_iota(jnp.int32, shape, 1)
    heads = plan.heads * plan.groups
    row = jnp.zeros((1, plan.model), jnp.float32)
    for head in range(plan.heads):
        places = (lane == bucket * heads + chip * plan.heads + head) & (lane < heads * table_ref.shape[1])
        row = row + split_dot(
            table_grad[head : head + 1, :], places.astype(jnp.float32).astype(jnp.bfloat16), dot_nn
        )
    small_mine[4:5, :] = row
    small_copy = started(
        remote(
            small_mine, small_half, chain_send.at[5, 0], chain_recv.at[5, 0], links.pair()
        )
    )

    small_copy.wait()
    small_sum[...] = small_mine[...] + small_half[...]
    small_copies = to_chips(
        links, small_sum, small_part, plane_send.at[5], plane_recv.at[5], by_step=True, whole=True
    )

    loads["cots"].wait()
    wait_all(rows_own)
    wait_all(rows_lines)
    slots = plan.copies * plan.cycle * plan.capacity
    stores = []
    for e in range(plan.experts):
        picked = slice(e * plan.capacity, (e + 1) * plan.capacity)
        rows = rows_all[:, :, picked, :].reshape(slots, plan.model)
        cots = cots_all[:, :, picked, :].reshape(slots, plan.model)
        loads["ein%d" % e].wait()
        loads["eout%d" % e].wait()
        for low in range(0, part, plan.wide):
            units = slice(e * part + low, e * part + low + plan.wide)
            pre = dot_nn(rows, up[:, units])
            active = to_half(smooth_act(pre))
            d_pre = to_half(dot_nt(cots, down[units, :]) * smooth_slope(pre))
            weights[e, :, low : low + plan.wide] = to_half(dot_tn(rows, d_pre))
            weights[plan.experts + e, low : low + plan.wide, :] = to_half(dot_tn(active, cots))
        stores.append(local(weights.at[e], ein_grad.at[e], own_sem.at[1 + 2 * e]))
        stores.append(
            local(weights.at[plan.experts + e], eout_grad.at[e], own_sem.at[2 + 2 * e])
        )
        if e == 0:
            wait_all(small_copies)
            value = small_sum[...]
            for step in range(1, plan.chips):
                value = value + small_part[step]
            small_row[...] = value
            small_copies = to_lines(
                links, small_row, small_in, line_send.at[6], line_recv.at[6], whole=True
            )

    wait_all(small_copies)
    value = small_row[...]
    for step in range(1, plan.copies):
        value = value + small_in[step]
    small_ref[...] = value
    three_finish(1, three_lines)
    o_finish(1, one_lines[1])
    wait_all(dense_copies)
    value = widen(dense_pair[core, chip])
    for step in range(1, plan.chips):
        value = value + widen(dense_part[step])
    dense_ref[...] = value
    three_finish(0, three_zero)
    o_finish(0, o_zero)
    wait_all(stores)


def whole_backward(plan, values, caches, weights, dense, experts):
    f32, half = jnp.float32, jnp.bfloat16
    whole = pl.BlockSpec(memory_space=VMEM)
    hbm = pl.BlockSpec(memory_space=pl.ANY)
    dma = pltpu.SemaphoreType.DMA
    total = plan.groups * plan.rows
    model, share = plan.model, plan.share
    units = dense[0].shape[1]
    part = units // plan.copies
    slabs = (plan.cycle, plan.slab, model)
    window = (plan.rows, plan.wide)
    row = (plan.rows, model)
    height = 2 * part // plan.cycle
    o_rows, three_rows = -(-share // 16) * 16, -(-3 * share // 16) * 16
    small = (8, model)
    outs = [
        (row, f32),
        (row, f32),
        ((2, 3 * share, model), f32),
        ((2, share, model), f32),
        ((height, model), f32),
        (small, f32),
        ((plan.experts, model, part), half),
        ((plan.experts, part, model), half),
    ]
    chip_o = (plan.chips, plan.copies * share, model)
    chip_dense = (plan.chips, height, model)
    scratch = [
        (slabs, half),
        ((plan.chips, 2) + row, half),
        ((plan.cycle,) + window, half),
        ((plan.cycle,) + window, half),
        ((plan.groups,) + window, half),
        ((plan.groups,) + window, half),
        ((4, model, model), half),
        ((model, units), half),
        ((units, model), half),
        ((plan.copies,) + slabs, half),
        ((plan.copies,) + slabs, half),
        ((16, 2 * plan.length), f32),
        ((plan.heads, plan.rows, 2 * plan.length), f32),
        ((plan.heads, plan.rows, 2 * plan.length), f32),
        ((2, plan.groups) + window, half),
        ((2, plan.groups) + window, half),
        ((plan.wide, plan.length), half),
        ((plan.wide, total), f32),
        ((plan.heads, total, plan.wide), half),
        ((plan.heads, total, plan.wide), half),
        ((plan.cycle,) + window, half),
        ((plan.cycle,) + window, half),
        ((plan.chips, 2) + window, half),
        ((2, plan.chips, 2) + window, half),
        ((plan.chips, 2) + window, half),
        ((2, plan.groups, 2) + window, half),
        ((plan.wide, total), f32),
        ((2, plan.groups) + window, half),
        ((2, plan.groups) + window, half),
        (row, f32),
        ((max(model, 3 * plan.wide), model), f32),
        ((2,) + chip_o, half),
        ((2,) + chip_o, half),
        ((2,) + chip_o, half),
        ((2, plan.copies, o_rows, model), half),
        ((2, plan.copies, o_rows, model), half),
        ((2, 3, plan.chips * share, model), half),
        ((2, 3, plan.chips * share, model), half),
        ((2, plan.chips, three_rows, model), half),
        ((2, plan.chips, three_rows, model), half),
        ((2, plan.copies, three_rows, model), half),
        ((plan.copies,) + row, half),
        ((2,) + chip_dense, half),
        (chip_dense, half),
        (chip_dense, half),
        (small, f32),
        (small, f32),
        (small, f32),
        ((plan.chips,) + small, f32),
        (small, f32),
        ((plan.copies,) + small, f32),
    ]
    chips, copies = plan.chips, plan.copies
    sems = [(28,), (2 * plan.experts + plan.copies,)]
    sems += [(2, chips)] * 8
    sems += [(6, 1)] * 2 + [(6, chips)] * 2 + [(8, copies)] * 2
    sems += [(plan.cycle,)] * 2
    return pl.pallas_call(
        functools.partial(whole_backward_kernel, plan),
        out_shape=tuple(jax.ShapeDtypeStruct(*out) for out in outs),
        in_specs=[whole] * len(values) + [hbm] * (len(caches) + 8),
        out_specs=(whole,) * (len(outs) - 2) + (hbm,) * 2,
        scratch_shapes=[VMEM(*one) for one in scratch] + [dma(one) for one in sems],
        compiler_params=pltpu.CompilerParams(
            collective_id=1, has_side_effects=True, vmem_limit_bytes=63 * 1024 * 1024
        ),
        name="whole_backward",
    )(*values, *caches, *weights, *dense, *experts)


def rms_backward(hidden, inv_rms, gains, d_normed):
    d_gains = jnp.sum(d_normed * hidden * inv_rms, axis=0)
    return (norm_slope(hidden, inv_rms, gains, d_normed), d_gains)


def body(
    inputs,
    w_query,
    w_key,
    w_value,
    w_out,
    norm_gain,
    bias_table,
    dense_in,
    dense_out,
    expert_in,
    expert_out,
    routes,
    gate_scale,
    buckets,
    cotangent,
):
    group_rows, model_width = inputs.shape
    head_count = bias_table.shape[1]
    plan = Plan(
        lax.axis_size("dp"),
        lax.axis_size(("ctx", "exp")),
        lax.axis_size("exp"),
        head_count,
        model_width // head_count,
        group_rows,
        expert_in.shape[0],
    )
    attention = (w_query, w_key, w_value, w_out)
    dense = (dense_in, dense_out)
    experts = (expert_in, expert_out)
    if not plan.fused:
        return separate_body(
            plan,
            inputs,
            attention,
            norm_gain,
            bias_table,
            dense,
            experts,
            routes,
            gate_scale,
            jnp.concatenate([buckets[:1], buckets[:0:-1]]),
            cotangent,
        )
    bucket_row, table = buckets[None], bias_table.T
    (
        last_mid,
        grad,
        last_gain,
        stream,
        mid,
        attended,
        log_norm,
        dense_normed,
        _,
        rows,
        produced,
        cots,
        rows_early,
        *kept,
    ) = whole_forward(
        plan,
        inputs,
        norm_gain,
        table,
        bucket_row,
        routes.T,
        gate_scale.T,
        cotangent,
        attention,
        dense,
        experts,
    )
    output, input_grad, three, out, dense_share, small, grad_ein, grad_eout = whole_backward(
        plan,
        (
            grad,
            stream,
            inputs,
            mid,
            norm_gain,
            last_gain,
            table,
            bucket_row,
            attended,
            log_norm,
            dense_normed,
            last_mid,
            produced,
            routes.T,
            gate_scale.T,
        ),
        (*kept, cots, rows, rows_early),
        attention,
        dense,
        experts,
    )
    share = plan.share
    place = lax.axis_index(("dp", "ctx", "exp"))
    three = jnp.transpose(three.reshape(2, 3, share, model_width), (1, 0, 3, 2))
    gains = lax.dynamic_slice_in_dim(small[:4], place * share, share, 1)
    bucket_count = bias_table.shape[0]
    table_share = bucket_count * head_count // (plan.copies * plan.cycle)
    table = lax.dynamic_slice_in_dim(small[4], place * table_share, table_share, 0)
    half_rows = dense_share.shape[0] // 2
    return (
        output,
        input_grad,
        three[0],
        three[1],
        three[2],
        jnp.transpose(out, (0, 2, 1)),
        gains,
        table,
        dense_share[:half_rows].T,
        dense_share[half_rows:],
        widen(grad_ein),
        widen(grad_eout),
    )


def separate_body(
    plan,
    inputs,
    attention,
    norm_gain,
    bias_table,
    dense,
    experts,
    routes,
    gate_scale,
    reversed_buckets,
    cotangent,
):
    group_rows, model_width = inputs.shape
    bucket_count, head_count = bias_table.shape
    dense_in, dense_out = dense
    expert_in, expert_out = experts
    cycle_size = plan.cycle
    my_group = lax.axis_index(("ctx", "exp")) // plan.splits
    bucket_hits = (
        reversed_buckets[None, :] == jnp.arange(bucket_count, dtype=jnp.int32)[:, None]
    ).astype(jnp.float32)
    my_table = lax.dynamic_slice_in_dim(bias_table.T, my_group * plan.heads, plan.heads, 0)
    bias_rows = jnp.dot(my_table, bucket_hits, precision=highest)
    local_experts = expert_in.shape[0]
    expert_total = local_experts * cycle_size
    capacity = 2 * group_rows // expert_total
    recv_rows = cycle_size * capacity
    flat_routes = routes[:, 0]
    route_hits = (
        flat_routes[:, None] == jnp.arange(expert_total, dtype=jnp.int32)[None, :]
    ).astype(jnp.int32)
    slot_order = jnp.sum((jnp.cumsum(route_hits, axis=0) - 1) * route_hits, axis=1)
    target = flat_routes * capacity + slot_order
    dispatch = (
        target[None, :] == jnp.arange(expert_total * capacity, dtype=jnp.int32)[:, None]
    ).astype(jnp.bfloat16)

    def to_owners(rows_half):
        placed = jnp.dot(dispatch, rows_half, preferred_element_type=jnp.float32)
        return lax.all_to_all(
            to_half(placed).reshape(cycle_size, local_experts, capacity, model_width),
            ("ctx", "exp"),
            split_axis=0,
            concat_axis=2,
            tiled=True,
        ).reshape(local_experts, recv_rows, model_width)

    def from_owners(produced):
        returned = lax.all_to_all(
            produced.reshape(1, local_experts, recv_rows, model_width),
            ("ctx", "exp"),
            split_axis=2,
            concat_axis=0,
            tiled=True,
        )
        return jnp.einsum(
            "sc,sd->cd",
            dispatch,
            returned.reshape(expert_total * capacity, model_width),
            preferred_element_type=jnp.float32,
        )

    mid_zero, *cache_zero = attention_forward(
        plan, 0, inputs, norm_gain, bias_rows, *attention, 0
    )
    inv_rms_one = lax.rsqrt(jnp.mean(mid_zero * mid_zero, axis=-1, keepdims=True) + epsilon)
    normed_half = to_half(mid_zero * inv_rms_one * norm_gain[1])
    pre_act = jnp.dot(normed_half, dense_in, preferred_element_type=jnp.float32)
    active = to_half(smooth_act(pre_act))
    stream = mid_zero + jnp.dot(active, dense_out, preferred_element_type=jnp.float32)
    mid_one, *cache_one = attention_forward(plan, 1, stream, norm_gain, bias_rows, *attention, 1)
    grad_rows = to_owners(to_half(gate_scale * cotangent))
    inv_rms_three = lax.rsqrt(jnp.mean(mid_one * mid_one, axis=-1, keepdims=True) + epsilon)
    rows = to_owners(to_half(mid_one * inv_rms_three * norm_gain[3]))
    expert_pre = jnp.einsum("erd,edf->erf", rows, expert_in, preferred_element_type=jnp.float32)
    expert_active = to_half(smooth_act(expert_pre))
    produced = to_half(
        jnp.einsum("erf,efd->erd", expert_active, expert_out, preferred_element_type=jnp.float32)
    )
    d_active = jnp.einsum("erd,efd->erf", grad_rows, expert_out, preferred_element_type=jnp.float32)
    expert_d_pre = to_half(d_active * smooth_slope(expert_pre))
    d_rows = to_half(
        jnp.einsum("erf,edf->erd", expert_d_pre, expert_in, preferred_element_type=jnp.float32)
    )
    output = mid_one + gate_scale * from_owners(produced)
    d_hidden, gains_four = rms_backward(mid_one, inv_rms_three, norm_gain[3], from_owners(d_rows))
    grad_three = cotangent + d_hidden

    grad_two, gains_three, attn_two, bias_two = attention_backward(
        plan, 1, grad_three, [stream] + cache_one, norm_gain, bias_rows, *attention, 2
    )
    grad_half = to_half(grad_two)
    d_active = jnp.dot(grad_half, dense_out.T, preferred_element_type=jnp.float32)
    d_pre = to_half(d_active * smooth_slope(pre_act))
    d_normed = jnp.dot(d_pre, dense_in.T, preferred_element_type=jnp.float32)
    d_hidden, gains_two = rms_backward(mid_zero, inv_rms_one, norm_gain[1], d_normed)
    input_grad, gains_one, attn_one, bias_one = attention_backward(
        plan, 0, grad_two + d_hidden, [inputs] + cache_zero, norm_gain, bias_rows, *attention, 3
    )

    my_table_grad = jnp.dot(bucket_hits, (bias_one + bias_two).T, precision=highest)
    table_grad = lax.dynamic_update_slice(
        jnp.zeros((bucket_count, head_count), jnp.float32),
        my_table_grad,
        (0, my_group * plan.heads),
    ).reshape(bucket_count * head_count)
    gains_all = jnp.stack([gains_one[0], gains_two, gains_three[0], gains_four])
    everyone = ("dp", "ctx", "exp")
    grad_dout = jnp.dot(active.T, grad_half, preferred_element_type=jnp.float32)
    grad_din = jnp.dot(normed_half.T, d_pre, preferred_element_type=jnp.float32)
    grad_ein = jnp.einsum("erd,erf->edf", rows, expert_d_pre, preferred_element_type=jnp.float32)
    grad_eout = jnp.einsum(
        "erf,erd->efd", expert_active, grad_rows, preferred_element_type=jnp.float32
    )
    grad_ein = lax.psum_scatter(to_half(grad_ein), "dp", scatter_dimension=2, tiled=True)
    grad_eout = lax.psum_scatter(to_half(grad_eout), "dp", scatter_dimension=1, tiled=True)
    attn = lax.psum_scatter(
        jnp.stack([attn_one, attn_two], axis=1), everyone, scatter_dimension=3, tiled=True
    ).astype(jnp.float32)
    gains = lax.psum_scatter(gains_all, everyone, scatter_dimension=1, tiled=True)
    table = lax.psum_scatter(table_grad, everyone, scatter_dimension=0, tiled=True)
    din = lax.psum_scatter(to_half(grad_din), everyone, scatter_dimension=1, tiled=True)
    dout = lax.psum_scatter(to_half(grad_dout), everyone, scatter_dimension=0, tiled=True)
    return (
        output,
        input_grad,
        attn[0],
        attn[1],
        attn[2],
        attn[3],
        gains,
        table,
        widen(din),
        widen(dout),
        widen(grad_ein),
        widen(grad_eout),
    )


def solution(mesh):
    in_specs = (
        P(("dp", "ctx", "exp"), None),
        P(),
        P(),
        P(),
        P(),
        P(),
        P(),
        P(),
        P(),
        P(("ctx", "exp"), None, None),
        P(("ctx", "exp"), None, None),
        P(("dp", "ctx", "exp"), None),
        P(("dp", "ctx", "exp"), None),
        P(),
        P(("dp", "ctx", "exp"), None),
    )
    out_specs = (
        P(("dp", "ctx", "exp"), None),
        P(("dp", "ctx", "exp"), None),
        P(None, None, ("dp", "ctx", "exp")),
        P(None, None, ("dp", "ctx", "exp")),
        P(None, None, ("dp", "ctx", "exp")),
        P(None, None, ("dp", "ctx", "exp")),
        P(None, ("dp", "ctx", "exp")),
        P(("dp", "ctx", "exp")),
        P(None, ("dp", "ctx", "exp")),
        P(("dp", "ctx", "exp"), None),
        P(("ctx", "exp"), None, "dp"),
        P(("ctx", "exp"), "dp", None),
    )
    return jax.shard_map(body, mesh=mesh, in_specs=in_specs, out_specs=out_specs, check_vma=False)
```
